32 devices in a mesh: expert: 4 (over z), ctx: 4 (over y, x), dp: 2 (over core).
Axes of the slice: x: 2, y: 2, z: 4, core: 2. Of those that a mesh axis runs over, the one named last changes fastest.
Arguments:
- x_in: bfloat16 [64, 256, 512], P(('expert', 'dp'), 'ctx'), may hold values from -6 to 6
- d_out: bfloat16 [64, 256, 512], P(('expert', 'dp'), 'ctx'), may hold values from -6 to 6
- key_mask: int32 [64, 256], P(('expert', 'dp'), 'ctx'), may hold values from 0 to 1, as said below
- expert_ids: int32 [64, 256, 2], P(('expert', 'dp'), 'ctx'), may hold values from 0 to 3, all different within a row; in each aligned block of 64 rows (0 to 63, 64 to 127, ..., all dimensions but the last counted through in order) at most 40 rows name the same one
- norm_params: float32 [4, 512], replicated, as said below
- w_qkv: bfloat16 [512, 1536], replicated, as said below
- w_proj: bfloat16 [512, 512], replicated, as said below
- w_router: float32 [512, 4], replicated, may hold values from -0.1875 to 0.1875
- w_in: bfloat16 [4, 512, 2048], P('expert', None, 'ctx'), as said below
- w_out: bfloat16 [4, 512, 2048], P('expert', None, 'ctx'), as said below
- mom_norm: float32 [4, 512], P(None, 'ctx'), as said below
- mom_router: float32 [512, 4], P(None, 'ctx'), as said below
- mom_qkv: float32 [512, 1536], P(None, 'ctx'), as said below
- mom_proj: float32 [512, 512], P(None, 'ctx'), as said below
- mom_in: float32 [4, 512, 2048], P('expert', None, 'ctx'), as said below
- mom_out: float32 [4, 512, 2048], P('expert', None, 'ctx'), as said below
Outputs:
- block_out: bfloat16 [64, 256, 512], P(('expert', 'dp'), 'ctx')
- d_x: float32 [64, 256, 512], P(('expert', 'dp'), 'ctx')
- g_norm: float32 [4, 512], P(None, 'ctx')
- g_router: float32 [512, 4], P(None, 'ctx')
- g_qkv: float32 [512, 1536], P(None, 'ctx')
- g_proj: float32 [512, 512], P(None, 'ctx')
- g_in: float32 [4, 512, 2048], P('expert', None, 'ctx')
- g_out: float32 [4, 512, 2048], P('expert', None, 'ctx')
- m_norm: float32 [4, 512], P(None, 'ctx')
- m_router: float32 [512, 4], P(None, 'ctx')
- m_qkv: float32 [512, 1536], P(None, 'ctx')
- m_proj: float32 [512, 512], P(None, 'ctx')
- m_in: float32 [4, 512, 2048], P('expert', None, 'ctx')
- m_out: float32 [4, 512, 2048], P('expert', None, 'ctx')
- n_norm: float32 [4, 512], P(None, 'ctx')
- n_router: float32 [512, 4], P(None, 'ctx')
- n_qkv: float32 [512, 1536], P(None, 'ctx')
- n_proj: float32 [512, 512], P(None, 'ctx')
- n_in: float32 [4, 512, 2048], P('expert', None, 'ctx')
- n_out: float32 [4, 512, 2048], P('expert', None, 'ctx')
- b_qkv: bfloat16 [512, 1536], P(None, 'ctx')
- b_proj: bfloat16 [512, 512], P(None, 'ctx')
- b_in: bfloat16 [4, 512, 2048], P('expert', None, 'ctx')
- b_out: bfloat16 [4, 512, 2048], P('expert', None, 'ctx')
The draws below stay inside these ranges and needn't reach their ends.
Inputs may be any that keep to these rules, and one draw needn't show every extreme that they name: `key_mask`: each image holds its real tokens first, more than 192 of them. `expert_ids`: each token names 2 different experts; among the 64 positions of one image on one device no expert is named by more than 40 of them, and in some such blocks one expert is named by exactly 40. `norm_params`: gains and shifts of the two norms. `w_qkv`: projection weights. `w_proj`: projection weights. `w_in`: expert weights. `w_out`: expert weights. `mom_norm`: earlier momentum. `mom_router`: earlier momentum. `mom_qkv`: earlier momentum. `mom_proj`: earlier momentum. `mom_in`: earlier momentum. `mom_out`: earlier momentum.
All inputs are finite; a program needn't handle non-finite values.
Results may differ from the reference program's by a relative error of at most 0.025.
Values may be sent and summed in bfloat16 or wider, within the bound.
A program may use at most 192 MiB of HBM per device.

```python
import math
import jax
import jax.numpy as jnp
import numpy as np
from jax import lax

D = 512
HEADS = 8
HEAD_DIM = 64
HID = 2048
EXPERTS = 4
TOP = 2
SEQ_DEV = 64
SEQ = 256
CAP = 40
IMG_MB = 4
MICRO = 2
IMAGES = 64
NS_ITERS = 4
N_CTX = 4


def column_lift(key, count):
    lift = 1.0 + 2.0 * jnp.arange(count, dtype=jnp.float32) / max(count - 1, 1)
    rough = jax.random.uniform(key, (count,), jnp.float32, 0.7, 1.4)
    return lift * rough


def draw_key_mask(key, part):
    key = jax.random.fold_in(key, 3)
    lengths = jax.random.randint(key, (IMAGES,), 3 * SEQ_DEV + 1, SEQ + 1)
    positions = jnp.arange(SEQ, dtype=jnp.int32)
    return (positions[None, :] < lengths[:, None]).astype(jnp.int32)


def draw_norm_params(key, part):
    key = jax.random.fold_in(key, 5)
    gains = jax.random.uniform(jax.random.fold_in(key, 1), (2, D), jnp.float32, 0.6, 1.6)
    shifts = 0.2 * jax.random.normal(key, (2, D), jnp.float32)
    return jnp.stack([gains[0], shifts[0], gains[1], shifts[1]])


def draw_w_qkv(key, part):
    key = jax.random.fold_in(key, 7)
    base = jax.random.normal(key, (D, 3 * D), jnp.float32)
    lift = column_lift(jax.random.fold_in(key, 1), 3 * D)
    return (base * lift[None, :] / math.sqrt(2 * D)).astype(jnp.bfloat16)


def draw_w_proj(key, part):
    key = jax.random.fold_in(key, 9)
    base = jax.random.normal(key, (D, D), jnp.float32)
    lift = column_lift(jax.random.fold_in(key, 1), D)
    return (base * lift[None, :] * 1.2 / math.sqrt(D)).astype(jnp.bfloat16)


def draw_w_in(key, part):
    key = jax.random.fold_in(key, 11)
    base = jax.random.normal(key, (EXPERTS, D, HID), jnp.float32)
    lift = column_lift(jax.random.fold_in(key, 1), HID)
    return (base * lift / math.sqrt(D)).astype(jnp.bfloat16)


def draw_w_out(key, part):
    key = jax.random.fold_in(key, 13)
    base = jax.random.normal(key, (EXPERTS, D, HID), jnp.float32)
    lift = column_lift(jax.random.fold_in(key, 1), HID)
    return (base * lift / math.sqrt(4 * HID)).astype(jnp.bfloat16)


def draw_mom_norm(key, part):
    key = jax.random.fold_in(key, 15)
    base = jax.random.normal(key, (4, D), jnp.float32)
    return base * 2.0 * math.sqrt(IMAGES * SEQ)


def draw_mom_router(key, part):
    key = jax.random.fold_in(key, 17)
    base = jax.random.normal(key, (D, EXPERTS), jnp.float32)
    return base * 2.0 * math.sqrt(IMAGES * SEQ)


def draw_mom_qkv(key, part):
    key = jax.random.fold_in(key, 19)
    base = jax.random.normal(key, (D, 3 * D), jnp.float32)
    lift = column_lift(jax.random.fold_in(key, 1), 3 * D)
    return base * lift[None, :] * 0.1 * math.sqrt(IMAGES * SEQ)


def draw_mom_proj(key, part):
    key = jax.random.fold_in(key, 21)
    base = jax.random.normal(key, (D, D), jnp.float32)
    lift = column_lift(jax.random.fold_in(key, 1), D)
    return base * lift[None, :] * 0.2 * math.sqrt(IMAGES * SEQ)


def draw_mom_in(key, part):
    key = jax.random.fold_in(key, 23)
    base = jax.random.normal(key, (EXPERTS, D, HID), jnp.float32)
    lift = column_lift(jax.random.fold_in(key, 1), HID)
    return base * lift * 0.15 * math.sqrt(2.0 * IMAGES * SEQ / EXPERTS)


def draw_mom_out(key, part):
    key = jax.random.fold_in(key, 25)
    base = jax.random.normal(key, (EXPERTS, D, HID), jnp.float32)
    lift = column_lift(jax.random.fold_in(key, 1), HID)
    return base * lift * 0.4 * math.sqrt(2.0 * IMAGES * SEQ / EXPERTS)


def shard_levels(own_key, extent, cuts, low, top_value):
    factor_of, own = 1.0, jax.random.fold_in(own_key, 6)
    for axis_at, shards_of in cuts:
        heights = jnp.exp(jax.random.uniform(jax.random.fold_in(own, axis_at), (shards_of,), jnp.float32, low / len(cuts), top_value / len(cuts)))
        factor_of = factor_of * jnp.repeat(heights, extent[axis_at] // shards_of).reshape([-1 if axis == axis_at else 1 for axis in range(len(extent))])
    return factor_of


def routed_block(rng, own, number, rows, number_of, top, bound, lean):
    sequence = jax.random.permutation(rng, number_of)
    crowded, common = shares(number_of, rows * top, bound, lean, True), shares(number_of, rows * top, bound, lean, False)
    places = jnp.arange(number_of)

    def named(sizes, rotation):
        used = int((sizes > 0).sum())
        fixed = max(1, used // 4)
        shifted = fixed + (places - fixed + rotation * (used - fixed)) % max(1, number_of - fixed)
        return jnp.zeros((number_of,), jnp.int32).at[sequence[jnp.where(places < fixed, places, shifted)]].set(jnp.asarray(sizes, jnp.int32))

    sizes = jnp.where(number % 4 == 0, named(crowded, number // 4), named(common, number - number // 4 - 1))
    mixed = jax.random.permutation(jax.random.fold_in(own, 3), number_of)
    donor, sink = mixed[0:number_of // 2 * 2:2], mixed[1:number_of // 2 * 2:2]
    margin = jnp.minimum(sizes[donor] - 1, bound - sizes[sink]) // 2
    margin = jnp.where((donor == sequence[0]) | (sink == sequence[0]) | (sizes[sink] == 0), 0, jnp.maximum(margin, 0))
    shifted = jax.random.randint(jax.random.fold_in(own, 4), (number_of // 2,), 0, 1 << 20) % (margin + 1)
    sizes = sizes.at[donor].add(-shifted).at[sink].add(shifted)
    members = jnp.searchsorted(jnp.cumsum(sizes), jnp.arange(rows * top), side="right").astype(jnp.int32)
    table = members.reshape(top, rows).T
    table = table[jax.random.permutation(jax.random.fold_in(own, 1), rows)]
    rotation = jax.random.randint(jax.random.fold_in(own, 2), (rows, 1), 0, top)
    return jnp.take_along_axis(table, (jnp.arange(top)[None, :] + rotation) % top, axis=1)


def shares(count, total, reach, slope, full):
    portions = [(1 << 20) // math.isqrt(grade ** slope) + 1 for grade in range(1, count + 1)]
    largest = reach if full else min(reach, max(-(-total // count), total * portions[0] // sum(portions)))
    least = 1 if total - largest >= count - 1 else 0
    given, spare = [largest] + [least] * (count - 1), total - largest - least * (count - 1)
    while spare > 0:
        candidates = [i for i in range(1, count) if given[i] < largest] or [i for i in range(1, count) if given[i] < reach]
        pool, remaining = sum([portions[i] for i in candidates]), spare
        for i in candidates:
            addition = min(reach - given[i], max(1, remaining * portions[i] // pool), spare)
            given[i] = given[i] + addition
            spare = spare - addition
    return np.array(given)


def scatter_about(stream_key, extent, scale, most, shards=(), kind=jnp.bfloat16):
    values = scale * jax.random.normal(stream_key, extent, jnp.float32)
    if shards:
        values = values * shard_levels(stream_key, extent, shards, -0.22, 0.18)
    return jnp.clip(values, -most, most).astype(kind)


def setup_inputs(seed: int = 0) -> dict:
    arg_keys = jax.random.split(jax.random.key(seed), 17)
    x_in = scatter_about(arg_keys[0], (IMAGES, SEQ, D), 1.0, 6.0, ((0, 8), (1, 4)))
    d_out = scatter_about(arg_keys[1], (IMAGES, SEQ, D), 1.0, 6.0, ((0, 8), (1, 4)))
    key_mask = draw_key_mask(jax.random.fold_in(arg_keys[16], 71), 0)
    expert_ids_keys = jax.random.split(jax.random.fold_in(arg_keys[3], 1), IMAGES * SEQ // SEQ_DEV)
    expert_ids_turns = jax.random.permutation(jax.random.fold_in(arg_keys[3], 3), IMAGES * SEQ // SEQ_DEV)
    expert_ids = jax.vmap(lambda own, number: routed_block(jax.random.fold_in(arg_keys[3], 2), own, number, SEQ_DEV, EXPERTS, TOP, CAP, 1))(expert_ids_keys, expert_ids_turns).reshape((IMAGES, SEQ, TOP))
    norm_params = draw_norm_params(jax.random.fold_in(arg_keys[16], 71), 0)
    w_qkv = draw_w_qkv(jax.random.fold_in(arg_keys[16], 71), 0)
    w_proj = draw_w_proj(jax.random.fold_in(arg_keys[16], 71), 0)
    w_router = scatter_about(arg_keys[7], (D, EXPERTS), (2 * D) ** -0.5, 0.1875, (), jnp.float32)
    w_in = draw_w_in(jax.random.fold_in(arg_keys[16], 71), 0)
    w_out = draw_w_out(jax.random.fold_in(arg_keys[16], 71), 0)
    mom_norm = draw_mom_norm(jax.random.fold_in(arg_keys[16], 71), 0)
    mom_router = draw_mom_router(jax.random.fold_in(arg_keys[16], 71), 0)
    mom_qkv = draw_mom_qkv(jax.random.fold_in(arg_keys[16], 71), 0)
    mom_proj = draw_mom_proj(jax.random.fold_in(arg_keys[16], 71), 0)
    mom_in = draw_mom_in(jax.random.fold_in(arg_keys[16], 71), 0)
    mom_out = draw_mom_out(jax.random.fold_in(arg_keys[16], 71), 0)
    return {"x_in": x_in, "d_out": d_out, "key_mask": key_mask, "expert_ids": expert_ids, "norm_params": norm_params, "w_qkv": w_qkv, "w_proj": w_proj, "w_router": w_router, "w_in": w_in, "w_out": w_out, "mom_norm": mom_norm, "mom_router": mom_router, "mom_qkv": mom_qkv, "mom_proj": mom_proj, "mom_in": mom_in, "mom_out": mom_out}


@jax.custom_vjp
def low(v):
    return lax.optimization_barrier(v.astype(jnp.bfloat16)).astype(jnp.float32)

@jax.custom_vjp
def low_back(v):
    return v

def low_keep(v):
    return (low(v), None)

def low_pass(kept, grad):
    return (grad,)

def back_keep(v):
    return (v, None)

def back_low(kept, grad):
    return (low(grad),)
low.defvjp(low_keep, low_pass)
low_back.defvjp(back_keep, back_low)
HIGH = lax.Precision.HIGHEST
NS_A = 3.4445
NS_B = -4.775
NS_C = 2.0315
DECAY = 0.5
RATE_MAT = 0.3
RATE_GAIN = 0.3
RATE_ROUTER = 0.05
EPS_NORM = 1e-06
EPS_ORTHO = 1e-07
NEG = -1e+30

def layer_norm(values, gain, shift):
    center = lax.optimization_barrier(jnp.mean(values, axis=-1, keepdims=True))
    spread = values - center
    power = lax.optimization_barrier(jnp.mean(spread * spread, axis=-1, keepdims=True))
    return spread * lax.rsqrt(power + EPS_NORM) * gain + shift

def route_slots(idents):
    count = idents.shape[0]
    blocks = idents.reshape(count * N_CTX, SEQ_DEV * TOP)
    onehot = (blocks[:, :, None] == jnp.arange(EXPERTS, dtype=jnp.int32)).astype(jnp.int32)
    before = jnp.cumsum(onehot, axis=1) - onehot
    ranked = lax.optimization_barrier(jnp.sum(before * onehot, axis=-1))
    offsets = (jnp.arange(count * N_CTX, dtype=jnp.int32) * CAP)[:, None]
    return (ranked + offsets).reshape(idents.shape)

def block_forward(x_part, params, idents, slots, mask):
    norm_params, w_qkv, w_proj, w_router, w_in, w_out = params
    count = x_part.shape[0]
    normed_first = low(layer_norm(x_part, norm_params[0], norm_params[1]))
    qkv = low_back(low(jnp.einsum('csd,de->cse', normed_first, w_qkv, precision=HIGH)))
    qkv = qkv.reshape(count, SEQ, 3, HEADS, HEAD_DIM)
    query = qkv[:, :, 0]
    keys = qkv[:, :, 1]
    values = qkv[:, :, 2]
    scores = low_back(jnp.einsum('cqhd,ckhd->chqk', query, keys, precision=HIGH) * HEAD_DIM ** (-0.5))
    scores = jnp.where(mask[:, None, None, :] > 0, scores, NEG)
    probs = low(jax.nn.softmax(scores, axis=-1))
    attended = low_back(low(jnp.einsum('chqk,ckhd->cqhd', probs, values, precision=HIGH)))
    branch = low_back(jnp.einsum('cse,ed->csd', attended.reshape(count, SEQ, D), w_proj, precision=HIGH))
    mid = x_part + branch
    normed_second = layer_norm(mid, norm_params[2], norm_params[3])
    logits = jnp.einsum('csd,de->cse', normed_second, w_router, precision=HIGH)
    onehot = (idents[..., None] == jnp.arange(EXPERTS, dtype=jnp.int32)).astype(jnp.float32)
    chosen = lax.optimization_barrier(jnp.sum(onehot * logits[:, :, None, :], axis=-1))
    gates = jax.nn.softmax(chosen, axis=-1)
    routed = low_back(jnp.broadcast_to(low(normed_second)[:, :, None, :], (count, SEQ, TOP, D)))
    flat_ids = idents.reshape(-1)
    flat_slots = slots.reshape(-1)
    buffer = jnp.zeros((EXPERTS, count * N_CTX * CAP, D), jnp.float32)
    buffer = buffer.at[flat_ids, flat_slots].set(routed.reshape(-1, D))
    pre = low_back(jnp.einsum('erd,edh->erh', buffer, w_in, precision=HIGH))
    act = low(jax.nn.gelu(pre, approximate=False))
    made = low_back(low(jnp.einsum('erh,edh->erd', act, w_out, precision=HIGH)))
    returned = made[flat_ids, flat_slots].reshape(count, SEQ, TOP, D)
    return mid + lax.optimization_barrier(jnp.sum(gates[..., None] * returned, axis=2))

def orthogonal(moment):
    iterate = moment / (jnp.sqrt(jnp.sum(moment * moment)) + EPS_ORTHO)
    for turn_index in range(NS_ITERS):
        gram = jnp.dot(iterate, iterate.T, precision=HIGH)
        mixer = NS_B * gram + NS_C * jnp.dot(gram, gram, precision=HIGH)
        iterate = NS_A * iterate + jnp.dot(mixer, iterate, precision=HIGH)
    return iterate

def muon(weight, grad, moment):
    fresh = DECAY * moment + grad
    factor = RATE_MAT * 0.2 * math.sqrt(max(weight.shape[-2], weight.shape[-1]))
    return (fresh, weight - factor * orthogonal(fresh))

def expert_muon(item):
    weight, grad, moment = item
    return muon(weight, grad, moment)

def steady(weight, grad, moment, rate):
    fresh = DECAY * moment + grad
    return (fresh, weight - rate * fresh * lax.rsqrt(jnp.mean(fresh * fresh) + EPS_NORM))

def reference(x_in, d_out, key_mask, expert_ids, norm_params, w_qkv, w_proj, w_router, w_in, w_out, mom_norm, mom_router, mom_qkv, mom_proj, mom_in, mom_out):
    params = (norm_params, w_qkv.astype(jnp.float32), w_proj.astype(jnp.float32), w_router, w_in.astype(jnp.float32), w_out.astype(jnp.float32))
    span = IMG_MB * MICRO
    groups = IMAGES // span

    def shape_spans(array):
        return array.reshape((groups, span) + array.shape[1:])
    inputs = (shape_spans(x_in), shape_spans(d_out), shape_spans(key_mask), shape_spans(expert_ids))

    def step(total, item):
        x_part, cotangent, mask, idents = item
        slots = route_slots(idents)

        def forward(x_value, param_value):
            return block_forward(x_value, param_value, idents, slots, mask)
        result, pull = jax.vjp(forward, x_part.astype(jnp.float32), params)
        d_input, d_params = pull(cotangent.astype(jnp.float32))
        return (jax.tree.map(jnp.add, total, d_params), (result.astype(jnp.bfloat16), d_input))
    zeros = jax.tree.map(jnp.zeros_like, params)
    grads, (results, d_inputs) = lax.scan(step, zeros, inputs)
    g_norm, g_qkv, g_proj, g_router, g_in, g_out = grads
    block_out = results.reshape(IMAGES, SEQ, D)
    d_x = d_inputs.reshape(IMAGES, SEQ, D)
    m_norm, n_norm = steady(norm_params, g_norm, mom_norm, RATE_GAIN)
    m_router, n_router = steady(w_router, g_router, mom_router, RATE_ROUTER)
    m_qkv, n_qkv = muon(w_qkv.astype(jnp.float32), g_qkv, mom_qkv)
    m_proj, n_proj = muon(w_proj.astype(jnp.float32), g_proj, mom_proj)
    m_in, n_in = lax.map(expert_muon, (w_in.astype(jnp.float32), g_in, mom_in))
    m_out, n_out = lax.map(expert_muon, (w_out.astype(jnp.float32), g_out, mom_out))
    return (block_out, d_x, g_norm, g_router, g_qkv, g_proj, g_in, g_out, m_norm, m_router, m_qkv, m_proj, m_in, m_out, n_norm, n_router, n_qkv, n_proj, n_in, n_out, n_qkv.astype(jnp.bfloat16), n_proj.astype(jnp.bfloat16), n_in.astype(jnp.bfloat16), n_out.astype(jnp.bfloat16))
```

```python
import functools
import math

import jax
import jax.numpy as jnp
from jax import lax
from jax.experimental import pallas as pl
from jax.experimental.pallas import tpu as pltpu
from jax.sharding import PartitionSpec as P

HEADS = 8
HEAD_DIM = 64
MICRO = 2
NS_ITERS = 4


HIGH = lax.Precision.HIGHEST
NS_A = 3.4445
NS_B = -4.775
NS_C = 2.0315
DECAY = 0.5
RATE_MAT = 0.3
RATE_GAIN = 0.3
RATE_ROUTER = 0.05
EPS_NORM = 1e-06
EPS_ORTHO = 1e-07
NEG = -1e30
LANES = 128
VMEM_LIMIT = 60 * 2**20
MESH = pl.DeviceIdType.MESH
NS_PRECISION = lax.Precision.HIGH


def as_sent(array):
    return jax.tree.map(lambda a: a.astype(jnp.bfloat16) if a.dtype == jnp.float32 else a, array)


def layer_norm(values, gain, shift):
    center = jnp.mean(values, axis=-1, keepdims=True)
    spread = values - center
    power = jnp.mean(spread * spread, axis=-1, keepdims=True)
    return spread * lax.rsqrt(power + EPS_NORM) * gain + shift


def gelu_exact(values):
    return jax.nn.gelu(values, approximate=False)


def add_block(total, piece):
    return total + piece


def masked_scores(query, key_piece, mask_piece, factor):
    scores = (
        jnp.einsum("bqhd,bkhd->bhqk", query, key_piece, preferred_element_type=jnp.float32) * factor
    )
    return jnp.where(mask_piece[:, None, None, :] > 0, scores, NEG)


def gram_list(matrices):
    return tuple(
        (jnp.einsum("...ik,...jk->...ij", matrix, matrix, precision=HIGH) for matrix in matrices)
    )


def schulz_turn(matrices, grams):
    result = []
    for matrix, gram in zip(matrices, grams):
        square = jnp.einsum("...ij,...jk->...ik", gram, gram, precision=HIGH)
        mixer = NS_B * gram + NS_C * square
        result.append(
            NS_A * matrix + jnp.einsum("...ij,...jk->...ik", mixer, matrix, precision=HIGH)
        )
    return tuple(result)


def exchanged(
    x_in,
    d_out,
    key_mask,
    expert_ids,
    norm_params,
    w_qkv,
    w_proj,
    w_router,
    w_in,
    w_out,
    mom_norm,
    mom_router,
    mom_qkv,
    mom_proj,
    mom_in,
    mom_out,
):
    ctx_count = lax.axis_size("ctx")
    ctx_place = lax.axis_index("ctx")
    owner_count = lax.axis_size("expert")
    local_images = x_in.shape[0]
    seq_dev = x_in.shape[1]
    width = x_in.shape[2]
    top_count = expert_ids.shape[-1]
    experts = w_router.shape[1]
    exp_dev = w_in.shape[0]
    hid_part = w_in.shape[2]
    capacity = max(2, (5 * top_count * seq_dev + 4 * experts - 1) // (4 * experts))
    batch = local_images // MICRO
    slot_count = batch * capacity
    seq_all = seq_dev * ctx_count
    factor = HEAD_DIM ** (-0.5)
    expert_iota = jnp.arange(experts, dtype=jnp.int32)
    recv_shape = (owner_count, exp_dev, slot_count, width)
    head_shape = (batch, seq_dev, HEADS, HEAD_DIM)

    def hidden_fold(step_fn, init):
        folded = step_fn(
            init,
            (
                lax.all_gather(w_in, "ctx", axis=2, tiled=True),
                lax.all_gather(w_out, "ctx", axis=2, tiled=True),
            ),
            jnp.int32(0),
        )
        return folded

    def to_owner(rows):
        return lax.all_to_all(rows, "expert", split_axis=0, concat_axis=0, tiled=True)

    def to_source(rows):
        return lax.all_to_all(rows, "expert", split_axis=0, concat_axis=0, tiled=True)

    def key_fold(keys, values, mask_low, step_fn, init):
        return step_fn(
            init,
            (
                lax.all_gather(keys, "ctx", axis=1, tiled=True),
                lax.all_gather(values, "ctx", axis=1, tiled=True),
                lax.all_gather(mask_low, "ctx", axis=1, tiled=True),
            ),
            jnp.int32(0),
        )

    grad_qkv = jnp.zeros(w_qkv.shape, jnp.float32)
    grad_proj = jnp.zeros(w_proj.shape, jnp.float32)
    grad_router = jnp.zeros(w_router.shape, jnp.float32)
    grad_norm = jnp.zeros((4, width), jnp.float32)
    grad_in = jnp.zeros((exp_dev, width, hid_part * ctx_count), jnp.float32)
    grad_out = jnp.zeros((exp_dev, width, hid_part * ctx_count), jnp.float32)
    outputs = []
    input_grads = []
    for micro_index in range(MICRO):
        first_image = micro_index * batch
        last_image = first_image + batch
        x_part = x_in[first_image:last_image].astype(jnp.float32)
        cotangent = d_out[first_image:last_image].astype(jnp.float32)
        mask_low = key_mask[first_image:last_image].astype(jnp.bfloat16)
        idents = expert_ids[first_image:last_image]
        normed_first, pull_first = jax.vjp(layer_norm, x_part, norm_params[0], norm_params[1])
        first_low = normed_first.astype(jnp.bfloat16).reshape(-1, width)
        qkv = jnp.dot(first_low, w_qkv, preferred_element_type=jnp.float32).astype(jnp.bfloat16)
        qkv = qkv.reshape(batch, seq_dev, 3, HEADS, HEAD_DIM)
        query = qkv[:, :, 0]
        keys = qkv[:, :, 1]
        values = qkv[:, :, 2]
        peak_old = jnp.full((batch, HEADS, seq_dev), NEG, jnp.float32)
        key_piece = lax.all_gather(keys, "ctx", axis=1, tiled=True)
        mask_piece = lax.all_gather(mask_low, "ctx", axis=1, tiled=True)
        scores = masked_scores(query, key_piece, mask_piece, factor)
        peak_new = jnp.maximum(peak_old, jnp.max(scores, axis=-1))
        total_new = jnp.sum(jnp.exp(scores - peak_new[..., None]), axis=-1)
        log_total = peak_new + jnp.log(total_new)

        def attend_step(acc, pieces, start):
            key_piece, value_piece, mask_piece = pieces
            weights = jnp.exp(
                masked_scores(query, key_piece, mask_piece, factor) - log_total[..., None]
            )
            return jnp.einsum(
                "bhqk,bkhd->bqhd",
                weights.astype(jnp.bfloat16),
                value_piece,
                preferred_element_type=jnp.float32,
            )

        attended = key_fold(keys, values, mask_low, attend_step, jnp.zeros(head_shape, jnp.float32))
        attended_low = attended.astype(jnp.bfloat16).reshape(-1, width)
        branch = jnp.dot(attended_low, w_proj, preferred_element_type=jnp.float32).reshape(
            batch, seq_dev, width
        )
        mid = x_part + branch
        normed_second, pull_second = jax.vjp(layer_norm, mid, norm_params[2], norm_params[3])
        routed_low = normed_second.astype(jnp.bfloat16)
        logits = jnp.einsum("bsd,de->bse", normed_second, w_router, precision=HIGH)
        onehot = (idents[..., None] == expert_iota).astype(jnp.float32)
        chosen = jnp.sum(onehot * logits[:, :, None, :], axis=-1)
        gates = jax.nn.softmax(chosen, axis=-1)
        flat_ids = idents.reshape(batch, seq_dev * top_count)
        hits = (flat_ids[..., None] == expert_iota).astype(jnp.int32)
        ranked = jnp.sum((jnp.cumsum(hits, axis=1) - hits) * hits, axis=-1)
        slot = (ranked + (jnp.arange(batch, dtype=jnp.int32) * capacity)[:, None]).reshape(-1)
        target = flat_ids.reshape(-1)
        routed_rows = jnp.broadcast_to(
            routed_low[:, :, None, :], (batch, seq_dev, top_count, width)
        ).reshape(-1, width)
        send = (
            jnp.zeros((experts, slot_count, width), jnp.bfloat16).at[target, slot].set(routed_rows)
        )
        received = to_owner(send.reshape(recv_shape))

        def expert_step(acc, pieces, start):
            piece_in, piece_out = pieces
            pre = jnp.einsum(
                "nesd,edh->nesh", received, piece_in, preferred_element_type=jnp.float32
            )
            act = gelu_exact(pre).astype(jnp.bfloat16)
            return jnp.einsum("nesh,edh->nesd", act, piece_out, preferred_element_type=jnp.float32)

        made = hidden_fold(expert_step, jnp.zeros(recv_shape, jnp.float32))
        back_rows = to_source(made.astype(jnp.bfloat16)).reshape(experts, slot_count, width)
        returned = (
            back_rows[target, slot].reshape(batch, seq_dev, top_count, width).astype(jnp.float32)
        )
        result = mid + jnp.sum(gates[..., None] * returned, axis=2)
        outputs.append(result.astype(jnp.bfloat16))
        dgates = jnp.sum(cotangent[:, :, None, :] * returned, axis=-1)
        dchosen = gates * (dgates - jnp.sum(gates * dgates, axis=-1, keepdims=True))
        dlogits = jnp.sum(dchosen[..., None] * onehot, axis=2)
        grad_router = grad_router + jnp.einsum(
            "bsd,bse->de", normed_second, dlogits, precision=HIGH
        )
        dsecond = jnp.einsum("bse,de->bsd", dlogits, w_router, precision=HIGH)
        dreturned = (
            (gates[..., None] * cotangent[:, :, None, :]).astype(jnp.bfloat16).reshape(-1, width)
        )
        dsend = (
            jnp.zeros((experts, slot_count, width), jnp.bfloat16).at[target, slot].set(dreturned)
        )
        dreceived = to_owner(dsend.reshape(recv_shape))

        def expert_back(carry, pieces, start):
            drows, dins, douts = carry
            piece_in, piece_out = pieces
            pre = jnp.einsum(
                "nesd,edh->nesh", received, piece_in, preferred_element_type=jnp.float32
            )
            act_full, pull_act = jax.vjp(gelu_exact, pre)
            act = act_full.astype(jnp.bfloat16)
            dact = jnp.einsum(
                "nesd,edh->nesh", dreceived, piece_out, preferred_element_type=jnp.float32
            )
            dpre = pull_act(dact)[0].astype(jnp.bfloat16)
            douts = add_block(
                douts,
                jnp.einsum("nesd,nesh->edh", dreceived, act, preferred_element_type=jnp.float32),
            )
            dins = add_block(
                dins,
                jnp.einsum("nesd,nesh->edh", received, dpre, preferred_element_type=jnp.float32),
            )
            drows = jnp.einsum("nesh,edh->nesd", dpre, piece_in, preferred_element_type=jnp.float32)
            return (drows, dins, douts)

        drows, grad_in, grad_out = hidden_fold(
            expert_back, (jnp.zeros(recv_shape, jnp.float32), grad_in, grad_out)
        )
        dback = to_source(drows.astype(jnp.bfloat16)).reshape(experts, slot_count, width)
        dsecond = dsecond + jnp.sum(
            dback[target, slot].reshape(batch, seq_dev, top_count, width).astype(jnp.float32),
            axis=2,
        )
        dmid, dgain_two, dshift_two = pull_second(dsecond)
        dmid = dmid + cotangent
        dbranch = dmid.astype(jnp.bfloat16).reshape(-1, width)
        grad_proj = grad_proj + jnp.einsum(
            "sd,se->de", attended_low, dbranch, preferred_element_type=jnp.float32
        )
        dattended = jnp.einsum("se,de->sd", dbranch, w_proj, preferred_element_type=jnp.float32)
        dattended = dattended.astype(jnp.bfloat16).reshape(head_shape)
        delta = jnp.einsum("bqhd,bqhd->bhq", dattended.astype(jnp.float32), attended)

        def attend_back(carry, pieces, start):
            dquery, dkeys, dvalues = carry
            key_piece, value_piece, mask_piece = pieces
            weights = jnp.exp(
                masked_scores(query, key_piece, mask_piece, factor) - log_total[..., None]
            )
            probs = weights.astype(jnp.bfloat16)
            dvalue_piece = jnp.einsum(
                "bhqk,bqhd->bkhd", probs, dattended, preferred_element_type=jnp.float32
            )
            dprobs = jnp.einsum(
                "bqhd,bkhd->bhqk", dattended, value_piece, preferred_element_type=jnp.float32
            )
            dscores = (weights * (dprobs - delta[..., None])).astype(jnp.bfloat16)
            dquery = factor * jnp.einsum(
                "bhqk,bkhd->bqhd", dscores, key_piece, preferred_element_type=jnp.float32
            )
            dkey_piece = factor * jnp.einsum(
                "bhqk,bqhd->bkhd", dscores, query, preferred_element_type=jnp.float32
            )
            return (dquery, add_block(dkeys, dkey_piece), add_block(dvalues, dvalue_piece))

        all_shape = (batch, seq_all, HEADS, HEAD_DIM)
        back_init = (
            jnp.zeros(head_shape, jnp.float32),
            jnp.zeros(all_shape, jnp.float32),
            jnp.zeros(all_shape, jnp.float32),
        )
        dquery, dkeys_all, dvalues_all = key_fold(keys, values, mask_low, attend_back, back_init)
        dkeys, dvalues = (
            lax.psum_scatter(
                dkeys_all.astype(jnp.bfloat16), "ctx", scatter_dimension=1, tiled=True
            ).astype(jnp.float32),
            lax.psum_scatter(
                dvalues_all.astype(jnp.bfloat16), "ctx", scatter_dimension=1, tiled=True
            ).astype(jnp.float32),
        )
        dqkv = (
            jnp.stack([dquery, dkeys, dvalues], axis=2).astype(jnp.bfloat16).reshape(-1, 3 * width)
        )
        grad_qkv = grad_qkv + jnp.einsum(
            "sd,se->de", first_low, dqkv, preferred_element_type=jnp.float32
        )
        dfirst = jnp.einsum("se,de->sd", dqkv, w_qkv, preferred_element_type=jnp.float32).reshape(
            batch, seq_dev, width
        )
        dx_part, dgain_one, dshift_one = pull_first(dfirst)
        grad_norm = grad_norm + jnp.stack([dgain_one, dshift_one, dgain_two, dshift_two])
        input_grads.append(dx_part + dmid)
    block_out = jnp.concatenate(outputs, axis=0)
    d_x = jnp.concatenate(input_grads, axis=0)
    shared = (
        lax.psum_scatter(
            grad_in.astype(jnp.bfloat16), "ctx", scatter_dimension=2, tiled=True
        ).astype(jnp.float32),
        lax.psum_scatter(
            grad_out.astype(jnp.bfloat16), "ctx", scatter_dimension=2, tiled=True
        ).astype(jnp.float32),
        lax.psum_scatter(
            grad_qkv[None].astype(jnp.bfloat16), "ctx", scatter_dimension=2, tiled=True
        ).astype(jnp.float32),
        lax.psum_scatter(
            grad_proj[None].astype(jnp.bfloat16), "ctx", scatter_dimension=2, tiled=True
        ).astype(jnp.float32),
        lax.psum_scatter(
            grad_norm[None].astype(jnp.bfloat16), "ctx", scatter_dimension=2, tiled=True
        ).astype(jnp.float32),
        lax.psum_scatter(
            grad_router[None].astype(jnp.bfloat16), "ctx", scatter_dimension=2, tiled=True
        ).astype(jnp.float32),
    )
    g_in, g_out = (
        lax.psum(shared[0].astype(jnp.bfloat16), "dp").astype(jnp.float32),
        lax.psum(shared[1].astype(jnp.bfloat16), "dp").astype(jnp.float32),
    )
    g_qkv, g_proj, g_norm, g_router = lax.psum(
        (shared[2][0], shared[3][0], shared[4][0], shared[5][0]), ("expert", "dp")
    )
    own_qkv = lax.dynamic_slice_in_dim(w_qkv, ctx_place * g_qkv.shape[1], g_qkv.shape[1], 1).astype(
        jnp.float32
    )
    own_proj = lax.dynamic_slice_in_dim(
        w_proj, ctx_place * g_proj.shape[1], g_proj.shape[1], 1
    ).astype(jnp.float32)
    own_norm = lax.dynamic_slice_in_dim(
        norm_params, ctx_place * g_norm.shape[1], g_norm.shape[1], 1
    )
    own_router = lax.dynamic_slice_in_dim(
        w_router, ctx_place * g_router.shape[1], g_router.shape[1], 1
    )
    m_qkv = DECAY * mom_qkv + g_qkv
    m_proj = DECAY * mom_proj + g_proj
    m_in = DECAY * mom_in + g_in
    m_out = DECAY * mom_out + g_out
    m_norm = DECAY * mom_norm + g_norm
    m_router = DECAY * mom_router + g_router
    matrices = (m_qkv, m_proj, m_in, m_out)
    vector_squares = (jnp.sum(m_norm * m_norm), jnp.sum(m_router * m_router))
    sums = lax.psum(
        tuple((jnp.sum(matrix * matrix, axis=(-2, -1)) for matrix in matrices)) + vector_squares,
        "ctx",
    )
    vector_totals = sums[4:]
    iterates = tuple(
        (
            matrix / jnp.expand_dims(jnp.sqrt(square) + EPS_ORTHO, (-2, -1))
            for matrix, square in zip(matrices, sums[:4])
        )
    )
    for turn_index in range(NS_ITERS):
        iterates = schulz_turn(
            iterates,
            jax.tree.map(
                lambda part: part.astype(jnp.float32), lax.psum(as_sent(gram_list(iterates)), "ctx")
            ),
        )
    n_qkv = (
        own_qkv - RATE_MAT * 0.2 * math.sqrt(max(width, g_qkv.shape[1] * ctx_count)) * iterates[0]
    )
    n_proj = (
        own_proj - RATE_MAT * 0.2 * math.sqrt(max(width, g_proj.shape[1] * ctx_count)) * iterates[1]
    )
    n_in = (
        w_in.astype(jnp.float32)
        - RATE_MAT * 0.2 * math.sqrt(max(width, hid_part * ctx_count)) * iterates[2]
    )
    n_out = (
        w_out.astype(jnp.float32)
        - RATE_MAT * 0.2 * math.sqrt(max(width, hid_part * ctx_count)) * iterates[3]
    )
    n_norm = own_norm - RATE_GAIN * m_norm * lax.rsqrt(vector_totals[0] / (4 * width) + EPS_NORM)
    n_router = own_router - RATE_ROUTER * m_router * lax.rsqrt(
        vector_totals[1] / (width * experts) + EPS_NORM
    )
    return (
        block_out,
        d_x,
        g_norm,
        g_router,
        g_qkv,
        g_proj,
        g_in,
        g_out,
        m_norm,
        m_router,
        m_qkv,
        m_proj,
        m_in,
        m_out,
        n_norm,
        n_router,
        n_qkv,
        n_proj,
        n_in,
        n_out,
        n_qkv.astype(jnp.bfloat16),
        n_proj.astype(jnp.bfloat16),
        n_in.astype(jnp.bfloat16),
        n_out.astype(jnp.bfloat16),
    )


def dot(left, right, precision=None):
    return jnp.dot(left, right, precision=precision, preferred_element_type=jnp.float32)


def dot_nt(left, right, precision=None):
    return lax.dot_general(
        left, right, (((1,), (1,)), ((), ())), precision=precision, preferred_element_type=jnp.float32
    )


def dot_tn(left, right, precision=None):
    return lax.dot_general(
        left, right, (((0,), (0,)), ((), ())), precision=precision, preferred_element_type=jnp.float32
    )


def places():
    return lax.axis_index("expert"), lax.axis_index("ctx"), lax.axis_index("dp")


def ctx_partner(ctx, step):
    column, row = lax.rem(ctx, 2), ctx // 2
    column = lax.rem(column + lax.rem(step, 2), 2)
    row = lax.rem(row + step // 2, 2)
    return row * 2 + column


def z_partner(expert, step, count):
    return lax.rem(expert + step, count)


def greet(partners):
    barrier = pltpu.get_barrier_semaphore()
    for partner in partners:
        pl.semaphore_signal(barrier, inc=1, device_id=partner, device_id_type=MESH)
    pl.semaphore_wait(barrier, len(partners))


def send(source, target, send_sem, recv_sem, partner):
    copy = pltpu.make_async_remote_copy(
        src_ref=source,
        dst_ref=target,
        send_sem=send_sem,
        recv_sem=recv_sem,
        device_id=partner,
        device_id_type=MESH,
    )
    copy.start()
    return copy


def normalize(values):
    center = jnp.mean(values, axis=-1, keepdims=True)
    spread = values - center
    power = jnp.mean(spread * spread, axis=-1, keepdims=True)
    scale = lax.rsqrt(power + EPS_NORM)
    return spread * scale, scale


def normalize_back(grad, unit, scale):
    first = jnp.mean(grad, axis=-1, keepdims=True)
    second = jnp.mean(grad * unit, axis=-1, keepdims=True)
    return scale * (grad - first - unit * second)


def group_rows(meta_ref, image):
    pairs = [
        meta_ref[2 * half, image] + meta_ref[2 * half + 1, image]
        for half in range(meta_ref.shape[0] // 2)
    ]
    return jnp.concatenate(pairs, axis=1)


def forward_kernel(
    n_exp,
    experts,
    x_ref,
    d_ref,
    meta_ref,
    w_ref,
    norm_ref,
    wqkv_ref,
    wproj_ref,
    x_all,
    d_all,
    meta_all,
    w_all,
    first_ref,
    qkv_ref,
    lse_ref,
    att_ref,
    mid_ref,
    routed_ref,
    x_send,
    x_recv,
    m_send,
    m_recv,
    d_send,
    d_recv,
    w_send,
    w_recv,
    s_send,
    s_recv,
    own_sem,
):
    expert, ctx, dp = places()
    own_images, n_ctx, seq_dev, width = x_all.shape
    seq = n_ctx * seq_dev
    ctx_steps = list(range(1, n_ctx))
    z_steps = [1, n_exp - 1] + list(range(2, n_exp - 1))
    ctx_ids = [(expert, ctx_partner(ctx, step), dp) for step in ctx_steps]
    z_ids = [(z_partner(expert, step, n_exp), ctx, dp) for step in z_steps]
    twin = (expert, ctx, 1 - dp)
    greet(ctx_ids + z_ids + [twin])
    own = [
        pltpu.make_async_copy(
            x_ref.at[pl.ds(ctx * own_images, own_images)], x_all.at[:, ctx], own_sem.at[0]
        ),
        pltpu.make_async_copy(meta_ref, meta_all.at[ctx], own_sem.at[1]),
        pltpu.make_async_copy(d_ref, d_all.at[:, ctx], own_sem.at[2]),
        pltpu.make_async_copy(w_ref, w_all.at[:, expert], own_sem.at[3]),
    ]
    for copy in own:
        copy.start()
    x_copies = []
    m_copies = []
    for at, partner in enumerate(ctx_ids):
        x_copies.append(
            send(
                x_ref.at[pl.ds(partner[1] * own_images, own_images)],
                x_all.at[:, ctx],
                x_send.at[at],
                x_recv.at[at],
                partner,
            )
        )
        m_copies.append(
            send(meta_ref, meta_all.at[ctx], m_send.at[at], m_recv.at[at], partner)
        )
    w_copies = [
        send(w_ref.at[dp], w_all.at[dp, expert], w_send.at[at], w_recv.at[at], partner)
        for at, partner in enumerate(z_ids)
    ]
    for copy in own:
        copy.wait()
    for copy in x_copies + m_copies:
        copy.wait()
    d_copies = [
        send(d_ref, d_all.at[:, ctx], d_send.at[at], d_recv.at[at], partner)
        for at, partner in enumerate(ctx_ids)
    ]
    lane = lax.broadcasted_iota(jnp.int32, (seq, LANES), 1)
    low_half = lane < HEAD_DIM
    for image in range(own_images):
        rows = pl.ds(image * seq, seq)
        values = x_all[image].reshape(seq, width).astype(jnp.float32)
        unit, _ = normalize(values)
        first = (unit * norm_ref[0:1] + norm_ref[1:2]).astype(jnp.bfloat16)
        first_ref[rows] = first
        qkv_ref[rows] = dot(first, wqkv_ref[...]).astype(jnp.bfloat16)
        key_mask = group_rows(meta_all, ctx * own_images + image)[experts : experts + 1]
        bias = jnp.where(key_mask > 0, 0.0, NEG)
        totals = jnp.zeros((seq, LANES), jnp.float32)
        for pair in range(HEADS // 2):
            query = qkv_ref[rows, pair * LANES : (pair + 1) * LANES]
            keys = qkv_ref[rows, width + pair * LANES : width + (pair + 1) * LANES]
            heads = qkv_ref[rows, 2 * width + pair * LANES : 2 * width + (pair + 1) * LANES]
            query = query * jnp.bfloat16(HEAD_DIM**-0.5)
            parts = []
            for half in range(2):
                chosen = low_half if half == 0 else ~low_half
                part = jnp.where(chosen, query, jnp.zeros_like(query))
                scores = dot_nt(part, keys) + bias
                peak = jnp.max(scores, axis=-1, keepdims=True)
                raised = jnp.exp(scores - peak)
                total = jnp.sum(raised, axis=-1, keepdims=True)
                probs = (raised * (1.0 / total)).astype(jnp.bfloat16)
                parts.append(dot(probs, heads))
                totals = jnp.where(lane == 2 * pair + half, peak + jnp.log(total), totals)
            att_ref[rows, pair * LANES : (pair + 1) * LANES] = jnp.where(
                low_half, parts[0], parts[1]
            ).astype(jnp.bfloat16)
        lse_ref[rows] = totals
        mid = values + dot(att_ref[rows], wproj_ref[...])
        mid_ref[rows] = mid
        unit, _ = normalize(mid)
        routed_ref[rows] = (unit * norm_ref[2:3] + norm_ref[3:4]).astype(jnp.bfloat16)
    s_copies = []
    for at, step in enumerate(z_steps):
        w_copies[at].wait()
        source = z_partner(expert, n_exp - step, n_exp)
        s_copies.append(
            send(
                w_all.at[dp, source], w_all.at[dp, source], s_send.at[at], s_recv.at[at], twin
            )
        )
    for copy in d_copies + s_copies:
        copy.wait()


def expert_kernel(
    experts,
    routed_ref,
    d_all,
    meta_all,
    w_all,
    router_ref,
    mid_ref,
    out_ref,
    dsecond_ref,
    grads_ref,
    grouter_ref,
    r_all,
    out_send,
    out_recv,
    ds_send,
    ds_recv,
    acc_out,
    acc_ds,
    acc_grads,
    acc_router,
    gates_ref,
    dgates_ref,
    r_turn,
    d_turn,
    r_sems,
    ds_sems,
    out_sems,
):
    expert, ctx, dp = places()
    n_ctx, rows, width = d_all.shape
    images = out_ref.shape[0]
    own_images = images // n_ctx
    seq_dev = out_ref.shape[1]
    ctx_ids = [(expert, ctx_partner(ctx, step), dp) for step in range(1, n_ctx)]
    greet(ctx_ids)
    r_copies = [
        send(routed_ref, r_all.at[ctx], r_sems.at[0, at], r_sems.at[1, at], partner)
        for at, partner in enumerate(ctx_ids)
    ]
    r_all[ctx] = routed_ref[...]
    acc_grads[...] = jnp.zeros_like(acc_grads)
    acc_router[...] = jnp.zeros_like(acc_router)
    lane = lax.broadcasted_iota(jnp.int32, (rows, LANES), 1)

    def piece_copies(step):
        owner = ctx_partner(ctx, step)
        copies = []
        for at in range(n_ctx - 1):
            target = ctx_partner(ctx, at + 1)
            copies.append(
                pltpu.make_async_remote_copy(
                    src_ref=out_send.at[step, :, target],
                    dst_ref=out_recv.at[ctx, pl.ds(owner * own_images, own_images)],
                    send_sem=out_sems.at[0, step, at],
                    recv_sem=out_sems.at[1, step, at],
                    device_id=(expert, target, dp),
                    device_id_type=MESH,
                )
            )
        return copies

    def chunk(step):
        owner = ctx_partner(ctx, step)
        if step > 0:
            r_copies[step - 1].wait_recv()
        routed = r_all[owner]
        cotangent = d_all[owner]
        r_turn[...] = routed.T
        d_turn[...] = cotangent.T
        present = jnp.concatenate(
            [group_rows(meta_all, owner * own_images + image) for image in range(own_images)], axis=1
        )
        present = jnp.concatenate(
            [present, jnp.zeros((LANES - present.shape[0], rows), jnp.float32)], axis=0
        ).T
        present = (present > 0) & (lane < experts)
        logits = dot(routed, router_ref[0]) + dot(routed, router_ref[1])
        peak = jnp.max(jnp.where(present, logits, NEG), axis=-1, keepdims=True)
        raised = jnp.where(present, jnp.exp(jnp.where(present, logits - peak, 0.0)), 0.0)
        gates_ref[...] = raised / jnp.sum(raised, axis=-1, keepdims=True)
        acc_out[...] = jnp.zeros_like(acc_out)
        acc_ds[...] = jnp.zeros_like(acc_ds)
        dgates_ref[...] = jnp.zeros_like(dgates_ref)

        def one_expert(index, carry):
            w_in = w_all[0, index]
            w_out = w_all[1, index]
            for half in range(2):
                part = pl.ds(half * (rows // 2), rows // 2)
                cols = lane[: rows // 2]
                gate = jnp.sum(
                    jnp.where(cols == index, gates_ref[part], 0.0), axis=-1, keepdims=True
                )
                pre = dot(r_all[owner, part], w_in)
                dact = dot(d_all[owner, part], w_out)
                cdf = 0.5 + 0.5 * lax.erf(pre * (0.5**0.5))
                act = pre * cdf
                slope = cdf + pre * (jnp.exp(-0.5 * pre * pre) * (1.0 / math.sqrt(2 * math.pi)))
                dgate = jnp.sum(dact * act, axis=-1, keepdims=True)
                dgates_ref[part] = jnp.where(cols == index, dgate, dgates_ref[part])
                act_low = (gate * act).astype(jnp.bfloat16)
                dpre = (gate * dact * slope).astype(jnp.bfloat16)
                acc_out[part] += dot_nt(act_low, w_out)
                acc_ds[part] += dot_nt(dpre, w_in)
                acc_grads[0, index] += dot(r_turn[:, half * (rows // 2) : (half + 1) * (rows // 2)], dpre)
                acc_grads[1, index] += dot(d_turn[:, half * (rows // 2) : (half + 1) * (rows // 2)], act_low)
            return carry

        lax.fori_loop(0, experts, one_expert, 0)
        gates = gates_ref[...]
        dgates = dgates_ref[...]
        dlogits = gates * (dgates - jnp.sum(gates * dgates, axis=-1, keepdims=True))
        high = dlogits.astype(jnp.bfloat16)
        low = (dlogits - high.astype(jnp.float32)).astype(jnp.bfloat16)
        acc_router[...] += dot(r_turn[...], high) + dot(r_turn[...], low)
        acc_ds[...] += (
            dot_nt(high, router_ref[0]) + dot_nt(high, router_ref[1]) + dot_nt(low, router_ref[0])
        )
        if step == 0:
            acc_out[...] += mid_ref[...]
            dsecond_ref[...] = acc_ds[...]
        else:
            ds_send[step - 1] = acc_ds[...].astype(jnp.bfloat16)
        out_send[step] = acc_out[...].astype(jnp.bfloat16).reshape(out_send.shape[1:])
        if step > 0:
            ds_copies.append(
                send(
                    ds_send.at[step - 1],
                    ds_recv.at[step - 1],
                    ds_sems.at[0, step - 1],
                    ds_sems.at[1, step - 1],
                    ctx_ids[step - 1],
                )
            )
        for copy in piece_copies(step):
            copy.start()

    ds_copies = []
    for step in range(n_ctx):
        chunk(step)
    grads_ref[...] = acc_grads[...].astype(jnp.bfloat16)
    grouter_ref[...] = acc_router[...].T[: grouter_ref.shape[0]]
    for copy in r_copies:
        copy.wait_send()
    for copy in ds_copies:
        copy.wait()
    for step in range(n_ctx):
        for copy in piece_copies(step):
            copy.wait()
    for at in range(n_ctx - 1):
        dsecond_ref[...] += ds_recv[at].astype(jnp.float32)
    for step in range(n_ctx):
        start = ctx_partner(ctx, step) * own_images
        for image in range(own_images):
            total = out_send[step, image, ctx].astype(jnp.float32)
            for at in range(n_ctx - 1):
                total += out_recv[ctx_partner(ctx, at + 1), start + image].astype(jnp.float32)
            out_ref[start + image] = total.astype(jnp.bfloat16)


def backward_kernel(
    n_exp,
    experts,
    x_ref,
    d_all,
    meta_all,
    first_ref,
    qkv_ref,
    lse_ref,
    att_ref,
    mid_ref,
    dsecond_ref,
    grads_ref,
    norm_ref,
    wqkv_ref,
    wproj_ref,
    dx_ref,
    shared_ref,
    gnorm_ref,
    gexp_ref,
    twin_recv,
    z_send,
    z_recv,
    dmid_ref,
    dbranch_ref,
    datt_ref,
    dqkv_ref,
    gqkv_ref,
    dx_send,
    dx_recv,
    t_sems,
    z_sems,
    f_sems,
    dx_sems,
):
    expert, ctx, dp = places()
    own_images, n_ctx, seq_dev, width = dx_send.shape
    seq = n_ctx * seq_dev
    ctx_ids = [(expert, ctx_partner(ctx, step), dp) for step in range(1, n_ctx)]
    z_steps = [1, n_exp - 1] + list(range(2, n_exp - 1))
    z_ids = [(z_partner(expert, step, n_exp), ctx, dp) for step in z_steps]
    twin = (expert, ctx, 1 - dp)
    greet(ctx_ids + z_ids + [twin])
    t_copy = send(grads_ref.at[1 - dp], twin_recv, t_sems.at[0], t_sems.at[1], twin)
    gain_one, gain_two = norm_ref[0:1], norm_ref[2:3]
    sums = [jnp.zeros((1, width), jnp.float32) for _ in range(4)]
    for image in range(own_images):
        rows = pl.ds(image * seq, seq)
        unit, scale = normalize(mid_ref[rows])
        grad = dsecond_ref[rows]
        sums[2] += jnp.sum(grad * unit, axis=0, keepdims=True)
        sums[3] += jnp.sum(grad, axis=0, keepdims=True)
        dmid = normalize_back(grad * gain_two, unit, scale) + d_all[ctx, rows].astype(jnp.float32)
        dmid_ref[rows] = dmid
        dbranch = dmid.astype(jnp.bfloat16)
        dbranch_ref[rows] = dbranch
        datt_ref[rows] = dot_nt(dbranch, wproj_ref[...]).astype(jnp.bfloat16)
    gproj = dot_tn(att_ref[...], dbranch_ref[...]).astype(jnp.bfloat16)
    part = width // n_ctx
    for place in range(n_ctx):
        shared_ref[place, :, 3 * part : 4 * part] = gproj[:, place * part : (place + 1) * part]
    t_copy.wait()
    for index in range(n_exp):
        z_send[index] = (
            grads_ref[dp, index].astype(jnp.float32) + twin_recv[index].astype(jnp.float32)
        ).astype(jnp.bfloat16)
    z_copies = [
        send(z_send.at[partner[0]], z_recv.at[at], z_sems.at[0, at], z_sems.at[1, at], partner)
        for at, partner in enumerate(z_ids)
    ]
    lane = lax.broadcasted_iota(jnp.int32, (seq, LANES), 1)
    low_half = lane < HEAD_DIM
    factor = HEAD_DIM**-0.5
    for image in range(own_images):
        rows = pl.ds(image * seq, seq)
        key_mask = group_rows(meta_all, ctx * own_images + image)[experts : experts + 1]
        bias = jnp.where(key_mask > 0, 0.0, NEG)
        totals = lse_ref[rows]
        for pair in range(HEADS // 2):
            at = pair * LANES
            query = qkv_ref[rows, at : at + LANES] * jnp.bfloat16(factor)
            keys = qkv_ref[rows, width + at : width + at + LANES]
            heads = qkv_ref[rows, 2 * width + at : 2 * width + at + LANES]
            datt = datt_ref[rows, at : at + LANES]
            dquery, dkeys, dheads = [], [], []
            for half in range(2):
                chosen = low_half if half == 0 else ~low_half
                scores = dot_nt(jnp.where(chosen, query, jnp.zeros_like(query)), keys) + bias
                head = 2 * pair + half
                weights = jnp.exp(scores - totals[:, head : head + 1])
                dprobs = dot_nt(jnp.where(chosen, datt, jnp.zeros_like(datt)), heads)
                delta = jnp.sum(weights * dprobs, axis=-1, keepdims=True)
                dscores = (weights * (dprobs - delta)).astype(jnp.bfloat16)
                dquery.append(dot(dscores, keys))
                dkeys.append(dot_tn(dscores, query))
                dheads.append(dot_tn(weights.astype(jnp.bfloat16), datt))
            dqkv_ref[rows, at : at + LANES] = (
                jnp.where(low_half, dquery[0], dquery[1]) * factor
            ).astype(jnp.bfloat16)
            dqkv_ref[rows, width + at : width + at + LANES] = jnp.where(
                low_half, dkeys[0], dkeys[1]
            ).astype(jnp.bfloat16)
            dqkv_ref[rows, 2 * width + at : 2 * width + at + LANES] = jnp.where(
                low_half, dheads[0], dheads[1]
            ).astype(jnp.bfloat16)
    for image in range(own_images):
        rows = pl.ds(image * seq, seq)
        grad = dot_nt(dqkv_ref[rows], wqkv_ref[...])
        unit, scale = normalize(x_ref[rows].astype(jnp.float32))
        sums[0] += jnp.sum(grad * unit, axis=0, keepdims=True)
        sums[1] += jnp.sum(grad, axis=0, keepdims=True)
        dx = dmid_ref[rows] + normalize_back(grad * gain_one, unit, scale)
        dx_send[image] = dx.astype(jnp.bfloat16).reshape(n_ctx, seq_dev, width)
    dx_copies = [
        send(
            dx_send.at[:, partner[1]],
            dx_recv.at[pl.ds(ctx * own_images, own_images)],
            dx_sems.at[0, at],
            dx_sems.at[1, at],
            partner,
        )
        for at, partner in enumerate(ctx_ids)
    ]
    for at, total in enumerate(sums):
        gnorm_ref[at : at + 1] = total
    gnorm_ref[4:8] = jnp.zeros((4, width), jnp.float32)
    gqkv_ref[...] = dot_tn(first_ref[...], dqkv_ref[...]).astype(jnp.bfloat16)
    for place in range(n_ctx):
        shared_ref[place, :, : 3 * part] = gqkv_ref[:, 3 * part * place : 3 * part * (place + 1)]
    for copy in z_copies:
        copy.wait()
    total = z_send[expert].astype(jnp.float32)
    for at in range(n_exp - 1):
        total += z_recv[at].astype(jnp.float32)
    gexp_ref[dp] = total.astype(jnp.bfloat16)
    f_copy = send(gexp_ref.at[dp], gexp_ref.at[dp], f_sems.at[0], f_sems.at[1], twin)
    for copy in dx_copies:
        copy.wait()
    for step in range(n_ctx):
        start = ctx_partner(ctx, step) * own_images
        for image in range(own_images):
            block = dx_send[image, ctx] if step == 0 else dx_recv[start + image]
            dx_ref[start + image] = block.astype(jnp.float32)
    f_copy.wait()


def orthogonal(gram_ref, mix_ref, total_ref, stage_waits):
    size = gram_ref.shape[0]
    eye = (
        lax.broadcasted_iota(jnp.int32, (size, size), 0)
        == lax.broadcasted_iota(jnp.int32, (size, size), 1)
    ).astype(jnp.float32)
    for turn in range(NS_ITERS):
        gram = gram_ref[...]
        mix_ref[...] = NS_A * eye + NS_B * gram + NS_C * dot(gram, gram, NS_PRECISION)
        if turn == 0:
            total_ref[...] = mix_ref[...]
        else:
            total_ref[...] = dot(mix_ref[...], total_ref[...], NS_PRECISION)
        if turn < NS_ITERS - 1:
            gram_ref[...] = dot(
                dot(mix_ref[...], gram_ref[...], NS_PRECISION), mix_ref[...], NS_PRECISION
            )
        stage_waits(turn)


def update_kernel(
    n_exp,
    experts,
    shared_ref,
    gnorm_ref,
    grouter_ref,
    gexp_ref,
    mexp_ref,
    mqkv_ref,
    mproj_ref,
    mnorm_ref,
    mrouter_ref,
    wexp_ref,
    wqkv_ref,
    wproj_ref,
    norm_ref,
    router_ref,
    o_gnorm,
    o_grouter,
    o_gqkv,
    o_gproj,
    o_gin,
    o_gout,
    o_mnorm,
    o_mrouter,
    o_mqkv,
    o_mproj,
    o_min,
    o_mout,
    o_nnorm,
    o_nrouter,
    o_nqkv,
    o_nproj,
    o_nin,
    o_nout,
    o_bqkv,
    o_bproj,
    o_bin,
    o_bout,
    small_ref,
    small_twin,
    small_ctx,
    small_z,
    half_recv,
    sum_one,
    ctx_recv,
    sum_two,
    z_all,
    whole_ref,
    mat_ref,
    gram_send,
    gram_recv,
    gram_ref,
    mix_ref,
    total_ref,
    step_ref,
    norm_send,
    norm_recv,
    t_sems,
    c_sems,
    z_sems,
    f_sems,
    g_sems,
    x_sems,
):
    expert, ctx, dp = places()
    n_ctx, width, part = shared_ref.shape
    half = width // 2
    cols = part // 4
    ctx_ids = [(expert, ctx_partner(ctx, step), dp) for step in range(1, n_ctx)]
    z_steps = [1, n_exp - 1] + list(range(2, n_exp - 1))
    z_ids = [(z_partner(expert, step, n_exp), ctx, dp) for step in z_steps]
    twin = (expert, ctx, 1 - dp)
    greet(ctx_ids + z_ids + [twin])
    own_half = pl.ds(pl.multiple_of(dp * half, half), half)
    other_half = pl.ds(pl.multiple_of((1 - dp) * half, half), half)
    small_ref[0:8] = gnorm_ref[...]
    small_ref[8:16] = grouter_ref[...]
    one = [
        send(shared_ref.at[:, other_half], half_recv, t_sems.at[0, 0], t_sems.at[1, 0], twin),
        send(small_ref, small_twin, t_sems.at[0, 1], t_sems.at[1, 1], twin),
    ]

    def gram_of(which, matrix):
        low = matrix.astype(jnp.bfloat16)
        gram_send[which] = dot_nt(low, low).astype(jnp.bfloat16)
        return [
            send(
                gram_send.at[which],
                gram_recv.at[which, at],
                g_sems.at[0, which, at],
                g_sems.at[1, which, at],
                partner,
            )
            for at, partner in enumerate(ctx_ids)
        ]

    def gram_total(which, copies):
        for copy in copies:
            copy.wait()
        total = gram_send[which].astype(jnp.float32)
        for at in range(n_ctx - 1):
            total += gram_recv[which, at].astype(jnp.float32)
        size = total.shape[0]
        diagonal = lax.broadcasted_iota(jnp.int32, (size, size), 0) == lax.broadcasted_iota(
            jnp.int32, (size, size), 1
        )
        square = jnp.sum(jnp.where(diagonal, total, 0.0), keepdims=True)
        scale = 1.0 / (jnp.sqrt(square) + EPS_ORTHO)
        gram_ref[...] = total * (scale * scale)
        return scale

    def step_of(which, matrix, scale):
        cut = pl.ds(0, matrix.shape[1])
        step_ref[which, dp, :, cut] = (
            dot(total_ref[...].astype(jnp.bfloat16), (matrix * scale).astype(jnp.bfloat16))
        ).astype(jnp.bfloat16)
        return send(
            step_ref.at[which, dp, :, cut],
            step_ref.at[which, dp, :, cut],
            x_sems.at[0, which],
            x_sems.at[1, which],
            twin,
        )

    for index, (o_g, o_m) in enumerate(((o_gin, o_min), (o_gout, o_mout))):
        grad = gexp_ref[index].astype(jnp.float32)
        o_g[0] = grad
        fresh = DECAY * mexp_ref[index] + grad
        o_m[0] = fresh
        mat_ref[index] = fresh
    exp_copies = gram_of(0, mat_ref[dp])
    for copy in one:
        copy.wait()
    small_ref[...] += small_twin[...]
    for place in range(n_ctx):
        sum_one[place] = (
            shared_ref[place, own_half].astype(jnp.float32) + half_recv[place].astype(jnp.float32)
        ).astype(jnp.bfloat16)
    small_ctx[ctx] = small_ref[...]
    two = [
        send(sum_one.at[partner[1]], ctx_recv.at[at], c_sems.at[0, 0, at], c_sems.at[1, 0, at], partner)
        for at, partner in enumerate(ctx_ids)
    ] + [
        send(small_ref, small_ctx.at[ctx], c_sems.at[0, 1, at], c_sems.at[1, 1, at], partner)
        for at, partner in enumerate(ctx_ids)
    ]
    exp_scale = gram_total(0, exp_copies)
    later = []

    def stages(turn):
        if turn == 0:
            for copy in two:
                copy.wait()
            total = sum_one[ctx].astype(jnp.float32)
            for at in range(n_ctx - 1):
                total += ctx_recv[at].astype(jnp.float32)
            z_all[expert] = total.astype(jnp.bfloat16)
            small = small_ctx[0]
            for place in range(1, n_ctx):
                small += small_ctx[place]
            small_z[expert] = small
            later.append(
                [
                    send(
                        z_all.at[expert],
                        z_all.at[expert],
                        z_sems.at[0, 0, at],
                        z_sems.at[1, 0, at],
                        partner,
                    )
                    for at, partner in enumerate(z_ids)
                ]
                + [
                    send(
                        small_z.at[expert],
                        small_z.at[expert],
                        z_sems.at[0, 1, at],
                        z_sems.at[1, 1, at],
                        partner,
                    )
                    for at, partner in enumerate(z_ids)
                ]
            )
        if turn == 2:
            for copy in later[0]:
                copy.wait()
            total = z_all[0].astype(jnp.float32)
            for place in range(1, n_exp):
                total += z_all[place].astype(jnp.float32)
            whole_ref[own_half] = total.astype(jnp.bfloat16)
            later.append(
                send(whole_ref.at[own_half], whole_ref.at[own_half], f_sems.at[0], f_sems.at[1], twin)
            )

    orthogonal(gram_ref, mix_ref, total_ref, stages)
    exp_step = step_of(0, mat_ref[dp], exp_scale)
    later[1].wait()
    grad = whole_ref[...].astype(jnp.float32)
    o_gqkv[...] = grad[:, : 3 * cols]
    o_gproj[...] = grad[:, 3 * cols :]
    fresh_qkv = DECAY * mqkv_ref[...] + grad[:, : 3 * cols]
    fresh_proj = DECAY * mproj_ref[...] + grad[:, 3 * cols :]
    o_mqkv[...] = fresh_qkv
    o_mproj[...] = fresh_proj
    mat_ref[2, :, : 3 * cols] = fresh_qkv
    mat_ref[3, :, :cols] = fresh_proj
    mat_ref[3, :, cols : 3 * cols] = jnp.zeros((width, 2 * cols), jnp.float32)
    small = small_z[0]
    for place in range(1, n_exp):
        small += small_z[place]
    small_ref[...] = small
    lane_part = pl.ds(pl.multiple_of(ctx * cols, cols), cols)
    own_norm = small_ref[0:4, lane_part]
    own_router = small_ref[pl.ds(8 + ctx, 1)]
    fresh_norm = DECAY * mnorm_ref[...] + own_norm
    fresh_router = DECAY * mrouter_ref[...] + own_router
    o_gnorm[...] = own_norm
    o_grouter[...] = own_router
    o_mnorm[...] = fresh_norm
    o_mrouter[...] = fresh_router
    row = lax.broadcasted_iota(jnp.int32, (8, LANES), 0)
    norm_send[...] = jnp.where(
        row == 0,
        jnp.sum(fresh_norm * fresh_norm, keepdims=True),
        jnp.sum(fresh_router * fresh_router, keepdims=True),
    )
    norm_recv[ctx] = norm_send[...]
    norm_copies = [
        send(norm_send, norm_recv.at[ctx], c_sems.at[0, 2, at], c_sems.at[1, 2, at], partner)
        for at, partner in enumerate(ctx_ids)
    ]
    own_matrix = mat_ref[2 + dp, :, : 3 * cols]
    shared_copies = gram_of(1, own_matrix)
    exp_step.wait()
    rate = RATE_MAT * 0.2 * math.sqrt(max(width, part * n_ctx))
    for index, (o_n, o_b) in enumerate(((o_nin, o_bin), (o_nout, o_bout))):
        new = wexp_ref[index].astype(jnp.float32) - rate * step_ref[0, index].astype(jnp.float32)
        o_n[0] = new
        o_b[0] = new.astype(jnp.bfloat16)
    for copy in norm_copies:
        copy.wait()
    squares = norm_recv[0]
    for place in range(1, n_ctx):
        squares += norm_recv[place]
    o_nnorm[...] = norm_ref[:, lane_part] - RATE_GAIN * fresh_norm * lax.rsqrt(
        squares[0:1] / (4 * width) + EPS_NORM
    )
    o_nrouter[...] = router_ref[...] - RATE_ROUTER * fresh_router * lax.rsqrt(
        squares[1:2, 0:1] / (width * experts) + EPS_NORM
    )
    shared_scale = gram_total(1, shared_copies)
    orthogonal(gram_ref, mix_ref, total_ref, lambda turn: None)
    shared_step = step_of(1, own_matrix, shared_scale)
    shared_step.wait()
    rate = RATE_MAT * 0.2 * math.sqrt(max(width, 3 * cols * n_ctx))
    new = wqkv_ref[:, pl.ds(pl.multiple_of(ctx * 3 * cols, 3 * cols), 3 * cols)].astype(
        jnp.float32
    ) - rate * step_ref[1, 0, :, : 3 * cols].astype(jnp.float32)
    o_nqkv[...] = new
    o_bqkv[...] = new.astype(jnp.bfloat16)
    rate = RATE_MAT * 0.2 * math.sqrt(max(width, cols * n_ctx))
    new = wproj_ref[:, lane_part].astype(jnp.float32) - rate * step_ref[1, 1, :, :cols].astype(
        jnp.float32
    )
    o_nproj[...] = new
    o_bproj[...] = new.astype(jnp.bfloat16)


def call(kernel, ident, outs, scratch, operands, flops=0):
    spec = pl.BlockSpec(memory_space=pltpu.VMEM)
    return pl.pallas_call(
        kernel,
        out_shape=[jax.ShapeDtypeStruct(shape, dtype) for shape, dtype in outs],
        in_specs=[spec] * len(operands),
        out_specs=[spec] * len(outs),
        scratch_shapes=scratch,
        cost_estimate=pl.CostEstimate(flops=flops, bytes_accessed=2**22, transcendentals=0),
        compiler_params=pltpu.CompilerParams(
            collective_id=ident, has_side_effects=True, vmem_limit_bytes=VMEM_LIMIT
        ),
    )(*operands)


def gathered(
    x_in,
    d_out,
    key_mask,
    expert_ids,
    norm_params,
    w_qkv,
    w_proj,
    w_router,
    w_in,
    w_out,
    mom_norm,
    mom_router,
    mom_qkv,
    mom_proj,
    mom_in,
    mom_out,
):
    n_exp = lax.axis_size("expert")
    n_ctx = lax.axis_size("ctx")
    ctx = lax.axis_index("ctx")
    images, seq_dev, width = x_in.shape
    experts = w_router.shape[1]
    own_images = images // n_ctx
    seq = n_ctx * seq_dev
    rows = own_images * seq
    hid = w_in.shape[2]
    low, full = jnp.bfloat16, jnp.float32
    dma = lambda *shape: pltpu.SemaphoreType.DMA(shape)
    vmem = lambda shape, dtype: pltpu.VMEM(shape, dtype)

    present = jnp.any(
        expert_ids[..., None] == jnp.arange(experts, dtype=jnp.int32), axis=2
    ).astype(full)
    meta = jnp.concatenate(
        [present, key_mask[..., None].astype(full), jnp.zeros((images, seq_dev, 7 - experts), full)],
        axis=-1,
    ).swapaxes(1, 2)
    odd = (ctx % 2).astype(full)
    meta = jnp.concatenate([meta * (1 - odd), meta * odd], axis=-1)
    weights = jnp.stack([w_in[0], w_out[0]])
    router = jnp.pad(w_router, ((0, 0), (0, LANES - experts)))
    router_high = router.astype(low)
    router_two = jnp.stack([router_high, (router - router_high.astype(full)).astype(low)])

    x_all, d_all, meta_all, w_all, first, qkv, lse, att, mid, routed = call(
        functools.partial(forward_kernel, n_exp, experts),
        1,
        [
            ((own_images, n_ctx, seq_dev, width), low),
            ((images, n_ctx, seq_dev, width), low),
            ((n_ctx,) + meta.shape, full),
            ((2, n_exp, width, hid), low),
            ((rows, width), low),
            ((rows, 3 * width), low),
            ((rows, LANES), full),
            ((rows, width), low),
            ((rows, width), full),
            ((rows, width), low),
        ],
        [dma(n_ctx - 1)] * 6 + [dma(n_exp - 1)] * 4 + [dma(4)],
        (x_in, d_out, meta, weights, norm_params, w_qkv, w_proj),
    )
    d_all = d_all.reshape(n_ctx, rows, width)
    block_out, dsecond, grads, grouter = call(
        functools.partial(expert_kernel, experts),
        2,
        [
            ((images, seq_dev, width), low),
            ((rows, width), full),
            ((2, n_exp, width, hid), low),
            ((8, width), full),
        ],
        [
            vmem((n_ctx, rows, width), low),
            vmem((n_ctx, own_images, n_ctx, seq_dev, width), low),
            vmem((n_ctx, images, seq_dev, width), low),
            vmem((n_ctx - 1, rows, width), low),
            vmem((n_ctx - 1, rows, width), low),
            vmem((rows, width), full),
            vmem((rows, width), full),
            vmem((2, n_exp, width, hid), full),
            vmem((width, LANES), full),
            vmem((rows, LANES), full),
            vmem((rows, LANES), full),
            vmem((width, rows), low),
            vmem((width, rows), low),
            dma(2, n_ctx - 1),
            dma(2, n_ctx - 1),
            dma(2, n_ctx, n_ctx - 1),
        ],
        (routed, d_all, meta_all, w_all, router_two, mid),
    )
    d_x, shared, gnorm, gexp = call(
        functools.partial(backward_kernel, n_exp, experts),
        3,
        [
            ((images, seq_dev, width), full),
            ((n_ctx, width, width), low),
            ((8, width), full),
            ((2, width, hid), low),
        ],
        [
            vmem((n_exp, width, hid), low),
            vmem((n_exp, width, hid), low),
            vmem((n_exp - 1, width, hid), low),
            vmem((rows, width), full),
            vmem((rows, width), low),
            vmem((rows, width), low),
            vmem((rows, 3 * width), low),
            vmem((width, 3 * width), low),
            vmem((own_images, n_ctx, seq_dev, width), low),
            vmem((images, seq_dev, width), low),
            dma(2),
            dma(2, n_exp - 1),
            dma(2),
            dma(2, n_ctx - 1),
        ],
        (
            x_all.reshape(rows, width),
            d_all,
            meta_all,
            first,
            qkv,
            lse,
            att,
            mid,
            dsecond,
            grads,
            norm_params,
            w_qkv,
            w_proj,
        ),
    )
    cols = width // n_ctx
    own_router = lax.dynamic_slice_in_dim(w_router, ctx, 1, 1).reshape(1, width)
    pieces = ((4, cols), (1, width), (width, 3 * cols), (width, cols), (1, width, hid), (1, width, hid))
    results = call(
        functools.partial(update_kernel, n_exp, experts),
        4,
        [(piece, full) for piece in pieces * 3] + [(piece, low) for piece in pieces[2:]],
        [
            vmem((16, width), full),
            vmem((16, width), full),
            vmem((n_ctx, 16, width), full),
            vmem((n_exp, 16, width), full),
            vmem((n_ctx, width // 2, width), low),
            vmem((n_ctx, width // 2, width), low),
            vmem((n_ctx - 1, width // 2, width), low),
            vmem((8, LANES), full),
            vmem((n_exp, width // 2, width), low),
            vmem((width, width), low),
            vmem((4, width, hid), full),
            vmem((2, width, width), low),
            vmem((2, n_ctx - 1, width, width), low),
            vmem((width, width), full),
            vmem((width, width), full),
            vmem((width, width), full),
            vmem((2, 2, width, hid), low),
            vmem((8, LANES), full),
            vmem((n_ctx, 8, LANES), full),
            dma(2, 2),
            dma(2, 3, n_ctx - 1),
            dma(2, 2, n_exp - 1),
            dma(2),
            dma(2, 2, n_ctx - 1),
            dma(2, 2),
        ],
        (
            shared,
            gnorm,
            grouter,
            gexp,
            jnp.stack([mom_in[0], mom_out[0]]),
            mom_qkv,
            mom_proj,
            mom_norm,
            mom_router.reshape(1, width),
            weights,
            w_qkv,
            w_proj,
            norm_params,
            own_router,
        ),
    )
    results = [
        value.reshape(width, 1) if value.shape == (1, width) else value for value in results
    ]
    return (block_out, d_x, *results)


def solution(mesh):
    in_specs = (
        P(("expert", "dp"), "ctx", None),
        P(("expert", "dp"), "ctx", None),
        P(("expert", "dp"), "ctx"),
        P(("expert", "dp"), "ctx", None),
        P(),
        P(),
        P(),
        P(),
        P("expert", None, "ctx"),
        P("expert", None, "ctx"),
        P(None, "ctx"),
        P(None, "ctx"),
        P(None, "ctx"),
        P(None, "ctx"),
        P("expert", None, "ctx"),
        P("expert", None, "ctx"),
    )
    out_specs = (
        P(("expert", "dp"), "ctx", None),
        P(("expert", "dp"), "ctx", None),
        P(None, "ctx"),
        P(None, "ctx"),
        P(None, "ctx"),
        P(None, "ctx"),
        P("expert", None, "ctx"),
        P("expert", None, "ctx"),
        P(None, "ctx"),
        P(None, "ctx"),
        P(None, "ctx"),
        P(None, "ctx"),
        P("expert", None, "ctx"),
        P("expert", None, "ctx"),
        P(None, "ctx"),
        P(None, "ctx"),
        P(None, "ctx"),
        P(None, "ctx"),
        P("expert", None, "ctx"),
        P("expert", None, "ctx"),
        P(None, "ctx"),
        P(None, "ctx"),
        P("expert", None, "ctx"),
        P("expert", None, "ctx"),
    )
    experts = mesh.shape["expert"]
    square = mesh.shape["ctx"] == 4 and mesh.shape["dp"] == 2

    def local(*arrays):
        whole = (
            square
            and arrays[7].shape[1] == experts <= 7
            and arrays[8].shape[0] == 1
            and 2 * arrays[0].shape[1] == LANES
        )
        return (gathered if whole else exchanged)(*arrays)

    return jax.shard_map(local, mesh=mesh, in_specs=in_specs, out_specs=out_specs, check_vma=False)
```

```python
import functools
import math

import jax
import jax.numpy as jnp
from jax import lax
from jax.experimental import pallas as pl
from jax.experimental.pallas import tpu as pltpu
from jax.sharding import PartitionSpec as P

HEADS = 8
HEAD_DIM = 64
MICRO = 2
NS_ITERS = 4


HIGH = lax.Precision.HIGHEST
NS_A = 3.4445
NS_B = -4.775
NS_C = 2.0315
DECAY = 0.5
RATE_MAT = 0.3
RATE_GAIN = 0.3
RATE_ROUTER = 0.05
EPS_NORM = 1e-06
EPS_ORTHO = 1e-07
NEG = -1e30
LANES = 128
VMEM_LIMIT = 60 * 2**20
MESH = pl.DeviceIdType.MESH


def as_sent(array):
    return jax.tree.map(lambda a: a.astype(jnp.bfloat16) if a.dtype == jnp.float32 else a, array)


def layer_norm(values, gain, shift):
    center = jnp.mean(values, axis=-1, keepdims=True)
    spread = values - center
    power = jnp.mean(spread * spread, axis=-1, keepdims=True)
    return spread * lax.rsqrt(power + EPS_NORM) * gain + shift


def gelu_exact(values):
    return jax.nn.gelu(values, approximate=False)


def add_block(total, piece):
    return total + piece


def masked_scores(query, key_piece, mask_piece, factor):
    scores = (
        jnp.einsum("bqhd,bkhd->bhqk", query, key_piece, preferred_element_type=jnp.float32) * factor
    )
    return jnp.where(mask_piece[:, None, None, :] > 0, scores, NEG)


def gram_list(matrices):
    return tuple(
        (jnp.einsum("...ik,...jk->...ij", matrix, matrix, precision=HIGH) for matrix in matrices)
    )


def schulz_turn(matrices, grams):
    result = []
    for matrix, gram in zip(matrices, grams):
        square = jnp.einsum("...ij,...jk->...ik", gram, gram, precision=HIGH)
        mixer = NS_B * gram + NS_C * square
        result.append(
            NS_A * matrix + jnp.einsum("...ij,...jk->...ik", mixer, matrix, precision=HIGH)
        )
    return tuple(result)


def exchanged(
    x_in,
    d_out,
    key_mask,
    expert_ids,
    norm_params,
    w_qkv,
    w_proj,
    w_router,
    w_in,
    w_out,
    mom_norm,
    mom_router,
    mom_qkv,
    mom_proj,
    mom_in,
    mom_out,
):
    ctx_count = lax.axis_size("ctx")
    ctx_place = lax.axis_index("ctx")
    owner_count = lax.axis_size("expert")
    local_images = x_in.shape[0]
    seq_dev = x_in.shape[1]
    width = x_in.shape[2]
    top_count = expert_ids.shape[-1]
    experts = w_router.shape[1]
    exp_dev = w_in.shape[0]
    hid_part = w_in.shape[2]
    capacity = max(2, (5 * top_count * seq_dev + 4 * experts - 1) // (4 * experts))
    batch = local_images // MICRO
    slot_count = batch * capacity
    seq_all = seq_dev * ctx_count
    factor = HEAD_DIM ** (-0.5)
    expert_iota = jnp.arange(experts, dtype=jnp.int32)
    recv_shape = (owner_count, exp_dev, slot_count, width)
    head_shape = (batch, seq_dev, HEADS, HEAD_DIM)

    def hidden_fold(step_fn, init):
        folded = step_fn(
            init,
            (
                lax.all_gather(w_in, "ctx", axis=2, tiled=True),
                lax.all_gather(w_out, "ctx", axis=2, tiled=True),
            ),
            jnp.int32(0),
        )
        return folded

    def to_owner(rows):
        return lax.all_to_all(rows, "expert", split_axis=0, concat_axis=0, tiled=True)

    def to_source(rows):
        return lax.all_to_all(rows, "expert", split_axis=0, concat_axis=0, tiled=True)

    def key_fold(keys, values, mask_low, step_fn, init):
        return step_fn(
            init,
            (
                lax.all_gather(keys, "ctx", axis=1, tiled=True),
                lax.all_gather(values, "ctx", axis=1, tiled=True),
                lax.all_gather(mask_low, "ctx", axis=1, tiled=True),
            ),
            jnp.int32(0),
        )

    grad_qkv = jnp.zeros(w_qkv.shape, jnp.float32)
    grad_proj = jnp.zeros(w_proj.shape, jnp.float32)
    grad_router = jnp.zeros(w_router.shape, jnp.float32)
    grad_norm = jnp.zeros((4, width), jnp.float32)
    grad_in = jnp.zeros((exp_dev, width, hid_part * ctx_count), jnp.float32)
    grad_out = jnp.zeros((exp_dev, width, hid_part * ctx_count), jnp.float32)
    outputs = []
    input_grads = []
    for micro_index in range(MICRO):
        first_image = micro_index * batch
        last_image = first_image + batch
        x_part = x_in[first_image:last_image].astype(jnp.float32)
        cotangent = d_out[first_image:last_image].astype(jnp.float32)
        mask_low = key_mask[first_image:last_image].astype(jnp.bfloat16)
        idents = expert_ids[first_image:last_image]
        normed_first, pull_first = jax.vjp(layer_norm, x_part, norm_params[0], norm_params[1])
        first_low = normed_first.astype(jnp.bfloat16).reshape(-1, width)
        qkv = jnp.dot(first_low, w_qkv, preferred_element_type=jnp.float32).astype(jnp.bfloat16)
        qkv = qkv.reshape(batch, seq_dev, 3, HEADS, HEAD_DIM)
        query = qkv[:, :, 0]
        keys = qkv[:, :, 1]
        values = qkv[:, :, 2]
        peak_old = jnp.full((batch, HEADS, seq_dev), NEG, jnp.float32)
        key_piece = lax.all_gather(keys, "ctx", axis=1, tiled=True)
        mask_piece = lax.all_gather(mask_low, "ctx", axis=1, tiled=True)
        scores = masked_scores(query, key_piece, mask_piece, factor)
        peak_new = jnp.maximum(peak_old, jnp.max(scores, axis=-1))
        total_new = jnp.sum(jnp.exp(scores - peak_new[..., None]), axis=-1)
        log_total = peak_new + jnp.log(total_new)

        def attend_step(acc, pieces, start):
            key_piece, value_piece, mask_piece = pieces
            weights = jnp.exp(
                masked_scores(query, key_piece, mask_piece, factor) - log_total[..., None]
            )
            return jnp.einsum(
                "bhqk,bkhd->bqhd",
                weights.astype(jnp.bfloat16),
                value_piece,
                preferred_element_type=jnp.float32,
            )

        attended = key_fold(keys, values, mask_low, attend_step, jnp.zeros(head_shape, jnp.float32))
        attended_low = attended.astype(jnp.bfloat16).reshape(-1, width)
        branch = jnp.dot(attended_low, w_proj, preferred_element_type=jnp.float32).reshape(
            batch, seq_dev, width
        )
        mid = x_part + branch
        normed_second, pull_second = jax.vjp(layer_norm, mid, norm_params[2], norm_params[3])
        routed_low = normed_second.astype(jnp.bfloat16)
        logits = jnp.einsum("bsd,de->bse", normed_second, w_router, precision=HIGH)
        onehot = (idents[..., None] == expert_iota).astype(jnp.float32)
        chosen = jnp.sum(onehot * logits[:, :, None, :], axis=-1)
        gates = jax.nn.softmax(chosen, axis=-1)
        flat_ids = idents.reshape(batch, seq_dev * top_count)
        hits = (flat_ids[..., None] == expert_iota).astype(jnp.int32)
        ranked = jnp.sum((jnp.cumsum(hits, axis=1) - hits) * hits, axis=-1)
        slot = (ranked + (jnp.arange(batch, dtype=jnp.int32) * capacity)[:, None]).reshape(-1)
        target = flat_ids.reshape(-1)
        routed_rows = jnp.broadcast_to(
            routed_low[:, :, None, :], (batch, seq_dev, top_count, width)
        ).reshape(-1, width)
        send = (
            jnp.zeros((experts, slot_count, width), jnp.bfloat16).at[target, slot].set(routed_rows)
        )
        received = to_owner(send.reshape(recv_shape))

        def expert_step(acc, pieces, start):
            piece_in, piece_out = pieces
            pre = jnp.einsum(
                "nesd,edh->nesh", received, piece_in, preferred_element_type=jnp.float32
            )
            act = gelu_exact(pre).astype(jnp.bfloat16)
            return jnp.einsum("nesh,edh->nesd", act, piece_out, preferred_element_type=jnp.float32)

        made = hidden_fold(expert_step, jnp.zeros(recv_shape, jnp.float32))
        back_rows = to_source(made.astype(jnp.bfloat16)).reshape(experts, slot_count, width)
        returned = (
            back_rows[target, slot].reshape(batch, seq_dev, top_count, width).astype(jnp.float32)
        )
        result = mid + jnp.sum(gates[..., None] * returned, axis=2)
        outputs.append(result.astype(jnp.bfloat16))
        dgates = jnp.sum(cotangent[:, :, None, :] * returned, axis=-1)
        dchosen = gates * (dgates - jnp.sum(gates * dgates, axis=-1, keepdims=True))
        dlogits = jnp.sum(dchosen[..., None] * onehot, axis=2)
        grad_router = grad_router + jnp.einsum(
            "bsd,bse->de", normed_second, dlogits, precision=HIGH
        )
        dsecond = jnp.einsum("bse,de->bsd", dlogits, w_router, precision=HIGH)
        dreturned = (
            (gates[..., None] * cotangent[:, :, None, :]).astype(jnp.bfloat16).reshape(-1, width)
        )
        dsend = (
            jnp.zeros((experts, slot_count, width), jnp.bfloat16).at[target, slot].set(dreturned)
        )
        dreceived = to_owner(dsend.reshape(recv_shape))

        def expert_back(carry, pieces, start):
            drows, dins, douts = carry
            piece_in, piece_out = pieces
            pre = jnp.einsum(
                "nesd,edh->nesh", received, piece_in, preferred_element_type=jnp.float32
            )
            act_full, pull_act = jax.vjp(gelu_exact, pre)
            act = act_full.astype(jnp.bfloat16)
            dact = jnp.einsum(
                "nesd,edh->nesh", dreceived, piece_out, preferred_element_type=jnp.float32
            )
            dpre = pull_act(dact)[0].astype(jnp.bfloat16)
            douts = add_block(
                douts,
                jnp.einsum("nesd,nesh->edh", dreceived, act, preferred_element_type=jnp.float32),
            )
            dins = add_block(
                dins,
                jnp.einsum("nesd,nesh->edh", received, dpre, preferred_element_type=jnp.float32),
            )
            drows = jnp.einsum("nesh,edh->nesd", dpre, piece_in, preferred_element_type=jnp.float32)
            return (drows, dins, douts)

        drows, grad_in, grad_out = hidden_fold(
            expert_back, (jnp.zeros(recv_shape, jnp.float32), grad_in, grad_out)
        )
        dback = to_source(drows.astype(jnp.bfloat16)).reshape(experts, slot_count, width)
        dsecond = dsecond + jnp.sum(
            dback[target, slot].reshape(batch, seq_dev, top_count, width).astype(jnp.float32),
            axis=2,
        )
        dmid, dgain_two, dshift_two = pull_second(dsecond)
        dmid = dmid + cotangent
        dbranch = dmid.astype(jnp.bfloat16).reshape(-1, width)
        grad_proj = grad_proj + jnp.einsum(
            "sd,se->de", attended_low, dbranch, preferred_element_type=jnp.float32
        )
        dattended = jnp.einsum("se,de->sd", dbranch, w_proj, preferred_element_type=jnp.float32)
        dattended = dattended.astype(jnp.bfloat16).reshape(head_shape)
        delta = jnp.einsum("bqhd,bqhd->bhq", dattended.astype(jnp.float32), attended)

        def attend_back(carry, pieces, start):
            dquery, dkeys, dvalues = carry
            key_piece, value_piece, mask_piece = pieces
            weights = jnp.exp(
                masked_scores(query, key_piece, mask_piece, factor) - log_total[..., None]
            )
            probs = weights.astype(jnp.bfloat16)
            dvalue_piece = jnp.einsum(
                "bhqk,bqhd->bkhd", probs, dattended, preferred_element_type=jnp.float32
            )
            dprobs = jnp.einsum(
                "bqhd,bkhd->bhqk", dattended, value_piece, preferred_element_type=jnp.float32
            )
            dscores = (weights * (dprobs - delta[..., None])).astype(jnp.bfloat16)
            dquery = factor * jnp.einsum(
                "bhqk,bkhd->bqhd", dscores, key_piece, preferred_element_type=jnp.float32
            )
            dkey_piece = factor * jnp.einsum(
                "bhqk,bqhd->bkhd", dscores, query, preferred_element_type=jnp.float32
            )
            return (dquery, add_block(dkeys, dkey_piece), add_block(dvalues, dvalue_piece))

        all_shape = (batch, seq_all, HEADS, HEAD_DIM)
        back_init = (
            jnp.zeros(head_shape, jnp.float32),
            jnp.zeros(all_shape, jnp.float32),
            jnp.zeros(all_shape, jnp.float32),
        )
        dquery, dkeys_all, dvalues_all = key_fold(keys, values, mask_low, attend_back, back_init)
        dkeys, dvalues = (
            lax.psum_scatter(
                dkeys_all.astype(jnp.bfloat16), "ctx", scatter_dimension=1, tiled=True
            ).astype(jnp.float32),
            lax.psum_scatter(
                dvalues_all.astype(jnp.bfloat16), "ctx", scatter_dimension=1, tiled=True
            ).astype(jnp.float32),
        )
        dqkv = (
            jnp.stack([dquery, dkeys, dvalues], axis=2).astype(jnp.bfloat16).reshape(-1, 3 * width)
        )
        grad_qkv = grad_qkv + jnp.einsum(
            "sd,se->de", first_low, dqkv, preferred_element_type=jnp.float32
        )
        dfirst = jnp.einsum("se,de->sd", dqkv, w_qkv, preferred_element_type=jnp.float32).reshape(
            batch, seq_dev, width
        )
        dx_part, dgain_one, dshift_one = pull_first(dfirst)
        grad_norm = grad_norm + jnp.stack([dgain_one, dshift_one, dgain_two, dshift_two])
        input_grads.append(dx_part + dmid)
    block_out = jnp.concatenate(outputs, axis=0)
    d_x = jnp.concatenate(input_grads, axis=0)
    shared = (
        lax.psum_scatter(
            grad_in.astype(jnp.bfloat16), "ctx", scatter_dimension=2, tiled=True
        ).astype(jnp.float32),
        lax.psum_scatter(
            grad_out.astype(jnp.bfloat16), "ctx", scatter_dimension=2, tiled=True
        ).astype(jnp.float32),
        lax.psum_scatter(
            grad_qkv[None].astype(jnp.bfloat16), "ctx", scatter_dimension=2, tiled=True
        ).astype(jnp.float32),
        lax.psum_scatter(
            grad_proj[None].astype(jnp.bfloat16), "ctx", scatter_dimension=2, tiled=True
        ).astype(jnp.float32),
        lax.psum_scatter(
            grad_norm[None].astype(jnp.bfloat16), "ctx", scatter_dimension=2, tiled=True
        ).astype(jnp.float32),
        lax.psum_scatter(
            grad_router[None].astype(jnp.bfloat16), "ctx", scatter_dimension=2, tiled=True
        ).astype(jnp.float32),
    )
    g_in, g_out = (
        lax.psum(shared[0].astype(jnp.bfloat16), "dp").astype(jnp.float32),
        lax.psum(shared[1].astype(jnp.bfloat16), "dp").astype(jnp.float32),
    )
    g_qkv, g_proj, g_norm, g_router = lax.psum(
        (shared[2][0], shared[3][0], shared[4][0], shared[5][0]), ("expert", "dp")
    )
    own_qkv = lax.dynamic_slice_in_dim(w_qkv, ctx_place * g_qkv.shape[1], g_qkv.shape[1], 1).astype(
        jnp.float32
    )
    own_proj = lax.dynamic_slice_in_dim(
        w_proj, ctx_place * g_proj.shape[1], g_proj.shape[1], 1
    ).astype(jnp.float32)
    own_norm = lax.dynamic_slice_in_dim(
        norm_params, ctx_place * g_norm.shape[1], g_norm.shape[1], 1
    )
    own_router = lax.dynamic_slice_in_dim(
        w_router, ctx_place * g_router.shape[1], g_router.shape[1], 1
    )
    m_qkv = DECAY * mom_qkv + g_qkv
    m_proj = DECAY * mom_proj + g_proj
    m_in = DECAY * mom_in + g_in
    m_out = DECAY * mom_out + g_out
    m_norm = DECAY * mom_norm + g_norm
    m_router = DECAY * mom_router + g_router
    matrices = (m_qkv, m_proj, m_in, m_out)
    vector_squares = (jnp.sum(m_norm * m_norm), jnp.sum(m_router * m_router))
    sums = lax.psum(
        tuple((jnp.sum(matrix * matrix, axis=(-2, -1)) for matrix in matrices)) + vector_squares,
        "ctx",
    )
    vector_totals = sums[4:]
    iterates = tuple(
        (
            matrix / jnp.expand_dims(jnp.sqrt(square) + EPS_ORTHO, (-2, -1))
            for matrix, square in zip(matrices, sums[:4])
        )
    )
    for turn_index in range(NS_ITERS):
        iterates = schulz_turn(
            iterates,
            jax.tree.map(
                lambda part: part.astype(jnp.float32), lax.psum(as_sent(gram_list(iterates)), "ctx")
            ),
        )
    n_qkv = (
        own_qkv - RATE_MAT * 0.2 * math.sqrt(max(width, g_qkv.shape[1] * ctx_count)) * iterates[0]
    )
    n_proj = (
        own_proj - RATE_MAT * 0.2 * math.sqrt(max(width, g_proj.shape[1] * ctx_count)) * iterates[1]
    )
    n_in = (
        w_in.astype(jnp.float32)
        - RATE_MAT * 0.2 * math.sqrt(max(width, hid_part * ctx_count)) * iterates[2]
    )
    n_out = (
        w_out.astype(jnp.float32)
        - RATE_MAT * 0.2 * math.sqrt(max(width, hid_part * ctx_count)) * iterates[3]
    )
    n_norm = own_norm - RATE_GAIN * m_norm * lax.rsqrt(vector_totals[0] / (4 * width) + EPS_NORM)
    n_router = own_router - RATE_ROUTER * m_router * lax.rsqrt(
        vector_totals[1] / (width * experts) + EPS_NORM
    )
    return (
        block_out,
        d_x,
        g_norm,
        g_router,
        g_qkv,
        g_proj,
        g_in,
        g_out,
        m_norm,
        m_router,
        m_qkv,
        m_proj,
        m_in,
        m_out,
        n_norm,
        n_router,
        n_qkv,
        n_proj,
        n_in,
        n_out,
        n_qkv.astype(jnp.bfloat16),
        n_proj.astype(jnp.bfloat16),
        n_in.astype(jnp.bfloat16),
        n_out.astype(jnp.bfloat16),
    )


def dot(left, right, precision=None):
    return jnp.dot(left, right, precision=precision, preferred_element_type=jnp.float32)


def dot_nt(left, right, precision=None):
    return lax.dot_general(
        left, right, (((1,), (1,)), ((), ())), precision=precision, preferred_element_type=jnp.float32
    )


def dot_tn(left, right, precision=None):
    return lax.dot_general(
        left, right, (((0,), (0,)), ((), ())), precision=precision, preferred_element_type=jnp.float32
    )


def places():
    return lax.axis_index("expert"), lax.axis_index("ctx"), lax.axis_index("dp")


def ctx_partner(ctx, step):
    column, row = lax.rem(ctx, 2), ctx // 2
    column = lax.rem(column + lax.rem(step, 2), 2)
    row = lax.rem(row + step // 2, 2)
    return row * 2 + column


def z_partner(expert, step, count):
    return lax.rem(expert + step, count)


def greet(partners):
    barrier = pltpu.get_barrier_semaphore()
    for partner in partners:
        pl.semaphore_signal(barrier, inc=1, device_id=partner, device_id_type=MESH)
    pl.semaphore_wait(barrier, len(partners))


def send(source, target, send_sem, recv_sem, partner):
    copy = pltpu.make_async_remote_copy(
        src_ref=source,
        dst_ref=target,
        send_sem=send_sem,
        recv_sem=recv_sem,
        device_id=partner,
        device_id_type=MESH,
    )
    copy.start()
    return copy


def normalize(values):
    center = jnp.mean(values, axis=-1, keepdims=True)
    spread = values - center
    power = jnp.mean(spread * spread, axis=-1, keepdims=True)
    scale = lax.rsqrt(power + EPS_NORM)
    return spread * scale, scale


def normalize_back(grad, unit, scale):
    first = jnp.mean(grad, axis=-1, keepdims=True)
    second = jnp.mean(grad * unit, axis=-1, keepdims=True)
    return scale * (grad - first - unit * second)


def group_rows(meta_ref, image):
    pairs = [
        meta_ref[2 * half, image] + meta_ref[2 * half + 1, image]
        for half in range(meta_ref.shape[0] // 2)
    ]
    return jnp.concatenate(pairs, axis=1)


def forward_kernel(
    n_exp,
    experts,
    x_ref,
    d_ref,
    meta_ref,
    w_ref,
    norm_ref,
    wqkv_ref,
    wproj_ref,
    x_all,
    d_all,
    meta_all,
    w_all,
    first_ref,
    qkv_ref,
    lse_ref,
    att_ref,
    mid_ref,
    routed_ref,
    d_own,
    mask_own,
    x_send,
    x_recv,
    m_send,
    m_recv,
    d_send,
    d_recv,
    w_send,
    w_recv,
    s_send,
    s_recv,
    own_sem,
):
    expert, ctx, dp = places()
    own_images, n_ctx, seq_dev, width = x_all.shape
    seq = n_ctx * seq_dev
    ctx_steps = list(range(1, n_ctx))
    z_steps = [1, n_exp - 1] + list(range(2, n_exp - 1))
    ctx_ids = [(expert, ctx_partner(ctx, step), dp) for step in ctx_steps]
    z_ids = [(z_partner(expert, step, n_exp), ctx, dp) for step in z_steps]
    twin = (expert, ctx, 1 - dp)
    greet(ctx_ids + z_ids + [twin])
    own = [
        pltpu.make_async_copy(
            x_ref.at[pl.ds(ctx * own_images, own_images)], x_all.at[:, ctx], own_sem.at[0]
        ),
        pltpu.make_async_copy(meta_ref, meta_all.at[ctx], own_sem.at[1]),
        pltpu.make_async_copy(d_ref, d_all.at[:, ctx], own_sem.at[2]),
        pltpu.make_async_copy(w_ref, w_all.at[:, expert], own_sem.at[3]),
    ]
    for copy in own:
        copy.start()
    x_copies = []
    m_copies = []
    for at, partner in enumerate(ctx_ids):
        x_copies.append(
            send(
                x_ref.at[pl.ds(partner[1] * own_images, own_images)],
                x_all.at[:, ctx],
                x_send.at[at],
                x_recv.at[at],
                partner,
            )
        )
        m_copies.append(
            send(meta_ref, meta_all.at[ctx], m_send.at[at], m_recv.at[at], partner)
        )
    w_copies = [
        send(w_ref.at[dp], w_all.at[dp, expert], w_send.at[at], w_recv.at[at], partner)
        for at, partner in enumerate(z_ids)
    ]
    for copy in own:
        copy.wait()
    for copy in x_copies + m_copies:
        copy.wait()
    d_copies = [
        send(d_ref, d_all.at[:, ctx], d_send.at[at], d_recv.at[at], partner)
        for at, partner in enumerate(ctx_ids)
    ]
    lane = lax.broadcasted_iota(jnp.int32, (seq, LANES), 1)
    low_half = lane < HEAD_DIM
    for image in range(own_images):
        rows = pl.ds(image * seq, seq)
        values = x_all[image].reshape(seq, width).astype(jnp.float32)
        unit, _ = normalize(values)
        first = (unit * norm_ref[0:1] + norm_ref[1:2]).astype(jnp.bfloat16)
        first_ref[rows] = first
        qkv_ref[rows] = dot(first, wqkv_ref[...]).astype(jnp.bfloat16)
        key_mask = group_rows(meta_all, ctx * own_images + image)[experts : experts + 1]
        mask_own[image] = jnp.broadcast_to(key_mask, mask_own.shape[1:])
        bias = jnp.where(key_mask > 0, 0.0, NEG)
        totals = jnp.zeros((seq, LANES), jnp.float32)
        for pair in range(HEADS // 2):
            query = qkv_ref[rows, pair * LANES : (pair + 1) * LANES]
            keys = qkv_ref[rows, width + pair * LANES : width + (pair + 1) * LANES]
            heads = qkv_ref[rows, 2 * width + pair * LANES : 2 * width + (pair + 1) * LANES]
            query = query * jnp.bfloat16(HEAD_DIM**-0.5)
            parts = []
            for half in range(2):
                chosen = low_half if half == 0 else ~low_half
                part = jnp.where(chosen, query, jnp.zeros_like(query))
                scores = dot_nt(part, keys) + bias
                peak = jnp.max(scores, axis=-1, keepdims=True)
                raised = jnp.exp(scores - peak)
                total = jnp.sum(raised, axis=-1, keepdims=True)
                probs = (raised * (1.0 / total)).astype(jnp.bfloat16)
                parts.append(dot(probs, heads))
                totals = jnp.where(lane == 2 * pair + half, peak + jnp.log(total), totals)
            att_ref[rows, pair * LANES : (pair + 1) * LANES] = jnp.where(
                low_half, parts[0], parts[1]
            ).astype(jnp.bfloat16)
        lse_ref[rows] = totals
        mid = values + dot(att_ref[rows], wproj_ref[...])
        mid_ref[rows] = mid
        unit, _ = normalize(mid)
        routed_ref[rows] = (unit * norm_ref[2:3] + norm_ref[3:4]).astype(jnp.bfloat16)
    s_copies = []
    for at, step in enumerate(z_steps):
        w_copies[at].wait()
        source = z_partner(expert, n_exp - step, n_exp)
        s_copies.append(
            send(
                w_all.at[dp, source], w_all.at[dp, source], s_send.at[at], s_recv.at[at], twin
            )
        )
    for copy in d_copies + s_copies:
        copy.wait()
    for image in range(own_images):
        d_own[pl.ds(image * seq, seq)] = d_all[ctx * own_images + image].reshape(seq, width)


def expert_kernel(
    experts,
    routed_ref,
    d_all,
    meta_all,
    w_all,
    router_ref,
    mid_ref,
    out_send,
    dsecond_ref,
    grads_ref,
    grouter_ref,
    r_all,
    ds_send,
    ds_recv,
    acc_out,
    acc_ds,
    acc_grads,
    acc_router,
    gates_ref,
    dgates_ref,
    r_turn,
    d_turn,
    r_sems,
    ds_sems,
):
    expert, ctx, dp = places()
    n_ctx, rows, width = d_all.shape
    own_images = out_send.shape[1]
    ctx_ids = [(expert, ctx_partner(ctx, step), dp) for step in range(1, n_ctx)]
    greet(ctx_ids)
    r_copies = [
        send(routed_ref, r_all.at[ctx], r_sems.at[0, at], r_sems.at[1, at], partner)
        for at, partner in enumerate(ctx_ids)
    ]
    r_all[ctx] = routed_ref[...]
    acc_grads[...] = jnp.zeros_like(acc_grads)
    acc_router[...] = jnp.zeros_like(acc_router)
    lane = lax.broadcasted_iota(jnp.int32, (rows, LANES), 1)

    def chunk(step):
        owner = ctx_partner(ctx, step)
        if step > 0:
            r_copies[step - 1].wait_recv()
        routed = r_all[owner]
        cotangent = d_all[owner]
        r_turn[...] = routed.T
        d_turn[...] = cotangent.T
        present = jnp.concatenate(
            [group_rows(meta_all, owner * own_images + image) for image in range(own_images)], axis=1
        )
        present = jnp.concatenate(
            [present, jnp.zeros((LANES - present.shape[0], rows), jnp.float32)], axis=0
        ).T
        present = (present > 0) & (lane < experts)
        logits = dot(routed, router_ref[0]) + dot(routed, router_ref[1])
        peak = jnp.max(jnp.where(present, logits, NEG), axis=-1, keepdims=True)
        raised = jnp.where(present, jnp.exp(jnp.where(present, logits - peak, 0.0)), 0.0)
        gates_ref[...] = raised / jnp.sum(raised, axis=-1, keepdims=True)
        acc_out[...] = jnp.zeros_like(acc_out)
        acc_ds[...] = jnp.zeros_like(acc_ds)
        dgates_ref[...] = jnp.zeros_like(dgates_ref)

        def one_expert(index, carry):
            w_in = w_all[0, index]
            w_out = w_all[1, index]
            for half in range(2):
                part = pl.ds(half * (rows // 2), rows // 2)
                cols = lane[: rows // 2]
                gate = jnp.sum(
                    jnp.where(cols == index, gates_ref[part], 0.0), axis=-1, keepdims=True
                )
                pre = dot(r_all[owner, part], w_in)
                dact = dot(d_all[owner, part], w_out)
                cdf = 0.5 + 0.5 * lax.erf(pre * (0.5**0.5))
                act = pre * cdf
                slope = cdf + pre * (jnp.exp(-0.5 * pre * pre) * (1.0 / math.sqrt(2 * math.pi)))
                dgate = jnp.sum(dact * act, axis=-1, keepdims=True)
                dgates_ref[part] = jnp.where(cols == index, dgate, dgates_ref[part])
                act_low = (gate * act).astype(jnp.bfloat16)
                dpre = (gate * dact * slope).astype(jnp.bfloat16)
                acc_out[part] += dot_nt(act_low, w_out)
                acc_ds[part] += dot_nt(dpre, w_in)
                acc_grads[0, index] += dot(r_turn[:, half * (rows // 2) : (half + 1) * (rows // 2)], dpre)
                acc_grads[1, index] += dot(d_turn[:, half * (rows // 2) : (half + 1) * (rows // 2)], act_low)
            return carry

        lax.fori_loop(0, experts, one_expert, 0)
        gates = gates_ref[...]
        dgates = dgates_ref[...]
        dlogits = gates * (dgates - jnp.sum(gates * dgates, axis=-1, keepdims=True))
        high = dlogits.astype(jnp.bfloat16)
        low = (dlogits - high.astype(jnp.float32)).astype(jnp.bfloat16)
        acc_router[...] += dot(r_turn[...], high) + dot(r_turn[...], low)
        acc_ds[...] += (
            dot_nt(high, router_ref[0]) + dot_nt(high, router_ref[1]) + dot_nt(low, router_ref[0])
        )
        if step == 0:
            acc_out[...] += mid_ref[...]
            dsecond_ref[...] = acc_ds[...]
        else:
            ds_send[step - 1] = acc_ds[...].astype(jnp.bfloat16)
        out_send[step] = acc_out[...].astype(jnp.bfloat16).reshape(out_send.shape[1:])
        if step > 0:
            ds_copies.append(
                send(
                    ds_send.at[step - 1],
                    ds_recv.at[step - 1],
                    ds_sems.at[0, step - 1],
                    ds_sems.at[1, step - 1],
                    ctx_ids[step - 1],
                )
            )

    ds_copies = []
    for step in range(n_ctx):
        chunk(step)
    grads_ref[...] = acc_grads[...].astype(jnp.bfloat16)
    grouter_ref[...] = acc_router[...].T[: grouter_ref.shape[0]]
    for copy in r_copies:
        copy.wait_send()
    for copy in ds_copies:
        copy.wait()
    for at in range(n_ctx - 1):
        dsecond_ref[...] += ds_recv[at].astype(jnp.float32)


def split(values):
    high = values.astype(jnp.bfloat16)
    return high, (values - high.astype(jnp.float32)).astype(jnp.bfloat16)


def gram_blocks(matrix, packed_ref):
    size = matrix.shape[0]
    index = 0
    for row in range(size // LANES):
        strip = dot_nt(matrix[row * LANES : (row + 1) * LANES], matrix[row * LANES :])
        for col in range(size // LANES - row):
            packed_ref[index] = strip[:, col * LANES : (col + 1) * LANES].reshape(
                packed_ref.shape[1:]
            )
            index += 1


def gram_whole(packed_ref, high_ref, low_ref):
    count = high_ref.shape[0] // LANES
    diagonal = lax.broadcasted_iota(jnp.int32, (LANES, LANES), 0) == lax.broadcasted_iota(
        jnp.int32, (LANES, LANES), 1
    )
    places_of = {}
    square = jnp.zeros((1, 1), jnp.float32)
    index = 0
    for row in range(count):
        for col in range(row, count):
            places_of[index] = (row, col)
            if row == col:
                block = packed_ref[index].reshape(LANES, LANES)
                square += jnp.sum(jnp.where(diagonal, block, 0.0), keepdims=True)
            index += 1
    scale = 1.0 / (jnp.sqrt(square) + EPS_ORTHO)
    for index, (row, col) in places_of.items():
        block = packed_ref[index].reshape(LANES, LANES) * (scale * scale)
        rows, cols = pl.ds(row * LANES, LANES), pl.ds(col * LANES, LANES)
        high_ref[rows, cols], low_ref[rows, cols] = split(block)
        if row != col:
            high_ref[cols, rows], low_ref[cols, rows] = split(block.T)
    return scale


def orthogonal(high_ref, low_ref, mix_ref, total_ref, after):
    size = high_ref.shape[0]
    eye = lax.broadcasted_iota(jnp.int32, (size, size), 0) == lax.broadcasted_iota(
        jnp.int32, (size, size), 1
    )
    for turn in range(NS_ITERS):
        high, low = high_ref[...], low_ref[...]
        square = dot(high, high)
        if turn == NS_ITERS - 1:
            square += dot(high, low) + dot(low, high)
        mix_ref[...] = (
            jnp.where(eye, NS_A, 0.0)
            + NS_B * (high.astype(jnp.float32) + low.astype(jnp.float32))
            + NS_C * square
        ).astype(jnp.bfloat16)
        mix = mix_ref[...]
        if turn == 0:
            total_ref[...] = mix.astype(jnp.float32)
        else:
            total_high, total_low = split(total_ref[...])
            total_ref[...] = dot(mix, total_high) + dot(mix, total_low)
        if turn < NS_ITERS - 1:
            turned_high, turned_low = split(dot(mix, high) + dot(mix, low))
            high_ref[...], low_ref[...] = split(dot(turned_high, mix) + dot(turned_low, mix))
        after(turn)


def backward_kernel(
    n_exp,
    experts,
    x_ref,
    d_ref,
    mask_ref,
    first_ref,
    qkv_ref,
    lse_ref,
    att_ref,
    mid_ref,
    dsecond_ref,
    grads_ref,
    grouter_ref,
    norm_ref,
    wqkv_ref,
    wproj_ref,
    out_send,
    mexp_ref,
    mqkv_ref,
    mproj_ref,
    mnorm_ref,
    mrouter_ref,
    out_ref,
    dx_ref,
    gexp_ref,
    step_ref,
    whole_ref,
    sums_ref,
    squares_ref,
    out_recv,
    twin_recv,
    z_send,
    z_recv,
    dmid_ref,
    dbranch_ref,
    datt_ref,
    dqkv_ref,
    dx_send,
    shared_ref,
    half_recv,
    sum_one,
    ctx_recv,
    piece_send,
    piece_recv,
    mat_ref,
    packed_ref,
    packed_recv,
    gathered_ref,
    high_ref,
    low_ref,
    mix_ref,
    total_ref,
    small_ref,
    small_twin,
    small_ctx,
    small_z,
    out_sems,
    t_sems,
    z_sems,
    f_sems,
    dx_sems,
    h_sems,
    c_sems,
    s_sems,
    p_sems,
    w_sems,
    g_sems,
    a_sems,
    x_sems,
    n_sems,
):
    expert, ctx, dp = places()
    own_images, n_ctx, seq_dev, width = dx_send.shape
    images = own_images * n_ctx
    seq = n_ctx * seq_dev
    half = width // 2
    cols = width // n_ctx
    ctx_ids = [(expert, ctx_partner(ctx, step), dp) for step in range(1, n_ctx)]
    z_steps = [1, n_exp - 1] + list(range(2, n_exp - 1))
    z_ids = [(z_partner(expert, step, n_exp), ctx, dp) for step in z_steps]
    twin = (expert, ctx, 1 - dp)
    greet(ctx_ids + z_ids + [twin])

    def to_each(partners, source, target, sems):
        return [
            send(source(at, partner), target(at, partner), sems.at[0, at], sems.at[1, at], partner)
            for at, partner in enumerate(partners)
        ]

    t_copy = send(grads_ref.at[1 - dp], twin_recv, t_sems.at[0], t_sems.at[1], twin)
    out_copies = []
    for step in range(n_ctx):
        first_image = ctx_partner(ctx, step) * own_images
        for at, partner in enumerate(ctx_ids):
            out_copies.append(
                send(
                    out_send.at[step, :, partner[1]],
                    out_recv.at[ctx, pl.ds(first_image, own_images)],
                    out_sems.at[0, step, at],
                    out_sems.at[1, step, at],
                    partner,
                )
            )
    gain_one, gain_two = norm_ref[0:1], norm_ref[2:3]
    sums = [jnp.zeros((1, width), jnp.float32) for _ in range(4)]
    for image in range(own_images):
        rows = pl.ds(image * seq, seq)
        unit, scale = normalize(mid_ref[rows])
        grad = dsecond_ref[rows]
        sums[2] += jnp.sum(grad * unit, axis=0, keepdims=True)
        sums[3] += jnp.sum(grad, axis=0, keepdims=True)
        dmid = normalize_back(grad * gain_two, unit, scale) + d_ref[rows].astype(jnp.float32)
        dmid_ref[rows] = dmid
        dbranch = dmid.astype(jnp.bfloat16)
        dbranch_ref[rows] = dbranch
        datt_ref[rows] = dot_nt(dbranch, wproj_ref[...]).astype(jnp.bfloat16)
    t_copy.wait()
    for index in range(n_exp):
        z_send[index] = (
            grads_ref[dp, index].astype(jnp.float32) + twin_recv[index].astype(jnp.float32)
        ).astype(jnp.bfloat16)
    z_copies = to_each(
        z_ids, lambda at, partner: z_send.at[partner[0]], lambda at, partner: z_recv.at[at], z_sems
    )
    gproj = dot_tn(att_ref[...], dbranch_ref[...]).astype(jnp.bfloat16)
    for place in range(n_ctx):
        shared_ref[place, :, 3 * cols :] = gproj[:, place * cols : (place + 1) * cols]
    lane = lax.broadcasted_iota(jnp.int32, (seq, LANES), 1)
    low_half = lane < HEAD_DIM
    factor = HEAD_DIM**-0.5
    for image in range(own_images):
        rows = pl.ds(image * seq, seq)
        bias = jnp.where(mask_ref[image, 0:1] > 0, 0.0, NEG)
        totals = lse_ref[rows]
        for pair in range(HEADS // 2):
            at = pair * LANES
            query = qkv_ref[rows, at : at + LANES] * jnp.bfloat16(factor)
            keys = qkv_ref[rows, width + at : width + at + LANES]
            heads = qkv_ref[rows, 2 * width + at : 2 * width + at + LANES]
            datt = datt_ref[rows, at : at + LANES]
            dquery, dkeys, dheads = [], [], []
            for part in range(2):
                chosen = low_half if part == 0 else ~low_half
                scores = dot_nt(jnp.where(chosen, query, jnp.zeros_like(query)), keys) + bias
                head = 2 * pair + part
                weights = jnp.exp(scores - totals[:, head : head + 1])
                dprobs = dot_nt(jnp.where(chosen, datt, jnp.zeros_like(datt)), heads)
                delta = jnp.sum(weights * dprobs, axis=-1, keepdims=True)
                dscores = (weights * (dprobs - delta)).astype(jnp.bfloat16)
                dquery.append(dot(dscores, keys))
                dkeys.append(dot_tn(dscores, query))
                dheads.append(dot_tn(weights.astype(jnp.bfloat16), datt))
            dqkv_ref[rows, at : at + LANES] = (
                jnp.where(low_half, dquery[0], dquery[1]) * factor
            ).astype(jnp.bfloat16)
            dqkv_ref[rows, width + at : width + at + LANES] = jnp.where(
                low_half, dkeys[0], dkeys[1]
            ).astype(jnp.bfloat16)
            dqkv_ref[rows, 2 * width + at : 2 * width + at + LANES] = jnp.where(
                low_half, dheads[0], dheads[1]
            ).astype(jnp.bfloat16)
    gqkv = dot_tn(first_ref[...], dqkv_ref[...]).astype(jnp.bfloat16)
    for place in range(n_ctx):
        shared_ref[place, :, : 3 * cols] = gqkv[:, 3 * cols * place : 3 * cols * (place + 1)]
    own_half = pl.ds(pl.multiple_of(dp * half, half), half)
    other_half = pl.ds(pl.multiple_of((1 - dp) * half, half), half)
    h_copy = send(shared_ref.at[:, other_half], half_recv, h_sems.at[0, 0], h_sems.at[1, 0], twin)
    for image in range(own_images):
        rows = pl.ds(image * seq, seq)
        grad = dot_nt(dqkv_ref[rows], wqkv_ref[...])
        unit, scale = normalize(x_ref[rows].astype(jnp.float32))
        sums[0] += jnp.sum(grad * unit, axis=0, keepdims=True)
        sums[1] += jnp.sum(grad, axis=0, keepdims=True)
        dx = dmid_ref[rows] + normalize_back(grad * gain_one, unit, scale)
        dx_send[image] = dx.astype(jnp.bfloat16).reshape(n_ctx, seq_dev, width)
    for at, total in enumerate(sums):
        small_ref[at : at + 1] = total
    small_ref[4:8] = jnp.zeros((4, width), jnp.float32)
    small_ref[8:16] = grouter_ref[...]
    s_copy = send(small_ref, small_twin, h_sems.at[0, 1], h_sems.at[1, 1], twin)
    h_copy.wait()
    for place in range(n_ctx):
        sum_one[place] = (
            shared_ref[place, own_half].astype(jnp.float32) + half_recv[place].astype(jnp.float32)
        ).astype(jnp.bfloat16)
    c_copies = to_each(
        ctx_ids, lambda at, partner: sum_one.at[partner[1]], lambda at, partner: ctx_recv.at[at], c_sems
    )
    dx_copies = to_each(
        ctx_ids,
        lambda at, partner: dx_send.at[:, partner[1]],
        lambda at, partner: dx_ref.at[pl.ds(ctx * own_images, own_images)],
        dx_sems,
    )
    for image in range(own_images):
        dx_ref[ctx * own_images + image] = dx_send[image, ctx]
    s_copy.wait()
    small_ctx[ctx] = small_ref[...] + small_twin[...]
    s_copies = to_each(
        ctx_ids, lambda at, partner: small_ctx.at[ctx], lambda at, partner: small_ctx.at[ctx], s_sems
    )
    for copy in out_copies:
        copy.wait()
    for step in range(n_ctx):
        start = ctx_partner(ctx, step) * own_images
        for image in range(own_images):
            total = out_send[step, image, ctx].astype(jnp.float32)
            for at in range(n_ctx - 1):
                total += out_recv[ctx_partner(ctx, at + 1), start + image].astype(jnp.float32)
            out_ref[start + image] = total.astype(jnp.bfloat16)
    for copy in c_copies:
        copy.wait()
    total = sum_one[ctx].astype(jnp.float32)
    for at in range(n_ctx - 1):
        total += ctx_recv[at].astype(jnp.float32)
    piece_send[...] = total.astype(jnp.bfloat16).reshape(piece_send.shape)
    p_copies = to_each(
        z_ids,
        lambda at, partner: piece_send.at[partner[0]],
        lambda at, partner: piece_recv.at[at],
        p_sems,
    )
    for copy in s_copies:
        copy.wait()
    total = small_ctx[0]
    for place in range(1, n_ctx):
        total += small_ctx[place]
    small_z[expert] = total
    s_copies = to_each(
        z_ids,
        lambda at, partner: small_z.at[expert],
        lambda at, partner: small_z.at[expert],
        n_sems.at[0],
    )

    def gram_start(which, matrix):
        gram_blocks(matrix.astype(jnp.bfloat16), packed_ref.at[which])
        return to_each(
            ctx_ids,
            lambda at, partner: packed_ref.at[which, :, partner[1]],
            lambda at, partner: packed_recv.at[which, at],
            g_sems.at[which],
        )

    def gram_middle(which, copies):
        for copy in copies:
            copy.wait()
        total = packed_ref[which, :, ctx]
        for at in range(n_ctx - 1):
            total += packed_recv[which, at]
        gathered_ref[which, :, ctx] = total
        return to_each(
            ctx_ids,
            lambda at, partner: gathered_ref.at[which, :, ctx],
            lambda at, partner: gathered_ref.at[which, :, ctx],
            a_sems.at[which],
        )

    def step_of(which, matrix, scale):
        total_high, total_low = split(total_ref[...])
        high, low = split(matrix * scale)
        cut = pl.ds(0, matrix.shape[1])
        step_ref[which, dp, :, cut] = (
            dot(total_high, high) + dot(total_high, low) + dot(total_low, high)
        ).astype(jnp.bfloat16)
        return send(
            step_ref.at[which, dp, :, cut],
            step_ref.at[which, dp, :, cut],
            x_sems.at[0, which],
            x_sems.at[1, which],
            twin,
        )

    for copy in z_copies:
        copy.wait()
    total = z_send[expert].astype(jnp.float32)
    for at in range(n_exp - 1):
        total += z_recv[at].astype(jnp.float32)
    gexp_ref[dp] = total.astype(jnp.bfloat16)
    f_copy = send(gexp_ref.at[dp], gexp_ref.at[dp], f_sems.at[0], f_sems.at[1], twin)
    mat_ref[0] = DECAY * mexp_ref[dp] + gexp_ref[dp].astype(jnp.float32)
    exp_copies = gram_start(0, mat_ref[0])
    for copy in p_copies:
        copy.wait()
    total = piece_send[expert].astype(jnp.float32)
    for at in range(n_exp - 1):
        total += piece_recv[at].astype(jnp.float32)
    whole_ref[dp, expert] = total.astype(jnp.bfloat16)
    p_copies = to_each(
        z_ids,
        lambda at, partner: whole_ref.at[dp, expert],
        lambda at, partner: whole_ref.at[dp, expert],
        w_sems,
    )
    exp_copies = gram_middle(0, exp_copies)
    for copy in p_copies:
        copy.wait()
    w_copy = send(whole_ref.at[dp], whole_ref.at[dp], f_sems.at[2], f_sems.at[3], twin)
    for copy in s_copies:
        copy.wait()
    total = small_z[0]
    for place in range(1, n_exp):
        total += small_z[place]
    sums_ref[...] = total
    lane_part = pl.ds(pl.multiple_of(ctx * cols, cols), cols)
    fresh_norm = DECAY * mnorm_ref[...] + sums_ref[0:4, lane_part]
    fresh_router = DECAY * mrouter_ref[...] + sums_ref[pl.ds(8 + ctx, 1)]
    row = lax.broadcasted_iota(jnp.int32, (8, LANES), 0)
    squares_ref[ctx] = jnp.where(
        row == 0,
        jnp.sum(fresh_norm * fresh_norm, keepdims=True),
        jnp.sum(fresh_router * fresh_router, keepdims=True),
    )
    n_copies = to_each(
        ctx_ids,
        lambda at, partner: squares_ref.at[ctx],
        lambda at, partner: squares_ref.at[ctx],
        n_sems.at[1],
    )
    w_copy.wait()
    grad = whole_ref[...].reshape(width, width).astype(jnp.float32)
    mat_ref[1, :, : 3 * cols] = DECAY * mqkv_ref[...] + grad[:, : 3 * cols]
    mat_ref[2, :, :cols] = DECAY * mproj_ref[...] + grad[:, 3 * cols :]
    mat_ref[2, :, cols : 3 * cols] = jnp.zeros((width, 2 * cols), jnp.float32)
    shared_copies = [gram_start(1, mat_ref[1 + dp, :, : 3 * cols])]
    for copy in exp_copies:
        copy.wait()
    exp_scale = gram_whole(gathered_ref.at[0], high_ref, low_ref)

    def after(turn):
        if turn == 1:
            shared_copies[0] = gram_middle(1, shared_copies[0])

    orthogonal(high_ref, low_ref, mix_ref, total_ref, after)
    exp_step = step_of(0, mat_ref[0], exp_scale)
    for copy in shared_copies[0]:
        copy.wait()
    shared_scale = gram_whole(gathered_ref.at[1], high_ref, low_ref)
    orthogonal(high_ref, low_ref, mix_ref, total_ref, lambda turn: None)
    shared_step = step_of(1, mat_ref[1 + dp, :, : 3 * cols], shared_scale)
    for copy in dx_copies + n_copies + [f_copy, exp_step, shared_step]:
        copy.wait()


def finish_kernel(
    experts,
    n_ctx,
    ctx_ref,
    gexp_ref,
    step_ref,
    whole_ref,
    sums_ref,
    squares_ref,
    dx_in,
    out_in,
    mexp_ref,
    mqkv_ref,
    mproj_ref,
    mnorm_ref,
    mrouter_ref,
    wexp_ref,
    wqkv_ref,
    wproj_ref,
    norm_ref,
    router_ref,
    o_out,
    o_dx,
    o_gnorm,
    o_grouter,
    o_gqkv,
    o_gproj,
    o_gin,
    o_gout,
    o_mnorm,
    o_mrouter,
    o_mqkv,
    o_mproj,
    o_min,
    o_mout,
    o_nnorm,
    o_nrouter,
    o_nqkv,
    o_nproj,
    o_nin,
    o_nout,
    o_bqkv,
    o_bproj,
    o_bin,
    o_bout,
):
    width = norm_ref.shape[1]
    cols = width // n_ctx
    o_out[...] = out_in[...]
    o_dx[...] = dx_in[...].astype(jnp.float32)

    def update(grad, moment, weight, step, columns, outs):
        o_g, o_m, o_n, o_b = outs
        rate = RATE_MAT * 0.2 * math.sqrt(max(width, columns))
        new = weight.astype(jnp.float32) - rate * step.astype(jnp.float32)
        o_g[...] = grad.reshape(o_g.shape)
        o_m[...] = (DECAY * moment + grad).reshape(o_m.shape)
        o_n[...] = new.reshape(o_n.shape)
        o_b[...] = new.astype(jnp.bfloat16).reshape(o_b.shape)

    for index, outs in enumerate(((o_gin, o_min, o_nin, o_bin), (o_gout, o_mout, o_nout, o_bout))):
        update(
            gexp_ref[index].astype(jnp.float32),
            mexp_ref[index],
            wexp_ref[index],
            step_ref[0, index],
            n_ctx * gexp_ref.shape[2],
            outs,
        )
    grad = whole_ref[...].astype(jnp.float32)
    update(
        grad[:, : 3 * cols],
        mqkv_ref[...],
        wqkv_ref[...],
        step_ref[1, 0, :, : 3 * cols],
        3 * width,
        (o_gqkv, o_mqkv, o_nqkv, o_bqkv),
    )
    update(
        grad[:, 3 * cols :],
        mproj_ref[...],
        wproj_ref[...],
        step_ref[1, 1, :, :cols],
        width,
        (o_gproj, o_mproj, o_nproj, o_bproj),
    )
    ctx = ctx_ref[0]
    own_norm = sums_ref[0:4, pl.ds(pl.multiple_of(ctx * cols, cols), cols)]
    own_router = sums_ref[pl.ds(8 + ctx, 1)]
    fresh_norm = DECAY * mnorm_ref[...] + own_norm
    fresh_router = DECAY * mrouter_ref[...] + own_router
    o_gnorm[...] = own_norm
    o_grouter[...] = own_router
    o_mnorm[...] = fresh_norm
    o_mrouter[...] = fresh_router
    squares = squares_ref[0]
    for place in range(1, n_ctx):
        squares += squares_ref[place]
    o_nnorm[...] = norm_ref[:, pl.ds(pl.multiple_of(ctx * cols, cols), cols)] - (
        RATE_GAIN * fresh_norm * lax.rsqrt(squares[0:1] / (4 * width) + EPS_NORM)
    )
    o_nrouter[...] = router_ref[...] - RATE_ROUTER * fresh_router * lax.rsqrt(
        squares[1:2, 0:1] / (width * experts) + EPS_NORM
    )


def call(kernel, ident, outs, scratch, operands):
    spec = pl.BlockSpec(memory_space=pltpu.VMEM)
    return pl.pallas_call(
        kernel,
        out_shape=[jax.ShapeDtypeStruct(shape, dtype) for shape, dtype in outs],
        in_specs=[spec] * len(operands),
        out_specs=[spec] * len(outs),
        scratch_shapes=scratch,
        compiler_params=pltpu.CompilerParams(
            collective_id=ident, has_side_effects=True, vmem_limit_bytes=VMEM_LIMIT
        ),
    )(*operands)


def gathered(
    x_in,
    d_out,
    key_mask,
    expert_ids,
    norm_params,
    w_qkv,
    w_proj,
    w_router,
    w_in,
    w_out,
    mom_norm,
    mom_router,
    mom_qkv,
    mom_proj,
    mom_in,
    mom_out,
):
    n_exp = lax.axis_size("expert")
    n_ctx = lax.axis_size("ctx")
    ctx = lax.axis_index("ctx")
    images, seq_dev, width = x_in.shape
    experts = w_router.shape[1]
    own_images = images // n_ctx
    seq = n_ctx * seq_dev
    rows = own_images * seq
    hid = w_in.shape[2]
    low, full = jnp.bfloat16, jnp.float32
    dma = lambda *shape: pltpu.SemaphoreType.DMA(shape)
    vmem = lambda shape, dtype: pltpu.VMEM(shape, dtype)

    present = jnp.any(
        expert_ids[..., None] == jnp.arange(experts, dtype=jnp.int32), axis=2
    ).astype(full)
    meta = jnp.concatenate(
        [present, key_mask[..., None].astype(full), jnp.zeros((images, seq_dev, 7 - experts), full)],
        axis=-1,
    ).swapaxes(1, 2)
    odd = (ctx % 2).astype(full)
    meta = jnp.concatenate([meta * (1 - odd), meta * odd], axis=-1)
    weights = jnp.stack([w_in[0], w_out[0]])
    router = jnp.pad(w_router, ((0, 0), (0, LANES - experts)))
    router_high = router.astype(low)
    router_two = jnp.stack([router_high, (router - router_high.astype(full)).astype(low)])

    x_all, d_all, meta_all, w_all, first, qkv, lse, att, mid, routed, d_own, mask_own = call(
        functools.partial(forward_kernel, n_exp, experts),
        1,
        [
            ((own_images, n_ctx, seq_dev, width), low),
            ((images, n_ctx, seq_dev, width), low),
            ((n_ctx,) + meta.shape, full),
            ((2, n_exp, width, hid), low),
            ((rows, width), low),
            ((rows, 3 * width), low),
            ((rows, LANES), full),
            ((rows, width), low),
            ((rows, width), full),
            ((rows, width), low),
            ((rows, width), low),
            ((own_images, 8, seq), full),
        ],
        [dma(n_ctx - 1)] * 6 + [dma(n_exp - 1)] * 4 + [dma(4)],
        (x_in, d_out, meta, weights, norm_params, w_qkv, w_proj),
    )
    d_all = d_all.reshape(n_ctx, rows, width)
    out_parts, dsecond, grads, grouter = call(
        functools.partial(expert_kernel, experts),
        2,
        [
            ((n_ctx, own_images, n_ctx, seq_dev, width), low),
            ((rows, width), full),
            ((2, n_exp, width, hid), low),
            ((8, width), full),
        ],
        [
            vmem((n_ctx, rows, width), low),
            vmem((n_ctx - 1, rows, width), low),
            vmem((n_ctx - 1, rows, width), low),
            vmem((rows, width), full),
            vmem((rows, width), full),
            vmem((2, n_exp, width, hid), full),
            vmem((width, LANES), full),
            vmem((rows, LANES), full),
            vmem((rows, LANES), full),
            vmem((width, rows), low),
            vmem((width, rows), low),
            dma(2, n_ctx - 1),
            dma(2, n_ctx - 1),
        ],
        (routed, d_all, meta_all, w_all, router_two, mid),
    )
    cols = width // n_ctx
    blocks = (width // LANES) * (width // LANES + 1) // 2
    block_rows = LANES // n_ctx
    moments = (
        jnp.stack([mom_in[0], mom_out[0]]),
        mom_qkv,
        mom_proj,
        mom_norm,
        mom_router.reshape(1, width),
    )
    out_low, dx_low, gexp, steps, whole, sums, squares = call(
        functools.partial(backward_kernel, n_exp, experts),
        3,
        [
            ((images, seq_dev, width), low),
            ((images, seq_dev, width), low),
            ((2, width, hid), low),
            ((2, 2, width, hid), low),
            ((2, n_exp, width // 2 // n_exp, width), low),
            ((16, width), full),
            ((n_ctx, 8, LANES), full),
        ],
        [
            vmem((n_ctx, images, seq_dev, width), low),
            vmem((n_exp, width, hid), low),
            vmem((n_exp, width, hid), low),
            vmem((n_exp - 1, width, hid), low),
            vmem((rows, width), full),
            vmem((rows, width), low),
            vmem((rows, width), low),
            vmem((rows, 3 * width), low),
            vmem((own_images, n_ctx, seq_dev, width), low),
            vmem((n_ctx, width, width), low),
            vmem((n_ctx, width // 2, width), low),
            vmem((n_ctx, width // 2, width), low),
            vmem((n_ctx - 1, width // 2, width), low),
            vmem((n_exp, width // 2 // n_exp, width), low),
            vmem((n_exp - 1, width // 2 // n_exp, width), low),
            vmem((3, width, hid), full),
            vmem((2, blocks, n_ctx, block_rows, LANES), full),
            vmem((2, n_ctx - 1, blocks, block_rows, LANES), full),
            vmem((2, blocks, n_ctx, block_rows, LANES), full),
            vmem((width, width), low),
            vmem((width, width), low),
            vmem((width, width), low),
            vmem((width, width), full),
            vmem((16, width), full),
            vmem((16, width), full),
            vmem((n_ctx, 16, width), full),
            vmem((n_exp, 16, width), full),
            dma(2, n_ctx, n_ctx - 1),
            dma(2),
            dma(2, n_exp - 1),
            dma(4),
            dma(2, n_ctx - 1),
            dma(2, 2),
            dma(2, n_ctx - 1),
            dma(2, n_ctx - 1),
            dma(2, n_exp - 1),
            dma(2, n_exp - 1),
            dma(2, 2, n_ctx - 1),
            dma(2, 2, n_ctx - 1),
            dma(2, 2),
            dma(2, 2, max(n_ctx, n_exp) - 1),
        ],
        (
            x_all.reshape(rows, width),
            d_own,
            mask_own,
            first,
            qkv,
            lse,
            att,
            mid,
            dsecond,
            grads,
            grouter,
            norm_params,
            w_qkv,
            w_proj,
            out_parts,
        )
        + moments,
    )
    cut = lambda array, count: lax.dynamic_slice_in_dim(array, ctx * count, count, 1)
    pieces = ((4, cols), (1, width), (width, 3 * cols), (width, cols), (1, width, hid), (1, width, hid))
    spec = pl.BlockSpec(memory_space=pltpu.VMEM)
    outs = (
        [((images, seq_dev, width), low), ((images, seq_dev, width), full)]
        + [(piece, full) for piece in pieces * 3]
        + [(piece, low) for piece in pieces[2:]]
    )
    results = pl.pallas_call(
        functools.partial(finish_kernel, experts, n_ctx),
        out_shape=[jax.ShapeDtypeStruct(shape, dtype) for shape, dtype in outs],
        in_specs=[pl.BlockSpec(memory_space=pltpu.SMEM)] + [spec] * 17,
        out_specs=[spec] * len(outs),
        compiler_params=pltpu.CompilerParams(vmem_limit_bytes=VMEM_LIMIT),
    )(
        ctx.reshape(1),
        gexp,
        steps,
        whole.reshape(width, width),
        sums,
        squares,
        dx_low,
        out_low,
        *moments,
        weights,
        cut(w_qkv, 3 * cols),
        cut(w_proj, cols),
        norm_params,
        cut(w_router, 1).reshape(1, width),
    )
    return tuple(
        value.reshape(width, 1) if value.shape == (1, width) else value for value in results
    )


def solution(mesh):
    in_specs = (
        P(("expert", "dp"), "ctx", None),
        P(("expert", "dp"), "ctx", None),
        P(("expert", "dp"), "ctx"),
        P(("expert", "dp"), "ctx", None),
        P(),
        P(),
        P(),
        P(),
        P("expert", None, "ctx"),
        P("expert", None, "ctx"),
        P(None, "ctx"),
        P(None, "ctx"),
        P(None, "ctx"),
        P(None, "ctx"),
        P("expert", None, "ctx"),
        P("expert", None, "ctx"),
    )
    out_specs = (
        P(("expert", "dp"), "ctx", None),
        P(("expert", "dp"), "ctx", None),
        P(None, "ctx"),
        P(None, "ctx"),
        P(None, "ctx"),
        P(None, "ctx"),
        P("expert", None, "ctx"),
        P("expert", None, "ctx"),
        P(None, "ctx"),
        P(None, "ctx"),
        P(None, "ctx"),
        P(None, "ctx"),
        P("expert", None, "ctx"),
        P("expert", None, "ctx"),
        P(None, "ctx"),
        P(None, "ctx"),
        P(None, "ctx"),
        P(None, "ctx"),
        P("expert", None, "ctx"),
        P("expert", None, "ctx"),
        P(None, "ctx"),
        P(None, "ctx"),
        P("expert", None, "ctx"),
        P("expert", None, "ctx"),
    )
    experts = mesh.shape["expert"]
    square = mesh.shape["ctx"] == 4 and mesh.shape["dp"] == 2

    def local(*arrays):
        whole = (
            square
            and arrays[7].shape[1] == experts <= 7
            and arrays[8].shape[0] == 1
            and 2 * arrays[0].shape[1] == LANES
        )
        return (gathered if whole else exchanged)(*arrays)

    return jax.shard_map(local, mesh=mesh, in_specs=in_specs, out_specs=out_specs, check_vma=False)
```

```python
import functools
import math

import jax
import jax.numpy as jnp
from jax import lax
from jax.experimental import pallas as pl
from jax.experimental.pallas import tpu as pltpu
from jax.sharding import PartitionSpec as P

HEADS = 8
HEAD_DIM = 64
MICRO = 2
NS_ITERS = 4


HIGH = lax.Precision.HIGHEST
NS_A = 3.4445
NS_B = -4.775
NS_C = 2.0315
DECAY = 0.5
RATE_MAT = 0.3
RATE_GAIN = 0.3
RATE_ROUTER = 0.05
EPS_NORM = 1e-06
EPS_ORTHO = 1e-07
NEG = -1e30
LANES = 128
VMEM_LIMIT = 60 * 2**20
MESH = pl.DeviceIdType.MESH


def as_sent(array):
    return jax.tree.map(lambda a: a.astype(jnp.bfloat16) if a.dtype == jnp.float32 else a, array)


def layer_norm(values, gain, shift):
    center = jnp.mean(values, axis=-1, keepdims=True)
    spread = values - center
    power = jnp.mean(spread * spread, axis=-1, keepdims=True)
    return spread * lax.rsqrt(power + EPS_NORM) * gain + shift


def gelu_exact(values):
    return jax.nn.gelu(values, approximate=False)


def add_block(total, piece):
    return total + piece


def masked_scores(query, key_piece, mask_piece, factor):
    scores = (
        jnp.einsum("bqhd,bkhd->bhqk", query, key_piece, preferred_element_type=jnp.float32) * factor
    )
    return jnp.where(mask_piece[:, None, None, :] > 0, scores, NEG)


def gram_list(matrices):
    return tuple(
        (jnp.einsum("...ik,...jk->...ij", matrix, matrix, precision=HIGH) for matrix in matrices)
    )


def schulz_turn(matrices, grams):
    result = []
    for matrix, gram in zip(matrices, grams):
        square = jnp.einsum("...ij,...jk->...ik", gram, gram, precision=HIGH)
        mixer = NS_B * gram + NS_C * square
        result.append(
            NS_A * matrix + jnp.einsum("...ij,...jk->...ik", mixer, matrix, precision=HIGH)
        )
    return tuple(result)


def exchanged(
    x_in,
    d_out,
    key_mask,
    expert_ids,
    norm_params,
    w_qkv,
    w_proj,
    w_router,
    w_in,
    w_out,
    mom_norm,
    mom_router,
    mom_qkv,
    mom_proj,
    mom_in,
    mom_out,
):
    ctx_count = lax.axis_size("ctx")
    ctx_place = lax.axis_index("ctx")
    owner_count = lax.axis_size("expert")
    local_images = x_in.shape[0]
    seq_dev = x_in.shape[1]
    width = x_in.shape[2]
    top_count = expert_ids.shape[-1]
    experts = w_router.shape[1]
    exp_dev = w_in.shape[0]
    hid_part = w_in.shape[2]
    capacity = max(2, (5 * top_count * seq_dev + 4 * experts - 1) // (4 * experts))
    batch = local_images // MICRO
    slot_count = batch * capacity
    seq_all = seq_dev * ctx_count
    factor = HEAD_DIM ** (-0.5)
    expert_iota = jnp.arange(experts, dtype=jnp.int32)
    recv_shape = (owner_count, exp_dev, slot_count, width)
    head_shape = (batch, seq_dev, HEADS, HEAD_DIM)

    def hidden_fold(step_fn, init):
        folded = step_fn(
            init,
            (
                lax.all_gather(w_in, "ctx", axis=2, tiled=True),
                lax.all_gather(w_out, "ctx", axis=2, tiled=True),
            ),
            jnp.int32(0),
        )
        return folded

    def to_owner(rows):
        return lax.all_to_all(rows, "expert", split_axis=0, concat_axis=0, tiled=True)

    def to_source(rows):
        return lax.all_to_all(rows, "expert", split_axis=0, concat_axis=0, tiled=True)

    def key_fold(keys, values, mask_low, step_fn, init):
        return step_fn(
            init,
            (
                lax.all_gather(keys, "ctx", axis=1, tiled=True),
                lax.all_gather(values, "ctx", axis=1, tiled=True),
                lax.all_gather(mask_low, "ctx", axis=1, tiled=True),
            ),
            jnp.int32(0),
        )

    grad_qkv = jnp.zeros(w_qkv.shape, jnp.float32)
    grad_proj = jnp.zeros(w_proj.shape, jnp.float32)
    grad_router = jnp.zeros(w_router.shape, jnp.float32)
    grad_norm = jnp.zeros((4, width), jnp.float32)
    grad_in = jnp.zeros((exp_dev, width, hid_part * ctx_count), jnp.float32)
    grad_out = jnp.zeros((exp_dev, width, hid_part * ctx_count), jnp.float32)
    outputs = []
    input_grads = []
    for micro_index in range(MICRO):
        first_image = micro_index * batch
        last_image = first_image + batch
        x_part = x_in[first_image:last_image].astype(jnp.float32)
        cotangent = d_out[first_image:last_image].astype(jnp.float32)
        mask_low = key_mask[first_image:last_image].astype(jnp.bfloat16)
        idents = expert_ids[first_image:last_image]
        normed_first, pull_first = jax.vjp(layer_norm, x_part, norm_params[0], norm_params[1])
        first_low = normed_first.astype(jnp.bfloat16).reshape(-1, width)
        qkv = jnp.dot(first_low, w_qkv, preferred_element_type=jnp.float32).astype(jnp.bfloat16)
        qkv = qkv.reshape(batch, seq_dev, 3, HEADS, HEAD_DIM)
        query = qkv[:, :, 0]
        keys = qkv[:, :, 1]
        values = qkv[:, :, 2]
        peak_old = jnp.full((batch, HEADS, seq_dev), NEG, jnp.float32)
        key_piece = lax.all_gather(keys, "ctx", axis=1, tiled=True)
        mask_piece = lax.all_gather(mask_low, "ctx", axis=1, tiled=True)
        scores = masked_scores(query, key_piece, mask_piece, factor)
        peak_new = jnp.maximum(peak_old, jnp.max(scores, axis=-1))
        total_new = jnp.sum(jnp.exp(scores - peak_new[..., None]), axis=-1)
        log_total = peak_new + jnp.log(total_new)

        def attend_step(acc, pieces, start):
            key_piece, value_piece, mask_piece = pieces
            weights = jnp.exp(
                masked_scores(query, key_piece, mask_piece, factor) - log_total[..., None]
            )
            return jnp.einsum(
                "bhqk,bkhd->bqhd",
                weights.astype(jnp.bfloat16),
                value_piece,
                preferred_element_type=jnp.float32,
            )

        attended = key_fold(keys, values, mask_low, attend_step, jnp.zeros(head_shape, jnp.float32))
        attended_low = attended.astype(jnp.bfloat16).reshape(-1, width)
        branch = jnp.dot(attended_low, w_proj, preferred_element_type=jnp.float32).reshape(
            batch, seq_dev, width
        )
        mid = x_part + branch
        normed_second, pull_second = jax.vjp(layer_norm, mid, norm_params[2], norm_params[3])
        routed_low = normed_second.astype(jnp.bfloat16)
        logits = jnp.einsum("bsd,de->bse", normed_second, w_router, precision=HIGH)
        onehot = (idents[..., None] == expert_iota).astype(jnp.float32)
        chosen = jnp.sum(onehot * logits[:, :, None, :], axis=-1)
        gates = jax.nn.softmax(chosen, axis=-1)
        flat_ids = idents.reshape(batch, seq_dev * top_count)
        hits = (flat_ids[..., None] == expert_iota).astype(jnp.int32)
        ranked = jnp.sum((jnp.cumsum(hits, axis=1) - hits) * hits, axis=-1)
        slot = (ranked + (jnp.arange(batch, dtype=jnp.int32) * capacity)[:, None]).reshape(-1)
        target = flat_ids.reshape(-1)
        routed_rows = jnp.broadcast_to(
            routed_low[:, :, None, :], (batch, seq_dev, top_count, width)
        ).reshape(-1, width)
        send = (
            jnp.zeros((experts, slot_count, width), jnp.bfloat16).at[target, slot].set(routed_rows)
        )
        received = to_owner(send.reshape(recv_shape))

        def expert_step(acc, pieces, start):
            piece_in, piece_out = pieces
            pre = jnp.einsum(
                "nesd,edh->nesh", received, piece_in, preferred_element_type=jnp.float32
            )
            act = gelu_exact(pre).astype(jnp.bfloat16)
            return jnp.einsum("nesh,edh->nesd", act, piece_out, preferred_element_type=jnp.float32)

        made = hidden_fold(expert_step, jnp.zeros(recv_shape, jnp.float32))
        back_rows = to_source(made.astype(jnp.bfloat16)).reshape(experts, slot_count, width)
        returned = (
            back_rows[target, slot].reshape(batch, seq_dev, top_count, width).astype(jnp.float32)
        )
        result = mid + jnp.sum(gates[..., None] * returned, axis=2)
        outputs.append(result.astype(jnp.bfloat16))
        dgates = jnp.sum(cotangent[:, :, None, :] * returned, axis=-1)
        dchosen = gates * (dgates - jnp.sum(gates * dgates, axis=-1, keepdims=True))
        dlogits = jnp.sum(dchosen[..., None] * onehot, axis=2)
        grad_router = grad_router + jnp.einsum(
            "bsd,bse->de", normed_second, dlogits, precision=HIGH
        )
        dsecond = jnp.einsum("bse,de->bsd", dlogits, w_router, precision=HIGH)
        dreturned = (
            (gates[..., None] * cotangent[:, :, None, :]).astype(jnp.bfloat16).reshape(-1, width)
        )
        dsend = (
            jnp.zeros((experts, slot_count, width), jnp.bfloat16).at[target, slot].set(dreturned)
        )
        dreceived = to_owner(dsend.reshape(recv_shape))

        def expert_back(carry, pieces, start):
            drows, dins, douts = carry
            piece_in, piece_out = pieces
            pre = jnp.einsum(
                "nesd,edh->nesh", received, piece_in, preferred_element_type=jnp.float32
            )
            act_full, pull_act = jax.vjp(gelu_exact, pre)
            act = act_full.astype(jnp.bfloat16)
            dact = jnp.einsum(
                "nesd,edh->nesh", dreceived, piece_out, preferred_element_type=jnp.float32
            )
            dpre = pull_act(dact)[0].astype(jnp.bfloat16)
            douts = add_block(
                douts,
                jnp.einsum("nesd,nesh->edh", dreceived, act, preferred_element_type=jnp.float32),
            )
            dins = add_block(
                dins,
                jnp.einsum("nesd,nesh->edh", received, dpre, preferred_element_type=jnp.float32),
            )
            drows = jnp.einsum("nesh,edh->nesd", dpre, piece_in, preferred_element_type=jnp.float32)
            return (drows, dins, douts)

        drows, grad_in, grad_out = hidden_fold(
            expert_back, (jnp.zeros(recv_shape, jnp.float32), grad_in, grad_out)
        )
        dback = to_source(drows.astype(jnp.bfloat16)).reshape(experts, slot_count, width)
        dsecond = dsecond + jnp.sum(
            dback[target, slot].reshape(batch, seq_dev, top_count, width).astype(jnp.float32),
            axis=2,
        )
        dmid, dgain_two, dshift_two = pull_second(dsecond)
        dmid = dmid + cotangent
        dbranch = dmid.astype(jnp.bfloat16).reshape(-1, width)
        grad_proj = grad_proj + jnp.einsum(
            "sd,se->de", attended_low, dbranch, preferred_element_type=jnp.float32
        )
        dattended = jnp.einsum("se,de->sd", dbranch, w_proj, preferred_element_type=jnp.float32)
        dattended = dattended.astype(jnp.bfloat16).reshape(head_shape)
        delta = jnp.einsum("bqhd,bqhd->bhq", dattended.astype(jnp.float32), attended)

        def attend_back(carry, pieces, start):
            dquery, dkeys, dvalues = carry
            key_piece, value_piece, mask_piece = pieces
            weights = jnp.exp(
                masked_scores(query, key_piece, mask_piece, factor) - log_total[..., None]
            )
            probs = weights.astype(jnp.bfloat16)
            dvalue_piece = jnp.einsum(
                "bhqk,bqhd->bkhd", probs, dattended, preferred_element_type=jnp.float32
            )
            dprobs = jnp.einsum(
                "bqhd,bkhd->bhqk", dattended, value_piece, preferred_element_type=jnp.float32
            )
            dscores = (weights * (dprobs - delta[..., None])).astype(jnp.bfloat16)
            dquery = factor * jnp.einsum(
                "bhqk,bkhd->bqhd", dscores, key_piece, preferred_element_type=jnp.float32
            )
            dkey_piece = factor * jnp.einsum(
                "bhqk,bqhd->bkhd", dscores, query, preferred_element_type=jnp.float32
            )
            return (dquery, add_block(dkeys, dkey_piece), add_block(dvalues, dvalue_piece))

        all_shape = (batch, seq_all, HEADS, HEAD_DIM)
        back_init = (
            jnp.zeros(head_shape, jnp.float32),
            jnp.zeros(all_shape, jnp.float32),
            jnp.zeros(all_shape, jnp.float32),
        )
        dquery, dkeys_all, dvalues_all = key_fold(keys, values, mask_low, attend_back, back_init)
        dkeys, dvalues = (
            lax.psum_scatter(
                dkeys_all.astype(jnp.bfloat16), "ctx", scatter_dimension=1, tiled=True
            ).astype(jnp.float32),
            lax.psum_scatter(
                dvalues_all.astype(jnp.bfloat16), "ctx", scatter_dimension=1, tiled=True
            ).astype(jnp.float32),
        )
        dqkv = (
            jnp.stack([dquery, dkeys, dvalues], axis=2).astype(jnp.bfloat16).reshape(-1, 3 * width)
        )
        grad_qkv = grad_qkv + jnp.einsum(
            "sd,se->de", first_low, dqkv, preferred_element_type=jnp.float32
        )
        dfirst = jnp.einsum("se,de->sd", dqkv, w_qkv, preferred_element_type=jnp.float32).reshape(
            batch, seq_dev, width
        )
        dx_part, dgain_one, dshift_one = pull_first(dfirst)
        grad_norm = grad_norm + jnp.stack([dgain_one, dshift_one, dgain_two, dshift_two])
        input_grads.append(dx_part + dmid)
    block_out = jnp.concatenate(outputs, axis=0)
    d_x = jnp.concatenate(input_grads, axis=0)
    shared = (
        lax.psum_scatter(
            grad_in.astype(jnp.bfloat16), "ctx", scatter_dimension=2, tiled=True
        ).astype(jnp.float32),
        lax.psum_scatter(
            grad_out.astype(jnp.bfloat16), "ctx", scatter_dimension=2, tiled=True
        ).astype(jnp.float32),
        lax.psum_scatter(
            grad_qkv[None].astype(jnp.bfloat16), "ctx", scatter_dimension=2, tiled=True
        ).astype(jnp.float32),
        lax.psum_scatter(
            grad_proj[None].astype(jnp.bfloat16), "ctx", scatter_dimension=2, tiled=True
        ).astype(jnp.float32),
        lax.psum_scatter(
            grad_norm[None].astype(jnp.bfloat16), "ctx", scatter_dimension=2, tiled=True
        ).astype(jnp.float32),
        lax.psum_scatter(
            grad_router[None].astype(jnp.bfloat16), "ctx", scatter_dimension=2, tiled=True
        ).astype(jnp.float32),
    )
    g_in, g_out = (
        lax.psum(shared[0].astype(jnp.bfloat16), "dp").astype(jnp.float32),
        lax.psum(shared[1].astype(jnp.bfloat16), "dp").astype(jnp.float32),
    )
    g_qkv, g_proj, g_norm, g_router = lax.psum(
        (shared[2][0], shared[3][0], shared[4][0], shared[5][0]), ("expert", "dp")
    )
    own_qkv = lax.dynamic_slice_in_dim(w_qkv, ctx_place * g_qkv.shape[1], g_qkv.shape[1], 1).astype(
        jnp.float32
    )
    own_proj = lax.dynamic_slice_in_dim(
        w_proj, ctx_place * g_proj.shape[1], g_proj.shape[1], 1
    ).astype(jnp.float32)
    own_norm = lax.dynamic_slice_in_dim(
        norm_params, ctx_place * g_norm.shape[1], g_norm.shape[1], 1
    )
    own_router = lax.dynamic_slice_in_dim(
        w_router, ctx_place * g_router.shape[1], g_router.shape[1], 1
    )
    m_qkv = DECAY * mom_qkv + g_qkv
    m_proj = DECAY * mom_proj + g_proj
    m_in = DECAY * mom_in + g_in
    m_out = DECAY * mom_out + g_out
    m_norm = DECAY * mom_norm + g_norm
    m_router = DECAY * mom_router + g_router
    matrices = (m_qkv, m_proj, m_in, m_out)
    vector_squares = (jnp.sum(m_norm * m_norm), jnp.sum(m_router * m_router))
    sums = lax.psum(
        tuple((jnp.sum(matrix * matrix, axis=(-2, -1)) for matrix in matrices)) + vector_squares,
        "ctx",
    )
    vector_totals = sums[4:]
    iterates = tuple(
        (
            matrix / jnp.expand_dims(jnp.sqrt(square) + EPS_ORTHO, (-2, -1))
            for matrix, square in zip(matrices, sums[:4])
        )
    )
    for turn_index in range(NS_ITERS):
        iterates = schulz_turn(
            iterates,
            jax.tree.map(
                lambda part: part.astype(jnp.float32), lax.psum(as_sent(gram_list(iterates)), "ctx")
            ),
        )
    n_qkv = (
        own_qkv - RATE_MAT * 0.2 * math.sqrt(max(width, g_qkv.shape[1] * ctx_count)) * iterates[0]
    )
    n_proj = (
        own_proj - RATE_MAT * 0.2 * math.sqrt(max(width, g_proj.shape[1] * ctx_count)) * iterates[1]
    )
    n_in = (
        w_in.astype(jnp.float32)
        - RATE_MAT * 0.2 * math.sqrt(max(width, hid_part * ctx_count)) * iterates[2]
    )
    n_out = (
        w_out.astype(jnp.float32)
        - RATE_MAT * 0.2 * math.sqrt(max(width, hid_part * ctx_count)) * iterates[3]
    )
    n_norm = own_norm - RATE_GAIN * m_norm * lax.rsqrt(vector_totals[0] / (4 * width) + EPS_NORM)
    n_router = own_router - RATE_ROUTER * m_router * lax.rsqrt(
        vector_totals[1] / (width * experts) + EPS_NORM
    )
    return (
        block_out,
        d_x,
        g_norm,
        g_router,
        g_qkv,
        g_proj,
        g_in,
        g_out,
        m_norm,
        m_router,
        m_qkv,
        m_proj,
        m_in,
        m_out,
        n_norm,
        n_router,
        n_qkv,
        n_proj,
        n_in,
        n_out,
        n_qkv.astype(jnp.bfloat16),
        n_proj.astype(jnp.bfloat16),
        n_in.astype(jnp.bfloat16),
        n_out.astype(jnp.bfloat16),
    )


def dot(left, right, precision=None):
    return jnp.dot(left, right, precision=precision, preferred_element_type=jnp.float32)


def dot_nt(left, right, precision=None):
    return lax.dot_general(
        left, right, (((1,), (1,)), ((), ())), precision=precision, preferred_element_type=jnp.float32
    )


def dot_tn(left, right, precision=None):
    return lax.dot_general(
        left, right, (((0,), (0,)), ((), ())), precision=precision, preferred_element_type=jnp.float32
    )


def places():
    return lax.axis_index("expert"), lax.axis_index("ctx"), lax.axis_index("dp")


def ctx_partner(ctx, step):
    column, row = lax.rem(ctx, 2), ctx // 2
    column = lax.rem(column + lax.rem(step, 2), 2)
    row = lax.rem(row + step // 2, 2)
    return row * 2 + column


def z_partner(expert, step, count):
    return lax.rem(expert + step, count)


def greet(partners):
    barrier = pltpu.get_barrier_semaphore()
    for partner in partners:
        pl.semaphore_signal(barrier, inc=1, device_id=partner, device_id_type=MESH)
    pl.semaphore_wait(barrier, len(partners))


def send(source, target, send_sem, recv_sem, partner):
    copy = pltpu.make_async_remote_copy(
        src_ref=source,
        dst_ref=target,
        send_sem=send_sem,
        recv_sem=recv_sem,
        device_id=partner,
        device_id_type=MESH,
    )
    copy.start()
    return copy


def normalize(values):
    center = jnp.mean(values, axis=-1, keepdims=True)
    spread = values - center
    power = jnp.mean(spread * spread, axis=-1, keepdims=True)
    scale = lax.rsqrt(power + EPS_NORM)
    return spread * scale, scale


def normalize_back(grad, unit, scale):
    first = jnp.mean(grad, axis=-1, keepdims=True)
    second = jnp.mean(grad * unit, axis=-1, keepdims=True)
    return scale * (grad - first - unit * second)


def group_rows(meta_ref, image):
    pairs = [
        meta_ref[2 * half, image] + meta_ref[2 * half + 1, image]
        for half in range(meta_ref.shape[0] // 2)
    ]
    return jnp.concatenate(pairs, axis=1)


def gelu_parts(values):
    size = jnp.abs(values)
    density = jnp.exp(-0.5 * values * values)
    turn = pl.reciprocal(1.0 + (0.3275911 * 0.5**0.5) * size, approx=True)
    series = turn * (
        0.5 * 0.254829592
        + turn
        * (
            0.5 * -0.284496736
            + turn * (0.5 * 1.421413741 + turn * (0.5 * -1.453152027 + turn * (0.5 * 1.061405429)))
        )
    )
    tail = series * density
    return jnp.where(values > 0, 1.0 - tail, tail), density * (1.0 / math.sqrt(2 * math.pi))


def forward_kernel(
    n_exp,
    experts,
    x_ref,
    d_ref,
    meta_ref,
    win_ref,
    wout_ref,
    norm_ref,
    wqkv_hbm,
    wproj_hbm,
    router_ref,
    x_all,
    first_ref,
    qkv_ref,
    lse_ref,
    att_ref,
    mid_ref,
    d_own,
    mask_own,
    out_send,
    dsecond_ref,
    grads_ref,
    grouter_ref,
    d_all,
    w_all,
    r_all,
    meta_all,
    wqkv_ref,
    wproj_ref,
    ds_send,
    ds_recv,
    acc_out,
    acc_ds,
    acc_router,
    gates_ref,
    dgates_ref,
    r_turn,
    d_turn,
    act_all,
    dpre_all,
    x_sems,
    m_sems,
    d_sems,
    r_sems,
    ds_sems,
    dr_sems,
    rr_sems,
    z_sems,
    s_sems,
    own_sem,
):
    expert, ctx, dp = places()
    own_images, n_ctx, seq_dev, width = x_all.shape
    seq = n_ctx * seq_dev
    rows = own_images * seq
    ctx_ids = [(expert, ctx_partner(ctx, step), dp) for step in range(1, n_ctx)]
    side_ids = ctx_ids[:2]
    twin = (expert, ctx, 1 - dp)
    right, left = lax.rem(expert + 1, n_exp), lax.rem(expert + n_exp - 1, n_exp)
    greet(ctx_ids + [(right, ctx, dp), (left, ctx, dp), twin])
    own = [
        pltpu.make_async_copy(source, target, own_sem.at[at])
        for at, (source, target) in enumerate(
            (
                (win_ref.at[0], w_all.at[0, expert]),
                (wout_ref.at[0], w_all.at[1, expert]),
                (x_ref.at[pl.ds(ctx * own_images, own_images)], x_all.at[:, ctx]),
                (meta_ref, meta_all.at[ctx]),
                (wqkv_hbm, wqkv_ref),
                (wproj_hbm, wproj_ref),
                (d_ref, d_all.at[:, :, ctx]),
            )
        )
    ]
    for copy in own:
        copy.start()
    x_copies = [
        send(
            x_ref.at[pl.ds(partner[1] * own_images, own_images)],
            x_all.at[:, ctx],
            x_sems.at[0, at],
            x_sems.at[1, at],
            partner,
        )
        for at, partner in enumerate(ctx_ids)
    ] + [
        send(meta_ref, meta_all.at[ctx], m_sems.at[0, at], m_sems.at[1, at], partner)
        for at, partner in enumerate(ctx_ids)
    ]

    def hop(phase, side):
        share = expert - phase if side == 0 else expert + phase
        able = (share >= 0) & (expert < n_exp - 1) if side == 0 else (share < n_exp) & (expert > 0)
        share = jnp.clip(share, 0, n_exp - 1)
        return able, pltpu.make_async_remote_copy(
            src_ref=w_all.at[dp, share],
            dst_ref=w_all.at[dp, share],
            send_sem=z_sems.at[0, phase, side],
            recv_sem=z_sems.at[1, phase, side],
            device_id=(right if side == 0 else left, ctx, dp),
            device_id_type=MESH,
        )

    def landed(phase, side):
        share = expert - 1 - phase if side == 0 else expert + 1 + phase
        able = share >= 0 if side == 0 else share < n_exp
        share = jnp.clip(share, 0, n_exp - 1)
        place = w_all.at[dp, share]
        return (
            able,
            pltpu.make_async_remote_copy(
                src_ref=place,
                dst_ref=place,
                send_sem=z_sems.at[0, phase, side],
                recv_sem=z_sems.at[1, phase, side],
                device_id=(left if side == 0 else right, ctx, dp),
                device_id_type=MESH,
            ),
            pltpu.make_async_remote_copy(
                src_ref=place,
                dst_ref=place,
                send_sem=s_sems.at[0, phase, side],
                recv_sem=s_sems.at[1, phase, side],
                device_id=twin,
                device_id_type=MESH,
            ),
        )

    def start_hops(phase):
        for side in range(2):
            able, copy = hop(phase, side)
            pl.when(able)(copy.start)

    def take_hops(phase):
        for side in range(2):
            able, copy, shared = landed(phase, side)

            @pl.when(able)
            def _():
                copy.wait_recv()
                shared.start()

    def take_shared(phase):
        for side in range(2):
            able, _, shared = landed(phase, side)
            pl.when(able)(shared.wait_recv)

    own[0].wait()
    own[1].wait()
    start_hops(0)
    for copy in own[2:]:
        copy.wait()

    def d_copy(at, order):
        group = ctx_partner(ctx_ids[at][1], order)
        return pltpu.make_async_remote_copy(
            src_ref=d_ref.at[group],
            dst_ref=d_all.at[group, :, ctx],
            send_sem=d_sems.at[0, at, order],
            recv_sem=d_sems.at[1, at, order],
            device_id=ctx_ids[at],
            device_id_type=MESH,
        )

    def d_relay(image, order):
        target = side_ids[1 - image]
        place = d_all.at[ctx_partner(target[1], order), image, side_ids[image][1]]
        return pltpu.make_async_remote_copy(
            src_ref=place,
            dst_ref=place,
            send_sem=dr_sems.at[0, image, order],
            recv_sem=dr_sems.at[1, image, order],
            device_id=target,
            device_id_type=MESH,
        )

    def r_copy(at, image):
        return pltpu.make_async_remote_copy(
            src_ref=r_all.at[ctx, image],
            dst_ref=r_all.at[ctx, image],
            send_sem=r_sems.at[0, at, image],
            recv_sem=r_sems.at[1, at, image],
            device_id=side_ids[at],
            device_id_type=MESH,
        )

    def r_relay(image):
        place = r_all.at[side_ids[image][1], image]
        return pltpu.make_async_remote_copy(
            src_ref=place,
            dst_ref=place,
            send_sem=rr_sems.at[0, image],
            recv_sem=rr_sems.at[1, image],
            device_id=side_ids[1 - image],
            device_id_type=MESH,
        )

    for at in range(n_ctx - 1):
        d_copy(at, 0).start()
    for copy in x_copies:
        copy.wait()
    for order in range(1, n_ctx):
        for at in range(2):
            d_copy(at, order).start()
    lane = lax.broadcasted_iota(jnp.int32, (seq, LANES), 1)
    low_half = lane < HEAD_DIM
    for image in range(own_images):
        part = pl.ds(image * seq, seq)
        values = x_all[image].reshape(seq, width).astype(jnp.float32)
        unit, _ = normalize(values)
        first = (unit * norm_ref[0:1] + norm_ref[1:2]).astype(jnp.bfloat16)
        first_ref[part] = first
        qkv_ref[part] = dot(first, wqkv_ref[...]).astype(jnp.bfloat16)
        key_mask = group_rows(meta_all, ctx * own_images + image)[experts : experts + 1]
        mask_own[image] = jnp.broadcast_to(key_mask, mask_own.shape[1:])
        bias = jnp.where(key_mask > 0, 0.0, NEG)
        totals = jnp.zeros((seq, LANES), jnp.float32)
        for pair in range(HEADS // 2):
            query = qkv_ref[part, pair * LANES : (pair + 1) * LANES]
            keys = qkv_ref[part, width + pair * LANES : width + (pair + 1) * LANES]
            heads = qkv_ref[part, 2 * width + pair * LANES : 2 * width + (pair + 1) * LANES]
            query = query * jnp.bfloat16(HEAD_DIM**-0.5)
            parts = []
            for half in range(2):
                chosen = low_half if half == 0 else ~low_half
                scores = dot_nt(jnp.where(chosen, query, jnp.zeros_like(query)), keys) + bias
                peak = jnp.max(scores, axis=-1, keepdims=True)
                raised = jnp.exp(scores - peak)
                total = jnp.sum(raised, axis=-1, keepdims=True)
                probs = (raised * (1.0 / total)).astype(jnp.bfloat16)
                parts.append(dot(probs, heads))
                totals = jnp.where(lane == 2 * pair + half, peak + jnp.log(total), totals)
            att_ref[part, pair * LANES : (pair + 1) * LANES] = jnp.where(
                low_half, parts[0], parts[1]
            ).astype(jnp.bfloat16)
        lse_ref[part] = totals
        mid = values + dot(att_ref[part], wproj_ref[...])
        mid_ref[part] = mid
        unit, _ = normalize(mid)
        r_all[ctx, image] = (unit * norm_ref[2:3] + norm_ref[3:4]).astype(jnp.bfloat16)
        for at in range(2):
            r_copy(at, image).start()
        if image == 0:
            take_hops(0)
            start_hops(1)

    near = jnp.where(expert < n_exp // 2, expert + 1, expert - 1)
    last = jnp.where(expert < n_exp // 2, n_exp - 1, 0)
    middle = n_exp * (n_exp - 1) // 2 - expert - near - last

    def start_chunk(chunk, slot, owner):
        columns = pl.ds(pl.multiple_of(chunk * rows, rows), rows)
        routed = r_all[owner].reshape(rows, width)
        r_turn[:, columns] = routed.T
        d_turn[:, columns] = d_all[owner].reshape(rows, width).T
        wide = lax.broadcasted_iota(jnp.int32, (rows, LANES), 1)
        present = jnp.concatenate(
            [group_rows(meta_all, owner * own_images + image) for image in range(own_images)], axis=1
        )
        present = jnp.concatenate(
            [present, jnp.zeros((LANES - present.shape[0], rows), jnp.float32)], axis=0
        ).T
        present = (present > 0) & (wide < experts)
        logits = dot(routed, router_ref[0]) + dot(routed, router_ref[1])
        peak = jnp.max(jnp.where(present, logits, NEG), axis=-1, keepdims=True)
        raised = jnp.where(present, jnp.exp(jnp.where(present, logits - peak, 0.0)), 0.0)
        gates_ref[slot] = raised / jnp.sum(raised, axis=-1, keepdims=True)
        dgates_ref[slot] = jnp.zeros((rows, LANES), jnp.float32)
        acc_out[slot] = jnp.zeros(acc_out.shape[1:], jnp.float32)
        acc_ds[slot] = jnp.zeros(acc_ds.shape[1:], jnp.float32)

    def end_chunk(chunk, slot):
        columns = pl.ds(pl.multiple_of(chunk * rows, rows), rows)
        gates = gates_ref[slot]
        dgates = dgates_ref[slot]
        dlogits = gates * (dgates - jnp.sum(gates * dgates, axis=-1, keepdims=True))
        high, low = split(dlogits)
        turned = r_turn[:, columns]
        acc_router[...] += dot(turned, high) + dot(turned, low)
        total = (
            acc_ds[slot]
            + dot_nt(high, router_ref[0])
            + dot_nt(high, router_ref[1])
            + dot_nt(low, router_ref[0])
        )
        if chunk == 0:
            dsecond_ref[...] = total
            out = acc_out[slot] + mid_ref[...]
        else:
            ds_send[chunk - 1] = total.astype(jnp.bfloat16)
            out = acc_out[slot]
        out_send[chunk] = out.astype(jnp.bfloat16).reshape(out_send.shape[1:])

    def ds_copy(chunk):
        return pltpu.make_async_remote_copy(
            src_ref=ds_send.at[chunk - 1],
            dst_ref=ds_recv.at[chunk - 1],
            send_sem=ds_sems.at[0, chunk - 1],
            recv_sem=ds_sems.at[1, chunk - 1],
            device_id=ctx_ids[chunk - 1],
            device_id_type=MESH,
        )

    acc_router[...] = jnp.zeros_like(acc_router)

    def one_step(step, carry):
        chunk = jnp.where(
            step < 8, jnp.where((step < 3) | (step == 6), 0, 1), step // 4
        )
        rank = jnp.where(
            step < 8,
            jnp.where(step < 3, step, jnp.where(step < 6, step - 3, 3)),
            lax.rem(step, 4),
        )
        slot = lax.rem(chunk, 2)
        owner = ctx_partner(ctx, chunk)
        index = jnp.where(
            rank == 0, expert, jnp.where(rank == 1, near, jnp.where(rank == 2, middle, last))
        )

        @pl.when(step == 0)
        def _():
            for at in range(n_ctx - 1):
                d_copy(at, 0).wait_recv()
            start_chunk(0, 0, ctx)

        @pl.when(step == 1)
        def _():
            take_shared(0)
            for order in range(1, n_ctx):
                for at in range(2):
                    d_copy(at, order).wait_recv()
            for order in range(1, n_ctx):
                for image in range(2):
                    d_relay(image, order).start()

        @pl.when(step == 2)
        def _():
            take_hops(1)
            start_hops(2)
            take_shared(1)

        @pl.when(step == 3)
        def _():
            for image in range(2):
                r_copy(0, image).wait_recv()
                d_relay(image, 1).wait_recv()
            r_relay(0).start()
            start_chunk(1, 1, ctx_ids[0][1])

        @pl.when(step == 4)
        def _():
            for image in range(2):
                r_copy(1, image).wait_recv()
            r_relay(1).start()

        @pl.when(step == 6)
        def _():
            take_hops(2)
            take_shared(2)

        @pl.when(step == 8)
        def _():
            for image in range(2):
                d_relay(image, 2).wait_recv()
            start_chunk(2, 0, ctx_ids[1][1])

        @pl.when(step == 12)
        def _():
            for image in range(2):
                d_relay(image, 3).wait_recv()
                r_relay(image).wait_recv()
            start_chunk(3, 1, ctx_ids[2][1])

        w_in = w_all[0, index]
        w_out = w_all[1, index]
        for image in range(own_images):
            part = pl.ds(image * seq, seq)
            gate = jnp.sum(
                jnp.where(lane == index, gates_ref[slot, part], 0.0), axis=-1, keepdims=True
            )
            pre = dot(r_all[owner, image], w_in)
            dact = dot(d_all[owner, image].reshape(seq, width), w_out)
            cdf, density = gelu_parts(pre)
            act = pre * cdf
            dgate = jnp.sum(dact * act, axis=-1, keepdims=True)
            dgates_ref[slot, part] = jnp.where(lane == index, dgate, dgates_ref[slot, part])
            act_low = (gate * act).astype(jnp.bfloat16)
            dpre = (gate * dact * (cdf + pre * density)).astype(jnp.bfloat16)
            kept = pl.ds(pl.multiple_of(chunk * rows + image * seq, seq), seq)
            act_all[index, kept] = act_low
            dpre_all[index, kept] = dpre
            acc_out[slot, part] += dot_nt(act_low, w_out)
            acc_ds[slot, part] += dot_nt(dpre, w_in)

        @pl.when(step == 6)
        def _():
            end_chunk(0, 0)

        @pl.when(step == 7)
        def _():
            end_chunk(1, 1)
            ds_copy(1).start()

        @pl.when(step == 11)
        def _():
            end_chunk(2, 0)
            ds_copy(2).start()

        @pl.when(step == 15)
        def _():
            end_chunk(3, 1)
            ds_copy(3).start()

        return carry

    lax.fori_loop(0, n_ctx * n_exp, one_step, 0)

    def one_expert(index, carry):
        grads_ref[0, index] = dot(r_turn[...], dpre_all[index]).astype(jnp.bfloat16)
        grads_ref[1, index] = dot(d_turn[...], act_all[index]).astype(jnp.bfloat16)
        return carry

    lax.fori_loop(0, n_exp, one_expert, 0)
    grouter_ref[...] = acc_router[...].T[: grouter_ref.shape[0]]
    d_own[...] = d_all[ctx].reshape(rows, width)
    for phase in range(n_exp - 1):
        for side in range(2):
            able, copy = hop(phase, side)
            pl.when(able)(copy.wait_send)
            able, _, shared = landed(phase, side)
            pl.when(able)(shared.wait_send)
    for at in range(n_ctx - 1):
        for order in range(n_ctx if at < 2 else 1):
            d_copy(at, order).wait_send()
    for image in range(2):
        r_relay(image).wait_send()
        for at in range(2):
            r_copy(at, image).wait_send()
        for order in range(1, n_ctx):
            d_relay(image, order).wait_send()
    for chunk in range(1, n_ctx):
        ds_copy(chunk).wait()
        dsecond_ref[...] += ds_recv[chunk - 1].astype(jnp.float32)


def split(values):
    high = values.astype(jnp.bfloat16)
    return high, (values - high.astype(jnp.float32)).astype(jnp.bfloat16)


def gram_blocks(matrix, packed_ref):
    size = matrix.shape[0]
    index = 0
    for row in range(size // LANES):
        strip = dot_nt(matrix[row * LANES : (row + 1) * LANES], matrix[row * LANES :])
        for col in range(size // LANES - row):
            packed_ref[index] = strip[:, col * LANES : (col + 1) * LANES].reshape(
                packed_ref.shape[1:]
            )
            index += 1


def gram_whole(packed_ref, high_ref, low_ref):
    count = high_ref.shape[0] // LANES
    diagonal = lax.broadcasted_iota(jnp.int32, (LANES, LANES), 0) == lax.broadcasted_iota(
        jnp.int32, (LANES, LANES), 1
    )
    places_of = {}
    square = jnp.zeros((1, 1), jnp.float32)
    index = 0
    for row in range(count):
        for col in range(row, count):
            places_of[index] = (row, col)
            if row == col:
                block = packed_ref[index].reshape(LANES, LANES)
                square += jnp.sum(jnp.where(diagonal, block, 0.0), keepdims=True)
            index += 1
    scale = 1.0 / (jnp.sqrt(square) + EPS_ORTHO)
    for index, (row, col) in places_of.items():
        block = packed_ref[index].reshape(LANES, LANES) * (scale * scale)
        rows, cols = pl.ds(row * LANES, LANES), pl.ds(col * LANES, LANES)
        high_ref[rows, cols], low_ref[rows, cols] = split(block)
        if row != col:
            high_ref[cols, rows], low_ref[cols, rows] = split(block.T)
    return scale


def orthogonal(high_ref, low_ref, mix_ref, total_ref, after):
    size = high_ref.shape[0]
    eye = lax.broadcasted_iota(jnp.int32, (size, size), 0) == lax.broadcasted_iota(
        jnp.int32, (size, size), 1
    )
    for turn in range(NS_ITERS):
        high, low = high_ref[...], low_ref[...]
        square = dot(high, high)
        if turn == NS_ITERS - 1:
            square += dot(high, low) + dot(low, high)
        mix_ref[...] = (
            jnp.where(eye, NS_A, 0.0)
            + NS_B * (high.astype(jnp.float32) + low.astype(jnp.float32))
            + NS_C * square
        ).astype(jnp.bfloat16)
        mix = mix_ref[...]
        if turn == 0:
            total_ref[...] = mix.astype(jnp.float32)
        else:
            total_high, total_low = split(total_ref[...])
            total_ref[...] = dot(mix, total_high) + dot(mix, total_low)
        if turn < NS_ITERS - 1:
            turned_high, turned_low = split(dot(mix, high) + dot(mix, low))
            high_ref[...], low_ref[...] = split(dot(turned_high, mix) + dot(turned_low, mix))
        after(turn)


def backward_kernel(
    n_exp,
    experts,
    x_ref,
    d_ref,
    mask_ref,
    first_ref,
    qkv_ref,
    lse_ref,
    att_ref,
    mid_ref,
    dsecond_ref,
    grads_ref,
    grouter_ref,
    norm_ref,
    wqkv_ref,
    wproj_ref,
    out_send,
    mexp_ref,
    mqkv_ref,
    mproj_ref,
    mnorm_ref,
    mrouter_ref,
    out_ref,
    dx_ref,
    gexp_ref,
    step_ref,
    whole_ref,
    sums_ref,
    squares_ref,
    out_recv,
    twin_recv,
    z_send,
    z_recv,
    dmid_ref,
    dbranch_ref,
    datt_ref,
    dqkv_ref,
    dx_send,
    shared_ref,
    half_recv,
    sum_one,
    ctx_recv,
    piece_send,
    piece_recv,
    mat_ref,
    packed_ref,
    packed_recv,
    gathered_ref,
    high_ref,
    low_ref,
    mix_ref,
    total_ref,
    small_ref,
    small_twin,
    small_ctx,
    small_z,
    out_sems,
    t_sems,
    z_sems,
    f_sems,
    dx_sems,
    h_sems,
    c_sems,
    s_sems,
    p_sems,
    w_sems,
    g_sems,
    a_sems,
    x_sems,
    n_sems,
):
    expert, ctx, dp = places()
    own_images, n_ctx, seq_dev, width = dx_send.shape
    images = own_images * n_ctx
    seq = n_ctx * seq_dev
    half = width // 2
    cols = width // n_ctx
    ctx_ids = [(expert, ctx_partner(ctx, step), dp) for step in range(1, n_ctx)]
    z_steps = [1, n_exp - 1] + list(range(2, n_exp - 1))
    z_ids = [(z_partner(expert, step, n_exp), ctx, dp) for step in z_steps]
    twin = (expert, ctx, 1 - dp)
    greet(ctx_ids + z_ids + [twin])

    def to_each(partners, source, target, sems):
        return [
            send(source(at, partner), target(at, partner), sems.at[0, at], sems.at[1, at], partner)
            for at, partner in enumerate(partners)
        ]

    t_copy = send(grads_ref.at[1 - dp], twin_recv, t_sems.at[0], t_sems.at[1], twin)
    out_copies = []
    for step in range(n_ctx):
        first_image = ctx_partner(ctx, step) * own_images
        for at, partner in enumerate(ctx_ids):
            out_copies.append(
                send(
                    out_send.at[step, :, partner[1]],
                    out_recv.at[ctx, pl.ds(first_image, own_images)],
                    out_sems.at[0, step, at],
                    out_sems.at[1, step, at],
                    partner,
                )
            )
    gain_one, gain_two = norm_ref[0:1], norm_ref[2:3]
    sums = [jnp.zeros((1, width), jnp.float32) for _ in range(4)]
    for image in range(own_images):
        rows = pl.ds(image * seq, seq)
        unit, scale = normalize(mid_ref[rows])
        grad = dsecond_ref[rows]
        sums[2] += jnp.sum(grad * unit, axis=0, keepdims=True)
        sums[3] += jnp.sum(grad, axis=0, keepdims=True)
        dmid = normalize_back(grad * gain_two, unit, scale) + d_ref[rows].astype(jnp.float32)
        dmid_ref[rows] = dmid
        dbranch = dmid.astype(jnp.bfloat16)
        dbranch_ref[rows] = dbranch
        datt_ref[rows] = dot_nt(dbranch, wproj_ref[...]).astype(jnp.bfloat16)
    t_copy.wait()
    for index in range(n_exp):
        z_send[index] = (
            grads_ref[dp, index].astype(jnp.float32) + twin_recv[index].astype(jnp.float32)
        ).astype(jnp.bfloat16)
    z_copies = to_each(
        z_ids, lambda at, partner: z_send.at[partner[0]], lambda at, partner: z_recv.at[at], z_sems
    )
    gproj = dot_tn(att_ref[...], dbranch_ref[...]).astype(jnp.bfloat16)
    for place in range(n_ctx):
        shared_ref[place, :, 3 * cols :] = gproj[:, place * cols : (place + 1) * cols]
    lane = lax.broadcasted_iota(jnp.int32, (seq, LANES), 1)
    low_half = lane < HEAD_DIM
    factor = HEAD_DIM**-0.5
    for image in range(own_images):
        rows = pl.ds(image * seq, seq)
        bias = jnp.where(mask_ref[image, 0:1] > 0, 0.0, NEG)
        totals = lse_ref[rows]
        for pair in range(HEADS // 2):
            at = pair * LANES
            query = qkv_ref[rows, at : at + LANES] * jnp.bfloat16(factor)
            keys = qkv_ref[rows, width + at : width + at + LANES]
            heads = qkv_ref[rows, 2 * width + at : 2 * width + at + LANES]
            datt = datt_ref[rows, at : at + LANES]
            dquery, dkeys, dheads = [], [], []
            for part in range(2):
                chosen = low_half if part == 0 else ~low_half
                scores = dot_nt(jnp.where(chosen, query, jnp.zeros_like(query)), keys) + bias
                head = 2 * pair + part
                weights = jnp.exp(scores - totals[:, head : head + 1])
                dprobs = dot_nt(jnp.where(chosen, datt, jnp.zeros_like(datt)), heads)
                delta = jnp.sum(weights * dprobs, axis=-1, keepdims=True)
                dscores = (weights * (dprobs - delta)).astype(jnp.bfloat16)
                dquery.append(dot(dscores, keys))
                dkeys.append(dot_tn(dscores, query))
                dheads.append(dot_tn(weights.astype(jnp.bfloat16), datt))
            dqkv_ref[rows, at : at + LANES] = (
                jnp.where(low_half, dquery[0], dquery[1]) * factor
            ).astype(jnp.bfloat16)
            dqkv_ref[rows, width + at : width + at + LANES] = jnp.where(
                low_half, dkeys[0], dkeys[1]
            ).astype(jnp.bfloat16)
            dqkv_ref[rows, 2 * width + at : 2 * width + at + LANES] = jnp.where(
                low_half, dheads[0], dheads[1]
            ).astype(jnp.bfloat16)
    gqkv = dot_tn(first_ref[...], dqkv_ref[...]).astype(jnp.bfloat16)
    for place in range(n_ctx):
        shared_ref[place, :, : 3 * cols] = gqkv[:, 3 * cols * place : 3 * cols * (place + 1)]
    own_half = pl.ds(pl.multiple_of(dp * half, half), half)
    other_half = pl.ds(pl.multiple_of((1 - dp) * half, half), half)
    h_copy = send(shared_ref.at[:, other_half], half_recv, h_sems.at[0, 0], h_sems.at[1, 0], twin)
    for image in range(own_images):
        rows = pl.ds(image * seq, seq)
        grad = dot_nt(dqkv_ref[rows], wqkv_ref[...])
        unit, scale = normalize(x_ref[rows].astype(jnp.float32))
        sums[0] += jnp.sum(grad * unit, axis=0, keepdims=True)
        sums[1] += jnp.sum(grad, axis=0, keepdims=True)
        dx = dmid_ref[rows] + normalize_back(grad * gain_one, unit, scale)
        dx_send[image] = dx.astype(jnp.bfloat16).reshape(n_ctx, seq_dev, width)
    for at, total in enumerate(sums):
        small_ref[at : at + 1] = total
    small_ref[4:8] = jnp.zeros((4, width), jnp.float32)
    small_ref[8:16] = grouter_ref[...]
    s_copy = send(small_ref, small_twin, h_sems.at[0, 1], h_sems.at[1, 1], twin)
    h_copy.wait()
    for place in range(n_ctx):
        sum_one[place] = (
            shared_ref[place, own_half].astype(jnp.float32) + half_recv[place].astype(jnp.float32)
        ).astype(jnp.bfloat16)
    c_copies = to_each(
        ctx_ids, lambda at, partner: sum_one.at[partner[1]], lambda at, partner: ctx_recv.at[at], c_sems
    )
    dx_copies = to_each(
        ctx_ids,
        lambda at, partner: dx_send.at[:, partner[1]],
        lambda at, partner: dx_ref.at[pl.ds(ctx * own_images, own_images)],
        dx_sems,
    )
    for image in range(own_images):
        dx_ref[ctx * own_images + image] = dx_send[image, ctx]
    s_copy.wait()
    small_ctx[ctx] = small_ref[...] + small_twin[...]
    s_copies = to_each(
        ctx_ids, lambda at, partner: small_ctx.at[ctx], lambda at, partner: small_ctx.at[ctx], s_sems
    )
    for copy in out_copies:
        copy.wait()
    for step in range(n_ctx):
        start = ctx_partner(ctx, step) * own_images
        for image in range(own_images):
            total = out_send[step, image, ctx].astype(jnp.float32)
            for at in range(n_ctx - 1):
                total += out_recv[ctx_partner(ctx, at + 1), start + image].astype(jnp.float32)
            out_ref[start + image] = total.astype(jnp.bfloat16)
    for copy in c_copies:
        copy.wait()
    total = sum_one[ctx].astype(jnp.float32)
    for at in range(n_ctx - 1):
        total += ctx_recv[at].astype(jnp.float32)
    piece_send[...] = total.astype(jnp.bfloat16).reshape(piece_send.shape)
    p_copies = to_each(
        z_ids,
        lambda at, partner: piece_send.at[partner[0]],
        lambda at, partner: piece_recv.at[at],
        p_sems,
    )
    for copy in s_copies:
        copy.wait()
    total = small_ctx[0]
    for place in range(1, n_ctx):
        total += small_ctx[place]
    small_z[expert] = total
    s_copies = to_each(
        z_ids,
        lambda at, partner: small_z.at[expert],
        lambda at, partner: small_z.at[expert],
        n_sems.at[0],
    )

    def gram_start(which, matrix):
        gram_blocks(matrix.astype(jnp.bfloat16), packed_ref.at[which])
        return to_each(
            ctx_ids,
            lambda at, partner: packed_ref.at[which, :, partner[1]],
            lambda at, partner: packed_recv.at[which, at],
            g_sems.at[which],
        )

    def gram_middle(which, copies):
        for copy in copies:
            copy.wait()
        total = packed_ref[which, :, ctx]
        for at in range(n_ctx - 1):
            total += packed_recv[which, at]
        gathered_ref[which, :, ctx] = total
        return to_each(
            ctx_ids,
            lambda at, partner: gathered_ref.at[which, :, ctx],
            lambda at, partner: gathered_ref.at[which, :, ctx],
            a_sems.at[which],
        )

    def step_of(which, matrix, scale):
        total_high, total_low = split(total_ref[...])
        high, low = split(matrix * scale)
        cut = pl.ds(0, matrix.shape[1])
        step_ref[which, dp, :, cut] = (
            dot(total_high, high) + dot(total_high, low) + dot(total_low, high)
        ).astype(jnp.bfloat16)
        return send(
            step_ref.at[which, dp, :, cut],
            step_ref.at[which, dp, :, cut],
            x_sems.at[0, which],
            x_sems.at[1, which],
            twin,
        )

    for copy in z_copies:
        copy.wait()
    total = z_send[expert].astype(jnp.float32)
    for at in range(n_exp - 1):
        total += z_recv[at].astype(jnp.float32)
    gexp_ref[dp] = total.astype(jnp.bfloat16)
    f_copy = send(gexp_ref.at[dp], gexp_ref.at[dp], f_sems.at[0], f_sems.at[1], twin)
    mat_ref[0] = DECAY * mexp_ref[dp] + gexp_ref[dp].astype(jnp.float32)
    exp_copies = gram_start(0, mat_ref[0])
    for copy in p_copies:
        copy.wait()
    total = piece_send[expert].astype(jnp.float32)
    for at in range(n_exp - 1):
        total += piece_recv[at].astype(jnp.float32)
    whole_ref[dp, expert] = total.astype(jnp.bfloat16)
    p_copies = to_each(
        z_ids,
        lambda at, partner: whole_ref.at[dp, expert],
        lambda at, partner: whole_ref.at[dp, expert],
        w_sems,
    )
    exp_copies = gram_middle(0, exp_copies)
    for copy in p_copies:
        copy.wait()
    w_copy = send(whole_ref.at[dp], whole_ref.at[dp], f_sems.at[2], f_sems.at[3], twin)
    for copy in s_copies:
        copy.wait()
    total = small_z[0]
    for place in range(1, n_exp):
        total += small_z[place]
    sums_ref[...] = total
    lane_part = pl.ds(pl.multiple_of(ctx * cols, cols), cols)
    fresh_norm = DECAY * mnorm_ref[...] + sums_ref[0:4, lane_part]
    fresh_router = DECAY * mrouter_ref[...] + sums_ref[pl.ds(8 + ctx, 1)]
    row = lax.broadcasted_iota(jnp.int32, (8, LANES), 0)
    squares_ref[ctx] = jnp.where(
        row == 0,
        jnp.sum(fresh_norm * fresh_norm, keepdims=True),
        jnp.sum(fresh_router * fresh_router, keepdims=True),
    )
    n_copies = to_each(
        ctx_ids,
        lambda at, partner: squares_ref.at[ctx],
        lambda at, partner: squares_ref.at[ctx],
        n_sems.at[1],
    )
    w_copy.wait()
    grad = whole_ref[...].reshape(width, width).astype(jnp.float32)
    mat_ref[1, :, : 3 * cols] = DECAY * mqkv_ref[...] + grad[:, : 3 * cols]
    mat_ref[2, :, :cols] = DECAY * mproj_ref[...] + grad[:, 3 * cols :]
    mat_ref[2, :, cols : 3 * cols] = jnp.zeros((width, 2 * cols), jnp.float32)
    shared_copies = [gram_start(1, mat_ref[1 + dp, :, : 3 * cols])]
    for copy in exp_copies:
        copy.wait()
    exp_scale = gram_whole(gathered_ref.at[0], high_ref, low_ref)

    def after(turn):
        if turn == 1:
            shared_copies[0] = gram_middle(1, shared_copies[0])

    orthogonal(high_ref, low_ref, mix_ref, total_ref, after)
    exp_step = step_of(0, mat_ref[0], exp_scale)
    for copy in shared_copies[0]:
        copy.wait()
    shared_scale = gram_whole(gathered_ref.at[1], high_ref, low_ref)
    orthogonal(high_ref, low_ref, mix_ref, total_ref, lambda turn: None)
    shared_step = step_of(1, mat_ref[1 + dp, :, : 3 * cols], shared_scale)
    for copy in dx_copies + n_copies + [f_copy, exp_step, shared_step]:
        copy.wait()


def finish_kernel(
    experts,
    n_ctx,
    ctx_ref,
    gexp_ref,
    step_ref,
    whole_ref,
    sums_ref,
    squares_ref,
    dx_in,
    out_in,
    mexp_ref,
    mqkv_ref,
    mproj_ref,
    mnorm_ref,
    mrouter_ref,
    win_ref,
    wout_ref,
    wqkv_ref,
    wproj_ref,
    norm_ref,
    router_ref,
    o_out,
    o_dx,
    o_gnorm,
    o_grouter,
    o_gqkv,
    o_gproj,
    o_gin,
    o_gout,
    o_mnorm,
    o_mrouter,
    o_mqkv,
    o_mproj,
    o_min,
    o_mout,
    o_nnorm,
    o_nrouter,
    o_nqkv,
    o_nproj,
    o_nin,
    o_nout,
    o_bqkv,
    o_bproj,
    o_bin,
    o_bout,
):
    width = norm_ref.shape[1]
    cols = width // n_ctx
    o_out[...] = out_in[...]
    o_dx[...] = dx_in[...].astype(jnp.float32)

    def update(grad, moment, weight, step, columns, outs):
        o_g, o_m, o_n, o_b = outs
        rate = RATE_MAT * 0.2 * math.sqrt(max(width, columns))
        new = weight.astype(jnp.float32) - rate * step.astype(jnp.float32)
        o_g[...] = grad.reshape(o_g.shape)
        o_m[...] = (DECAY * moment + grad).reshape(o_m.shape)
        o_n[...] = new.reshape(o_n.shape)
        o_b[...] = new.astype(jnp.bfloat16).reshape(o_b.shape)

    for index, outs in enumerate(((o_gin, o_min, o_nin, o_bin), (o_gout, o_mout, o_nout, o_bout))):
        update(
            gexp_ref[index].astype(jnp.float32),
            mexp_ref[index],
            (win_ref, wout_ref)[index][0],
            step_ref[0, index],
            n_ctx * gexp_ref.shape[2],
            outs,
        )
    grad = whole_ref[...].astype(jnp.float32)
    update(
        grad[:, : 3 * cols],
        mqkv_ref[...],
        wqkv_ref[...],
        step_ref[1, 0, :, : 3 * cols],
        3 * width,
        (o_gqkv, o_mqkv, o_nqkv, o_bqkv),
    )
    update(
        grad[:, 3 * cols :],
        mproj_ref[...],
        wproj_ref[...],
        step_ref[1, 1, :, :cols],
        width,
        (o_gproj, o_mproj, o_nproj, o_bproj),
    )
    ctx = ctx_ref[0]
    own_norm = sums_ref[0:4, pl.ds(pl.multiple_of(ctx * cols, cols), cols)]
    own_router = sums_ref[pl.ds(8 + ctx, 1)]
    fresh_norm = DECAY * mnorm_ref[...] + own_norm
    fresh_router = DECAY * mrouter_ref[...] + own_router
    o_gnorm[...] = own_norm
    o_grouter[...] = own_router
    o_mnorm[...] = fresh_norm
    o_mrouter[...] = fresh_router
    squares = squares_ref[0]
    for place in range(1, n_ctx):
        squares += squares_ref[place]
    o_nnorm[...] = norm_ref[:, pl.ds(pl.multiple_of(ctx * cols, cols), cols)] - (
        RATE_GAIN * fresh_norm * lax.rsqrt(squares[0:1] / (4 * width) + EPS_NORM)
    )
    o_nrouter[...] = router_ref[...] - RATE_ROUTER * fresh_router * lax.rsqrt(
        squares[1:2, 0:1] / (width * experts) + EPS_NORM
    )


def call(kernel, ident, outs, scratch, operands, spaces=None):
    spec = pl.BlockSpec(memory_space=pltpu.VMEM)
    spaces = spaces or [pltpu.VMEM] * len(operands)
    return pl.pallas_call(
        kernel,
        out_shape=[jax.ShapeDtypeStruct(shape, dtype) for shape, dtype in outs],
        in_specs=[pl.BlockSpec(memory_space=space) for space in spaces],
        out_specs=[spec] * len(outs),
        scratch_shapes=scratch,
        compiler_params=pltpu.CompilerParams(
            collective_id=ident, has_side_effects=True, vmem_limit_bytes=VMEM_LIMIT
        ),
    )(*operands)


def gathered(
    x_in,
    d_out,
    key_mask,
    expert_ids,
    norm_params,
    w_qkv,
    w_proj,
    w_router,
    w_in,
    w_out,
    mom_norm,
    mom_router,
    mom_qkv,
    mom_proj,
    mom_in,
    mom_out,
):
    n_exp = lax.axis_size("expert")
    n_ctx = lax.axis_size("ctx")
    ctx = lax.axis_index("ctx")
    images, seq_dev, width = x_in.shape
    experts = w_router.shape[1]
    own_images = images // n_ctx
    seq = n_ctx * seq_dev
    rows = own_images * seq
    hid = w_in.shape[2]
    low, full = jnp.bfloat16, jnp.float32
    dma = lambda *shape: pltpu.SemaphoreType.DMA(shape)
    vmem = lambda shape, dtype: pltpu.VMEM(shape, dtype)

    present = jnp.any(
        expert_ids[..., None] == jnp.arange(experts, dtype=jnp.int32), axis=2
    ).astype(full)
    meta = jnp.concatenate(
        [present, key_mask[..., None].astype(full), jnp.zeros((images, seq_dev, 7 - experts), full)],
        axis=-1,
    ).swapaxes(1, 2)
    odd = (ctx % 2).astype(full)
    meta = jnp.concatenate([meta * (1 - odd), meta * odd], axis=-1)
    router = jnp.pad(w_router, ((0, 0), (0, LANES - experts)))
    router_high = router.astype(low)
    router_two = jnp.stack([router_high, (router - router_high.astype(full)).astype(low)])

    vm, anywhere = pltpu.VMEM, pl.ANY
    (
        x_all,
        first,
        qkv,
        lse,
        att,
        mid,
        d_own,
        mask_own,
        out_parts,
        dsecond,
        grads,
        grouter,
    ) = call(
        functools.partial(forward_kernel, n_exp, experts),
        1,
        [
            ((own_images, n_ctx, seq_dev, width), low),
            ((rows, width), low),
            ((rows, 3 * width), low),
            ((rows, LANES), full),
            ((rows, width), low),
            ((rows, width), full),
            ((rows, width), low),
            ((own_images, 8, seq), full),
            ((n_ctx, own_images, n_ctx, seq_dev, width), low),
            ((rows, width), full),
            ((2, n_exp, width, hid), low),
            ((8, width), full),
        ],
        [
            vmem((n_ctx, own_images, n_ctx, seq_dev, width), low),
            vmem((2, n_exp, width, hid), low),
            vmem((n_ctx, own_images, seq, width), low),
            vmem((n_ctx,) + meta.shape, full),
            vmem((width, 3 * width), low),
            vmem((width, width), low),
            vmem((n_ctx - 1, rows, width), low),
            vmem((n_ctx - 1, rows, width), low),
            vmem((2, rows, width), full),
            vmem((2, rows, width), full),
            vmem((width, LANES), full),
            vmem((2, rows, LANES), full),
            vmem((2, rows, LANES), full),
            vmem((width, n_ctx * rows), low),
            vmem((width, n_ctx * rows), low),
            vmem((n_exp, n_ctx * rows, hid), low),
            vmem((n_exp, n_ctx * rows, hid), low),
            dma(2, n_ctx - 1),
            dma(2, n_ctx - 1),
            dma(2, n_ctx - 1, n_ctx),
            dma(2, 2, 2),
            dma(2, n_ctx - 1),
            dma(2, 2, n_ctx),
            dma(2, 2),
            dma(2, n_exp - 1, 2),
            dma(2, n_exp - 1, 2),
            dma(7),
        ],
        (
            x_in,
            d_out.reshape(n_ctx, own_images, seq_dev, width),
            meta,
            w_in,
            w_out,
            norm_params,
            w_qkv,
            w_proj,
            router_two,
        ),
        [anywhere, anywhere, vm, anywhere, anywhere, vm, anywhere, anywhere, vm],
    )
    cols = width // n_ctx
    blocks = (width // LANES) * (width // LANES + 1) // 2
    block_rows = LANES // n_ctx
    moments = (
        jnp.stack([mom_in[0], mom_out[0]]),
        mom_qkv,
        mom_proj,
        mom_norm,
        mom_router.reshape(1, width),
    )
    out_low, dx_low, gexp, steps, whole, sums, squares = call(
        functools.partial(backward_kernel, n_exp, experts),
        3,
        [
            ((images, seq_dev, width), low),
            ((images, seq_dev, width), low),
            ((2, width, hid), low),
            ((2, 2, width, hid), low),
            ((2, n_exp, width // 2 // n_exp, width), low),
            ((16, width), full),
            ((n_ctx, 8, LANES), full),
        ],
        [
            vmem((n_ctx, images, seq_dev, width), low),
            vmem((n_exp, width, hid), low),
            vmem((n_exp, width, hid), low),
            vmem((n_exp - 1, width, hid), low),
            vmem((rows, width), full),
            vmem((rows, width), low),
            vmem((rows, width), low),
            vmem((rows, 3 * width), low),
            vmem((own_images, n_ctx, seq_dev, width), low),
            vmem((n_ctx, width, width), low),
            vmem((n_ctx, width // 2, width), low),
            vmem((n_ctx, width // 2, width), low),
            vmem((n_ctx - 1, width // 2, width), low),
            vmem((n_exp, width // 2 // n_exp, width), low),
            vmem((n_exp - 1, width // 2 // n_exp, width), low),
            vmem((3, width, hid), full),
            vmem((2, blocks, n_ctx, block_rows, LANES), full),
            vmem((2, n_ctx - 1, blocks, block_rows, LANES), full),
            vmem((2, blocks, n_ctx, block_rows, LANES), full),
            vmem((width, width), low),
            vmem((width, width), low),
            vmem((width, width), low),
            vmem((width, width), full),
            vmem((16, width), full),
            vmem((16, width), full),
            vmem((n_ctx, 16, width), full),
            vmem((n_exp, 16, width), full),
            dma(2, n_ctx, n_ctx - 1),
            dma(2),
            dma(2, n_exp - 1),
            dma(4),
            dma(2, n_ctx - 1),
            dma(2, 2),
            dma(2, n_ctx - 1),
            dma(2, n_ctx - 1),
            dma(2, n_exp - 1),
            dma(2, n_exp - 1),
            dma(2, 2, n_ctx - 1),
            dma(2, 2, n_ctx - 1),
            dma(2, 2),
            dma(2, 2, max(n_ctx, n_exp) - 1),
        ],
        (
            x_all.reshape(rows, width),
            d_own,
            mask_own,
            first,
            qkv,
            lse,
            att,
            mid,
            dsecond,
            grads,
            grouter,
            norm_params,
            w_qkv,
            w_proj,
            out_parts,
        )
        + moments,
    )
    cut = lambda array, count: lax.dynamic_slice_in_dim(array, ctx * count, count, 1)
    pieces = ((4, cols), (1, width), (width, 3 * cols), (width, cols), (1, width, hid), (1, width, hid))
    spec = pl.BlockSpec(memory_space=pltpu.VMEM)
    outs = (
        [((images, seq_dev, width), low), ((images, seq_dev, width), full)]
        + [(piece, full) for piece in pieces * 3]
        + [(piece, low) for piece in pieces[2:]]
    )
    results = pl.pallas_call(
        functools.partial(finish_kernel, experts, n_ctx),
        out_shape=[jax.ShapeDtypeStruct(shape, dtype) for shape, dtype in outs],
        in_specs=[pl.BlockSpec(memory_space=pltpu.SMEM)] + [spec] * 18,
        out_specs=[spec] * len(outs),
        compiler_params=pltpu.CompilerParams(vmem_limit_bytes=VMEM_LIMIT),
    )(
        ctx.reshape(1),
        gexp,
        steps,
        whole.reshape(width, width),
        sums,
        squares,
        dx_low,
        out_low,
        *moments,
        w_in,
        w_out,
        cut(w_qkv, 3 * cols),
        cut(w_proj, cols),
        norm_params,
        cut(w_router, 1).reshape(1, width),
    )
    return tuple(
        value.reshape(width, 1) if value.shape == (1, width) else value for value in results
    )


def solution(mesh):
    in_specs = (
        P(("expert", "dp"), "ctx", None),
        P(("expert", "dp"), "ctx", None),
        P(("expert", "dp"), "ctx"),
        P(("expert", "dp"), "ctx", None),
        P(),
        P(),
        P(),
        P(),
        P("expert", None, "ctx"),
        P("expert", None, "ctx"),
        P(None, "ctx"),
        P(None, "ctx"),
        P(None, "ctx"),
        P(None, "ctx"),
        P("expert", None, "ctx"),
        P("expert", None, "ctx"),
    )
    out_specs = (
        P(("expert", "dp"), "ctx", None),
        P(("expert", "dp"), "ctx", None),
        P(None, "ctx"),
        P(None, "ctx"),
        P(None, "ctx"),
        P(None, "ctx"),
        P("expert", None, "ctx"),
        P("expert", None, "ctx"),
        P(None, "ctx"),
        P(None, "ctx"),
        P(None, "ctx"),
        P(None, "ctx"),
        P("expert", None, "ctx"),
        P("expert", None, "ctx"),
        P(None, "ctx"),
        P(None, "ctx"),
        P(None, "ctx"),
        P(None, "ctx"),
        P("expert", None, "ctx"),
        P("expert", None, "ctx"),
        P(None, "ctx"),
        P(None, "ctx"),
        P("expert", None, "ctx"),
        P("expert", None, "ctx"),
    )
    experts = mesh.shape["expert"]
    square = mesh.shape["ctx"] == 4 and mesh.shape["dp"] == 2

    def local(*arrays):
        whole = (
            square
            and arrays[7].shape[1] == experts <= 7
            and arrays[8].shape[0] == 1
            and 2 * arrays[0].shape[1] == LANES
        )
        return (gathered if whole else exchanged)(*arrays)

    return jax.shard_map(local, mesh=mesh, in_specs=in_specs, out_specs=out_specs, check_vma=False)
```

```python
import functools
import math

import jax
import jax.numpy as jnp
from jax import lax
from jax.experimental import pallas as pl
from jax.experimental.pallas import tpu as pltpu
from jax.sharding import PartitionSpec as P

HEADS = 8
HEAD_DIM = 64
MICRO = 2
NS_ITERS = 4


HIGH = lax.Precision.HIGHEST
NS_A = 3.4445
NS_B = -4.775
NS_C = 2.0315
DECAY = 0.5
RATE_MAT = 0.3
RATE_GAIN = 0.3
RATE_ROUTER = 0.05
EPS_NORM = 1e-06
EPS_ORTHO = 1e-07
NEG = -1e30
LANES = 128
VMEM_LIMIT = 60 * 2**20
MESH = pl.DeviceIdType.MESH


def as_sent(array):
    return jax.tree.map(lambda a: a.astype(jnp.bfloat16) if a.dtype == jnp.float32 else a, array)


def layer_norm(values, gain, shift):
    center = jnp.mean(values, axis=-1, keepdims=True)
    spread = values - center
    power = jnp.mean(spread * spread, axis=-1, keepdims=True)
    return spread * lax.rsqrt(power + EPS_NORM) * gain + shift


def gelu_exact(values):
    return jax.nn.gelu(values, approximate=False)


def add_block(total, piece):
    return total + piece


def masked_scores(query, key_piece, mask_piece, factor):
    scores = (
        jnp.einsum("bqhd,bkhd->bhqk", query, key_piece, preferred_element_type=jnp.float32) * factor
    )
    return jnp.where(mask_piece[:, None, None, :] > 0, scores, NEG)


def gram_list(matrices):
    return tuple(
        (jnp.einsum("...ik,...jk->...ij", matrix, matrix, precision=HIGH) for matrix in matrices)
    )


def schulz_turn(matrices, grams):
    result = []
    for matrix, gram in zip(matrices, grams):
        square = jnp.einsum("...ij,...jk->...ik", gram, gram, precision=HIGH)
        mixer = NS_B * gram + NS_C * square
        result.append(
            NS_A * matrix + jnp.einsum("...ij,...jk->...ik", mixer, matrix, precision=HIGH)
        )
    return tuple(result)


def exchanged(
    x_in,
    d_out,
    key_mask,
    expert_ids,
    norm_params,
    w_qkv,
    w_proj,
    w_router,
    w_in,
    w_out,
    mom_norm,
    mom_router,
    mom_qkv,
    mom_proj,
    mom_in,
    mom_out,
):
    ctx_count = lax.axis_size("ctx")
    ctx_place = lax.axis_index("ctx")
    owner_count = lax.axis_size("expert")
    local_images = x_in.shape[0]
    seq_dev = x_in.shape[1]
    width = x_in.shape[2]
    top_count = expert_ids.shape[-1]
    experts = w_router.shape[1]
    exp_dev = w_in.shape[0]
    hid_part = w_in.shape[2]
    capacity = max(2, (5 * top_count * seq_dev + 4 * experts - 1) // (4 * experts))
    batch = local_images // MICRO
    slot_count = batch * capacity
    seq_all = seq_dev * ctx_count
    factor = HEAD_DIM ** (-0.5)
    expert_iota = jnp.arange(experts, dtype=jnp.int32)
    recv_shape = (owner_count, exp_dev, slot_count, width)
    head_shape = (batch, seq_dev, HEADS, HEAD_DIM)

    def hidden_fold(step_fn, init):
        folded = step_fn(
            init,
            (
                lax.all_gather(w_in, "ctx", axis=2, tiled=True),
                lax.all_gather(w_out, "ctx", axis=2, tiled=True),
            ),
            jnp.int32(0),
        )
        return folded

    def to_owner(rows):
        return lax.all_to_all(rows, "expert", split_axis=0, concat_axis=0, tiled=True)

    def to_source(rows):
        return lax.all_to_all(rows, "expert", split_axis=0, concat_axis=0, tiled=True)

    def key_fold(keys, values, mask_low, step_fn, init):
        return step_fn(
            init,
            (
                lax.all_gather(keys, "ctx", axis=1, tiled=True),
                lax.all_gather(values, "ctx", axis=1, tiled=True),
                lax.all_gather(mask_low, "ctx", axis=1, tiled=True),
            ),
            jnp.int32(0),
        )

    grad_qkv = jnp.zeros(w_qkv.shape, jnp.float32)
    grad_proj = jnp.zeros(w_proj.shape, jnp.float32)
    grad_router = jnp.zeros(w_router.shape, jnp.float32)
    grad_norm = jnp.zeros((4, width), jnp.float32)
    grad_in = jnp.zeros((exp_dev, width, hid_part * ctx_count), jnp.float32)
    grad_out = jnp.zeros((exp_dev, width, hid_part * ctx_count), jnp.float32)
    outputs = []
    input_grads = []
    for micro_index in range(MICRO):
        first_image = micro_index * batch
        last_image = first_image + batch
        x_part = x_in[first_image:last_image].astype(jnp.float32)
        cotangent = d_out[first_image:last_image].astype(jnp.float32)
        mask_low = key_mask[first_image:last_image].astype(jnp.bfloat16)
        idents = expert_ids[first_image:last_image]
        normed_first, pull_first = jax.vjp(layer_norm, x_part, norm_params[0], norm_params[1])
        first_low = normed_first.astype(jnp.bfloat16).reshape(-1, width)
        qkv = jnp.dot(first_low, w_qkv, preferred_element_type=jnp.float32).astype(jnp.bfloat16)
        qkv = qkv.reshape(batch, seq_dev, 3, HEADS, HEAD_DIM)
        query = qkv[:, :, 0]
        keys = qkv[:, :, 1]
        values = qkv[:, :, 2]
        peak_old = jnp.full((batch, HEADS, seq_dev), NEG, jnp.float32)
        key_piece = lax.all_gather(keys, "ctx", axis=1, tiled=True)
        mask_piece = lax.all_gather(mask_low, "ctx", axis=1, tiled=True)
        scores = masked_scores(query, key_piece, mask_piece, factor)
        peak_new = jnp.maximum(peak_old, jnp.max(scores, axis=-1))
        total_new = jnp.sum(jnp.exp(scores - peak_new[..., None]), axis=-1)
        log_total = peak_new + jnp.log(total_new)

        def attend_step(acc, pieces, start):
            key_piece, value_piece, mask_piece = pieces
            weights = jnp.exp(
                masked_scores(query, key_piece, mask_piece, factor) - log_total[..., None]
            )
            return jnp.einsum(
                "bhqk,bkhd->bqhd",
                weights.astype(jnp.bfloat16),
                value_piece,
                preferred_element_type=jnp.float32,
            )

        attended = key_fold(keys, values, mask_low, attend_step, jnp.zeros(head_shape, jnp.float32))
        attended_low = attended.astype(jnp.bfloat16).reshape(-1, width)
        branch = jnp.dot(attended_low, w_proj, preferred_element_type=jnp.float32).reshape(
            batch, seq_dev, width
        )
        mid = x_part + branch
        normed_second, pull_second = jax.vjp(layer_norm, mid, norm_params[2], norm_params[3])
        routed_low = normed_second.astype(jnp.bfloat16)
        logits = jnp.einsum("bsd,de->bse", normed_second, w_router, precision=HIGH)
        onehot = (idents[..., None] == expert_iota).astype(jnp.float32)
        chosen = jnp.sum(onehot * logits[:, :, None, :], axis=-1)
        gates = jax.nn.softmax(chosen, axis=-1)
        flat_ids = idents.reshape(batch, seq_dev * top_count)
        hits = (flat_ids[..., None] == expert_iota).astype(jnp.int32)
        ranked = jnp.sum((jnp.cumsum(hits, axis=1) - hits) * hits, axis=-1)
        slot = (ranked + (jnp.arange(batch, dtype=jnp.int32) * capacity)[:, None]).reshape(-1)
        target = flat_ids.reshape(-1)
        routed_rows = jnp.broadcast_to(
            routed_low[:, :, None, :], (batch, seq_dev, top_count, width)
        ).reshape(-1, width)
        send = (
            jnp.zeros((experts, slot_count, width), jnp.bfloat16).at[target, slot].set(routed_rows)
        )
        received = to_owner(send.reshape(recv_shape))

        def expert_step(acc, pieces, start):
            piece_in, piece_out = pieces
            pre = jnp.einsum(
                "nesd,edh->nesh", received, piece_in, preferred_element_type=jnp.float32
            )
            act = gelu_exact(pre).astype(jnp.bfloat16)
            return jnp.einsum("nesh,edh->nesd", act, piece_out, preferred_element_type=jnp.float32)

        made = hidden_fold(expert_step, jnp.zeros(recv_shape, jnp.float32))
        back_rows = to_source(made.astype(jnp.bfloat16)).reshape(experts, slot_count, width)
        returned = (
            back_rows[target, slot].reshape(batch, seq_dev, top_count, width).astype(jnp.float32)
        )
        result = mid + jnp.sum(gates[..., None] * returned, axis=2)
        outputs.append(result.astype(jnp.bfloat16))
        dgates = jnp.sum(cotangent[:, :, None, :] * returned, axis=-1)
        dchosen = gates * (dgates - jnp.sum(gates * dgates, axis=-1, keepdims=True))
        dlogits = jnp.sum(dchosen[..., None] * onehot, axis=2)
        grad_router = grad_router + jnp.einsum(
            "bsd,bse->de", normed_second, dlogits, precision=HIGH
        )
        dsecond = jnp.einsum("bse,de->bsd", dlogits, w_router, precision=HIGH)
        dreturned = (
            (gates[..., None] * cotangent[:, :, None, :]).astype(jnp.bfloat16).reshape(-1, width)
        )
        dsend = (
            jnp.zeros((experts, slot_count, width), jnp.bfloat16).at[target, slot].set(dreturned)
        )
        dreceived = to_owner(dsend.reshape(recv_shape))

        def expert_back(carry, pieces, start):
            drows, dins, douts = carry
            piece_in, piece_out = pieces
            pre = jnp.einsum(
                "nesd,edh->nesh", received, piece_in, preferred_element_type=jnp.float32
            )
            act_full, pull_act = jax.vjp(gelu_exact, pre)
            act = act_full.astype(jnp.bfloat16)
            dact = jnp.einsum(
                "nesd,edh->nesh", dreceived, piece_out, preferred_element_type=jnp.float32
            )
            dpre = pull_act(dact)[0].astype(jnp.bfloat16)
            douts = add_block(
                douts,
                jnp.einsum("nesd,nesh->edh", dreceived, act, preferred_element_type=jnp.float32),
            )
            dins = add_block(
                dins,
                jnp.einsum("nesd,nesh->edh", received, dpre, preferred_element_type=jnp.float32),
            )
            drows = jnp.einsum("nesh,edh->nesd", dpre, piece_in, preferred_element_type=jnp.float32)
            return (drows, dins, douts)

        drows, grad_in, grad_out = hidden_fold(
            expert_back, (jnp.zeros(recv_shape, jnp.float32), grad_in, grad_out)
        )
        dback = to_source(drows.astype(jnp.bfloat16)).reshape(experts, slot_count, width)
        dsecond = dsecond + jnp.sum(
            dback[target, slot].reshape(batch, seq_dev, top_count, width).astype(jnp.float32),
            axis=2,
        )
        dmid, dgain_two, dshift_two = pull_second(dsecond)
        dmid = dmid + cotangent
        dbranch = dmid.astype(jnp.bfloat16).reshape(-1, width)
        grad_proj = grad_proj + jnp.einsum(
            "sd,se->de", attended_low, dbranch, preferred_element_type=jnp.float32
        )
        dattended = jnp.einsum("se,de->sd", dbranch, w_proj, preferred_element_type=jnp.float32)
        dattended = dattended.astype(jnp.bfloat16).reshape(head_shape)
        delta = jnp.einsum("bqhd,bqhd->bhq", dattended.astype(jnp.float32), attended)

        def attend_back(carry, pieces, start):
            dquery, dkeys, dvalues = carry
            key_piece, value_piece, mask_piece = pieces
            weights = jnp.exp(
                masked_scores(query, key_piece, mask_piece, factor) - log_total[..., None]
            )
            probs = weights.astype(jnp.bfloat16)
            dvalue_piece = jnp.einsum(
                "bhqk,bqhd->bkhd", probs, dattended, preferred_element_type=jnp.float32
            )
            dprobs = jnp.einsum(
                "bqhd,bkhd->bhqk", dattended, value_piece, preferred_element_type=jnp.float32
            )
            dscores = (weights * (dprobs - delta[..., None])).astype(jnp.bfloat16)
            dquery = factor * jnp.einsum(
                "bhqk,bkhd->bqhd", dscores, key_piece, preferred_element_type=jnp.float32
            )
            dkey_piece = factor * jnp.einsum(
                "bhqk,bqhd->bkhd", dscores, query, preferred_element_type=jnp.float32
            )
            return (dquery, add_block(dkeys, dkey_piece), add_block(dvalues, dvalue_piece))

        all_shape = (batch, seq_all, HEADS, HEAD_DIM)
        back_init = (
            jnp.zeros(head_shape, jnp.float32),
            jnp.zeros(all_shape, jnp.float32),
            jnp.zeros(all_shape, jnp.float32),
        )
        dquery, dkeys_all, dvalues_all = key_fold(keys, values, mask_low, attend_back, back_init)
        dkeys, dvalues = (
            lax.psum_scatter(
                dkeys_all.astype(jnp.bfloat16), "ctx", scatter_dimension=1, tiled=True
            ).astype(jnp.float32),
            lax.psum_scatter(
                dvalues_all.astype(jnp.bfloat16), "ctx", scatter_dimension=1, tiled=True
            ).astype(jnp.float32),
        )
        dqkv = (
            jnp.stack([dquery, dkeys, dvalues], axis=2).astype(jnp.bfloat16).reshape(-1, 3 * width)
        )
        grad_qkv = grad_qkv + jnp.einsum(
            "sd,se->de", first_low, dqkv, preferred_element_type=jnp.float32
        )
        dfirst = jnp.einsum("se,de->sd", dqkv, w_qkv, preferred_element_type=jnp.float32).reshape(
            batch, seq_dev, width
        )
        dx_part, dgain_one, dshift_one = pull_first(dfirst)
        grad_norm = grad_norm + jnp.stack([dgain_one, dshift_one, dgain_two, dshift_two])
        input_grads.append(dx_part + dmid)
    block_out = jnp.concatenate(outputs, axis=0)
    d_x = jnp.concatenate(input_grads, axis=0)
    shared = (
        lax.psum_scatter(
            grad_in.astype(jnp.bfloat16), "ctx", scatter_dimension=2, tiled=True
        ).astype(jnp.float32),
        lax.psum_scatter(
            grad_out.astype(jnp.bfloat16), "ctx", scatter_dimension=2, tiled=True
        ).astype(jnp.float32),
        lax.psum_scatter(
            grad_qkv[None].astype(jnp.bfloat16), "ctx", scatter_dimension=2, tiled=True
        ).astype(jnp.float32),
        lax.psum_scatter(
            grad_proj[None].astype(jnp.bfloat16), "ctx", scatter_dimension=2, tiled=True
        ).astype(jnp.float32),
        lax.psum_scatter(
            grad_norm[None].astype(jnp.bfloat16), "ctx", scatter_dimension=2, tiled=True
        ).astype(jnp.float32),
        lax.psum_scatter(
            grad_router[None].astype(jnp.bfloat16), "ctx", scatter_dimension=2, tiled=True
        ).astype(jnp.float32),
    )
    g_in, g_out = (
        lax.psum(shared[0].astype(jnp.bfloat16), "dp").astype(jnp.float32),
        lax.psum(shared[1].astype(jnp.bfloat16), "dp").astype(jnp.float32),
    )
    g_qkv, g_proj, g_norm, g_router = lax.psum(
        (shared[2][0], shared[3][0], shared[4][0], shared[5][0]), ("expert", "dp")
    )
    own_qkv = lax.dynamic_slice_in_dim(w_qkv, ctx_place * g_qkv.shape[1], g_qkv.shape[1], 1).astype(
        jnp.float32
    )
    own_proj = lax.dynamic_slice_in_dim(
        w_proj, ctx_place * g_proj.shape[1], g_proj.shape[1], 1
    ).astype(jnp.float32)
    own_norm = lax.dynamic_slice_in_dim(
        norm_params, ctx_place * g_norm.shape[1], g_norm.shape[1], 1
    )
    own_router = lax.dynamic_slice_in_dim(
        w_router, ctx_place * g_router.shape[1], g_router.shape[1], 1
    )
    m_qkv = DECAY * mom_qkv + g_qkv
    m_proj = DECAY * mom_proj + g_proj
    m_in = DECAY * mom_in + g_in
    m_out = DECAY * mom_out + g_out
    m_norm = DECAY * mom_norm + g_norm
    m_router = DECAY * mom_router + g_router
    matrices = (m_qkv, m_proj, m_in, m_out)
    vector_squares = (jnp.sum(m_norm * m_norm), jnp.sum(m_router * m_router))
    sums = lax.psum(
        tuple((jnp.sum(matrix * matrix, axis=(-2, -1)) for matrix in matrices)) + vector_squares,
        "ctx",
    )
    vector_totals = sums[4:]
    iterates = tuple(
        (
            matrix / jnp.expand_dims(jnp.sqrt(square) + EPS_ORTHO, (-2, -1))
            for matrix, square in zip(matrices, sums[:4])
        )
    )
    for turn_index in range(NS_ITERS):
        iterates = schulz_turn(
            iterates,
            jax.tree.map(
                lambda part: part.astype(jnp.float32), lax.psum(as_sent(gram_list(iterates)), "ctx")
            ),
        )
    n_qkv = (
        own_qkv - RATE_MAT * 0.2 * math.sqrt(max(width, g_qkv.shape[1] * ctx_count)) * iterates[0]
    )
    n_proj = (
        own_proj - RATE_MAT * 0.2 * math.sqrt(max(width, g_proj.shape[1] * ctx_count)) * iterates[1]
    )
    n_in = (
        w_in.astype(jnp.float32)
        - RATE_MAT * 0.2 * math.sqrt(max(width, hid_part * ctx_count)) * iterates[2]
    )
    n_out = (
        w_out.astype(jnp.float32)
        - RATE_MAT * 0.2 * math.sqrt(max(width, hid_part * ctx_count)) * iterates[3]
    )
    n_norm = own_norm - RATE_GAIN * m_norm * lax.rsqrt(vector_totals[0] / (4 * width) + EPS_NORM)
    n_router = own_router - RATE_ROUTER * m_router * lax.rsqrt(
        vector_totals[1] / (width * experts) + EPS_NORM
    )
    return (
        block_out,
        d_x,
        g_norm,
        g_router,
        g_qkv,
        g_proj,
        g_in,
        g_out,
        m_norm,
        m_router,
        m_qkv,
        m_proj,
        m_in,
        m_out,
        n_norm,
        n_router,
        n_qkv,
        n_proj,
        n_in,
        n_out,
        n_qkv.astype(jnp.bfloat16),
        n_proj.astype(jnp.bfloat16),
        n_in.astype(jnp.bfloat16),
        n_out.astype(jnp.bfloat16),
    )


def dot(left, right, precision=None):
    return jnp.dot(left, right, precision=precision, preferred_element_type=jnp.float32)


def dot_nt(left, right, precision=None):
    return lax.dot_general(
        left, right, (((1,), (1,)), ((), ())), precision=precision, preferred_element_type=jnp.float32
    )


def dot_tn(left, right, precision=None):
    return lax.dot_general(
        left, right, (((0,), (0,)), ((), ())), precision=precision, preferred_element_type=jnp.float32
    )


def places():
    return lax.axis_index("expert"), lax.axis_index("ctx"), lax.axis_index("dp")


def ctx_partner(ctx, step):
    column, row = lax.rem(ctx, 2), ctx // 2
    column = lax.rem(column + lax.rem(step, 2), 2)
    row = lax.rem(row + step // 2, 2)
    return row * 2 + column


def z_partner(expert, step, count):
    return lax.rem(expert + step, count)


def greet(partners):
    barrier = pltpu.get_barrier_semaphore()
    for partner in partners:
        pl.semaphore_signal(barrier, inc=1, device_id=partner, device_id_type=MESH)
    pl.semaphore_wait(barrier, len(partners))


def send(source, target, send_sem, recv_sem, partner):
    copy = pltpu.make_async_remote_copy(
        src_ref=source,
        dst_ref=target,
        send_sem=send_sem,
        recv_sem=recv_sem,
        device_id=partner,
        device_id_type=MESH,
    )
    copy.start()
    return copy


def normalize(values):
    center = jnp.mean(values, axis=-1, keepdims=True)
    spread = values - center
    power = jnp.mean(spread * spread, axis=-1, keepdims=True)
    scale = lax.rsqrt(power + EPS_NORM)
    return spread * scale, scale


def normalize_back(grad, unit, scale):
    first = jnp.mean(grad, axis=-1, keepdims=True)
    second = jnp.mean(grad * unit, axis=-1, keepdims=True)
    return scale * (grad - first - unit * second)


def group_rows(meta_ref, image):
    pairs = [
        meta_ref[2 * half, image] + meta_ref[2 * half + 1, image]
        for half in range(meta_ref.shape[0] // 2)
    ]
    return jnp.concatenate(pairs, axis=1)


def split(values):
    high = values.astype(jnp.bfloat16)
    return high, (values - high.astype(jnp.float32)).astype(jnp.bfloat16)


def gelu_parts(values):
    cdf = 0.5 + 0.5 * lax.erf(values * (0.5**0.5))
    return cdf, jnp.exp(-0.5 * values * values) * (1.0 / math.sqrt(2 * math.pi))


def forward_kernel(
    n_exp,
    experts,
    x_ref,
    d_ref,
    ids_ref,
    mask_ref,
    win_ref,
    wout_ref,
    norm_ref,
    wqkv_hbm,
    wproj_hbm,
    wrouter_ref,
    o_x,
    o_first,
    o_qkv,
    o_lse,
    o_att,
    o_mid,
    o_d,
    o_mask,
    o_out,
    o_dsecond,
    o_grads,
    o_grouter,
    x_all,
    first_ref,
    qkv_ref,
    lse_ref,
    att_ref,
    mid_ref,
    mask_own,
    out_send,
    dsecond_ref,
    grads_recv,
    grouter_ref,
    d_all,
    w_all,
    r_all,
    meta_ref,
    meta_all,
    wqkv_ref,
    wproj_ref,
    router_ref,
    ds_send,
    ds_recv,
    acc_out,
    acc_ds,
    acc_router,
    gates_ref,
    dgates_ref,
    r_turn,
    d_turn,
    act_all,
    dpre_all,
    x_sems,
    m_sems,
    d_sems,
    r_sems,
    ds_sems,
    dr_sems,
    rr_sems,
    z_sems,
    s_sems,
    t_sems,
    own_sem,
    o_sems,
):
    expert, ctx, dp = places()
    own_images, n_ctx, seq_dev, width = x_all.shape
    seq = n_ctx * seq_dev
    rows = own_images * seq
    ctx_ids = [(expert, ctx_partner(ctx, step), dp) for step in range(1, n_ctx)]
    side_ids = ctx_ids[:2]
    twin = (expert, ctx, 1 - dp)
    right, left = lax.rem(expert + 1, n_exp), lax.rem(expert + n_exp - 1, n_exp)
    row = lax.broadcasted_iota(jnp.int32, (8, seq_dev), 0)
    odd = lax.rem(ctx, 2).astype(jnp.float32)
    for image in range(ids_ref.shape[0]):
        named = jnp.zeros((8, seq_dev), jnp.bool_)
        for choice in range(ids_ref.shape[1]):
            named = named | (ids_ref[image, choice : choice + 1] == row)
        values = jnp.where(
            row == experts, mask_ref[image : image + 1].astype(jnp.float32), named.astype(jnp.float32)
        )
        meta_ref[image, :, :seq_dev] = values * (1.0 - odd)
        meta_ref[image, :, seq_dev:] = values * odd
    router_ref[...] = jnp.zeros_like(router_ref)
    router_high, router_low = split(wrouter_ref[...])
    router_ref[0, :experts] = router_high.astype(jnp.float32)
    router_ref[1, :experts] = router_low.astype(jnp.float32)
    greet(ctx_ids + [(right, ctx, dp), (left, ctx, dp), twin])
    own = [
        pltpu.make_async_copy(source, target, own_sem.at[at])
        for at, (source, target) in enumerate(
            (
                (win_ref.at[0], w_all.at[0, expert]),
                (wout_ref.at[0], w_all.at[1, expert]),
                (x_ref.at[pl.ds(ctx * own_images, own_images)], x_all.at[:, ctx]),
                (wqkv_hbm, wqkv_ref),
                (wproj_hbm, wproj_ref),
                (d_ref, d_all.at[:, :, ctx]),
            )
        )
    ]
    for copy in own:
        copy.start()
    meta_all[ctx] = meta_ref[...]
    x_copies = []
    for image in range(own_images):
        x_copies.append(
            [
                send(
                    x_ref.at[partner[1] * own_images + image],
                    x_all.at[image, ctx],
                    x_sems.at[0, image, at],
                    x_sems.at[1, image, at],
                    partner,
                )
                for at, partner in enumerate(ctx_ids)
            ]
        )
        if image == 0:
            m_copies = [
                send(meta_ref, meta_all.at[ctx], m_sems.at[0, at], m_sems.at[1, at], partner)
                for at, partner in enumerate(ctx_ids)
            ]

    def hop(phase, side):
        share = expert - phase if side == 0 else expert + phase
        able = (share >= 0) & (expert < n_exp - 1) if side == 0 else (share < n_exp) & (expert > 0)
        share = jnp.clip(share, 0, n_exp - 1)
        return able, pltpu.make_async_remote_copy(
            src_ref=w_all.at[dp, share],
            dst_ref=w_all.at[dp, share],
            send_sem=z_sems.at[0, phase, side],
            recv_sem=z_sems.at[1, phase, side],
            device_id=(right if side == 0 else left, ctx, dp),
            device_id_type=MESH,
        )

    def landed(phase, side):
        share = expert - 1 - phase if side == 0 else expert + 1 + phase
        able = share >= 0 if side == 0 else share < n_exp
        share = jnp.clip(share, 0, n_exp - 1)
        place = w_all.at[dp, share]
        return (
            able,
            pltpu.make_async_remote_copy(
                src_ref=place,
                dst_ref=place,
                send_sem=z_sems.at[0, phase, side],
                recv_sem=z_sems.at[1, phase, side],
                device_id=(left if side == 0 else right, ctx, dp),
                device_id_type=MESH,
            ),
            pltpu.make_async_remote_copy(
                src_ref=place,
                dst_ref=place,
                send_sem=s_sems.at[0, phase, side],
                recv_sem=s_sems.at[1, phase, side],
                device_id=twin,
                device_id_type=MESH,
            ),
        )

    def start_hops(phase):
        for side in range(2):
            able, copy = hop(phase, side)
            pl.when(able)(copy.start)

    def take_hops(phase):
        for side in range(2):
            able, copy, shared = landed(phase, side)

            @pl.when(able)
            def _():
                copy.wait_recv()
                shared.start()

    def take_shared(phase):
        for side in range(2):
            able, _, shared = landed(phase, side)
            pl.when(able)(shared.wait_recv)

    own[0].wait()
    own[1].wait()
    start_hops(0)
    for copy in own[2:]:
        copy.wait()

    def d_copy(at, order):
        group = ctx_partner(ctx_ids[at][1], order)
        return pltpu.make_async_remote_copy(
            src_ref=d_ref.at[group],
            dst_ref=d_all.at[group, :, ctx],
            send_sem=d_sems.at[0, at, order],
            recv_sem=d_sems.at[1, at, order],
            device_id=ctx_ids[at],
            device_id_type=MESH,
        )

    def d_relay(image, order):
        target = side_ids[1 - image]
        place = d_all.at[ctx_partner(target[1], order), image, side_ids[image][1]]
        return pltpu.make_async_remote_copy(
            src_ref=place,
            dst_ref=place,
            send_sem=dr_sems.at[0, image, order],
            recv_sem=dr_sems.at[1, image, order],
            device_id=target,
            device_id_type=MESH,
        )

    def r_copy(at, image):
        return pltpu.make_async_remote_copy(
            src_ref=r_all.at[ctx, image],
            dst_ref=r_all.at[ctx, image],
            send_sem=r_sems.at[0, at, image],
            recv_sem=r_sems.at[1, at, image],
            device_id=side_ids[at],
            device_id_type=MESH,
        )

    def r_relay(image):
        place = r_all.at[side_ids[image][1], image]
        return pltpu.make_async_remote_copy(
            src_ref=place,
            dst_ref=place,
            send_sem=rr_sems.at[0, image],
            recv_sem=rr_sems.at[1, image],
            device_id=side_ids[1 - image],
            device_id_type=MESH,
        )

    for at in range(n_ctx - 1):
        d_copy(at, 0).start()
    for copy in x_copies[0] + m_copies:
        copy.wait()
    for order in range(1, n_ctx):
        for at in range(2):
            d_copy(at, order).start()
    lane = lax.broadcasted_iota(jnp.int32, (seq, LANES), 1)
    low_half = lane < HEAD_DIM
    for image in range(own_images):
        part = pl.ds(image * seq, seq)
        if image > 0:
            for copy in x_copies[image]:
                copy.wait()
        values = x_all[image].reshape(seq, width).astype(jnp.float32)
        unit, _ = normalize(values)
        first = (unit * norm_ref[0:1] + norm_ref[1:2]).astype(jnp.bfloat16)
        first_ref[part] = first
        qkv_ref[part] = dot(first, wqkv_ref[...]).astype(jnp.bfloat16)
        key_mask = group_rows(meta_all, ctx * own_images + image)[experts : experts + 1]
        mask_own[image] = jnp.broadcast_to(key_mask, mask_own.shape[1:])
        bias = jnp.where(key_mask > 0, 0.0, NEG)
        totals = jnp.zeros((seq, LANES), jnp.float32)
        for pair in range(HEADS // 2):
            query = qkv_ref[part, pair * LANES : (pair + 1) * LANES]
            keys = qkv_ref[part, width + pair * LANES : width + (pair + 1) * LANES]
            heads = qkv_ref[part, 2 * width + pair * LANES : 2 * width + (pair + 1) * LANES]
            query = query * jnp.bfloat16(HEAD_DIM**-0.5)
            parts = []
            for half in range(2):
                chosen = low_half if half == 0 else ~low_half
                scores = dot_nt(jnp.where(chosen, query, jnp.zeros_like(query)), keys) + bias
                peak = jnp.max(scores, axis=-1, keepdims=True)
                raised = jnp.exp(scores - peak)
                total = jnp.sum(raised, axis=-1, keepdims=True)
                probs = (raised * (1.0 / total)).astype(jnp.bfloat16)
                parts.append(dot(probs, heads))
                totals = jnp.where(lane == 2 * pair + half, peak + jnp.log(total), totals)
            att_ref[part, pair * LANES : (pair + 1) * LANES] = jnp.where(
                low_half, parts[0], parts[1]
            ).astype(jnp.bfloat16)
        lse_ref[part] = totals
        mid = values + dot(att_ref[part], wproj_ref[...])
        mid_ref[part] = mid
        unit, _ = normalize(mid)
        r_all[ctx, image] = (unit * norm_ref[2:3] + norm_ref[3:4]).astype(jnp.bfloat16)
        for at in range(2):
            r_copy(at, image).start()
        if image == 0:
            take_hops(0)
            start_hops(1)

    kept_copies = [
        pltpu.make_async_copy(source, target, o_sems.at[at])
        for at, (source, target) in enumerate(
            (
                (x_all, o_x),
                (first_ref, o_first),
                (qkv_ref, o_qkv),
                (lse_ref, o_lse),
                (att_ref, o_att),
                (mid_ref, o_mid),
                (mask_own, o_mask),
            )
        )
    ]
    for copy in kept_copies:
        copy.start()

    def out_copy(chunk):
        return pltpu.make_async_copy(out_send.at[chunk], o_out.at[chunk], o_sems.at[8 + chunk])

    near = jnp.where(expert < n_exp // 2, expert + 1, expert - 1)
    last = jnp.where(expert < n_exp // 2, n_exp - 1, 0)
    middle = n_exp * (n_exp - 1) // 2 - expert - near - last

    def start_chunk(chunk, slot, owner):
        columns = pl.ds(pl.multiple_of(chunk * rows, rows), rows)
        routed = r_all[owner].reshape(rows, width)
        r_turn[:, columns] = routed.T
        d_turn[:, columns] = d_all[owner].reshape(rows, width).T
        present = jnp.concatenate(
            [group_rows(meta_all, owner * own_images + image) for image in range(own_images)], axis=1
        )
        present = jnp.concatenate(
            [present, jnp.zeros((LANES - present.shape[0], rows), jnp.float32)], axis=0
        ).T
        present = (present > 0) & (wide < experts)
        logits = dot_nt(routed, router_ref[0].astype(jnp.bfloat16)) + dot_nt(
            routed, router_ref[1].astype(jnp.bfloat16)
        )
        peak = jnp.max(jnp.where(present, logits, NEG), axis=-1, keepdims=True)
        raised = jnp.where(present, jnp.exp(jnp.where(present, logits - peak, 0.0)), 0.0)
        gates_ref[slot] = raised / jnp.sum(raised, axis=-1, keepdims=True)
        dgates_ref[slot] = jnp.zeros((rows, LANES), jnp.float32)
        acc_out[slot] = jnp.zeros(acc_out.shape[1:], jnp.float32)
        acc_ds[slot] = jnp.zeros(acc_ds.shape[1:], jnp.float32)

    def end_chunk(chunk, slot):
        columns = pl.ds(pl.multiple_of(chunk * rows, rows), rows)
        gates = gates_ref[slot]
        dgates = dgates_ref[slot]
        dlogits = gates * (dgates - jnp.sum(gates * dgates, axis=-1, keepdims=True))
        high, low = split(dlogits)
        turned = r_turn[:, columns]
        acc_router[...] += dot(turned, high) + dot(turned, low)
        total = (
            acc_ds[slot]
            + dot(high, router_ref[0].astype(jnp.bfloat16))
            + dot(high, router_ref[1].astype(jnp.bfloat16))
            + dot(low, router_ref[0].astype(jnp.bfloat16))
        )
        if chunk == 0:
            dsecond_ref[...] = total
            out = acc_out[slot] + mid_ref[...]
        else:
            ds_send[chunk - 1] = total.astype(jnp.bfloat16)
            out = acc_out[slot]
        out_send[chunk] = out.astype(jnp.bfloat16).reshape(out_send.shape[1:])
        out_copy(chunk).start()

    def ds_copy(chunk):
        return pltpu.make_async_remote_copy(
            src_ref=ds_send.at[chunk - 1],
            dst_ref=ds_recv.at[chunk - 1],
            send_sem=ds_sems.at[0, chunk - 1],
            recv_sem=ds_sems.at[1, chunk - 1],
            device_id=ctx_ids[chunk - 1],
            device_id_type=MESH,
        )

    acc_router[...] = jnp.zeros_like(acc_router)

    def place_of(step):
        chunk = jnp.where(
            step < 8, jnp.where((step < 3) | (step == 6), 0, 1), step // 4
        )
        rank = jnp.where(
            step < 8,
            jnp.where(step < 3, step, jnp.where(step < 6, step - 3, 3)),
            lax.rem(step, 4),
        )
        index = jnp.where(
            rank == 0, expert, jnp.where(rank == 1, near, jnp.where(rank == 2, middle, last))
        )
        return chunk, lax.rem(chunk, 2), index

    def hidden(step):
        chunk, slot, index = place_of(step)
        owner = ctx_partner(ctx, chunk)
        pre = dot(r_all[owner].reshape(rows, width), w_all[0, index])
        dact = dot(d_all[owner].reshape(rows, width), w_all[1, index])
        gate = jnp.sum(jnp.where(wide == index, gates_ref[slot], 0.0), axis=-1, keepdims=True)
        cdf, density = gelu_parts(pre)
        act = pre * cdf
        dgate = jnp.sum(dact * act, axis=-1, keepdims=True)
        dgates_ref[slot] = jnp.where(wide == index, dgate, dgates_ref[slot])
        kept = pl.ds(pl.multiple_of(chunk * rows, rows), rows)
        act_all[index, kept] = (gate * act).astype(jnp.bfloat16)
        dpre_all[index, kept] = (gate * dact * (cdf + pre * density)).astype(jnp.bfloat16)

    def back_out(step):
        chunk, slot, index = place_of(step)
        kept = pl.ds(pl.multiple_of(chunk * rows, rows), rows)
        acc_out[slot] += dot_nt(act_all[index, kept], w_all[1, index])
        acc_ds[slot] += dot_nt(dpre_all[index, kept], w_all[0, index])

    wide = lax.broadcasted_iota(jnp.int32, (rows, LANES), 1)
    for at in range(n_ctx - 1):
        d_copy(at, 0).wait_recv()
    start_chunk(0, 0, ctx)
    hidden(0)

    def one_step(step, carry):
        @pl.when(step == 1)
        def _():
            take_shared(0)
            for order in range(1, n_ctx):
                for at in range(2):
                    d_copy(at, order).wait_recv()
            for order in range(1, n_ctx):
                for image in range(2):
                    d_relay(image, order).start()

        @pl.when(step == 2)
        def _():
            take_hops(1)
            start_hops(2)
            take_shared(1)

        @pl.when(step == 3)
        def _():
            for image in range(2):
                r_copy(0, image).wait_recv()
                d_relay(image, 1).wait_recv()
            r_relay(0).start()
            start_chunk(1, 1, ctx_ids[0][1])

        @pl.when(step == 4)
        def _():
            for image in range(2):
                r_copy(1, image).wait_recv()
            r_relay(1).start()

        @pl.when(step == 6)
        def _():
            take_hops(2)
            take_shared(2)

        @pl.when(step == 8)
        def _():
            for image in range(2):
                d_relay(image, 2).wait_recv()
            start_chunk(2, 0, ctx_ids[1][1])

        @pl.when(step == 12)
        def _():
            for image in range(2):
                d_relay(image, 3).wait_recv()
                r_relay(image).wait_recv()
            start_chunk(3, 1, ctx_ids[2][1])

        back_out(step - 1)
        hidden(step)

        @pl.when(step == 7)
        def _():
            end_chunk(0, 0)

        @pl.when(step == 8)
        def _():
            end_chunk(1, 1)
            ds_copy(1).start()

        @pl.when(step == 12)
        def _():
            end_chunk(2, 0)
            ds_copy(2).start()

        return carry

    lax.fori_loop(1, n_ctx * n_exp, one_step, 0)
    back_out(n_ctx * n_exp - 1)
    end_chunk(3, 1)
    ds_copy(3).start()

    d_kept = pltpu.make_async_copy(d_all.at[ctx], o_d, o_sems.at[7])
    d_kept.start()

    def grad_at(which, index):
        return act_all.at[index, pl.ds(pl.multiple_of(which * width, width), width)]

    def t_copy(index):
        return pltpu.make_async_remote_copy(
            src_ref=grad_at(1 - dp, index),
            dst_ref=grads_recv.at[index],
            send_sem=t_sems.at[0, index],
            recv_sem=t_sems.at[1, index],
            device_id=twin,
            device_id_type=MESH,
        )

    def one_expert(index, carry):
        grad_out = dot(d_turn[...], act_all[index]).astype(jnp.bfloat16)
        grad_at(0, index)[...] = dot(r_turn[...], dpre_all[index]).astype(jnp.bfloat16)
        grad_at(1, index)[...] = grad_out
        t_copy(index).start()
        return carry

    lax.fori_loop(0, n_exp, one_expert, 0)
    grouter_ref[...] = acc_router[...].T[: grouter_ref.shape[0]]
    for index in range(n_exp):
        t_copy(index).wait()
        grad_at(dp, index)[...] = (
            grad_at(dp, index)[...].astype(jnp.float32) + grads_recv[index].astype(jnp.float32)
        ).astype(jnp.bfloat16)
    last_copies = [pltpu.make_async_copy(grouter_ref, o_grouter, o_sems.at[13])] + [
        pltpu.make_async_copy(grad_at(dp, index), o_grads.at[index], o_sems.at[15 + index])
        for index in range(n_exp)
    ]
    for copy in last_copies:
        copy.start()
    for phase in range(n_exp - 1):
        for side in range(2):
            able, copy = hop(phase, side)
            pl.when(able)(copy.wait_send)
            able, _, shared = landed(phase, side)
            pl.when(able)(shared.wait_send)
    for at in range(n_ctx - 1):
        for order in range(n_ctx if at < 2 else 1):
            d_copy(at, order).wait_send()
    for image in range(2):
        r_relay(image).wait_send()
        for at in range(2):
            r_copy(at, image).wait_send()
        for order in range(1, n_ctx):
            d_relay(image, order).wait_send()
    for chunk in range(1, n_ctx):
        ds_copy(chunk).wait()
        dsecond_ref[...] += ds_recv[chunk - 1].astype(jnp.float32)
    last_copies.append(pltpu.make_async_copy(dsecond_ref, o_dsecond, o_sems.at[14]))
    last_copies[-1].start()
    for copy in kept_copies + [d_kept] + last_copies:
        copy.wait()
    for chunk in range(n_ctx):
        out_copy(chunk).wait()


def gram_blocks(matrix, packed_ref):
    size = matrix.shape[0]
    index = 0
    for row in range(size // LANES):
        strip = dot_nt(matrix[row * LANES : (row + 1) * LANES], matrix[row * LANES :])
        for col in range(size // LANES - row):
            packed_ref[index] = strip[:, col * LANES : (col + 1) * LANES].reshape(
                packed_ref.shape[1:]
            )
            index += 1


def gram_whole(packed_ref, high_ref, low_ref):
    count = high_ref.shape[0] // LANES
    diagonal = lax.broadcasted_iota(jnp.int32, (LANES, LANES), 0) == lax.broadcasted_iota(
        jnp.int32, (LANES, LANES), 1
    )
    places_of = {}
    square = jnp.zeros((1, 1), jnp.float32)
    index = 0
    for row in range(count):
        for col in range(row, count):
            places_of[index] = (row, col)
            if row == col:
                block = packed_ref[index].reshape(LANES, LANES)
                square += jnp.sum(jnp.where(diagonal, block, 0.0), keepdims=True)
            index += 1
    scale = 1.0 / (jnp.sqrt(square) + EPS_ORTHO)
    for index, (row, col) in places_of.items():
        block = packed_ref[index].reshape(LANES, LANES) * (scale * scale)
        rows, cols = pl.ds(row * LANES, LANES), pl.ds(col * LANES, LANES)
        high_ref[rows, cols], low_ref[rows, cols] = split(block)
        if row != col:
            high_ref[cols, rows], low_ref[cols, rows] = split(block.T)
    return scale


def orthogonal(high_ref, low_ref, mix_ref, total_ref):
    size = high_ref.shape[0]
    eye = lax.broadcasted_iota(jnp.int32, (size, size), 0) == lax.broadcasted_iota(
        jnp.int32, (size, size), 1
    )
    for turn in range(NS_ITERS):
        high, low = high_ref[...], low_ref[...]
        square = dot(high, high)
        if turn == NS_ITERS - 1:
            square += dot(high, low) + dot(low, high)
        mix_ref[...] = (
            jnp.where(eye, NS_A, 0.0)
            + NS_B * (high.astype(jnp.float32) + low.astype(jnp.float32))
            + NS_C * square
        ).astype(jnp.bfloat16)
        mix = mix_ref[...]
        if turn == 0:
            total_ref[...] = mix.astype(jnp.float32)
        else:
            total_high, total_low = split(total_ref[...])
            total_ref[...] = dot(mix, total_high) + dot(mix, total_low)
        if turn < NS_ITERS - 1:
            turned_high, turned_low = split(dot(mix, high) + dot(mix, low))
            high_ref[...], low_ref[...] = split(dot(turned_high, mix) + dot(turned_low, mix))


def backward_kernel(
    n_exp,
    h_x,
    h_d,
    h_mask,
    h_first,
    h_qkv,
    h_lse,
    h_att,
    h_mid,
    h_dsecond,
    h_grads,
    grouter_ref,
    norm_ref,
    h_wqkv,
    h_wproj,
    h_out,
    h_min,
    h_mout,
    h_mqkv,
    h_mproj,
    mnorm_ref,
    mrouter_ref,
    out_ref,
    dx_ref,
    gexp_ref,
    step_ref,
    whole_ref,
    sums_ref,
    squares_ref,
    x_ref,
    d_ref,
    mask_ref,
    first_ref,
    qkv_ref,
    lse_ref,
    att_ref,
    mid_ref,
    dsecond_ref,
    own_grads,
    wqkv_ref,
    wproj_ref,
    out_own,
    mexp_ref,
    mqkv_ref,
    mproj_ref,
    out_recv,
    z_recv,
    dmid_ref,
    dbranch_ref,
    datt_ref,
    dqkv_ref,
    dx_send,
    shared_ref,
    half_recv,
    sum_one,
    ctx_recv,
    piece_send,
    piece_recv,
    mat_ref,
    packed_ref,
    packed_recv,
    gathered_ref,
    high_ref,
    low_ref,
    mix_ref,
    total_ref,
    small_ref,
    small_twin,
    small_ctx,
    small_z,
    in_sems,
    out_sems,
    z_sems,
    f_sems,
    dx_sems,
    h_sems,
    c_sems,
    s_sems,
    p_sems,
    w_sems,
    g_sems,
    a_sems,
    x_sems,
    n_sems,
):
    expert, ctx, dp = places()
    own_images, n_ctx, seq_dev, width = dx_send.shape
    seq = n_ctx * seq_dev
    half = width // 2
    cols = width // n_ctx
    loads = {}

    def load(name, source, target):
        loads[name] = pltpu.make_async_copy(source, target, in_sems.at[len(loads)])
        return loads[name]

    def take(*names):
        for name in names:
            loads[name].wait()

    for name, source, target in (
        ("mid", h_mid, mid_ref),
        ("dsecond", h_dsecond, dsecond_ref),
        ("d", h_d, d_ref),
        ("wproj", h_wproj, wproj_ref),
        ("qkv", h_qkv, qkv_ref),
        ("lse", h_lse, lse_ref),
        ("mask", h_mask, mask_ref),
        ("att", h_att, att_ref),
        ("first", h_first, first_ref),
        ("wqkv", h_wqkv, wqkv_ref),
        ("x", h_x, x_ref),
        ("grads", h_grads.at[expert], own_grads),
        ("out", h_out.at[:, :, ctx], out_own),
        ("mqkv", h_mqkv, mqkv_ref),
        ("mproj", h_mproj, mproj_ref),
    ):
        load(name, source, target).start()
    moment = [
        pltpu.make_async_copy(source.at[0], mexp_ref, in_sems.at[len(loads)])
        for source in (h_min, h_mout)
    ]
    pl.when(dp == 0)(moment[0].start)
    pl.when(dp == 1)(moment[1].start)
    ctx_ids = [(expert, ctx_partner(ctx, step), dp) for step in range(1, n_ctx)]
    z_steps = [1, n_exp - 1] + list(range(2, n_exp - 1))
    z_ids = [(z_partner(expert, step, n_exp), ctx, dp) for step in z_steps]
    twin = (expert, ctx, 1 - dp)
    greet(ctx_ids + z_ids + [twin])

    def to_each(partners, source, target, sems):
        return [
            send(source(at, partner), target(at, partner), sems.at[0, at], sems.at[1, at], partner)
            for at, partner in enumerate(partners)
        ]

    z_copies = to_each(
        z_ids, lambda at, partner: h_grads.at[partner[0]], lambda at, partner: z_recv.at[at], z_sems
    )
    out_copies = []
    for step in range(n_ctx):
        first_image = ctx_partner(ctx, step) * own_images
        for at, partner in enumerate(ctx_ids):
            out_copies.append(
                send(
                    h_out.at[step, :, partner[1]],
                    out_recv.at[ctx, pl.ds(first_image, own_images)],
                    out_sems.at[0, step, at],
                    out_sems.at[1, step, at],
                    partner,
                )
            )
    gain_one, gain_two = norm_ref[0:1], norm_ref[2:3]
    sums = [jnp.zeros((1, width), jnp.float32) for _ in range(4)]
    take("mid", "dsecond", "d", "wproj")
    for image in range(own_images):
        rows = pl.ds(image * seq, seq)
        unit, scale = normalize(mid_ref[rows])
        grad = dsecond_ref[rows]
        sums[2] += jnp.sum(grad * unit, axis=0, keepdims=True)
        sums[3] += jnp.sum(grad, axis=0, keepdims=True)
        dmid = normalize_back(grad * gain_two, unit, scale) + d_ref[rows].astype(jnp.float32)
        dmid_ref[rows] = dmid
        dbranch = dmid.astype(jnp.bfloat16)
        dbranch_ref[rows] = dbranch
        datt_ref[rows] = dot_nt(dbranch, wproj_ref[...]).astype(jnp.bfloat16)
    take("qkv", "lse", "mask")
    lane = lax.broadcasted_iota(jnp.int32, (seq, LANES), 1)
    low_half = lane < HEAD_DIM
    factor = HEAD_DIM**-0.5
    for image in range(own_images):
        rows = pl.ds(image * seq, seq)
        bias = jnp.where(mask_ref[image, 0:1] > 0, 0.0, NEG)
        totals = lse_ref[rows]
        for pair in range(HEADS // 2):
            at = pair * LANES
            query = qkv_ref[rows, at : at + LANES] * jnp.bfloat16(factor)
            keys = qkv_ref[rows, width + at : width + at + LANES]
            heads = qkv_ref[rows, 2 * width + at : 2 * width + at + LANES]
            datt = datt_ref[rows, at : at + LANES]
            dquery, dkeys, dheads = [], [], []
            for part in range(2):
                chosen = low_half if part == 0 else ~low_half
                scores = dot_nt(jnp.where(chosen, query, jnp.zeros_like(query)), keys) + bias
                head = 2 * pair + part
                weights = jnp.exp(scores - totals[:, head : head + 1])
                dprobs = dot_nt(jnp.where(chosen, datt, jnp.zeros_like(datt)), heads)
                delta = jnp.sum(weights * dprobs, axis=-1, keepdims=True)
                dscores = (weights * (dprobs - delta)).astype(jnp.bfloat16)
                dquery.append(dot(dscores, keys))
                dkeys.append(dot_tn(dscores, query))
                dheads.append(dot_tn(weights.astype(jnp.bfloat16), datt))
            dqkv_ref[rows, at : at + LANES] = (
                jnp.where(low_half, dquery[0], dquery[1]) * factor
            ).astype(jnp.bfloat16)
            dqkv_ref[rows, width + at : width + at + LANES] = jnp.where(
                low_half, dkeys[0], dkeys[1]
            ).astype(jnp.bfloat16)
            dqkv_ref[rows, 2 * width + at : 2 * width + at + LANES] = jnp.where(
                low_half, dheads[0], dheads[1]
            ).astype(jnp.bfloat16)
    take("att", "first")
    gproj = dot_tn(att_ref[...], dbranch_ref[...]).astype(jnp.bfloat16)
    gqkv = dot_tn(first_ref[...], dqkv_ref[...]).astype(jnp.bfloat16)
    for place in range(n_ctx):
        shared_ref[place, :, : 3 * cols] = gqkv[:, 3 * cols * place : 3 * cols * (place + 1)]
        shared_ref[place, :, 3 * cols :] = gproj[:, place * cols : (place + 1) * cols]
    own_half = pl.ds(pl.multiple_of(dp * half, half), half)
    other_half = pl.ds(pl.multiple_of((1 - dp) * half, half), half)
    h_copy = send(shared_ref.at[:, other_half], half_recv, h_sems.at[0, 0], h_sems.at[1, 0], twin)
    take("wqkv", "x")
    for image in range(own_images):
        rows = pl.ds(image * seq, seq)
        grad = dot_nt(dqkv_ref[rows], wqkv_ref[...])
        unit, scale = normalize(x_ref[rows].astype(jnp.float32))
        sums[0] += jnp.sum(grad * unit, axis=0, keepdims=True)
        sums[1] += jnp.sum(grad, axis=0, keepdims=True)
        dx = dmid_ref[rows] + normalize_back(grad * gain_one, unit, scale)
        dx_send[image] = dx.astype(jnp.bfloat16).reshape(n_ctx, seq_dev, width)
        if image == 0:
            h_copy.wait()
            for place in range(n_ctx):
                sum_one[place] = (
                    shared_ref[place, own_half].astype(jnp.float32)
                    + half_recv[place].astype(jnp.float32)
                ).astype(jnp.bfloat16)
            c_copies = to_each(
                ctx_ids,
                lambda at, partner: sum_one.at[partner[1]],
                lambda at, partner: ctx_recv.at[at],
                c_sems,
            )
    for at, total in enumerate(sums):
        small_ref[at : at + 1] = total
    small_ref[4:8] = jnp.zeros((4, width), jnp.float32)
    small_ref[8:16] = grouter_ref[...]
    s_copy = send(small_ref, small_twin, h_sems.at[0, 1], h_sems.at[1, 1], twin)
    dx_copies = to_each(
        ctx_ids,
        lambda at, partner: dx_send.at[:, partner[1]],
        lambda at, partner: dx_ref.at[pl.ds(ctx * own_images, own_images)],
        dx_sems,
    )
    for image in range(own_images):
        dx_ref[ctx * own_images + image] = dx_send[image, ctx]
    s_copy.wait()
    small_ctx[ctx] = small_ref[...] + small_twin[...]
    s_copies = to_each(
        ctx_ids, lambda at, partner: small_ctx.at[ctx], lambda at, partner: small_ctx.at[ctx], s_sems
    )
    take("out")
    for copy in out_copies:
        copy.wait()
    for step in range(n_ctx):
        start = ctx_partner(ctx, step) * own_images
        for image in range(own_images):
            total = out_own[step, image].astype(jnp.float32)
            for at in range(n_ctx - 1):
                total += out_recv[ctx_partner(ctx, at + 1), start + image].astype(jnp.float32)
            out_ref[start + image] = total.astype(jnp.bfloat16)
    for copy in c_copies:
        copy.wait()
    total = sum_one[ctx].astype(jnp.float32)
    for at in range(n_ctx - 1):
        total += ctx_recv[at].astype(jnp.float32)
    piece_send[...] = total.astype(jnp.bfloat16).reshape(piece_send.shape)
    p_copies = to_each(
        z_ids,
        lambda at, partner: piece_send.at[partner[0]],
        lambda at, partner: piece_recv.at[at],
        p_sems,
    )
    for copy in s_copies:
        copy.wait()
    total = small_ctx[0]
    for place in range(1, n_ctx):
        total += small_ctx[place]
    small_z[expert] = total
    s_copies = to_each(
        z_ids,
        lambda at, partner: small_z.at[expert],
        lambda at, partner: small_z.at[expert],
        n_sems.at[0],
    )

    def gram_start(which, matrix):
        gram_blocks(matrix.astype(jnp.bfloat16), packed_ref.at[which])
        return to_each(
            ctx_ids,
            lambda at, partner: packed_ref.at[which, :, partner[1]],
            lambda at, partner: packed_recv.at[which, at],
            g_sems.at[which],
        )

    def gram_middle(which, copies):
        for copy in copies:
            copy.wait()
        total = packed_ref[which, :, ctx]
        for at in range(n_ctx - 1):
            total += packed_recv[which, at]
        gathered_ref[which, :, ctx] = total
        return to_each(
            ctx_ids,
            lambda at, partner: gathered_ref.at[which, :, ctx],
            lambda at, partner: gathered_ref.at[which, :, ctx],
            a_sems.at[which],
        )

    def step_of(which, matrix, scale):
        total_high, total_low = split(total_ref[...])
        high, low = split(matrix * scale)
        cut = pl.ds(0, matrix.shape[1])
        step_ref[which, dp, :, cut] = (
            dot(total_high, high) + dot(total_high, low) + dot(total_low, high)
        ).astype(jnp.bfloat16)
        return send(
            step_ref.at[which, dp, :, cut],
            step_ref.at[which, dp, :, cut],
            x_sems.at[0, which],
            x_sems.at[1, which],
            twin,
        )

    for copy in p_copies:
        copy.wait()
    total = piece_send[expert].astype(jnp.float32)
    for at in range(n_exp - 1):
        total += piece_recv[at].astype(jnp.float32)
    whole_ref[dp, expert] = total.astype(jnp.bfloat16)
    p_copies = to_each(
        z_ids,
        lambda at, partner: whole_ref.at[dp, expert],
        lambda at, partner: whole_ref.at[dp, expert],
        w_sems,
    )
    take("grads")
    for copy in z_copies:
        copy.wait()
    total = own_grads[...].astype(jnp.float32)
    for at in range(n_exp - 1):
        total += z_recv[at].astype(jnp.float32)
    gexp_ref[dp] = total.astype(jnp.bfloat16)
    f_copy = send(gexp_ref.at[dp], gexp_ref.at[dp], f_sems.at[0], f_sems.at[1], twin)
    moment[0].wait()
    mat_ref[0] = DECAY * mexp_ref[...] + gexp_ref[dp].astype(jnp.float32)
    exp_copies = gram_start(0, mat_ref[0])
    for copy in p_copies:
        copy.wait()
    w_copy = send(whole_ref.at[dp], whole_ref.at[dp], f_sems.at[2], f_sems.at[3], twin)
    for copy in s_copies:
        copy.wait()
    total = small_z[0]
    for place in range(1, n_exp):
        total += small_z[place]
    sums_ref[...] = total
    lane_part = pl.ds(pl.multiple_of(ctx * cols, cols), cols)
    fresh_norm = DECAY * mnorm_ref[...] + sums_ref[0:4, lane_part]
    fresh_router = DECAY * mrouter_ref[...] + sums_ref[pl.ds(8 + ctx, 1)]
    row = lax.broadcasted_iota(jnp.int32, (8, LANES), 0)
    squares_ref[ctx] = jnp.where(
        row == 0,
        jnp.sum(fresh_norm * fresh_norm, keepdims=True),
        jnp.sum(fresh_router * fresh_router, keepdims=True),
    )
    n_copies = to_each(
        ctx_ids,
        lambda at, partner: squares_ref.at[ctx],
        lambda at, partner: squares_ref.at[ctx],
        n_sems.at[1],
    )
    w_copy.wait()
    take("mqkv", "mproj")
    grad = whole_ref[...].reshape(width, width).astype(jnp.float32)
    mat_ref[1, :, : 3 * cols] = DECAY * mqkv_ref[...] + grad[:, : 3 * cols]
    mat_ref[2, :, :cols] = DECAY * mproj_ref[...] + grad[:, 3 * cols :]
    mat_ref[2, :, cols : 3 * cols] = jnp.zeros((width, 2 * cols), jnp.float32)
    shared_copies = [gram_start(1, mat_ref[1 + dp, :, : 3 * cols])]
    exp_copies = gram_middle(0, exp_copies)
    shared_copies[0] = gram_middle(1, shared_copies[0])
    for copy in exp_copies:
        copy.wait()
    exp_scale = gram_whole(gathered_ref.at[0], high_ref, low_ref)

    orthogonal(high_ref, low_ref, mix_ref, total_ref)
    exp_step = step_of(0, mat_ref[0], exp_scale)
    for copy in shared_copies[0]:
        copy.wait()
    shared_scale = gram_whole(gathered_ref.at[1], high_ref, low_ref)
    orthogonal(high_ref, low_ref, mix_ref, total_ref)
    shared_step = step_of(1, mat_ref[1 + dp, :, : 3 * cols], shared_scale)
    for copy in dx_copies + n_copies + [f_copy, exp_step, shared_step]:
        copy.wait()


def finish_kernel(
    experts,
    n_ctx,
    width,
    ctx_ref,
    gexp_ref,
    step_ref,
    whole_ref,
    sums_ref,
    squares_ref,
    dx_in,
    out_in,
    min_ref,
    mout_ref,
    mqkv_ref,
    mproj_ref,
    mnorm_ref,
    mrouter_ref,
    win_ref,
    wout_ref,
    wqkv_ref,
    wproj_ref,
    norm_ref,
    router_ref,
    o_out,
    o_dx,
    o_gnorm,
    o_grouter,
    o_gqkv,
    o_gproj,
    o_gin,
    o_gout,
    o_mnorm,
    o_mrouter,
    o_mqkv,
    o_mproj,
    o_min,
    o_mout,
    o_nnorm,
    o_nrouter,
    o_nqkv,
    o_nproj,
    o_nin,
    o_nout,
    o_bqkv,
    o_bproj,
    o_bin,
    o_bout,
):
    cols = width // n_ctx
    o_out[...] = out_in[...]
    o_dx[...] = dx_in[...].astype(jnp.float32)

    def update(grad, moment, weight, step, columns, outs):
        o_g, o_m, o_n, o_b = outs
        rate = RATE_MAT * 0.2 * math.sqrt(max(width, columns))
        new = weight.astype(jnp.float32) - rate * step.astype(jnp.float32)
        o_g[...] = grad.reshape(o_g.shape)
        o_m[...] = (DECAY * moment + grad).reshape(o_m.shape)
        o_n[...] = new.reshape(o_n.shape)
        o_b[...] = new.astype(jnp.bfloat16).reshape(o_b.shape)

    for index, outs in enumerate(((o_gin, o_min, o_nin, o_bin), (o_gout, o_mout, o_nout, o_bout))):
        update(
            gexp_ref[index].astype(jnp.float32),
            (min_ref, mout_ref)[index][0],
            (win_ref, wout_ref)[index][0],
            step_ref[0, index],
            n_ctx * gexp_ref.shape[2],
            outs,
        )
    grad = whole_ref[...].astype(jnp.float32)
    update(
        grad[:, : 3 * cols],
        mqkv_ref[...],
        wqkv_ref[...],
        step_ref[1, 0, :, : 3 * cols],
        3 * width,
        (o_gqkv, o_mqkv, o_nqkv, o_bqkv),
    )
    update(
        grad[:, 3 * cols :],
        mproj_ref[...],
        wproj_ref[...],
        step_ref[1, 1, :, :cols],
        width,
        (o_gproj, o_mproj, o_nproj, o_bproj),
    )
    ctx = ctx_ref[0]
    own_norm = sums_ref[0:4, pl.ds(pl.multiple_of(ctx * cols, cols), cols)]
    own_router = sums_ref[pl.ds(8 + ctx, 1)]
    fresh_norm = DECAY * mnorm_ref[...] + own_norm
    fresh_router = DECAY * mrouter_ref[...] + own_router
    o_gnorm[...] = own_norm
    o_grouter[...] = own_router
    o_mnorm[...] = fresh_norm
    o_mrouter[...] = fresh_router
    squares = squares_ref[0]
    for place in range(1, n_ctx):
        squares += squares_ref[place]
    o_nnorm[...] = norm_ref[...] - (
        RATE_GAIN * fresh_norm * lax.rsqrt(squares[0:1] / (4 * width) + EPS_NORM)
    )
    o_nrouter[...] = router_ref[pl.ds(ctx, 1)] - RATE_ROUTER * fresh_router * lax.rsqrt(
        squares[1:2, 0:1] / (width * experts) + EPS_NORM
    )


def call(kernel, ident, outs, scratch, operands, spaces, out_spaces=None):
    out_spaces = out_spaces or [pltpu.VMEM] * len(outs)
    return pl.pallas_call(
        kernel,
        out_shape=[jax.ShapeDtypeStruct(shape, dtype) for shape, dtype in outs],
        in_specs=[pl.BlockSpec(memory_space=space) for space in spaces],
        out_specs=[pl.BlockSpec(memory_space=space) for space in out_spaces],
        scratch_shapes=scratch,
        compiler_params=pltpu.CompilerParams(
            collective_id=ident, has_side_effects=True, vmem_limit_bytes=VMEM_LIMIT
        ),
    )(*operands)


def gathered(
    x_in,
    d_out,
    key_mask,
    expert_ids,
    norm_params,
    w_qkv,
    w_proj,
    w_router,
    w_in,
    w_out,
    mom_norm,
    mom_router,
    mom_qkv,
    mom_proj,
    mom_in,
    mom_out,
):
    n_exp = lax.axis_size("expert")
    n_ctx = lax.axis_size("ctx")
    ctx = lax.axis_index("ctx")
    images, seq_dev, width = x_in.shape
    experts = w_router.shape[1]
    own_images = images // n_ctx
    seq = n_ctx * seq_dev
    rows = own_images * seq
    hid = w_in.shape[2]
    low, full = jnp.bfloat16, jnp.float32
    dma = lambda *shape: pltpu.SemaphoreType.DMA(shape)
    vmem = lambda shape, dtype: pltpu.VMEM(shape, dtype)

    vm, anywhere = pltpu.VMEM, pl.ANY
    block = (own_images, n_ctx, seq_dev, width)
    kept = [
        (block, low),
        ((rows, width), low),
        ((rows, 3 * width), low),
        ((rows, LANES), full),
        ((rows, width), low),
        ((rows, width), full),
        (block, low),
        ((own_images, 8, seq), full),
        ((n_ctx,) + block, low),
        ((rows, width), full),
        ((n_exp, width, hid), low),
        ((8, width), full),
    ]
    router_turned = w_router.T
    (x_all, first, qkv, lse, att, mid, d_own, mask_own, out_parts, dsecond, grads, grouter) = call(
        functools.partial(forward_kernel, n_exp, experts),
        1,
        kept,
        [vmem(*kept[at]) for at in (0, 1, 2, 3, 4, 5, 7, 8, 9)]
        + [
            vmem((n_exp, width, hid), low),
            vmem((8, width), full),
            vmem((n_ctx,) + block, low),
            vmem((2, n_exp, width, hid), low),
            vmem((n_ctx, own_images, seq, width), low),
            vmem((images, 8, LANES), full),
            vmem((n_ctx, images, 8, LANES), full),
            vmem((width, 3 * width), low),
            vmem((width, width), low),
            vmem((2, LANES, width), full),
            vmem((n_ctx - 1, rows, width), low),
            vmem((n_ctx - 1, rows, width), low),
            vmem((2, rows, width), full),
            vmem((2, rows, width), full),
            vmem((width, LANES), full),
            vmem((2, rows, LANES), full),
            vmem((2, rows, LANES), full),
            vmem((width, n_ctx * rows), low),
            vmem((width, n_ctx * rows), low),
            vmem((n_exp, n_ctx * rows, hid), low),
            vmem((n_exp, n_ctx * rows, hid), low),
            dma(2, own_images, n_ctx - 1),
            dma(2, n_ctx - 1),
            dma(2, n_ctx - 1, n_ctx),
            dma(2, 2, 2),
            dma(2, n_ctx - 1),
            dma(2, 2, n_ctx),
            dma(2, 2),
            dma(2, n_exp - 1, 2),
            dma(2, n_exp - 1, 2),
            dma(2, n_exp),
            dma(6),
            dma(15 + n_exp),
        ],
        (
            x_in,
            d_out.reshape(n_ctx, own_images, seq_dev, width),
            expert_ids.swapaxes(1, 2),
            key_mask,
            w_in,
            w_out,
            norm_params,
            w_qkv,
            w_proj,
            router_turned,
        ),
        [anywhere, anywhere, vm, vm, anywhere, anywhere, vm, anywhere, anywhere, vm],
        [anywhere] * 12,
    )
    cols = width // n_ctx
    blocks = (width // LANES) * (width // LANES + 1) // 2
    block_rows = LANES // n_ctx
    quarter = (n_exp, width // 2 // n_exp, width)
    moments = (mom_in, mom_out, mom_qkv, mom_proj, mom_norm, mom_router.reshape(1, width))
    out_low, dx_low, gexp, steps, whole, sums, squares = call(
        functools.partial(backward_kernel, n_exp),
        2,
        [
            ((images, seq_dev, width), low),
            ((images, seq_dev, width), low),
            ((2, width, hid), low),
            ((2, 2, width, hid), low),
            ((2,) + quarter, low),
            ((16, width), full),
            ((n_ctx, 8, LANES), full),
        ],
        [
            vmem((rows, width), low),
            vmem((rows, width), low),
            vmem((own_images, 8, seq), full),
            vmem((rows, width), low),
            vmem((rows, 3 * width), low),
            vmem((rows, LANES), full),
            vmem((rows, width), low),
            vmem((rows, width), full),
            vmem((rows, width), full),
            vmem((width, hid), low),
            vmem((width, 3 * width), low),
            vmem((width, width), low),
            vmem((n_ctx, own_images, seq_dev, width), low),
            vmem((width, hid), full),
            vmem((width, 3 * cols), full),
            vmem((width, cols), full),
            vmem((n_ctx, images, seq_dev, width), low),
            vmem((n_exp - 1, width, hid), low),
            vmem((rows, width), full),
            vmem((rows, width), low),
            vmem((rows, width), low),
            vmem((rows, 3 * width), low),
            vmem(block, low),
            vmem((n_ctx, width, width), low),
            vmem((n_ctx, width // 2, width), low),
            vmem((n_ctx, width // 2, width), low),
            vmem((n_ctx - 1, width // 2, width), low),
            vmem(quarter, low),
            vmem((n_exp - 1,) + quarter[1:], low),
            vmem((3, width, hid), full),
            vmem((2, blocks, n_ctx, block_rows, LANES), full),
            vmem((2, n_ctx - 1, blocks, block_rows, LANES), full),
            vmem((2, blocks, n_ctx, block_rows, LANES), full),
            vmem((width, width), low),
            vmem((width, width), low),
            vmem((width, width), low),
            vmem((width, width), full),
            vmem((16, width), full),
            vmem((16, width), full),
            vmem((n_ctx, 16, width), full),
            vmem((n_exp, 16, width), full),
            dma(16),
            dma(2, n_ctx, n_ctx - 1),
            dma(2, n_exp - 1),
            dma(4),
            dma(2, n_ctx - 1),
            dma(2, 2),
            dma(2, n_ctx - 1),
            dma(2, n_ctx - 1),
            dma(2, n_exp - 1),
            dma(2, n_exp - 1),
            dma(2, 2, n_ctx - 1),
            dma(2, 2, n_ctx - 1),
            dma(2, 2),
            dma(2, 2, max(n_ctx, n_exp) - 1),
        ],
        (
            x_all.reshape(rows, width),
            d_own.reshape(rows, width),
            mask_own,
            first,
            qkv,
            lse,
            att,
            mid,
            dsecond,
            grads,
            grouter,
            norm_params,
            w_qkv,
            w_proj,
            out_parts,
        )
        + moments,
        [anywhere] * 10 + [vm, vm] + [anywhere] * 7 + [vm, vm],
    )
    pieces = ((4, cols), (1, width), (width, 3 * cols), (width, cols), (1, width, hid), (1, width, hid))
    parts = width // LANES
    outs = (
        [((images, seq_dev, width), low), ((images, seq_dev, width), full)]
        + [(piece, full) for piece in pieces * 3]
        + [(piece, low) for piece in pieces[2:]]
    )

    def strip(shape, axis, last=None):
        def index_map(at, ctx_ref):
            place = [0] * len(shape)
            if axis is not None:
                place[axis] = at
            if last is not None:
                place[-1] = ctx_ref[0]
            return tuple(place)

        size = list(shape)
        if axis is not None:
            size[axis] //= parts
        if last is not None:
            size[-1] = last
        return pl.BlockSpec(tuple(size), index_map)

    def strips(shape):
        if len(shape) == 3:
            return strip(shape, 0 if shape[0] == images else 1)
        return strip(shape, 0 if shape[0] == width else None)

    results = pl.pallas_call(
        functools.partial(finish_kernel, experts, n_ctx, width),
        out_shape=[jax.ShapeDtypeStruct(shape, dtype) for shape, dtype in outs],
        grid_spec=pltpu.PrefetchScalarGridSpec(
            num_scalar_prefetch=1,
            grid=(parts,),
            in_specs=[
                strip((2, width, hid), 1),
                strip((2, 2, width, hid), 2),
                strip((width, width), 0),
                strip((16, width), None),
                strip((n_ctx, 8, LANES), None),
                strip((images, seq_dev, width), 0),
                strip((images, seq_dev, width), 0),
                strip((1, width, hid), 1),
                strip((1, width, hid), 1),
                strip((width, 3 * cols), 0),
                strip((width, cols), 0),
                strip((4, cols), None),
                strip((1, width), None),
                strip((1, width, hid), 1),
                strip((1, width, hid), 1),
                strip((width, 3 * width), 0, 3 * cols),
                strip((width, width), 0, cols),
                strip((4, width), None, cols),
                strip((experts, width), None),
            ],
            out_specs=[strips(shape) for shape, _ in outs],
        ),
        compiler_params=pltpu.CompilerParams(vmem_limit_bytes=VMEM_LIMIT),
    )(
        ctx.reshape(1),
        gexp,
        steps,
        whole.reshape(width, width),
        sums,
        squares,
        dx_low,
        out_low,
        *moments,
        w_in,
        w_out,
        w_qkv,
        w_proj,
        norm_params,
        router_turned,
    )
    return tuple(
        value.reshape(width, 1) if value.shape == (1, width) else value for value in results
    )


def solution(mesh):
    in_specs = (
        P(("expert", "dp"), "ctx", None),
        P(("expert", "dp"), "ctx", None),
        P(("expert", "dp"), "ctx"),
        P(("expert", "dp"), "ctx", None),
        P(),
        P(),
        P(),
        P(),
        P("expert", None, "ctx"),
        P("expert", None, "ctx"),
        P(None, "ctx"),
        P(None, "ctx"),
        P(None, "ctx"),
        P(None, "ctx"),
        P("expert", None, "ctx"),
        P("expert", None, "ctx"),
    )
    out_specs = (
        P(("expert", "dp"), "ctx", None),
        P(("expert", "dp"), "ctx", None),
        P(None, "ctx"),
        P(None, "ctx"),
        P(None, "ctx"),
        P(None, "ctx"),
        P("expert", None, "ctx"),
        P("expert", None, "ctx"),
        P(None, "ctx"),
        P(None, "ctx"),
        P(None, "ctx"),
        P(None, "ctx"),
        P("expert", None, "ctx"),
        P("expert", None, "ctx"),
        P(None, "ctx"),
        P(None, "ctx"),
        P(None, "ctx"),
        P(None, "ctx"),
        P("expert", None, "ctx"),
        P("expert", None, "ctx"),
        P(None, "ctx"),
        P(None, "ctx"),
        P("expert", None, "ctx"),
        P("expert", None, "ctx"),
    )
    experts = mesh.shape["expert"]
    square = mesh.shape["ctx"] == 4 and mesh.shape["dp"] == 2

    def local(*arrays):
        whole = (
            square
            and arrays[7].shape[1] == experts <= 7
            and arrays[8].shape[0] == 1
            and 2 * arrays[0].shape[1] == LANES
        )
        return (gathered if whole else exchanged)(*arrays)

    return jax.shard_map(local, mesh=mesh, in_specs=in_specs, out_specs=out_specs, check_vma=False)
```

```python
import functools
import math

import jax
import jax.numpy as jnp
from jax import lax
from jax.experimental import pallas as pl
from jax.experimental.pallas import tpu as pltpu
from jax.sharding import PartitionSpec as P

HEADS = 8
HEAD_DIM = 64
MICRO = 2
NS_ITERS = 4


HIGH = lax.Precision.HIGHEST
NS_A = 3.4445
NS_B = -4.775
NS_C = 2.0315
DECAY = 0.5
RATE_MAT = 0.3
RATE_GAIN = 0.3
RATE_ROUTER = 0.05
EPS_NORM = 1e-06
EPS_ORTHO = 1e-07
NEG = -1e30
LANES = 128
VMEM_LIMIT = 60 * 2**20
MESH = pl.DeviceIdType.MESH


def as_sent(array):
    return jax.tree.map(lambda a: a.astype(jnp.bfloat16) if a.dtype == jnp.float32 else a, array)


def layer_norm(values, gain, shift):
    center = jnp.mean(values, axis=-1, keepdims=True)
    spread = values - center
    power = jnp.mean(spread * spread, axis=-1, keepdims=True)
    return spread * lax.rsqrt(power + EPS_NORM) * gain + shift


def gelu_exact(values):
    return jax.nn.gelu(values, approximate=False)


def add_block(total, piece):
    return total + piece


def masked_scores(query, key_piece, mask_piece, factor):
    scores = (
        jnp.einsum("bqhd,bkhd->bhqk", query, key_piece, preferred_element_type=jnp.float32) * factor
    )
    return jnp.where(mask_piece[:, None, None, :] > 0, scores, NEG)


def gram_list(matrices):
    return tuple(
        (jnp.einsum("...ik,...jk->...ij", matrix, matrix, precision=HIGH) for matrix in matrices)
    )


def schulz_turn(matrices, grams):
    result = []
    for matrix, gram in zip(matrices, grams):
        square = jnp.einsum("...ij,...jk->...ik", gram, gram, precision=HIGH)
        mixer = NS_B * gram + NS_C * square
        result.append(
            NS_A * matrix + jnp.einsum("...ij,...jk->...ik", mixer, matrix, precision=HIGH)
        )
    return tuple(result)


def exchanged(
    x_in,
    d_out,
    key_mask,
    expert_ids,
    norm_params,
    w_qkv,
    w_proj,
    w_router,
    w_in,
    w_out,
    mom_norm,
    mom_router,
    mom_qkv,
    mom_proj,
    mom_in,
    mom_out,
):
    ctx_count = lax.axis_size("ctx")
    ctx_place = lax.axis_index("ctx")
    owner_count = lax.axis_size("expert")
    local_images = x_in.shape[0]
    seq_dev = x_in.shape[1]
    width = x_in.shape[2]
    top_count = expert_ids.shape[-1]
    experts = w_router.shape[1]
    exp_dev = w_in.shape[0]
    hid_part = w_in.shape[2]
    capacity = max(2, (5 * top_count * seq_dev + 4 * experts - 1) // (4 * experts))
    batch = local_images // MICRO
    slot_count = batch * capacity
    seq_all = seq_dev * ctx_count
    factor = HEAD_DIM ** (-0.5)
    expert_iota = jnp.arange(experts, dtype=jnp.int32)
    recv_shape = (owner_count, exp_dev, slot_count, width)
    head_shape = (batch, seq_dev, HEADS, HEAD_DIM)

    def hidden_fold(step_fn, init):
        folded = step_fn(
            init,
            (
                lax.all_gather(w_in, "ctx", axis=2, tiled=True),
                lax.all_gather(w_out, "ctx", axis=2, tiled=True),
            ),
            jnp.int32(0),
        )
        return folded

    def to_owner(rows):
        return lax.all_to_all(rows, "expert", split_axis=0, concat_axis=0, tiled=True)

    def to_source(rows):
        return lax.all_to_all(rows, "expert", split_axis=0, concat_axis=0, tiled=True)

    def key_fold(keys, values, mask_low, step_fn, init):
        return step_fn(
            init,
            (
                lax.all_gather(keys, "ctx", axis=1, tiled=True),
                lax.all_gather(values, "ctx", axis=1, tiled=True),
                lax.all_gather(mask_low, "ctx", axis=1, tiled=True),
            ),
            jnp.int32(0),
        )

    grad_qkv = jnp.zeros(w_qkv.shape, jnp.float32)
    grad_proj = jnp.zeros(w_proj.shape, jnp.float32)
    grad_router = jnp.zeros(w_router.shape, jnp.float32)
    grad_norm = jnp.zeros((4, width), jnp.float32)
    grad_in = jnp.zeros((exp_dev, width, hid_part * ctx_count), jnp.float32)
    grad_out = jnp.zeros((exp_dev, width, hid_part * ctx_count), jnp.float32)
    outputs = []
    input_grads = []
    for micro_index in range(MICRO):
        first_image = micro_index * batch
        last_image = first_image + batch
        x_part = x_in[first_image:last_image].astype(jnp.float32)
        cotangent = d_out[first_image:last_image].astype(jnp.float32)
        mask_low = key_mask[first_image:last_image].astype(jnp.bfloat16)
        idents = expert_ids[first_image:last_image]
        normed_first, pull_first = jax.vjp(layer_norm, x_part, norm_params[0], norm_params[1])
        first_low = normed_first.astype(jnp.bfloat16).reshape(-1, width)
        qkv = jnp.dot(first_low, w_qkv, preferred_element_type=jnp.float32).astype(jnp.bfloat16)
        qkv = qkv.reshape(batch, seq_dev, 3, HEADS, HEAD_DIM)
        query = qkv[:, :, 0]
        keys = qkv[:, :, 1]
        values = qkv[:, :, 2]
        peak_old = jnp.full((batch, HEADS, seq_dev), NEG, jnp.float32)
        key_piece = lax.all_gather(keys, "ctx", axis=1, tiled=True)
        mask_piece = lax.all_gather(mask_low, "ctx", axis=1, tiled=True)
        scores = masked_scores(query, key_piece, mask_piece, factor)
        peak_new = jnp.maximum(peak_old, jnp.max(scores, axis=-1))
        total_new = jnp.sum(jnp.exp(scores - peak_new[..., None]), axis=-1)
        log_total = peak_new + jnp.log(total_new)

        def attend_step(acc, pieces, start):
            key_piece, value_piece, mask_piece = pieces
            weights = jnp.exp(
                masked_scores(query, key_piece, mask_piece, factor) - log_total[..., None]
            )
            return jnp.einsum(
                "bhqk,bkhd->bqhd",
                weights.astype(jnp.bfloat16),
                value_piece,
                preferred_element_type=jnp.float32,
            )

        attended = key_fold(keys, values, mask_low, attend_step, jnp.zeros(head_shape, jnp.float32))
        attended_low = attended.astype(jnp.bfloat16).reshape(-1, width)
        branch = jnp.dot(attended_low, w_proj, preferred_element_type=jnp.float32).reshape(
            batch, seq_dev, width
        )
        mid = x_part + branch
        normed_second, pull_second = jax.vjp(layer_norm, mid, norm_params[2], norm_params[3])
        routed_low = normed_second.astype(jnp.bfloat16)
        logits = jnp.einsum("bsd,de->bse", normed_second, w_router, precision=HIGH)
        onehot = (idents[..., None] == expert_iota).astype(jnp.float32)
        chosen = jnp.sum(onehot * logits[:, :, None, :], axis=-1)
        gates = jax.nn.softmax(chosen, axis=-1)
        flat_ids = idents.reshape(batch, seq_dev * top_count)
        hits = (flat_ids[..., None] == expert_iota).astype(jnp.int32)
        ranked = jnp.sum((jnp.cumsum(hits, axis=1) - hits) * hits, axis=-1)
        slot = (ranked + (jnp.arange(batch, dtype=jnp.int32) * capacity)[:, None]).reshape(-1)
        target = flat_ids.reshape(-1)
        routed_rows = jnp.broadcast_to(
            routed_low[:, :, None, :], (batch, seq_dev, top_count, width)
        ).reshape(-1, width)
        send = (
            jnp.zeros((experts, slot_count, width), jnp.bfloat16).at[target, slot].set(routed_rows)
        )
        received = to_owner(send.reshape(recv_shape))

        def expert_step(acc, pieces, start):
            piece_in, piece_out = pieces
            pre = jnp.einsum(
                "nesd,edh->nesh", received, piece_in, preferred_element_type=jnp.float32
            )
            act = gelu_exact(pre).astype(jnp.bfloat16)
            return jnp.einsum("nesh,edh->nesd", act, piece_out, preferred_element_type=jnp.float32)

        made = hidden_fold(expert_step, jnp.zeros(recv_shape, jnp.float32))
        back_rows = to_source(made.astype(jnp.bfloat16)).reshape(experts, slot_count, width)
        returned = (
            back_rows[target, slot].reshape(batch, seq_dev, top_count, width).astype(jnp.float32)
        )
        result = mid + jnp.sum(gates[..., None] * returned, axis=2)
        outputs.append(result.astype(jnp.bfloat16))
        dgates = jnp.sum(cotangent[:, :, None, :] * returned, axis=-1)
        dchosen = gates * (dgates - jnp.sum(gates * dgates, axis=-1, keepdims=True))
        dlogits = jnp.sum(dchosen[..., None] * onehot, axis=2)
        grad_router = grad_router + jnp.einsum(
            "bsd,bse->de", normed_second, dlogits, precision=HIGH
        )
        dsecond = jnp.einsum("bse,de->bsd", dlogits, w_router, precision=HIGH)
        dreturned = (
            (gates[..., None] * cotangent[:, :, None, :]).astype(jnp.bfloat16).reshape(-1, width)
        )
        dsend = (
            jnp.zeros((experts, slot_count, width), jnp.bfloat16).at[target, slot].set(dreturned)
        )
        dreceived = to_owner(dsend.reshape(recv_shape))

        def expert_back(carry, pieces, start):
            drows, dins, douts = carry
            piece_in, piece_out = pieces
            pre = jnp.einsum(
                "nesd,edh->nesh", received, piece_in, preferred_element_type=jnp.float32
            )
            act_full, pull_act = jax.vjp(gelu_exact, pre)
            act = act_full.astype(jnp.bfloat16)
            dact = jnp.einsum(
                "nesd,edh->nesh", dreceived, piece_out, preferred_element_type=jnp.float32
            )
            dpre = pull_act(dact)[0].astype(jnp.bfloat16)
            douts = add_block(
                douts,
                jnp.einsum("nesd,nesh->edh", dreceived, act, preferred_element_type=jnp.float32),
            )
            dins = add_block(
                dins,
                jnp.einsum("nesd,nesh->edh", received, dpre, preferred_element_type=jnp.float32),
            )
            drows = jnp.einsum("nesh,edh->nesd", dpre, piece_in, preferred_element_type=jnp.float32)
            return (drows, dins, douts)

        drows, grad_in, grad_out = hidden_fold(
            expert_back, (jnp.zeros(recv_shape, jnp.float32), grad_in, grad_out)
        )
        dback = to_source(drows.astype(jnp.bfloat16)).reshape(experts, slot_count, width)
        dsecond = dsecond + jnp.sum(
            dback[target, slot].reshape(batch, seq_dev, top_count, width).astype(jnp.float32),
            axis=2,
        )
        dmid, dgain_two, dshift_two = pull_second(dsecond)
        dmid = dmid + cotangent
        dbranch = dmid.astype(jnp.bfloat16).reshape(-1, width)
        grad_proj = grad_proj + jnp.einsum(
            "sd,se->de", attended_low, dbranch, preferred_element_type=jnp.float32
        )
        dattended = jnp.einsum("se,de->sd", dbranch, w_proj, preferred_element_type=jnp.float32)
        dattended = dattended.astype(jnp.bfloat16).reshape(head_shape)
        delta = jnp.einsum("bqhd,bqhd->bhq", dattended.astype(jnp.float32), attended)

        def attend_back(carry, pieces, start):
            dquery, dkeys, dvalues = carry
            key_piece, value_piece, mask_piece = pieces
            weights = jnp.exp(
                masked_scores(query, key_piece, mask_piece, factor) - log_total[..., None]
            )
            probs = weights.astype(jnp.bfloat16)
            dvalue_piece = jnp.einsum(
                "bhqk,bqhd->bkhd", probs, dattended, preferred_element_type=jnp.float32
            )
            dprobs = jnp.einsum(
                "bqhd,bkhd->bhqk", dattended, value_piece, preferred_element_type=jnp.float32
            )
            dscores = (weights * (dprobs - delta[..., None])).astype(jnp.bfloat16)
            dquery = factor * jnp.einsum(
                "bhqk,bkhd->bqhd", dscores, key_piece, preferred_element_type=jnp.float32
            )
            dkey_piece = factor * jnp.einsum(
                "bhqk,bqhd->bkhd", dscores, query, preferred_element_type=jnp.float32
            )
            return (dquery, add_block(dkeys, dkey_piece), add_block(dvalues, dvalue_piece))

        all_shape = (batch, seq_all, HEADS, HEAD_DIM)
        back_init = (
            jnp.zeros(head_shape, jnp.float32),
            jnp.zeros(all_shape, jnp.float32),
            jnp.zeros(all_shape, jnp.float32),
        )
        dquery, dkeys_all, dvalues_all = key_fold(keys, values, mask_low, attend_back, back_init)
        dkeys, dvalues = (
            lax.psum_scatter(
                dkeys_all.astype(jnp.bfloat16), "ctx", scatter_dimension=1, tiled=True
            ).astype(jnp.float32),
            lax.psum_scatter(
                dvalues_all.astype(jnp.bfloat16), "ctx", scatter_dimension=1, tiled=True
            ).astype(jnp.float32),
        )
        dqkv = (
            jnp.stack([dquery, dkeys, dvalues], axis=2).astype(jnp.bfloat16).reshape(-1, 3 * width)
        )
        grad_qkv = grad_qkv + jnp.einsum(
            "sd,se->de", first_low, dqkv, preferred_element_type=jnp.float32
        )
        dfirst = jnp.einsum("se,de->sd", dqkv, w_qkv, preferred_element_type=jnp.float32).reshape(
            batch, seq_dev, width
        )
        dx_part, dgain_one, dshift_one = pull_first(dfirst)
        grad_norm = grad_norm + jnp.stack([dgain_one, dshift_one, dgain_two, dshift_two])
        input_grads.append(dx_part + dmid)
    block_out = jnp.concatenate(outputs, axis=0)
    d_x = jnp.concatenate(input_grads, axis=0)
    shared = (
        lax.psum_scatter(
            grad_in.astype(jnp.bfloat16), "ctx", scatter_dimension=2, tiled=True
        ).astype(jnp.float32),
        lax.psum_scatter(
            grad_out.astype(jnp.bfloat16), "ctx", scatter_dimension=2, tiled=True
        ).astype(jnp.float32),
        lax.psum_scatter(
            grad_qkv[None].astype(jnp.bfloat16), "ctx", scatter_dimension=2, tiled=True
        ).astype(jnp.float32),
        lax.psum_scatter(
            grad_proj[None].astype(jnp.bfloat16), "ctx", scatter_dimension=2, tiled=True
        ).astype(jnp.float32),
        lax.psum_scatter(
            grad_norm[None].astype(jnp.bfloat16), "ctx", scatter_dimension=2, tiled=True
        ).astype(jnp.float32),
        lax.psum_scatter(
            grad_router[None].astype(jnp.bfloat16), "ctx", scatter_dimension=2, tiled=True
        ).astype(jnp.float32),
    )
    g_in, g_out = (
        lax.psum(shared[0].astype(jnp.bfloat16), "dp").astype(jnp.float32),
        lax.psum(shared[1].astype(jnp.bfloat16), "dp").astype(jnp.float32),
    )
    g_qkv, g_proj, g_norm, g_router = lax.psum(
        (shared[2][0], shared[3][0], shared[4][0], shared[5][0]), ("expert", "dp")
    )
    own_qkv = lax.dynamic_slice_in_dim(w_qkv, ctx_place * g_qkv.shape[1], g_qkv.shape[1], 1).astype(
        jnp.float32
    )
    own_proj = lax.dynamic_slice_in_dim(
        w_proj, ctx_place * g_proj.shape[1], g_proj.shape[1], 1
    ).astype(jnp.float32)
    own_norm = lax.dynamic_slice_in_dim(
        norm_params, ctx_place * g_norm.shape[1], g_norm.shape[1], 1
    )
    own_router = lax.dynamic_slice_in_dim(
        w_router, ctx_place * g_router.shape[1], g_router.shape[1], 1
    )
    m_qkv = DECAY * mom_qkv + g_qkv
    m_proj = DECAY * mom_proj + g_proj
    m_in = DECAY * mom_in + g_in
    m_out = DECAY * mom_out + g_out
    m_norm = DECAY * mom_norm + g_norm
    m_router = DECAY * mom_router + g_router
    matrices = (m_qkv, m_proj, m_in, m_out)
    vector_squares = (jnp.sum(m_norm * m_norm), jnp.sum(m_router * m_router))
    sums = lax.psum(
        tuple((jnp.sum(matrix * matrix, axis=(-2, -1)) for matrix in matrices)) + vector_squares,
        "ctx",
    )
    vector_totals = sums[4:]
    iterates = tuple(
        (
            matrix / jnp.expand_dims(jnp.sqrt(square) + EPS_ORTHO, (-2, -1))
            for matrix, square in zip(matrices, sums[:4])
        )
    )
    for turn_index in range(NS_ITERS):
        iterates = schulz_turn(
            iterates,
            jax.tree.map(
                lambda part: part.astype(jnp.float32), lax.psum(as_sent(gram_list(iterates)), "ctx")
            ),
        )
    n_qkv = (
        own_qkv - RATE_MAT * 0.2 * math.sqrt(max(width, g_qkv.shape[1] * ctx_count)) * iterates[0]
    )
    n_proj = (
        own_proj - RATE_MAT * 0.2 * math.sqrt(max(width, g_proj.shape[1] * ctx_count)) * iterates[1]
    )
    n_in = (
        w_in.astype(jnp.float32)
        - RATE_MAT * 0.2 * math.sqrt(max(width, hid_part * ctx_count)) * iterates[2]
    )
    n_out = (
        w_out.astype(jnp.float32)
        - RATE_MAT * 0.2 * math.sqrt(max(width, hid_part * ctx_count)) * iterates[3]
    )
    n_norm = own_norm - RATE_GAIN * m_norm * lax.rsqrt(vector_totals[0] / (4 * width) + EPS_NORM)
    n_router = own_router - RATE_ROUTER * m_router * lax.rsqrt(
        vector_totals[1] / (width * experts) + EPS_NORM
    )
    return (
        block_out,
        d_x,
        g_norm,
        g_router,
        g_qkv,
        g_proj,
        g_in,
        g_out,
        m_norm,
        m_router,
        m_qkv,
        m_proj,
        m_in,
        m_out,
        n_norm,
        n_router,
        n_qkv,
        n_proj,
        n_in,
        n_out,
        n_qkv.astype(jnp.bfloat16),
        n_proj.astype(jnp.bfloat16),
        n_in.astype(jnp.bfloat16),
        n_out.astype(jnp.bfloat16),
    )


def dot(left, right, precision=None):
    return jnp.dot(left, right, precision=precision, preferred_element_type=jnp.float32)


def dot_nt(left, right, precision=None):
    return lax.dot_general(
        left, right, (((1,), (1,)), ((), ())), precision=precision, preferred_element_type=jnp.float32
    )


def dot_tn(left, right, precision=None):
    return lax.dot_general(
        left, right, (((0,), (0,)), ((), ())), precision=precision, preferred_element_type=jnp.float32
    )


def places():
    return lax.axis_index("expert"), lax.axis_index("ctx"), lax.axis_index("dp")


def ctx_partner(ctx, step):
    column, row = lax.rem(ctx, 2), ctx // 2
    column = lax.rem(column + lax.rem(step, 2), 2)
    row = lax.rem(row + step // 2, 2)
    return row * 2 + column


def z_partner(expert, step, count):
    return lax.rem(expert + step, count)


def greet(partners):
    barrier = pltpu.get_barrier_semaphore()
    for partner in partners:
        pl.semaphore_signal(barrier, inc=1, device_id=partner, device_id_type=MESH)
    pl.semaphore_wait(barrier, len(partners))


def send(source, target, send_sem, recv_sem, partner):
    copy = pltpu.make_async_remote_copy(
        src_ref=source,
        dst_ref=target,
        send_sem=send_sem,
        recv_sem=recv_sem,
        device_id=partner,
        device_id_type=MESH,
    )
    copy.start()
    return copy


def normalize(values):
    center = jnp.mean(values, axis=-1, keepdims=True)
    spread = values - center
    power = jnp.mean(spread * spread, axis=-1, keepdims=True)
    scale = lax.rsqrt(power + EPS_NORM)
    return spread * scale, scale


def normalize_back(grad, unit, scale):
    first = jnp.mean(grad, axis=-1, keepdims=True)
    second = jnp.mean(grad * unit, axis=-1, keepdims=True)
    return scale * (grad - first - unit * second)


def group_rows(meta_ref, image):
    pairs = [
        meta_ref[2 * half, image] + meta_ref[2 * half + 1, image]
        for half in range(meta_ref.shape[0] // 2)
    ]
    return jnp.concatenate(pairs, axis=1)


def split(values):
    high = values.astype(jnp.bfloat16)
    return high, (values - high.astype(jnp.float32)).astype(jnp.bfloat16)


def gelu_parts(values):
    cdf = 0.5 + 0.5 * lax.erf(values * (0.5**0.5))
    return cdf, jnp.exp(-0.5 * values * values) * (1.0 / math.sqrt(2 * math.pi))


def forward_kernel(
    n_exp,
    experts,
    x_ref,
    d_ref,
    ids_ref,
    mask_ref,
    win_ref,
    wout_ref,
    norm_ref,
    wqkv_hbm,
    wproj_hbm,
    wrouter_ref,
    o_x,
    o_first,
    o_qkv,
    o_lse,
    o_att,
    o_mid,
    o_d,
    o_mask,
    o_out,
    o_dsecond,
    o_grads,
    o_grouter,
    x_all,
    first_ref,
    qkv_ref,
    lse_ref,
    att_ref,
    mid_ref,
    mask_own,
    out_send,
    dsecond_ref,
    grads_recv,
    grouter_ref,
    d_all,
    w_all,
    r_all,
    meta_ref,
    meta_all,
    wqkv_ref,
    wproj_ref,
    router_ref,
    ds_send,
    ds_recv,
    acc_out,
    acc_ds,
    acc_router,
    gates_ref,
    dgates_ref,
    r_turn,
    d_turn,
    act_all,
    dpre_all,
    x_sems,
    m_sems,
    d_sems,
    r_sems,
    ds_sems,
    dr_sems,
    rr_sems,
    z_sems,
    s_sems,
    t_sems,
    own_sem,
    o_sems,
):
    expert, ctx, dp = places()
    own_images, n_ctx, seq_dev, width = x_all.shape
    seq = n_ctx * seq_dev
    rows = own_images * seq
    ctx_ids = [(expert, ctx_partner(ctx, step), dp) for step in range(1, n_ctx)]
    side_ids = ctx_ids[:2]
    twin = (expert, ctx, 1 - dp)
    right, left = lax.rem(expert + 1, n_exp), lax.rem(expert + n_exp - 1, n_exp)
    row = lax.broadcasted_iota(jnp.int32, (8, seq_dev), 0)
    odd = lax.rem(ctx, 2).astype(jnp.float32)
    for image in range(ids_ref.shape[0]):
        named = jnp.zeros((8, seq_dev), jnp.bool_)
        for choice in range(ids_ref.shape[1]):
            named = named | (ids_ref[image, choice : choice + 1] == row)
        values = jnp.where(
            row == experts, mask_ref[image : image + 1].astype(jnp.float32), named.astype(jnp.float32)
        )
        meta_ref[image, :, :seq_dev] = values * (1.0 - odd)
        meta_ref[image, :, seq_dev:] = values * odd
    router_ref[...] = jnp.zeros_like(router_ref)
    router_high, router_low = split(wrouter_ref[...])
    router_ref[0, :experts] = router_high.astype(jnp.float32)
    router_ref[1, :experts] = router_low.astype(jnp.float32)
    greet(ctx_ids + [(right, ctx, dp), (left, ctx, dp), twin])
    own = [
        pltpu.make_async_copy(source, target, own_sem.at[at])
        for at, (source, target) in enumerate(
            (
                (win_ref.at[0], w_all.at[0, expert]),
                (wout_ref.at[0], w_all.at[1, expert]),
                (x_ref.at[pl.ds(ctx * own_images, own_images)], x_all.at[:, ctx]),
                (wqkv_hbm, wqkv_ref),
                (wproj_hbm, wproj_ref),
                (d_ref, d_all.at[:, :, ctx]),
            )
        )
    ]
    for copy in own:
        copy.start()
    meta_all[ctx] = meta_ref[...]
    x_copies = []
    for image in range(own_images):
        x_copies.append(
            [
                send(
                    x_ref.at[partner[1] * own_images + image],
                    x_all.at[image, ctx],
                    x_sems.at[0, image, at],
                    x_sems.at[1, image, at],
                    partner,
                )
                for at, partner in enumerate(ctx_ids)
            ]
        )
        if image == 0:
            m_copies = [
                send(meta_ref, meta_all.at[ctx], m_sems.at[0, at], m_sems.at[1, at], partner)
                for at, partner in enumerate(ctx_ids)
            ]

    def hop(phase, side):
        share = expert - phase if side == 0 else expert + phase
        able = (share >= 0) & (expert < n_exp - 1) if side == 0 else (share < n_exp) & (expert > 0)
        share = jnp.clip(share, 0, n_exp - 1)
        return able, pltpu.make_async_remote_copy(
            src_ref=w_all.at[dp, share],
            dst_ref=w_all.at[dp, share],
            send_sem=z_sems.at[0, phase, side],
            recv_sem=z_sems.at[1, phase, side],
            device_id=(right if side == 0 else left, ctx, dp),
            device_id_type=MESH,
        )

    def landed(phase, side):
        share = expert - 1 - phase if side == 0 else expert + 1 + phase
        able = share >= 0 if side == 0 else share < n_exp
        share = jnp.clip(share, 0, n_exp - 1)
        place = w_all.at[dp, share]
        return (
            able,
            pltpu.make_async_remote_copy(
                src_ref=place,
                dst_ref=place,
                send_sem=z_sems.at[0, phase, side],
                recv_sem=z_sems.at[1, phase, side],
                device_id=(left if side == 0 else right, ctx, dp),
                device_id_type=MESH,
            ),
            pltpu.make_async_remote_copy(
                src_ref=place,
                dst_ref=place,
                send_sem=s_sems.at[0, phase, side],
                recv_sem=s_sems.at[1, phase, side],
                device_id=twin,
                device_id_type=MESH,
            ),
        )

    def start_hops(phase):
        for side in range(2):
            able, copy = hop(phase, side)
            pl.when(able)(copy.start)

    def take_hops(phase):
        for side in range(2):
            able, copy, shared = landed(phase, side)

            @pl.when(able)
            def _():
                copy.wait_recv()
                shared.start()

    def take_shared(phase):
        for side in range(2):
            able, _, shared = landed(phase, side)
            pl.when(able)(shared.wait_recv)

    own[0].wait()
    own[1].wait()
    start_hops(0)
    for copy in own[2:]:
        copy.wait()

    def d_copy(at, order):
        group = ctx_partner(ctx_ids[at][1], order)
        return pltpu.make_async_remote_copy(
            src_ref=d_ref.at[group],
            dst_ref=d_all.at[group, :, ctx],
            send_sem=d_sems.at[0, at, order],
            recv_sem=d_sems.at[1, at, order],
            device_id=ctx_ids[at],
            device_id_type=MESH,
        )

    def d_relay(image, order):
        target = side_ids[1 - image]
        place = d_all.at[ctx_partner(target[1], order), image, side_ids[image][1]]
        return pltpu.make_async_remote_copy(
            src_ref=place,
            dst_ref=place,
            send_sem=dr_sems.at[0, image, order],
            recv_sem=dr_sems.at[1, image, order],
            device_id=target,
            device_id_type=MESH,
        )

    def r_copy(at, image):
        return pltpu.make_async_remote_copy(
            src_ref=r_all.at[ctx, image],
            dst_ref=r_all.at[ctx, image],
            send_sem=r_sems.at[0, at, image],
            recv_sem=r_sems.at[1, at, image],
            device_id=side_ids[at],
            device_id_type=MESH,
        )

    def r_relay(image):
        place = r_all.at[side_ids[image][1], image]
        return pltpu.make_async_remote_copy(
            src_ref=place,
            dst_ref=place,
            send_sem=rr_sems.at[0, image],
            recv_sem=rr_sems.at[1, image],
            device_id=side_ids[1 - image],
            device_id_type=MESH,
        )

    for at in range(n_ctx - 1):
        d_copy(at, 0).start()
    for copy in x_copies[0] + m_copies:
        copy.wait()
    for order in range(1, n_ctx):
        for at in range(2):
            d_copy(at, order).start()
    lane = lax.broadcasted_iota(jnp.int32, (seq, LANES), 1)
    low_half = lane < HEAD_DIM
    for image in range(own_images):
        part = pl.ds(image * seq, seq)
        if image > 0:
            for copy in x_copies[image]:
                copy.wait()
        values = x_all[image].reshape(seq, width).astype(jnp.float32)
        unit, _ = normalize(values)
        first = (unit * norm_ref[0:1] + norm_ref[1:2]).astype(jnp.bfloat16)
        first_ref[part] = first
        qkv_ref[part] = dot(first, wqkv_ref[...]).astype(jnp.bfloat16)
        key_mask = group_rows(meta_all, ctx * own_images + image)[experts : experts + 1]
        mask_own[image] = jnp.broadcast_to(key_mask, mask_own.shape[1:])
        bias = jnp.where(key_mask > 0, 0.0, NEG)
        totals = jnp.zeros((seq, LANES), jnp.float32)
        for pair in range(HEADS // 2):
            query = qkv_ref[part, pair * LANES : (pair + 1) * LANES]
            keys = qkv_ref[part, width + pair * LANES : width + (pair + 1) * LANES]
            heads = qkv_ref[part, 2 * width + pair * LANES : 2 * width + (pair + 1) * LANES]
            query = query * jnp.bfloat16(HEAD_DIM**-0.5)
            parts = []
            for half in range(2):
                chosen = low_half if half == 0 else ~low_half
                scores = dot_nt(jnp.where(chosen, query, jnp.zeros_like(query)), keys) + bias
                peak = jnp.max(scores, axis=-1, keepdims=True)
                raised = jnp.exp(scores - peak)
                total = jnp.sum(raised, axis=-1, keepdims=True)
                probs = (raised * (1.0 / total)).astype(jnp.bfloat16)
                parts.append(dot(probs, heads))
                totals = jnp.where(lane == 2 * pair + half, peak + jnp.log(total), totals)
            att_ref[part, pair * LANES : (pair + 1) * LANES] = jnp.where(
                low_half, parts[0], parts[1]
            ).astype(jnp.bfloat16)
        lse_ref[part] = totals
        mid = values + dot(att_ref[part], wproj_ref[...])
        mid_ref[part] = mid
        unit, _ = normalize(mid)
        r_all[ctx, image] = (unit * norm_ref[2:3] + norm_ref[3:4]).astype(jnp.bfloat16)
        for at in range(2):
            r_copy(at, image).start()
        if image == 0:
            take_hops(0)
            start_hops(1)

    kept_copies = [
        pltpu.make_async_copy(source, target, o_sems.at[at])
        for at, (source, target) in enumerate(
            (
                (x_all, o_x),
                (first_ref, o_first),
                (qkv_ref, o_qkv),
                (lse_ref, o_lse),
                (att_ref, o_att),
                (mid_ref, o_mid),
                (mask_own, o_mask),
            )
        )
    ]
    for copy in kept_copies:
        copy.start()

    def out_copy(chunk):
        return pltpu.make_async_copy(out_send.at[chunk], o_out.at[chunk], o_sems.at[8 + chunk])

    near = jnp.where(expert < n_exp // 2, expert + 1, expert - 1)
    last = jnp.where(expert < n_exp // 2, n_exp - 1, 0)
    middle = n_exp * (n_exp - 1) // 2 - expert - near - last

    def start_chunk(chunk, slot, owner):
        columns = pl.ds(pl.multiple_of(chunk * rows, rows), rows)
        routed = r_all[owner].reshape(rows, width)
        r_turn[:, columns] = routed.T
        d_turn[:, columns] = d_all[owner].reshape(rows, width).T
        present = jnp.concatenate(
            [group_rows(meta_all, owner * own_images + image) for image in range(own_images)], axis=1
        )
        present = jnp.concatenate(
            [present, jnp.zeros((LANES - present.shape[0], rows), jnp.float32)], axis=0
        ).T
        present = (present > 0) & (wide < experts)
        logits = dot_nt(routed, router_ref[0].astype(jnp.bfloat16)) + dot_nt(
            routed, router_ref[1].astype(jnp.bfloat16)
        )
        peak = jnp.max(jnp.where(present, logits, NEG), axis=-1, keepdims=True)
        raised = jnp.where(present, jnp.exp(jnp.where(present, logits - peak, 0.0)), 0.0)
        gates_ref[slot] = raised / jnp.sum(raised, axis=-1, keepdims=True)
        dgates_ref[slot] = jnp.zeros((rows, LANES), jnp.float32)
        acc_out[slot] = jnp.zeros(acc_out.shape[1:], jnp.float32)
        acc_ds[slot] = jnp.zeros(acc_ds.shape[1:], jnp.float32)

    def end_chunk(chunk, slot):
        columns = pl.ds(pl.multiple_of(chunk * rows, rows), rows)
        gates = gates_ref[slot]
        dgates = dgates_ref[slot]
        dlogits = gates * (dgates - jnp.sum(gates * dgates, axis=-1, keepdims=True))
        high, low = split(dlogits)
        turned = r_turn[:, columns]
        acc_router[...] += dot(turned, high) + dot(turned, low)
        total = (
            acc_ds[slot]
            + dot(high, router_ref[0].astype(jnp.bfloat16))
            + dot(high, router_ref[1].astype(jnp.bfloat16))
            + dot(low, router_ref[0].astype(jnp.bfloat16))
        )
        if chunk == 0:
            dsecond_ref[...] = total
            out = acc_out[slot] + mid_ref[...]
        else:
            ds_send[chunk - 1] = total.astype(jnp.bfloat16)
            out = acc_out[slot]
        out_send[chunk] = out.astype(jnp.bfloat16).reshape(out_send.shape[1:])
        out_copy(chunk).start()

    def ds_copy(chunk):
        return pltpu.make_async_remote_copy(
            src_ref=ds_send.at[chunk - 1],
            dst_ref=ds_recv.at[chunk - 1],
            send_sem=ds_sems.at[0, chunk - 1],
            recv_sem=ds_sems.at[1, chunk - 1],
            device_id=ctx_ids[chunk - 1],
            device_id_type=MESH,
        )

    acc_router[...] = jnp.zeros_like(acc_router)

    def place_of(step):
        chunk = jnp.where(
            step < 8, jnp.where((step < 3) | (step == 6), 0, 1), step // 4
        )
        rank = jnp.where(
            step < 8,
            jnp.where(step < 3, step, jnp.where(step < 6, step - 3, 3)),
            lax.rem(step, 4),
        )
        index = jnp.where(
            rank == 0, expert, jnp.where(rank == 1, near, jnp.where(rank == 2, middle, last))
        )
        return chunk, lax.rem(chunk, 2), index

    def hidden(step):
        chunk, slot, index = place_of(step)
        owner = ctx_partner(ctx, chunk)
        pre = dot(r_all[owner].reshape(rows, width), w_all[0, index])
        dact = dot(d_all[owner].reshape(rows, width), w_all[1, index])
        gate = jnp.sum(jnp.where(wide == index, gates_ref[slot], 0.0), axis=-1, keepdims=True)
        cdf, density = gelu_parts(pre)
        act = pre * cdf
        dgate = jnp.sum(dact * act, axis=-1, keepdims=True)
        dgates_ref[slot] = jnp.where(wide == index, dgate, dgates_ref[slot])
        kept = pl.ds(pl.multiple_of(chunk * rows, rows), rows)
        act_all[index, kept] = (gate * act).astype(jnp.bfloat16)
        dpre_all[index, kept] = (gate * dact * (cdf + pre * density)).astype(jnp.bfloat16)

    def back_out(step):
        chunk, slot, index = place_of(step)
        kept = pl.ds(pl.multiple_of(chunk * rows, rows), rows)
        acc_out[slot] += dot_nt(act_all[index, kept], w_all[1, index])
        acc_ds[slot] += dot_nt(dpre_all[index, kept], w_all[0, index])

    wide = lax.broadcasted_iota(jnp.int32, (rows, LANES), 1)
    for at in range(n_ctx - 1):
        d_copy(at, 0).wait_recv()
    start_chunk(0, 0, ctx)
    hidden(0)

    def one_step(step, carry):
        @pl.when(step == 1)
        def _():
            take_shared(0)
            for order in range(1, n_ctx):
                for at in range(2):
                    d_copy(at, order).wait_recv()
            for order in range(1, n_ctx):
                for image in range(2):
                    d_relay(image, order).start()

        @pl.when(step == 2)
        def _():
            take_hops(1)
            start_hops(2)
            take_shared(1)

        @pl.when(step == 3)
        def _():
            for image in range(2):
                r_copy(0, image).wait_recv()
                d_relay(image, 1).wait_recv()
            r_relay(0).start()
            start_chunk(1, 1, ctx_ids[0][1])

        @pl.when(step == 4)
        def _():
            for image in range(2):
                r_copy(1, image).wait_recv()
            r_relay(1).start()

        @pl.when(step == 6)
        def _():
            take_hops(2)
            take_shared(2)

        @pl.when(step == 8)
        def _():
            for image in range(2):
                d_relay(image, 2).wait_recv()
            start_chunk(2, 0, ctx_ids[1][1])

        @pl.when(step == 12)
        def _():
            for image in range(2):
                d_relay(image, 3).wait_recv()
                r_relay(image).wait_recv()
            start_chunk(3, 1, ctx_ids[2][1])

        back_out(step - 1)
        hidden(step)

        @pl.when(step == 7)
        def _():
            end_chunk(0, 0)

        @pl.when(step == 8)
        def _():
            end_chunk(1, 1)
            ds_copy(1).start()

        @pl.when(step == 12)
        def _():
            end_chunk(2, 0)
            ds_copy(2).start()

        return carry

    lax.fori_loop(1, n_ctx * n_exp, one_step, 0)
    back_out(n_ctx * n_exp - 1)
    end_chunk(3, 1)
    ds_copy(3).start()

    d_kept = pltpu.make_async_copy(d_all.at[ctx], o_d, o_sems.at[7])
    d_kept.start()

    def grad_at(which, index):
        return act_all.at[index, pl.ds(pl.multiple_of(which * width, width), width)]

    def t_copy(index):
        return pltpu.make_async_remote_copy(
            src_ref=grad_at(1 - dp, index),
            dst_ref=grads_recv.at[index],
            send_sem=t_sems.at[0, index],
            recv_sem=t_sems.at[1, index],
            device_id=twin,
            device_id_type=MESH,
        )

    def one_expert(index, carry):
        grad_out = dot(d_turn[...], act_all[index]).astype(jnp.bfloat16)
        grad_at(0, index)[...] = dot(r_turn[...], dpre_all[index]).astype(jnp.bfloat16)
        grad_at(1, index)[...] = grad_out
        t_copy(index).start()
        return carry

    lax.fori_loop(0, n_exp, one_expert, 0)
    grouter_ref[...] = acc_router[...].T[: grouter_ref.shape[0]]
    for index in range(n_exp):
        t_copy(index).wait()
        grad_at(dp, index)[...] = (
            grad_at(dp, index)[...].astype(jnp.float32) + grads_recv[index].astype(jnp.float32)
        ).astype(jnp.bfloat16)
    last_copies = [pltpu.make_async_copy(grouter_ref, o_grouter, o_sems.at[13])] + [
        pltpu.make_async_copy(grad_at(dp, index), o_grads.at[index], o_sems.at[15 + index])
        for index in range(n_exp)
    ]
    for copy in last_copies:
        copy.start()
    for phase in range(n_exp - 1):
        for side in range(2):
            able, copy = hop(phase, side)
            pl.when(able)(copy.wait_send)
            able, _, shared = landed(phase, side)
            pl.when(able)(shared.wait_send)
    for at in range(n_ctx - 1):
        for order in range(n_ctx if at < 2 else 1):
            d_copy(at, order).wait_send()
    for image in range(2):
        r_relay(image).wait_send()
        for at in range(2):
            r_copy(at, image).wait_send()
        for order in range(1, n_ctx):
            d_relay(image, order).wait_send()
    for chunk in range(1, n_ctx):
        ds_copy(chunk).wait()
        dsecond_ref[...] += ds_recv[chunk - 1].astype(jnp.float32)
    last_copies.append(pltpu.make_async_copy(dsecond_ref, o_dsecond, o_sems.at[14]))
    last_copies[-1].start()
    for copy in kept_copies + [d_kept] + last_copies:
        copy.wait()
    for chunk in range(n_ctx):
        out_copy(chunk).wait()


def gram_blocks(matrix, packed_ref):
    size = matrix.shape[0]
    index = 0
    for row in range(size // LANES):
        strip = dot_nt(matrix[row * LANES : (row + 1) * LANES], matrix[row * LANES :])
        for col in range(size // LANES - row):
            packed_ref[index] = strip[:, col * LANES : (col + 1) * LANES].reshape(
                packed_ref.shape[1:]
            )
            index += 1


def gram_whole(packed_ref, high_ref, low_ref):
    count = high_ref.shape[0] // LANES
    diagonal = lax.broadcasted_iota(jnp.int32, (LANES, LANES), 0) == lax.broadcasted_iota(
        jnp.int32, (LANES, LANES), 1
    )
    places_of = {}
    square = jnp.zeros((1, 1), jnp.float32)
    index = 0
    for row in range(count):
        for col in range(row, count):
            places_of[index] = (row, col)
            if row == col:
                block = packed_ref[index].reshape(LANES, LANES)
                square += jnp.sum(jnp.where(diagonal, block, 0.0), keepdims=True)
            index += 1
    scale = 1.0 / (jnp.sqrt(square) + EPS_ORTHO)
    for index, (row, col) in places_of.items():
        block = packed_ref[index].reshape(LANES, LANES) * (scale * scale)
        rows, cols = pl.ds(row * LANES, LANES), pl.ds(col * LANES, LANES)
        high_ref[rows, cols], low_ref[rows, cols] = split(block)
        if row != col:
            high_ref[cols, rows], low_ref[cols, rows] = split(block.T)
    return scale


def orthogonal(high_ref, low_ref, mix_ref, total_ref):
    size = high_ref.shape[0]
    eye = lax.broadcasted_iota(jnp.int32, (size, size), 0) == lax.broadcasted_iota(
        jnp.int32, (size, size), 1
    )
    for turn in range(NS_ITERS):
        high, low = high_ref[...], low_ref[...]
        square = dot(high, high)
        if turn == NS_ITERS - 1:
            square += dot(high, low) + dot(low, high)
        mix_ref[...] = (
            jnp.where(eye, NS_A, 0.0)
            + NS_B * (high.astype(jnp.float32) + low.astype(jnp.float32))
            + NS_C * square
        ).astype(jnp.bfloat16)
        mix = mix_ref[...]
        if turn == 0:
            total_ref[...] = mix.astype(jnp.float32)
        else:
            total_high, total_low = split(total_ref[...])
            total_ref[...] = dot(mix, total_high) + dot(mix, total_low)
        if turn < NS_ITERS - 1:
            turned_high, turned_low = split(dot(mix, high) + dot(mix, low))
            high_ref[...], low_ref[...] = split(dot(turned_high, mix) + dot(turned_low, mix))


def backward_kernel(
    n_exp,
    h_x,
    h_d,
    h_mask,
    h_first,
    h_qkv,
    h_lse,
    h_att,
    h_mid,
    h_dsecond,
    h_grads,
    grouter_ref,
    norm_ref,
    h_wqkv,
    h_wproj,
    h_out,
    h_min,
    h_mout,
    h_mqkv,
    h_mproj,
    mnorm_ref,
    mrouter_ref,
    out_ref,
    dx_ref,
    gexp_ref,
    step_ref,
    whole_ref,
    sums_ref,
    squares_ref,
    x_ref,
    d_ref,
    mask_ref,
    first_ref,
    qkv_ref,
    lse_ref,
    att_ref,
    mid_ref,
    dsecond_ref,
    own_grads,
    passed_ref,
    wqkv_ref,
    wproj_ref,
    out_own,
    mexp_ref,
    mqkv_ref,
    mproj_ref,
    out_recv,
    z_recv,
    dmid_ref,
    dbranch_ref,
    datt_ref,
    dqkv_ref,
    dx_send,
    shared_ref,
    half_recv,
    sum_one,
    ctx_recv,
    piece_send,
    piece_recv,
    mat_ref,
    packed_ref,
    packed_recv,
    gathered_ref,
    high_ref,
    low_ref,
    mix_ref,
    total_ref,
    small_ref,
    small_twin,
    small_ctx,
    small_z,
    in_sems,
    out_sems,
    z_sems,
    f_sems,
    dx_sems,
    h_sems,
    c_sems,
    s_sems,
    p_sems,
    w_sems,
    g_sems,
    a_sems,
    x_sems,
    n_sems,
):
    expert, ctx, dp = places()
    own_images, n_ctx, seq_dev, width = dx_send.shape
    seq = n_ctx * seq_dev
    half = width // 2
    cols = width // n_ctx
    loads = {}

    def load(name, source, target):
        loads[name] = pltpu.make_async_copy(source, target, in_sems.at[len(loads)])
        return loads[name]

    def take(*names):
        for name in names:
            loads[name].wait()

    for name, source, target in (
        ("mid", h_mid, mid_ref),
        ("dsecond", h_dsecond, dsecond_ref),
        ("d", h_d, d_ref),
        ("wproj", h_wproj, wproj_ref),
        ("qkv", h_qkv, qkv_ref),
        ("lse", h_lse, lse_ref),
        ("mask", h_mask, mask_ref),
        ("att", h_att, att_ref),
        ("first", h_first, first_ref),
        ("wqkv", h_wqkv, wqkv_ref),
        ("x", h_x, x_ref),
        ("grads", h_grads.at[expert], own_grads),
        ("passed", h_grads.at[jnp.where(expert < n_exp // 2, n_exp - 1, 0)], passed_ref),
        ("out", h_out.at[:, :, ctx], out_own),
        ("mqkv", h_mqkv, mqkv_ref),
        ("mproj", h_mproj, mproj_ref),
    ):
        load(name, source, target).start()
    moment = [
        pltpu.make_async_copy(source.at[0], mexp_ref, in_sems.at[len(loads)])
        for source in (h_min, h_mout)
    ]
    pl.when(dp == 0)(moment[0].start)
    pl.when(dp == 1)(moment[1].start)
    ctx_ids = [(expert, ctx_partner(ctx, step), dp) for step in range(1, n_ctx)]
    z_steps = [1, n_exp - 1] + list(range(2, n_exp - 1))
    z_ids = [(z_partner(expert, step, n_exp), ctx, dp) for step in z_steps]
    twin = (expert, ctx, 1 - dp)
    greet(ctx_ids + z_ids + [twin])

    def to_each(partners, source, target, sems):
        return [
            send(source(at, partner), target(at, partner), sems.at[0, at], sems.at[1, at], partner)
            for at, partner in enumerate(partners)
        ]

    low_side = expert < n_exp // 2
    near_end = jnp.where(low_side, 0, n_exp - 1)
    far_end = n_exp - 1 - near_end
    near_mid = jnp.where(low_side, 1, n_exp - 2)
    far_mid = n_exp - 1 - near_mid
    at_end = expert == near_end

    def z_copy(target, source, slot, order):
        return pltpu.make_async_remote_copy(
            src_ref=source,
            dst_ref=z_recv.at[slot],
            send_sem=z_sems.at[0, order],
            recv_sem=z_sems.at[1, slot],
            device_id=(target, ctx, dp),
            device_id_type=MESH,
        )

    def end_copies():
        return [
            z_copy(near_mid, h_grads.at[far_end], 3, 0),
            z_copy(far_mid, h_grads.at[far_mid], 1, 1),
            z_copy(near_mid, h_grads.at[near_mid], 0, 2),
        ]

    def mid_copies():
        return [
            z_copy(far_mid, h_grads.at[far_mid], 2, 0),
            z_copy(near_end, h_grads.at[near_end], 0, 1),
            z_copy(far_end, passed_ref, 1, 2),
        ]

    @pl.when(at_end)
    def _():
        for copy in end_copies():
            copy.start()

    @pl.when(jnp.logical_not(at_end))
    def _():
        for copy in mid_copies()[:2]:
            copy.start()

    out_copies = []
    for step in range(n_ctx):
        first_image = ctx_partner(ctx, step) * own_images
        for at, partner in enumerate(ctx_ids):
            out_copies.append(
                send(
                    h_out.at[step, :, partner[1]],
                    out_recv.at[ctx, pl.ds(first_image, own_images)],
                    out_sems.at[0, step, at],
                    out_sems.at[1, step, at],
                    partner,
                )
            )
    gain_one, gain_two = norm_ref[0:1], norm_ref[2:3]
    sums = [jnp.zeros((1, width), jnp.float32) for _ in range(4)]
    take("mid", "dsecond", "d", "wproj")
    for image in range(own_images):
        rows = pl.ds(image * seq, seq)
        unit, scale = normalize(mid_ref[rows])
        grad = dsecond_ref[rows]
        sums[2] += jnp.sum(grad * unit, axis=0, keepdims=True)
        sums[3] += jnp.sum(grad, axis=0, keepdims=True)
        dmid = normalize_back(grad * gain_two, unit, scale) + d_ref[rows].astype(jnp.float32)
        dmid_ref[rows] = dmid
        dbranch = dmid.astype(jnp.bfloat16)
        dbranch_ref[rows] = dbranch
        datt_ref[rows] = dot_nt(dbranch, wproj_ref[...]).astype(jnp.bfloat16)
    take("qkv", "lse", "mask")
    lane = lax.broadcasted_iota(jnp.int32, (seq, LANES), 1)
    low_half = lane < HEAD_DIM
    factor = HEAD_DIM**-0.5
    for image in range(own_images):
        rows = pl.ds(image * seq, seq)
        bias = jnp.where(mask_ref[image, 0:1] > 0, 0.0, NEG)
        totals = lse_ref[rows]
        for pair in range(HEADS // 2):
            at = pair * LANES
            query = qkv_ref[rows, at : at + LANES] * jnp.bfloat16(factor)
            keys = qkv_ref[rows, width + at : width + at + LANES]
            heads = qkv_ref[rows, 2 * width + at : 2 * width + at + LANES]
            datt = datt_ref[rows, at : at + LANES]
            dquery, dkeys, dheads = [], [], []
            for part in range(2):
                chosen = low_half if part == 0 else ~low_half
                scores = dot_nt(jnp.where(chosen, query, jnp.zeros_like(query)), keys) + bias
                head = 2 * pair + part
                weights = jnp.exp(scores - totals[:, head : head + 1])
                dprobs = dot_nt(jnp.where(chosen, datt, jnp.zeros_like(datt)), heads)
                delta = jnp.sum(weights * dprobs, axis=-1, keepdims=True)
                dscores = (weights * (dprobs - delta)).astype(jnp.bfloat16)
                dquery.append(dot(dscores, keys))
                dkeys.append(dot_tn(dscores, query))
                dheads.append(dot_tn(weights.astype(jnp.bfloat16), datt))
            dqkv_ref[rows, at : at + LANES] = (
                jnp.where(low_half, dquery[0], dquery[1]) * factor
            ).astype(jnp.bfloat16)
            dqkv_ref[rows, width + at : width + at + LANES] = jnp.where(
                low_half, dkeys[0], dkeys[1]
            ).astype(jnp.bfloat16)
            dqkv_ref[rows, 2 * width + at : 2 * width + at + LANES] = jnp.where(
                low_half, dheads[0], dheads[1]
            ).astype(jnp.bfloat16)
    take("passed")

    @pl.when(jnp.logical_not(at_end))
    def _():
        copies = mid_copies()
        copies[0].wait_send()
        z_copy(near_mid, passed_ref, 3, 0).wait_recv()
        passed_ref[...] = (
            passed_ref[...].astype(jnp.float32) + z_recv[3].astype(jnp.float32)
        ).astype(jnp.bfloat16)
        copies[2].start()

    take("att", "first")
    gproj = dot_tn(att_ref[...], dbranch_ref[...]).astype(jnp.bfloat16)
    gqkv = dot_tn(first_ref[...], dqkv_ref[...]).astype(jnp.bfloat16)
    for place in range(n_ctx):
        shared_ref[place, :, : 3 * cols] = gqkv[:, 3 * cols * place : 3 * cols * (place + 1)]
        shared_ref[place, :, 3 * cols :] = gproj[:, place * cols : (place + 1) * cols]
    own_half = pl.ds(pl.multiple_of(dp * half, half), half)
    other_half = pl.ds(pl.multiple_of((1 - dp) * half, half), half)
    h_copy = send(shared_ref.at[:, other_half], half_recv, h_sems.at[0, 0], h_sems.at[1, 0], twin)
    take("wqkv", "x")
    for image in range(own_images):
        rows = pl.ds(image * seq, seq)
        grad = dot_nt(dqkv_ref[rows], wqkv_ref[...])
        unit, scale = normalize(x_ref[rows].astype(jnp.float32))
        sums[0] += jnp.sum(grad * unit, axis=0, keepdims=True)
        sums[1] += jnp.sum(grad, axis=0, keepdims=True)
        dx = dmid_ref[rows] + normalize_back(grad * gain_one, unit, scale)
        dx_send[image] = dx.astype(jnp.bfloat16).reshape(n_ctx, seq_dev, width)
        if image == 0:
            h_copy.wait()
            for place in range(n_ctx):
                sum_one[place] = (
                    shared_ref[place, own_half].astype(jnp.float32)
                    + half_recv[place].astype(jnp.float32)
                ).astype(jnp.bfloat16)
            c_copies = to_each(
                ctx_ids,
                lambda at, partner: sum_one.at[partner[1]],
                lambda at, partner: ctx_recv.at[at],
                c_sems,
            )
    for at, total in enumerate(sums):
        small_ref[at : at + 1] = total
    small_ref[4:8] = jnp.zeros((4, width), jnp.float32)
    small_ref[8:16] = grouter_ref[...]
    s_copy = send(small_ref, small_twin, h_sems.at[0, 1], h_sems.at[1, 1], twin)
    dx_copies = to_each(
        ctx_ids,
        lambda at, partner: dx_send.at[:, partner[1]],
        lambda at, partner: dx_ref.at[pl.ds(ctx * own_images, own_images)],
        dx_sems,
    )
    for image in range(own_images):
        dx_ref[ctx * own_images + image] = dx_send[image, ctx]
    s_copy.wait()
    small_ctx[ctx] = small_ref[...] + small_twin[...]
    s_copies = to_each(
        ctx_ids, lambda at, partner: small_ctx.at[ctx], lambda at, partner: small_ctx.at[ctx], s_sems
    )
    take("out")
    for copy in out_copies:
        copy.wait()
    for step in range(n_ctx):
        start = ctx_partner(ctx, step) * own_images
        for image in range(own_images):
            total = out_own[step, image].astype(jnp.float32)
            for at in range(n_ctx - 1):
                total += out_recv[ctx_partner(ctx, at + 1), start + image].astype(jnp.float32)
            out_ref[start + image] = total.astype(jnp.bfloat16)
    for copy in c_copies:
        copy.wait()
    total = sum_one[ctx].astype(jnp.float32)
    for at in range(n_ctx - 1):
        total += ctx_recv[at].astype(jnp.float32)
    piece_send[...] = total.astype(jnp.bfloat16).reshape(piece_send.shape)
    p_copies = to_each(
        z_ids,
        lambda at, partner: piece_send.at[partner[0]],
        lambda at, partner: piece_recv.at[at],
        p_sems,
    )
    for copy in s_copies:
        copy.wait()
    total = small_ctx[0]
    for place in range(1, n_ctx):
        total += small_ctx[place]
    small_z[expert] = total
    s_copies = to_each(
        z_ids,
        lambda at, partner: small_z.at[expert],
        lambda at, partner: small_z.at[expert],
        n_sems.at[0],
    )

    def gram_start(which, matrix):
        gram_blocks(matrix.astype(jnp.bfloat16), packed_ref.at[which])
        return to_each(
            ctx_ids,
            lambda at, partner: packed_ref.at[which, :, partner[1]],
            lambda at, partner: packed_recv.at[which, at],
            g_sems.at[which],
        )

    def gram_middle(which, copies):
        for copy in copies:
            copy.wait()
        total = packed_ref[which, :, ctx]
        for at in range(n_ctx - 1):
            total += packed_recv[which, at]
        gathered_ref[which, :, ctx] = total
        return to_each(
            ctx_ids,
            lambda at, partner: gathered_ref.at[which, :, ctx],
            lambda at, partner: gathered_ref.at[which, :, ctx],
            a_sems.at[which],
        )

    def step_of(which, matrix, scale):
        total_high, total_low = split(total_ref[...])
        high, low = split(matrix * scale)
        cut = pl.ds(0, matrix.shape[1])
        step_ref[which, dp, :, cut] = (
            dot(total_high, high) + dot(total_high, low) + dot(total_low, high)
        ).astype(jnp.bfloat16)
        return send(
            step_ref.at[which, dp, :, cut],
            step_ref.at[which, dp, :, cut],
            x_sems.at[0, which],
            x_sems.at[1, which],
            twin,
        )

    take("grads")

    @pl.when(at_end)
    def _():
        copies = end_copies()
        for copy in copies:
            copy.wait_send()
        copies[1].wait_recv()
        copies[2].wait_recv()
        total = own_grads[...].astype(jnp.float32)
        for slot in range(2):
            total += z_recv[slot].astype(jnp.float32)
        gexp_ref[dp] = total.astype(jnp.bfloat16)

    @pl.when(jnp.logical_not(at_end))
    def _():
        copies = mid_copies()
        copies[1].wait_send()
        copies[2].wait_send()
        for copy in copies:
            copy.wait_recv()
        total = own_grads[...].astype(jnp.float32)
        for slot in range(3):
            total += z_recv[slot].astype(jnp.float32)
        gexp_ref[dp] = total.astype(jnp.bfloat16)

    f_copy = send(gexp_ref.at[dp], gexp_ref.at[dp], f_sems.at[0], f_sems.at[1], twin)
    moment[0].wait()
    mat_ref[0] = DECAY * mexp_ref[...] + gexp_ref[dp].astype(jnp.float32)
    exp_copies = gram_start(0, mat_ref[0])
    for copy in p_copies:
        copy.wait()
    total = piece_send[expert].astype(jnp.float32)
    for at in range(n_exp - 1):
        total += piece_recv[at].astype(jnp.float32)
    whole_ref[dp, expert] = total.astype(jnp.bfloat16)
    p_copies = to_each(
        z_ids,
        lambda at, partner: whole_ref.at[dp, expert],
        lambda at, partner: whole_ref.at[dp, expert],
        w_sems,
    )
    for copy in p_copies:
        copy.wait()
    w_copy = send(whole_ref.at[dp], whole_ref.at[dp], f_sems.at[2], f_sems.at[3], twin)
    exp_copies = gram_middle(0, exp_copies)
    for copy in s_copies:
        copy.wait()
    total = small_z[0]
    for place in range(1, n_exp):
        total += small_z[place]
    sums_ref[...] = total
    lane_part = pl.ds(pl.multiple_of(ctx * cols, cols), cols)
    fresh_norm = DECAY * mnorm_ref[...] + sums_ref[0:4, lane_part]
    fresh_router = DECAY * mrouter_ref[...] + sums_ref[pl.ds(8 + ctx, 1)]
    row = lax.broadcasted_iota(jnp.int32, (8, LANES), 0)
    squares_ref[ctx] = jnp.where(
        row == 0,
        jnp.sum(fresh_norm * fresh_norm, keepdims=True),
        jnp.sum(fresh_router * fresh_router, keepdims=True),
    )
    n_copies = to_each(
        ctx_ids,
        lambda at, partner: squares_ref.at[ctx],
        lambda at, partner: squares_ref.at[ctx],
        n_sems.at[1],
    )
    w_copy.wait()
    take("mqkv", "mproj")
    grad = whole_ref[...].reshape(width, width).astype(jnp.float32)
    mat_ref[1, :, : 3 * cols] = DECAY * mqkv_ref[...] + grad[:, : 3 * cols]
    mat_ref[2, :, :cols] = DECAY * mproj_ref[...] + grad[:, 3 * cols :]
    mat_ref[2, :, cols : 3 * cols] = jnp.zeros((width, 2 * cols), jnp.float32)
    shared_copies = [gram_start(1, mat_ref[1 + dp, :, : 3 * cols])]
    for copy in exp_copies:
        copy.wait()
    exp_scale = gram_whole(gathered_ref.at[0], high_ref, low_ref)
    orthogonal(high_ref, low_ref, mix_ref, total_ref)
    exp_step = step_of(0, mat_ref[0], exp_scale)
    shared_copies[0] = gram_middle(1, shared_copies[0])
    for copy in shared_copies[0]:
        copy.wait()
    shared_scale = gram_whole(gathered_ref.at[1], high_ref, low_ref)
    orthogonal(high_ref, low_ref, mix_ref, total_ref)
    shared_step = step_of(1, mat_ref[1 + dp, :, : 3 * cols], shared_scale)
    for copy in dx_copies + n_copies + [f_copy, exp_step, shared_step]:
        copy.wait()


def finish_kernel(
    experts,
    n_ctx,
    width,
    ctx_ref,
    gexp_ref,
    step_ref,
    whole_ref,
    sums_ref,
    squares_ref,
    dx_in,
    out_in,
    min_ref,
    mout_ref,
    mqkv_ref,
    mproj_ref,
    mnorm_ref,
    mrouter_ref,
    win_ref,
    wout_ref,
    wqkv_ref,
    wproj_ref,
    norm_ref,
    router_ref,
    o_out,
    o_dx,
    o_gnorm,
    o_grouter,
    o_gqkv,
    o_gproj,
    o_gin,
    o_gout,
    o_mnorm,
    o_mrouter,
    o_mqkv,
    o_mproj,
    o_min,
    o_mout,
    o_nnorm,
    o_nrouter,
    o_nqkv,
    o_nproj,
    o_nin,
    o_nout,
    o_bqkv,
    o_bproj,
    o_bin,
    o_bout,
):
    cols = width // n_ctx
    o_out[...] = out_in[...]
    o_dx[...] = dx_in[...].astype(jnp.float32)

    def update(grad, moment, weight, step, columns, outs):
        o_g, o_m, o_n, o_b = outs
        rate = RATE_MAT * 0.2 * math.sqrt(max(width, columns))
        new = weight.astype(jnp.float32) - rate * step.astype(jnp.float32)
        o_g[...] = grad.reshape(o_g.shape)
        o_m[...] = (DECAY * moment + grad).reshape(o_m.shape)
        o_n[...] = new.reshape(o_n.shape)
        o_b[...] = new.astype(jnp.bfloat16).reshape(o_b.shape)

    for index, outs in enumerate(((o_gin, o_min, o_nin, o_bin), (o_gout, o_mout, o_nout, o_bout))):
        update(
            gexp_ref[index].astype(jnp.float32),
            (min_ref, mout_ref)[index][0],
            (win_ref, wout_ref)[index][0],
            step_ref[0, index],
            n_ctx * gexp_ref.shape[2],
            outs,
        )
    grad = whole_ref[...].astype(jnp.float32)
    update(
        grad[:, : 3 * cols],
        mqkv_ref[...],
        wqkv_ref[...],
        step_ref[1, 0, :, : 3 * cols],
        3 * width,
        (o_gqkv, o_mqkv, o_nqkv, o_bqkv),
    )
    update(
        grad[:, 3 * cols :],
        mproj_ref[...],
        wproj_ref[...],
        step_ref[1, 1, :, :cols],
        width,
        (o_gproj, o_mproj, o_nproj, o_bproj),
    )
    ctx = ctx_ref[0]
    own_norm = sums_ref[0:4, pl.ds(pl.multiple_of(ctx * cols, cols), cols)]
    own_router = sums_ref[pl.ds(8 + ctx, 1)]
    fresh_norm = DECAY * mnorm_ref[...] + own_norm
    fresh_router = DECAY * mrouter_ref[...] + own_router
    o_gnorm[...] = own_norm
    o_grouter[...] = own_router
    o_mnorm[...] = fresh_norm
    o_mrouter[...] = fresh_router
    squares = squares_ref[0]
    for place in range(1, n_ctx):
        squares += squares_ref[place]
    o_nnorm[...] = norm_ref[...] - (
        RATE_GAIN * fresh_norm * lax.rsqrt(squares[0:1] / (4 * width) + EPS_NORM)
    )
    o_nrouter[...] = router_ref[pl.ds(ctx, 1)] - RATE_ROUTER * fresh_router * lax.rsqrt(
        squares[1:2, 0:1] / (width * experts) + EPS_NORM
    )


def call(kernel, ident, outs, scratch, operands, spaces, out_spaces=None):
    out_spaces = out_spaces or [pltpu.VMEM] * len(outs)
    return pl.pallas_call(
        kernel,
        out_shape=[jax.ShapeDtypeStruct(shape, dtype) for shape, dtype in outs],
        in_specs=[pl.BlockSpec(memory_space=space) for space in spaces],
        out_specs=[pl.BlockSpec(memory_space=space) for space in out_spaces],
        scratch_shapes=scratch,
        compiler_params=pltpu.CompilerParams(
            collective_id=ident, has_side_effects=True, vmem_limit_bytes=VMEM_LIMIT
        ),
    )(*operands)


def gathered(
    x_in,
    d_out,
    key_mask,
    expert_ids,
    norm_params,
    w_qkv,
    w_proj,
    w_router,
    w_in,
    w_out,
    mom_norm,
    mom_router,
    mom_qkv,
    mom_proj,
    mom_in,
    mom_out,
):
    n_exp = lax.axis_size("expert")
    n_ctx = lax.axis_size("ctx")
    ctx = lax.axis_index("ctx")
    images, seq_dev, width = x_in.shape
    experts = w_router.shape[1]
    own_images = images // n_ctx
    seq = n_ctx * seq_dev
    rows = own_images * seq
    hid = w_in.shape[2]
    low, full = jnp.bfloat16, jnp.float32
    dma = lambda *shape: pltpu.SemaphoreType.DMA(shape)
    vmem = lambda shape, dtype: pltpu.VMEM(shape, dtype)

    vm, anywhere = pltpu.VMEM, pl.ANY
    block = (own_images, n_ctx, seq_dev, width)
    kept = [
        (block, low),
        ((rows, width), low),
        ((rows, 3 * width), low),
        ((rows, LANES), full),
        ((rows, width), low),
        ((rows, width), full),
        (block, low),
        ((own_images, 8, seq), full),
        ((n_ctx,) + block, low),
        ((rows, width), full),
        ((n_exp, width, hid), low),
        ((8, width), full),
    ]
    router_turned = w_router.T
    (x_all, first, qkv, lse, att, mid, d_own, mask_own, out_parts, dsecond, grads, grouter) = call(
        functools.partial(forward_kernel, n_exp, experts),
        1,
        kept,
        [vmem(*kept[at]) for at in (0, 1, 2, 3, 4, 5, 7, 8, 9)]
        + [
            vmem((n_exp, width, hid), low),
            vmem((8, width), full),
            vmem((n_ctx,) + block, low),
            vmem((2, n_exp, width, hid), low),
            vmem((n_ctx, own_images, seq, width), low),
            vmem((images, 8, LANES), full),
            vmem((n_ctx, images, 8, LANES), full),
            vmem((width, 3 * width), low),
            vmem((width, width), low),
            vmem((2, LANES, width), full),
            vmem((n_ctx - 1, rows, width), low),
            vmem((n_ctx - 1, rows, width), low),
            vmem((2, rows, width), full),
            vmem((2, rows, width), full),
            vmem((width, LANES), full),
            vmem((2, rows, LANES), full),
            vmem((2, rows, LANES), full),
            vmem((width, n_ctx * rows), low),
            vmem((width, n_ctx * rows), low),
            vmem((n_exp, n_ctx * rows, hid), low),
            vmem((n_exp, n_ctx * rows, hid), low),
            dma(2, own_images, n_ctx - 1),
            dma(2, n_ctx - 1),
            dma(2, n_ctx - 1, n_ctx),
            dma(2, 2, 2),
            dma(2, n_ctx - 1),
            dma(2, 2, n_ctx),
            dma(2, 2),
            dma(2, n_exp - 1, 2),
            dma(2, n_exp - 1, 2),
            dma(2, n_exp),
            dma(6),
            dma(15 + n_exp),
        ],
        (
            x_in,
            d_out.reshape(n_ctx, own_images, seq_dev, width),
            expert_ids.swapaxes(1, 2),
            key_mask,
            w_in,
            w_out,
            norm_params,
            w_qkv,
            w_proj,
            router_turned,
        ),
        [anywhere, anywhere, vm, vm, anywhere, anywhere, vm, anywhere, anywhere, vm],
        [anywhere] * 12,
    )
    cols = width // n_ctx
    blocks = (width // LANES) * (width // LANES + 1) // 2
    block_rows = LANES // n_ctx
    quarter = (n_exp, width // 2 // n_exp, width)
    moments = (mom_in, mom_out, mom_qkv, mom_proj, mom_norm, mom_router.reshape(1, width))
    out_low, dx_low, gexp, steps, whole, sums, squares = call(
        functools.partial(backward_kernel, n_exp),
        2,
        [
            ((images, seq_dev, width), low),
            ((images, seq_dev, width), low),
            ((2, width, hid), low),
            ((2, 2, width, hid), low),
            ((2,) + quarter, low),
            ((16, width), full),
            ((n_ctx, 8, LANES), full),
        ],
        [
            vmem((rows, width), low),
            vmem((rows, width), low),
            vmem((own_images, 8, seq), full),
            vmem((rows, width), low),
            vmem((rows, 3 * width), low),
            vmem((rows, LANES), full),
            vmem((rows, width), low),
            vmem((rows, width), full),
            vmem((rows, width), full),
            vmem((width, hid), low),
            vmem((width, hid), low),
            vmem((width, 3 * width), low),
            vmem((width, width), low),
            vmem((n_ctx, own_images, seq_dev, width), low),
            vmem((width, hid), full),
            vmem((width, 3 * cols), full),
            vmem((width, cols), full),
            vmem((n_ctx, images, seq_dev, width), low),
            vmem((n_exp, width, hid), low),
            vmem((rows, width), full),
            vmem((rows, width), low),
            vmem((rows, width), low),
            vmem((rows, 3 * width), low),
            vmem(block, low),
            vmem((n_ctx, width, width), low),
            vmem((n_ctx, width // 2, width), low),
            vmem((n_ctx, width // 2, width), low),
            vmem((n_ctx - 1, width // 2, width), low),
            vmem(quarter, low),
            vmem((n_exp - 1,) + quarter[1:], low),
            vmem((3, width, hid), full),
            vmem((2, blocks, n_ctx, block_rows, LANES), full),
            vmem((2, n_ctx - 1, blocks, block_rows, LANES), full),
            vmem((2, blocks, n_ctx, block_rows, LANES), full),
            vmem((width, width), low),
            vmem((width, width), low),
            vmem((width, width), low),
            vmem((width, width), full),
            vmem((16, width), full),
            vmem((16, width), full),
            vmem((n_ctx, 16, width), full),
            vmem((n_exp, 16, width), full),
            dma(17),
            dma(2, n_ctx, n_ctx - 1),
            dma(2, n_exp),
            dma(4),
            dma(2, n_ctx - 1),
            dma(2, 2),
            dma(2, n_ctx - 1),
            dma(2, n_ctx - 1),
            dma(2, n_exp - 1),
            dma(2, n_exp - 1),
            dma(2, 2, n_ctx - 1),
            dma(2, 2, n_ctx - 1),
            dma(2, 2),
            dma(2, 2, max(n_ctx, n_exp) - 1),
        ],
        (
            x_all.reshape(rows, width),
            d_own.reshape(rows, width),
            mask_own,
            first,
            qkv,
            lse,
            att,
            mid,
            dsecond,
            grads,
            grouter,
            norm_params,
            w_qkv,
            w_proj,
            out_parts,
        )
        + moments,
        [anywhere] * 10 + [vm, vm] + [anywhere] * 7 + [vm, vm],
    )
    pieces = ((4, cols), (1, width), (width, 3 * cols), (width, cols), (1, width, hid), (1, width, hid))
    parts = width // LANES
    outs = (
        [((images, seq_dev, width), low), ((images, seq_dev, width), full)]
        + [(piece, full) for piece in pieces * 3]
        + [(piece, low) for piece in pieces[2:]]
    )

    def strip(shape, axis, last=None):
        def index_map(at, ctx_ref):
            place = [0] * len(shape)
            if axis is not None:
                place[axis] = at
            if last is not None:
                place[-1] = ctx_ref[0]
            return tuple(place)

        size = list(shape)
        if axis is not None:
            size[axis] //= parts
        if last is not None:
            size[-1] = last
        return pl.BlockSpec(tuple(size), index_map)

    def strips(shape):
        if len(shape) == 3:
            return strip(shape, 0 if shape[0] == images else 1)
        return strip(shape, 0 if shape[0] == width else None)

    results = pl.pallas_call(
        functools.partial(finish_kernel, experts, n_ctx, width),
        out_shape=[jax.ShapeDtypeStruct(shape, dtype) for shape, dtype in outs],
        grid_spec=pltpu.PrefetchScalarGridSpec(
            num_scalar_prefetch=1,
            grid=(parts,),
            in_specs=[
                strip((2, width, hid), 1),
                strip((2, 2, width, hid), 2),
                strip((width, width), 0),
                strip((16, width), None),
                strip((n_ctx, 8, LANES), None),
                strip((images, seq_dev, width), 0),
                strip((images, seq_dev, width), 0),
                strip((1, width, hid), 1),
                strip((1, width, hid), 1),
                strip((width, 3 * cols), 0),
                strip((width, cols), 0),
                strip((4, cols), None),
                strip((1, width), None),
                strip((1, width, hid), 1),
                strip((1, width, hid), 1),
                strip((width, 3 * width), 0, 3 * cols),
                strip((width, width), 0, cols),
                strip((4, width), None, cols),
                strip((experts, width), None),
            ],
            out_specs=[strips(shape) for shape, _ in outs],
        ),
        compiler_params=pltpu.CompilerParams(vmem_limit_bytes=VMEM_LIMIT),
    )(
        ctx.reshape(1),
        gexp,
        steps,
        whole.reshape(width, width),
        sums,
        squares,
        dx_low,
        out_low,
        *moments,
        w_in,
        w_out,
        w_qkv,
        w_proj,
        norm_params,
        router_turned,
    )
    return tuple(
        value.reshape(width, 1) if value.shape == (1, width) else value for value in results
    )


def solution(mesh):
    in_specs = (
        P(("expert", "dp"), "ctx", None),
        P(("expert", "dp"), "ctx", None),
        P(("expert", "dp"), "ctx"),
        P(("expert", "dp"), "ctx", None),
        P(),
        P(),
        P(),
        P(),
        P("expert", None, "ctx"),
        P("expert", None, "ctx"),
        P(None, "ctx"),
        P(None, "ctx"),
        P(None, "ctx"),
        P(None, "ctx"),
        P("expert", None, "ctx"),
        P("expert", None, "ctx"),
    )
    out_specs = (
        P(("expert", "dp"), "ctx", None),
        P(("expert", "dp"), "ctx", None),
        P(None, "ctx"),
        P(None, "ctx"),
        P(None, "ctx"),
        P(None, "ctx"),
        P("expert", None, "ctx"),
        P("expert", None, "ctx"),
        P(None, "ctx"),
        P(None, "ctx"),
        P(None, "ctx"),
        P(None, "ctx"),
        P("expert", None, "ctx"),
        P("expert", None, "ctx"),
        P(None, "ctx"),
        P(None, "ctx"),
        P(None, "ctx"),
        P(None, "ctx"),
        P("expert", None, "ctx"),
        P("expert", None, "ctx"),
        P(None, "ctx"),
        P(None, "ctx"),
        P("expert", None, "ctx"),
        P("expert", None, "ctx"),
    )
    experts = mesh.shape["expert"]
    square = mesh.shape["ctx"] == 4 and mesh.shape["dp"] == 2

    def local(*arrays):
        whole = (
            square
            and arrays[7].shape[1] == experts <= 7
            and arrays[8].shape[0] == 1
            and 2 * arrays[0].shape[1] == LANES
        )
        return (gathered if whole else exchanged)(*arrays)

    return jax.shard_map(local, mesh=mesh, in_specs=in_specs, out_specs=out_specs, check_vma=False)
```

```python
import functools
import math

import jax
import jax.numpy as jnp
from jax import lax
from jax.experimental import pallas as pl
from jax.experimental.pallas import tpu as pltpu
from jax.sharding import PartitionSpec as P

HEADS = 8
HEAD_DIM = 64
MICRO = 2
NS_ITERS = 4


HIGH = lax.Precision.HIGHEST
NS_A = 3.4445
NS_B = -4.775
NS_C = 2.0315
DECAY = 0.5
RATE_MAT = 0.3
RATE_GAIN = 0.3
RATE_ROUTER = 0.05
EPS_NORM = 1e-06
EPS_ORTHO = 1e-07
NEG = -1e30
LANES = 128
VMEM_LIMIT = 60 * 2**20
MESH = pl.DeviceIdType.MESH


def as_sent(array):
    return jax.tree.map(lambda a: a.astype(jnp.bfloat16) if a.dtype == jnp.float32 else a, array)


def layer_norm(values, gain, shift):
    center = jnp.mean(values, axis=-1, keepdims=True)
    spread = values - center
    power = jnp.mean(spread * spread, axis=-1, keepdims=True)
    return spread * lax.rsqrt(power + EPS_NORM) * gain + shift


def gelu_exact(values):
    return jax.nn.gelu(values, approximate=False)


def add_block(total, piece):
    return total + piece


def masked_scores(query, key_piece, mask_piece, factor):
    scores = (
        jnp.einsum("bqhd,bkhd->bhqk", query, key_piece, preferred_element_type=jnp.float32) * factor
    )
    return jnp.where(mask_piece[:, None, None, :] > 0, scores, NEG)


def gram_list(matrices):
    return tuple(
        (jnp.einsum("...ik,...jk->...ij", matrix, matrix, precision=HIGH) for matrix in matrices)
    )


def schulz_turn(matrices, grams):
    result = []
    for matrix, gram in zip(matrices, grams):
        square = jnp.einsum("...ij,...jk->...ik", gram, gram, precision=HIGH)
        mixer = NS_B * gram + NS_C * square
        result.append(
            NS_A * matrix + jnp.einsum("...ij,...jk->...ik", mixer, matrix, precision=HIGH)
        )
    return tuple(result)


def exchanged(
    x_in,
    d_out,
    key_mask,
    expert_ids,
    norm_params,
    w_qkv,
    w_proj,
    w_router,
    w_in,
    w_out,
    mom_norm,
    mom_router,
    mom_qkv,
    mom_proj,
    mom_in,
    mom_out,
):
    ctx_count = lax.axis_size("ctx")
    ctx_place = lax.axis_index("ctx")
    owner_count = lax.axis_size("expert")
    local_images = x_in.shape[0]
    seq_dev = x_in.shape[1]
    width = x_in.shape[2]
    top_count = expert_ids.shape[-1]
    experts = w_router.shape[1]
    exp_dev = w_in.shape[0]
    hid_part = w_in.shape[2]
    capacity = max(2, (5 * top_count * seq_dev + 4 * experts - 1) // (4 * experts))
    batch = local_images // MICRO
    slot_count = batch * capacity
    seq_all = seq_dev * ctx_count
    factor = HEAD_DIM ** (-0.5)
    expert_iota = jnp.arange(experts, dtype=jnp.int32)
    recv_shape = (owner_count, exp_dev, slot_count, width)
    head_shape = (batch, seq_dev, HEADS, HEAD_DIM)

    def hidden_fold(step_fn, init):
        folded = step_fn(
            init,
            (
                lax.all_gather(w_in, "ctx", axis=2, tiled=True),
                lax.all_gather(w_out, "ctx", axis=2, tiled=True),
            ),
            jnp.int32(0),
        )
        return folded

    def to_owner(rows):
        return lax.all_to_all(rows, "expert", split_axis=0, concat_axis=0, tiled=True)

    def to_source(rows):
        return lax.all_to_all(rows, "expert", split_axis=0, concat_axis=0, tiled=True)

    def key_fold(keys, values, mask_low, step_fn, init):
        return step_fn(
            init,
            (
                lax.all_gather(keys, "ctx", axis=1, tiled=True),
                lax.all_gather(values, "ctx", axis=1, tiled=True),
                lax.all_gather(mask_low, "ctx", axis=1, tiled=True),
            ),
            jnp.int32(0),
        )

    grad_qkv = jnp.zeros(w_qkv.shape, jnp.float32)
    grad_proj = jnp.zeros(w_proj.shape, jnp.float32)
    grad_router = jnp.zeros(w_router.shape, jnp.float32)
    grad_norm = jnp.zeros((4, width), jnp.float32)
    grad_in = jnp.zeros((exp_dev, width, hid_part * ctx_count), jnp.float32)
    grad_out = jnp.zeros((exp_dev, width, hid_part * ctx_count), jnp.float32)
    outputs = []
    input_grads = []
    for micro_index in range(MICRO):
        first_image = micro_index * batch
        last_image = first_image + batch
        x_part = x_in[first_image:last_image].astype(jnp.float32)
        cotangent = d_out[first_image:last_image].astype(jnp.float32)
        mask_low = key_mask[first_image:last_image].astype(jnp.bfloat16)
        idents = expert_ids[first_image:last_image]
        normed_first, pull_first = jax.vjp(layer_norm, x_part, norm_params[0], norm_params[1])
        first_low = normed_first.astype(jnp.bfloat16).reshape(-1, width)
        qkv = jnp.dot(first_low, w_qkv, preferred_element_type=jnp.float32).astype(jnp.bfloat16)
        qkv = qkv.reshape(batch, seq_dev, 3, HEADS, HEAD_DIM)
        query = qkv[:, :, 0]
        keys = qkv[:, :, 1]
        values = qkv[:, :, 2]
        peak_old = jnp.full((batch, HEADS, seq_dev), NEG, jnp.float32)
        key_piece = lax.all_gather(keys, "ctx", axis=1, tiled=True)
        mask_piece = lax.all_gather(mask_low, "ctx", axis=1, tiled=True)
        scores = masked_scores(query, key_piece, mask_piece, factor)
        peak_new = jnp.maximum(peak_old, jnp.max(scores, axis=-1))
        total_new = jnp.sum(jnp.exp(scores - peak_new[..., None]), axis=-1)
        log_total = peak_new + jnp.log(total_new)

        def attend_step(acc, pieces, start):
            key_piece, value_piece, mask_piece = pieces
            weights = jnp.exp(
                masked_scores(query, key_piece, mask_piece, factor) - log_total[..., None]
            )
            return jnp.einsum(
                "bhqk,bkhd->bqhd",
                weights.astype(jnp.bfloat16),
                value_piece,
                preferred_element_type=jnp.float32,
            )

        attended = key_fold(keys, values, mask_low, attend_step, jnp.zeros(head_shape, jnp.float32))
        attended_low = attended.astype(jnp.bfloat16).reshape(-1, width)
        branch = jnp.dot(attended_low, w_proj, preferred_element_type=jnp.float32).reshape(
            batch, seq_dev, width
        )
        mid = x_part + branch
        normed_second, pull_second = jax.vjp(layer_norm, mid, norm_params[2], norm_params[3])
        routed_low = normed_second.astype(jnp.bfloat16)
        logits = jnp.einsum("bsd,de->bse", normed_second, w_router, precision=HIGH)
        onehot = (idents[..., None] == expert_iota).astype(jnp.float32)
        chosen = jnp.sum(onehot * logits[:, :, None, :], axis=-1)
        gates = jax.nn.softmax(chosen, axis=-1)
        flat_ids = idents.reshape(batch, seq_dev * top_count)
        hits = (flat_ids[..., None] == expert_iota).astype(jnp.int32)
        ranked = jnp.sum((jnp.cumsum(hits, axis=1) - hits) * hits, axis=-1)
        slot = (ranked + (jnp.arange(batch, dtype=jnp.int32) * capacity)[:, None]).reshape(-1)
        target = flat_ids.reshape(-1)
        routed_rows = jnp.broadcast_to(
            routed_low[:, :, None, :], (batch, seq_dev, top_count, width)
        ).reshape(-1, width)
        send = (
            jnp.zeros((experts, slot_count, width), jnp.bfloat16).at[target, slot].set(routed_rows)
        )
        received = to_owner(send.reshape(recv_shape))

        def expert_step(acc, pieces, start):
            piece_in, piece_out = pieces
            pre = jnp.einsum(
                "nesd,edh->nesh", received, piece_in, preferred_element_type=jnp.float32
            )
            act = gelu_exact(pre).astype(jnp.bfloat16)
            return jnp.einsum("nesh,edh->nesd", act, piece_out, preferred_element_type=jnp.float32)

        made = hidden_fold(expert_step, jnp.zeros(recv_shape, jnp.float32))
        back_rows = to_source(made.astype(jnp.bfloat16)).reshape(experts, slot_count, width)
        returned = (
            back_rows[target, slot].reshape(batch, seq_dev, top_count, width).astype(jnp.float32)
        )
        result = mid + jnp.sum(gates[..., None] * returned, axis=2)
        outputs.append(result.astype(jnp.bfloat16))
        dgates = jnp.sum(cotangent[:, :, None, :] * returned, axis=-1)
        dchosen = gates * (dgates - jnp.sum(gates * dgates, axis=-1, keepdims=True))
        dlogits = jnp.sum(dchosen[..., None] * onehot, axis=2)
        grad_router = grad_router + jnp.einsum(
            "bsd,bse->de", normed_second, dlogits, precision=HIGH
        )
        dsecond = jnp.einsum("bse,de->bsd", dlogits, w_router, precision=HIGH)
        dreturned = (
            (gates[..., None] * cotangent[:, :, None, :]).astype(jnp.bfloat16).reshape(-1, width)
        )
        dsend = (
            jnp.zeros((experts, slot_count, width), jnp.bfloat16).at[target, slot].set(dreturned)
        )
        dreceived = to_owner(dsend.reshape(recv_shape))

        def expert_back(carry, pieces, start):
            drows, dins, douts = carry
            piece_in, piece_out = pieces
            pre = jnp.einsum(
                "nesd,edh->nesh", received, piece_in, preferred_element_type=jnp.float32
            )
            act_full, pull_act = jax.vjp(gelu_exact, pre)
            act = act_full.astype(jnp.bfloat16)
            dact = jnp.einsum(
                "nesd,edh->nesh", dreceived, piece_out, preferred_element_type=jnp.float32
            )
            dpre = pull_act(dact)[0].astype(jnp.bfloat16)
            douts = add_block(
                douts,
                jnp.einsum("nesd,nesh->edh", dreceived, act, preferred_element_type=jnp.float32),
            )
            dins = add_block(
                dins,
                jnp.einsum("nesd,nesh->edh", received, dpre, preferred_element_type=jnp.float32),
            )
            drows = jnp.einsum("nesh,edh->nesd", dpre, piece_in, preferred_element_type=jnp.float32)
            return (drows, dins, douts)

        drows, grad_in, grad_out = hidden_fold(
            expert_back, (jnp.zeros(recv_shape, jnp.float32), grad_in, grad_out)
        )
        dback = to_source(drows.astype(jnp.bfloat16)).reshape(experts, slot_count, width)
        dsecond = dsecond + jnp.sum(
            dback[target, slot].reshape(batch, seq_dev, top_count, width).astype(jnp.float32),
            axis=2,
        )
        dmid, dgain_two, dshift_two = pull_second(dsecond)
        dmid = dmid + cotangent
        dbranch = dmid.astype(jnp.bfloat16).reshape(-1, width)
        grad_proj = grad_proj + jnp.einsum(
            "sd,se->de", attended_low, dbranch, preferred_element_type=jnp.float32
        )
        dattended = jnp.einsum("se,de->sd", dbranch, w_proj, preferred_element_type=jnp.float32)
        dattended = dattended.astype(jnp.bfloat16).reshape(head_shape)
        delta = jnp.einsum("bqhd,bqhd->bhq", dattended.astype(jnp.float32), attended)

        def attend_back(carry, pieces, start):
            dquery, dkeys, dvalues = carry
            key_piece, value_piece, mask_piece = pieces
            weights = jnp.exp(
                masked_scores(query, key_piece, mask_piece, factor) - log_total[..., None]
            )
            probs = weights.astype(jnp.bfloat16)
            dvalue_piece = jnp.einsum(
                "bhqk,bqhd->bkhd", probs, dattended, preferred_element_type=jnp.float32
            )
            dprobs = jnp.einsum(
                "bqhd,bkhd->bhqk", dattended, value_piece, preferred_element_type=jnp.float32
            )
            dscores = (weights * (dprobs - delta[..., None])).astype(jnp.bfloat16)
            dquery = factor * jnp.einsum(
                "bhqk,bkhd->bqhd", dscores, key_piece, preferred_element_type=jnp.float32
            )
            dkey_piece = factor * jnp.einsum(
                "bhqk,bqhd->bkhd", dscores, query, preferred_element_type=jnp.float32
            )
            return (dquery, add_block(dkeys, dkey_piece), add_block(dvalues, dvalue_piece))

        all_shape = (batch, seq_all, HEADS, HEAD_DIM)
        back_init = (
            jnp.zeros(head_shape, jnp.float32),
            jnp.zeros(all_shape, jnp.float32),
            jnp.zeros(all_shape, jnp.float32),
        )
        dquery, dkeys_all, dvalues_all = key_fold(keys, values, mask_low, attend_back, back_init)
        dkeys, dvalues = (
            lax.psum_scatter(
                dkeys_all.astype(jnp.bfloat16), "ctx", scatter_dimension=1, tiled=True
            ).astype(jnp.float32),
            lax.psum_scatter(
                dvalues_all.astype(jnp.bfloat16), "ctx", scatter_dimension=1, tiled=True
            ).astype(jnp.float32),
        )
        dqkv = (
            jnp.stack([dquery, dkeys, dvalues], axis=2).astype(jnp.bfloat16).reshape(-1, 3 * width)
        )
        grad_qkv = grad_qkv + jnp.einsum(
            "sd,se->de", first_low, dqkv, preferred_element_type=jnp.float32
        )
        dfirst = jnp.einsum("se,de->sd", dqkv, w_qkv, preferred_element_type=jnp.float32).reshape(
            batch, seq_dev, width
        )
        dx_part, dgain_one, dshift_one = pull_first(dfirst)
        grad_norm = grad_norm + jnp.stack([dgain_one, dshift_one, dgain_two, dshift_two])
        input_grads.append(dx_part + dmid)
    block_out = jnp.concatenate(outputs, axis=0)
    d_x = jnp.concatenate(input_grads, axis=0)
    shared = (
        lax.psum_scatter(
            grad_in.astype(jnp.bfloat16), "ctx", scatter_dimension=2, tiled=True
        ).astype(jnp.float32),
        lax.psum_scatter(
            grad_out.astype(jnp.bfloat16), "ctx", scatter_dimension=2, tiled=True
        ).astype(jnp.float32),
        lax.psum_scatter(
            grad_qkv[None].astype(jnp.bfloat16), "ctx", scatter_dimension=2, tiled=True
        ).astype(jnp.float32),
        lax.psum_scatter(
            grad_proj[None].astype(jnp.bfloat16), "ctx", scatter_dimension=2, tiled=True
        ).astype(jnp.float32),
        lax.psum_scatter(
            grad_norm[None].astype(jnp.bfloat16), "ctx", scatter_dimension=2, tiled=True
        ).astype(jnp.float32),
        lax.psum_scatter(
            grad_router[None].astype(jnp.bfloat16), "ctx", scatter_dimension=2, tiled=True
        ).astype(jnp.float32),
    )
    g_in, g_out = (
        lax.psum(shared[0].astype(jnp.bfloat16), "dp").astype(jnp.float32),
        lax.psum(shared[1].astype(jnp.bfloat16), "dp").astype(jnp.float32),
    )
    g_qkv, g_proj, g_norm, g_router = lax.psum(
        (shared[2][0], shared[3][0], shared[4][0], shared[5][0]), ("expert", "dp")
    )
    own_qkv = lax.dynamic_slice_in_dim(w_qkv, ctx_place * g_qkv.shape[1], g_qkv.shape[1], 1).astype(
        jnp.float32
    )
    own_proj = lax.dynamic_slice_in_dim(
        w_proj, ctx_place * g_proj.shape[1], g_proj.shape[1], 1
    ).astype(jnp.float32)
    own_norm = lax.dynamic_slice_in_dim(
        norm_params, ctx_place * g_norm.shape[1], g_norm.shape[1], 1
    )
    own_router = lax.dynamic_slice_in_dim(
        w_router, ctx_place * g_router.shape[1], g_router.shape[1], 1
    )
    m_qkv = DECAY * mom_qkv + g_qkv
    m_proj = DECAY * mom_proj + g_proj
    m_in = DECAY * mom_in + g_in
    m_out = DECAY * mom_out + g_out
    m_norm = DECAY * mom_norm + g_norm
    m_router = DECAY * mom_router + g_router
    matrices = (m_qkv, m_proj, m_in, m_out)
    vector_squares = (jnp.sum(m_norm * m_norm), jnp.sum(m_router * m_router))
    sums = lax.psum(
        tuple((jnp.sum(matrix * matrix, axis=(-2, -1)) for matrix in matrices)) + vector_squares,
        "ctx",
    )
    vector_totals = sums[4:]
    iterates = tuple(
        (
            matrix / jnp.expand_dims(jnp.sqrt(square) + EPS_ORTHO, (-2, -1))
            for matrix, square in zip(matrices, sums[:4])
        )
    )
    for turn_index in range(NS_ITERS):
        iterates = schulz_turn(
            iterates,
            jax.tree.map(
                lambda part: part.astype(jnp.float32), lax.psum(as_sent(gram_list(iterates)), "ctx")
            ),
        )
    n_qkv = (
        own_qkv - RATE_MAT * 0.2 * math.sqrt(max(width, g_qkv.shape[1] * ctx_count)) * iterates[0]
    )
    n_proj = (
        own_proj - RATE_MAT * 0.2 * math.sqrt(max(width, g_proj.shape[1] * ctx_count)) * iterates[1]
    )
    n_in = (
        w_in.astype(jnp.float32)
        - RATE_MAT * 0.2 * math.sqrt(max(width, hid_part * ctx_count)) * iterates[2]
    )
    n_out = (
        w_out.astype(jnp.float32)
        - RATE_MAT * 0.2 * math.sqrt(max(width, hid_part * ctx_count)) * iterates[3]
    )
    n_norm = own_norm - RATE_GAIN * m_norm * lax.rsqrt(vector_totals[0] / (4 * width) + EPS_NORM)
    n_router = own_router - RATE_ROUTER * m_router * lax.rsqrt(
        vector_totals[1] / (width * experts) + EPS_NORM
    )
    return (
        block_out,
        d_x,
        g_norm,
        g_router,
        g_qkv,
        g_proj,
        g_in,
        g_out,
        m_norm,
        m_router,
        m_qkv,
        m_proj,
        m_in,
        m_out,
        n_norm,
        n_router,
        n_qkv,
        n_proj,
        n_in,
        n_out,
        n_qkv.astype(jnp.bfloat16),
        n_proj.astype(jnp.bfloat16),
        n_in.astype(jnp.bfloat16),
        n_out.astype(jnp.bfloat16),
    )


def dot(left, right, precision=None):
    return jnp.dot(left, right, precision=precision, preferred_element_type=jnp.float32)


def dot_nt(left, right, precision=None):
    return lax.dot_general(
        left, right, (((1,), (1,)), ((), ())), precision=precision, preferred_element_type=jnp.float32
    )


def dot_tn(left, right, precision=None):
    return lax.dot_general(
        left, right, (((0,), (0,)), ((), ())), precision=precision, preferred_element_type=jnp.float32
    )


def places():
    return lax.axis_index("expert"), lax.axis_index("ctx"), lax.axis_index("dp")


def ctx_partner(ctx, step):
    column, row = lax.rem(ctx, 2), ctx // 2
    column = lax.rem(column + lax.rem(step, 2), 2)
    row = lax.rem(row + step // 2, 2)
    return row * 2 + column


def z_partner(expert, step, count):
    return lax.rem(expert + step, count)


def greet(partners):
    for partner in partners:
        pl.semaphore_signal(
            pltpu.get_barrier_semaphore(), inc=1, device_id=partner, device_id_type=MESH
        )


def await_greetings(partners):
    pl.semaphore_wait(pltpu.get_barrier_semaphore(), len(partners))


def send(source, target, send_sem, recv_sem, partner):
    copy = pltpu.make_async_remote_copy(
        src_ref=source,
        dst_ref=target,
        send_sem=send_sem,
        recv_sem=recv_sem,
        device_id=partner,
        device_id_type=MESH,
    )
    copy.start()
    return copy


def normalize(values):
    center = jnp.mean(values, axis=-1, keepdims=True)
    spread = values - center
    power = jnp.mean(spread * spread, axis=-1, keepdims=True)
    scale = lax.rsqrt(power + EPS_NORM)
    return spread * scale, scale


def normalize_back(grad, unit, scale):
    first = jnp.mean(grad, axis=-1, keepdims=True)
    second = jnp.mean(grad * unit, axis=-1, keepdims=True)
    return scale * (grad - first - unit * second)


def group_rows(meta_ref, image):
    pairs = [
        meta_ref[2 * half, image] + meta_ref[2 * half + 1, image]
        for half in range(meta_ref.shape[0] // 2)
    ]
    return jnp.concatenate(pairs, axis=1)


def split(values):
    high = values.astype(jnp.bfloat16)
    return high, (values - high.astype(jnp.float32)).astype(jnp.bfloat16)


def gelu_parts(values):
    cdf = 0.5 + 0.5 * lax.erf(values * (0.5**0.5))
    return cdf, jnp.exp(-0.5 * values * values) * (1.0 / math.sqrt(2 * math.pi))


def forward_kernel(
    n_exp,
    experts,
    x_ref,
    d_ref,
    ids_ref,
    mask_ref,
    win_ref,
    wout_ref,
    norm_ref,
    wqkv_hbm,
    wproj_hbm,
    wrouter_ref,
    o_x,
    o_first,
    o_qkv,
    o_lse,
    o_att,
    o_mid,
    o_d,
    o_out,
    o_dsecond,
    o_grads,
    o_grouter,
    x_all,
    first_ref,
    qkv_ref,
    lse_ref,
    att_ref,
    mid_ref,
    out_send,
    dsecond_ref,
    grads_recv,
    grouter_ref,
    d_all,
    w_all,
    r_all,
    meta_ref,
    meta_all,
    wqkv_ref,
    wproj_ref,
    router_ref,
    ds_send,
    ds_recv,
    acc_out,
    acc_ds,
    dlogits_ref,
    gates_ref,
    dgates_ref,
    r_turn,
    d_turn,
    act_all,
    dpre_all,
    x_sems,
    m_sems,
    d_sems,
    r_sems,
    ds_sems,
    dr_sems,
    rr_sems,
    z_sems,
    s_sems,
    t_sems,
    own_sem,
    o_sems,
):
    expert, ctx, dp = places()
    own_images, n_ctx, seq_dev, width = x_all.shape
    seq = n_ctx * seq_dev
    rows = own_images * seq
    ctx_ids = [(expert, ctx_partner(ctx, step), dp) for step in range(1, n_ctx)]
    side_ids = ctx_ids[:2]
    twin = (expert, ctx, 1 - dp)
    right, left = lax.rem(expert + 1, n_exp), lax.rem(expert + n_exp - 1, n_exp)
    greeted = ctx_ids + [(right, ctx, dp), (left, ctx, dp), twin]
    greet(greeted)
    row = lax.broadcasted_iota(jnp.int32, (8, seq_dev), 0)
    odd = lax.rem(ctx, 2).astype(jnp.float32)
    for image in range(ids_ref.shape[0]):
        named = jnp.zeros((8, seq_dev), jnp.bool_)
        for choice in range(ids_ref.shape[1]):
            named = named | (ids_ref[image, choice : choice + 1] == row)
        values = jnp.where(
            row == experts, mask_ref[image : image + 1].astype(jnp.float32), named.astype(jnp.float32)
        )
        meta_ref[image, :, :seq_dev] = values * (1.0 - odd)
        meta_ref[image, :, seq_dev:] = values * odd
    router_ref[...] = jnp.zeros_like(router_ref)
    router_high, router_low = split(wrouter_ref[...])
    router_ref[0, :experts] = router_high.astype(jnp.float32)
    router_ref[1, :experts] = router_low.astype(jnp.float32)
    own = [
        pltpu.make_async_copy(source, target, own_sem.at[at])
        for at, (source, target) in enumerate(
            (
                (win_ref.at[0], w_all.at[0, expert]),
                (wout_ref.at[0], w_all.at[1, expert]),
                (x_ref.at[pl.ds(ctx * own_images, own_images)], x_all.at[:, ctx]),
                (wqkv_hbm, wqkv_ref),
                (wproj_hbm, wproj_ref),
                (d_ref, d_all.at[:, :, ctx]),
            )
        )
    ]
    for copy in own:
        copy.start()
    meta_all[ctx] = meta_ref[...]
    await_greetings(greeted)
    x_copies = []
    for image in range(own_images):
        x_copies.append(
            [
                send(
                    x_ref.at[partner[1] * own_images + image],
                    x_all.at[image, ctx],
                    x_sems.at[0, image, at],
                    x_sems.at[1, image, at],
                    partner,
                )
                for at, partner in enumerate(ctx_ids)
            ]
        )
        if image == 0:
            m_copies = [
                send(meta_ref, meta_all.at[ctx], m_sems.at[0, at], m_sems.at[1, at], partner)
                for at, partner in enumerate(ctx_ids)
            ]

    def hop(phase, side):
        share = expert - phase if side == 0 else expert + phase
        able = (share >= 0) & (expert < n_exp - 1) if side == 0 else (share < n_exp) & (expert > 0)
        share = jnp.clip(share, 0, n_exp - 1)
        return able, pltpu.make_async_remote_copy(
            src_ref=w_all.at[dp, share],
            dst_ref=w_all.at[dp, share],
            send_sem=z_sems.at[0, phase, side],
            recv_sem=z_sems.at[1, phase, side],
            device_id=(right if side == 0 else left, ctx, dp),
            device_id_type=MESH,
        )

    def landed(phase, side):
        share = expert - 1 - phase if side == 0 else expert + 1 + phase
        able = share >= 0 if side == 0 else share < n_exp
        share = jnp.clip(share, 0, n_exp - 1)
        place = w_all.at[dp, share]
        return (
            able,
            pltpu.make_async_remote_copy(
                src_ref=place,
                dst_ref=place,
                send_sem=z_sems.at[0, phase, side],
                recv_sem=z_sems.at[1, phase, side],
                device_id=(left if side == 0 else right, ctx, dp),
                device_id_type=MESH,
            ),
            pltpu.make_async_remote_copy(
                src_ref=place,
                dst_ref=place,
                send_sem=s_sems.at[0, phase, side],
                recv_sem=s_sems.at[1, phase, side],
                device_id=twin,
                device_id_type=MESH,
            ),
        )

    def start_hops(phase):
        for side in range(2):
            able, copy = hop(phase, side)
            pl.when(able)(copy.start)

    def take_hops(phase):
        for side in range(2):
            able, copy, shared = landed(phase, side)

            @pl.when(able)
            def _():
                copy.wait_recv()
                shared.start()

    def take_shared(phase):
        for side in range(2):
            able, _, shared = landed(phase, side)
            pl.when(able)(shared.wait_recv)

    own[0].wait()
    own[1].wait()
    start_hops(0)
    for copy in own[2:]:
        copy.wait()

    def d_copy(at, order):
        group = ctx_partner(ctx_ids[at][1], order)
        return pltpu.make_async_remote_copy(
            src_ref=d_ref.at[group],
            dst_ref=d_all.at[group, :, ctx],
            send_sem=d_sems.at[0, at, order],
            recv_sem=d_sems.at[1, at, order],
            device_id=ctx_ids[at],
            device_id_type=MESH,
        )

    def d_relay(image, order):
        target = side_ids[1 - image]
        place = d_all.at[ctx_partner(target[1], order), image, side_ids[image][1]]
        return pltpu.make_async_remote_copy(
            src_ref=place,
            dst_ref=place,
            send_sem=dr_sems.at[0, image, order],
            recv_sem=dr_sems.at[1, image, order],
            device_id=target,
            device_id_type=MESH,
        )

    def r_copy(at, image):
        return pltpu.make_async_remote_copy(
            src_ref=r_all.at[ctx, image],
            dst_ref=r_all.at[ctx, image],
            send_sem=r_sems.at[0, at, image],
            recv_sem=r_sems.at[1, at, image],
            device_id=side_ids[at],
            device_id_type=MESH,
        )

    def r_relay(image):
        place = r_all.at[side_ids[image][1], image]
        return pltpu.make_async_remote_copy(
            src_ref=place,
            dst_ref=place,
            send_sem=rr_sems.at[0, image],
            recv_sem=rr_sems.at[1, image],
            device_id=side_ids[1 - image],
            device_id_type=MESH,
        )

    for at in range(n_ctx - 1):
        d_copy(at, 0).start()
    for copy in x_copies[0] + m_copies:
        copy.wait()
    for order in (3, 1):
        for at in range(2):
            d_copy(at, order).start()
    lane = lax.broadcasted_iota(jnp.int32, (seq, LANES), 1)
    low_half = lane < HEAD_DIM
    for image in range(own_images):
        part = pl.ds(image * seq, seq)
        if image > 0:
            for copy in x_copies[image]:
                copy.wait()
        values = x_all[image].reshape(seq, width).astype(jnp.float32)
        unit, _ = normalize(values)
        first = (unit * norm_ref[0:1] + norm_ref[1:2]).astype(jnp.bfloat16)
        first_ref[part] = first
        qkv_ref[part] = dot(first, wqkv_ref[...]).astype(jnp.bfloat16)
        key_mask = group_rows(meta_all, ctx * own_images + image)[experts : experts + 1]
        bias = jnp.where(key_mask > 0, 0.0, NEG)
        column = jnp.broadcast_to(bias, (LANES, seq)).T
        totals = jnp.where(lane == HEADS, column, 0.0)
        for pair in range(HEADS // 2):
            query = qkv_ref[part, pair * LANES : (pair + 1) * LANES]
            keys = qkv_ref[part, width + pair * LANES : width + (pair + 1) * LANES]
            heads = qkv_ref[part, 2 * width + pair * LANES : 2 * width + (pair + 1) * LANES]
            query = query * jnp.bfloat16(HEAD_DIM**-0.5)
            parts = []
            for half in range(2):
                chosen = low_half if half == 0 else ~low_half
                scores = dot_nt(jnp.where(chosen, query, jnp.zeros_like(query)), keys) + bias
                peak = jnp.max(scores, axis=-1, keepdims=True)
                raised = jnp.exp(scores - peak)
                total = jnp.sum(raised, axis=-1, keepdims=True)
                probs = (raised * (1.0 / total)).astype(jnp.bfloat16)
                parts.append(dot(probs, heads))
                totals = jnp.where(lane == 2 * pair + half, peak + jnp.log(total), totals)
            att_ref[part, pair * LANES : (pair + 1) * LANES] = jnp.where(
                low_half, parts[0], parts[1]
            ).astype(jnp.bfloat16)
        lse_ref[part] = totals
        mid = values + dot(att_ref[part], wproj_ref[...])
        mid_ref[part] = mid
        unit, _ = normalize(mid)
        r_all[ctx, image] = (unit * norm_ref[2:3] + norm_ref[3:4]).astype(jnp.bfloat16)
        for at in range(2):
            r_copy(at, image).start()
        if image == 0:
            take_hops(0)
            start_hops(1)
        if image == own_images - 1:
            for at in range(2):
                d_copy(at, 2).start()

    kept_copies = [
        pltpu.make_async_copy(source, target, o_sems.at[at])
        for at, (source, target) in enumerate(
            (
                (x_all, o_x),
                (first_ref, o_first),
                (qkv_ref, o_qkv),
                (lse_ref, o_lse),
                (att_ref, o_att),
                (mid_ref, o_mid),
            )
        )
    ]
    for copy in kept_copies:
        copy.start()

    def out_copy(chunk):
        return pltpu.make_async_copy(
            out_send.at[chunk % 2], o_out.at[chunk], o_sems.at[8 + chunk]
        )

    wide = lax.broadcasted_iota(jnp.int32, (rows, LANES), 1)
    near = jnp.where(expert < n_exp // 2, expert + 1, expert - 1)
    last = jnp.where(expert < n_exp // 2, n_exp - 1, 0)
    middle = n_exp * (n_exp - 1) // 2 - expert - near - last

    def start_chunk(chunk, owner):
        routed = r_all[owner].reshape(rows, width)
        present = jnp.concatenate(
            [group_rows(meta_all, owner * own_images + image) for image in range(own_images)], axis=1
        )
        present = jnp.concatenate(
            [present, jnp.zeros((LANES - present.shape[0], rows), jnp.float32)], axis=0
        ).T
        present = (present > 0) & (wide < experts)
        logits = dot_nt(routed, router_ref[0].astype(jnp.bfloat16)) + dot_nt(
            routed, router_ref[1].astype(jnp.bfloat16)
        )
        peak = jnp.max(jnp.where(present, logits, NEG), axis=-1, keepdims=True)
        raised = jnp.where(present, jnp.exp(jnp.where(present, logits - peak, 0.0)), 0.0)
        gates_ref[chunk] = raised / jnp.sum(raised, axis=-1, keepdims=True)
        dgates_ref[chunk] = jnp.zeros((rows, LANES), jnp.float32)

    def end_chunk(chunk):
        slot = 0 if chunk == 0 else 1
        gates = gates_ref[chunk]
        dgates = dgates_ref[chunk]
        dlogits = gates * (dgates - jnp.sum(gates * dgates, axis=-1, keepdims=True))
        high, low = split(dlogits)
        dlogits_ref[0, chunk * rows : (chunk + 1) * rows] = high
        dlogits_ref[1, chunk * rows : (chunk + 1) * rows] = low
        total = (
            acc_ds[slot]
            + dot(high, router_ref[0].astype(jnp.bfloat16))
            + dot(high, router_ref[1].astype(jnp.bfloat16))
            + dot(low, router_ref[0].astype(jnp.bfloat16))
        )
        if chunk == 0:
            dsecond_ref[...] = total
        else:
            ds_send[chunk - 1] = total.astype(jnp.bfloat16)
            ds_copy(chunk).start()
        out = acc_out[slot]
        if chunk == 0:
            out += mid_ref[...]
        if chunk in (3, 0):
            out_copy(1 if chunk == 3 else 2).wait()
        out_send[chunk % 2] = out.astype(jnp.bfloat16).reshape(out_send.shape[1:])
        out_copy(chunk).start()
        if chunk in (1, 2):
            acc_out[slot] = jnp.zeros(acc_out.shape[1:], jnp.float32)
            acc_ds[slot] = jnp.zeros(acc_ds.shape[1:], jnp.float32)

    def ds_copy(chunk):
        return pltpu.make_async_remote_copy(
            src_ref=ds_send.at[chunk - 1],
            dst_ref=ds_recv.at[chunk - 1],
            send_sem=ds_sems.at[0, chunk - 1],
            recv_sem=ds_sems.at[1, chunk - 1],
            device_id=ctx_ids[chunk - 1],
            device_id_type=MESH,
        )

    acc_out[...] = jnp.zeros_like(acc_out)
    acc_ds[...] = jnp.zeros_like(acc_ds)

    def place_of(step):
        own_chunk = (step < 3) | (step == n_ctx * n_exp - 1)
        chunk = jnp.where(own_chunk, 0, 1 + (step - 3) // n_exp)
        rank = jnp.where(step < 3, step, jnp.where(own_chunk, n_exp - 1, lax.rem(step - 3, n_exp)))
        index = jnp.where(
            rank == 0, expert, jnp.where(rank == 1, near, jnp.where(rank == 2, middle, last))
        )
        return chunk, jnp.where(own_chunk, 0, 1), index

    def hidden_products(step, image):
        chunk, _, index = place_of(step)
        owner = ctx_partner(ctx, chunk)
        return (
            dot(r_all[owner, image], w_all[0, index]),
            dot(d_all[owner, image].reshape(seq, width), w_all[1, index]),
        )

    def hidden(step, image, pre, dact):
        chunk, _, index = place_of(step)
        part = pl.ds(image * seq, seq)
        gate = jnp.sum(jnp.where(lane == index, gates_ref[chunk, part], 0.0), axis=-1, keepdims=True)
        cdf, density = gelu_parts(pre)
        act = pre * cdf
        dgate = jnp.sum(dact * act, axis=-1, keepdims=True)
        dgates_ref[chunk, part] = jnp.where(lane == index, dgate, dgates_ref[chunk, part])
        kept = pl.ds(pl.multiple_of(chunk * rows + image * seq, seq), seq)
        act_all[index, kept] = (gate * act).astype(jnp.bfloat16)
        dpre_all[index, kept] = (gate * dact * (cdf + pre * density)).astype(jnp.bfloat16)

    def back_out(step, image):
        chunk, slot, index = place_of(step)
        part = pl.ds(image * seq, seq)
        kept = pl.ds(pl.multiple_of(chunk * rows + image * seq, seq), seq)
        acc_out[slot, part] += dot_nt(act_all[index, kept], w_all[1, index])
        acc_ds[slot, part] += dot_nt(dpre_all[index, kept], w_all[0, index])

    for at in range(n_ctx - 1):
        d_copy(at, 0).wait_recv()
    start_chunk(0, ctx)
    for image in range(own_images):
        hidden(0, image, *hidden_products(0, image))

    def one_step(step, carry):
        @pl.when(step == 1)
        def _():
            take_shared(0)
            for order in (3, 1):
                for at in range(2):
                    d_copy(at, order).wait_recv()
            for order in range(1, n_ctx):
                d_relay(0, order).start()
            for order in (1, 2):
                d_relay(1, order).start()

        @pl.when(step == 2)
        def _():
            take_hops(1)
            start_hops(2)
            take_shared(1)

        @pl.when(step == 3)
        def _():
            for image in range(2):
                r_copy(0, image).wait_recv()
                d_relay(image, 1).wait_recv()
            r_relay(0).start()
            start_chunk(1, ctx_ids[0][1])

        @pl.when(step == 4)
        def _():
            for image in range(2):
                r_copy(1, image).wait_recv()
            r_relay(1).start()
            for at in range(2):
                d_copy(at, 2).wait_recv()
            d_relay(1, 3).start()

        @pl.when(step == 6)
        def _():
            take_hops(2)
            take_shared(2)

        @pl.when(step == 7)
        def _():
            for image in range(2):
                d_relay(image, 2).wait_recv()
            start_chunk(2, ctx_ids[1][1])

        @pl.when(step == 11)
        def _():
            for image in range(2):
                d_relay(image, 3).wait_recv()
                r_relay(image).wait_recv()
            start_chunk(3, ctx_ids[2][1])

        for image in range(own_images):
            products = hidden_products(step, image)
            back_out(step - 1, image)
            hidden(step, image, *products)

        for chunk in range(1, n_ctx):
            pl.when(step == 3 + chunk * n_exp)(functools.partial(end_chunk, chunk))

        return carry

    lax.fori_loop(1, n_ctx * n_exp, one_step, 0)
    for image in range(own_images):
        back_out(n_ctx * n_exp - 1, image)
    end_chunk(0)
    for chunk in range(n_ctx):
        owner = ctx_partner(ctx, chunk)
        r_turn[:, chunk * rows : (chunk + 1) * rows] = r_all[owner].reshape(rows, width).T
        d_turn[:, chunk * rows : (chunk + 1) * rows] = d_all[owner].reshape(rows, width).T

    d_kept = pltpu.make_async_copy(d_all.at[ctx], o_d, o_sems.at[7])
    d_kept.start()

    def grad_at(which, index):
        return act_all.at[index, pl.ds(pl.multiple_of(which * width, width), width)]

    def t_copy(index):
        return pltpu.make_async_remote_copy(
            src_ref=grad_at(1 - dp, index),
            dst_ref=grads_recv.at[index],
            send_sem=t_sems.at[0, index],
            recv_sem=t_sems.at[1, index],
            device_id=twin,
            device_id_type=MESH,
        )

    def one_expert(index, carry):
        grad_out = dot(d_turn[...], act_all[index]).astype(jnp.bfloat16)
        grad_at(0, index)[...] = dot(r_turn[...], dpre_all[index]).astype(jnp.bfloat16)
        grad_at(1, index)[...] = grad_out
        t_copy(index).start()
        return carry

    lax.fori_loop(0, n_exp, one_expert, 0)
    grouter = dot(r_turn[...], dlogits_ref[0]) + dot(r_turn[...], dlogits_ref[1])
    grouter_ref[...] = grouter.T[: grouter_ref.shape[0]]
    for index in range(n_exp):
        t_copy(index).wait()
        grad_at(dp, index)[...] = (
            grad_at(dp, index)[...].astype(jnp.float32) + grads_recv[index].astype(jnp.float32)
        ).astype(jnp.bfloat16)
    last_copies = [pltpu.make_async_copy(grouter_ref, o_grouter, o_sems.at[13])] + [
        pltpu.make_async_copy(grad_at(dp, index), o_grads.at[index], o_sems.at[15 + index])
        for index in range(n_exp)
    ]
    for copy in last_copies:
        copy.start()
    for phase in range(n_exp - 1):
        for side in range(2):
            able, copy = hop(phase, side)
            pl.when(able)(copy.wait_send)
            able, _, shared = landed(phase, side)
            pl.when(able)(shared.wait_send)
    for at in range(n_ctx - 1):
        for order in range(n_ctx if at < 2 else 1):
            d_copy(at, order).wait_send()
    for image in range(2):
        r_relay(image).wait_send()
        for at in range(2):
            r_copy(at, image).wait_send()
        for order in range(1, n_ctx):
            d_relay(image, order).wait_send()
    for chunk in range(1, n_ctx):
        ds_copy(chunk).wait()
        dsecond_ref[...] += ds_recv[chunk - 1].astype(jnp.float32)
    last_copies.append(pltpu.make_async_copy(dsecond_ref, o_dsecond, o_sems.at[14]))
    last_copies[-1].start()
    for copy in kept_copies + [d_kept] + last_copies:
        copy.wait()
    out_copy(3).wait()
    out_copy(0).wait()


def gram_blocks(matrix, packed_ref):
    size = matrix.shape[0]
    index = 0
    for row in range(size // LANES):
        strip = dot_nt(matrix[row * LANES : (row + 1) * LANES], matrix[row * LANES :])
        for col in range(size // LANES - row):
            packed_ref[index] = strip[:, col * LANES : (col + 1) * LANES].reshape(
                packed_ref.shape[1:]
            )
            index += 1


def gram_whole(packed_ref, high_ref, low_ref):
    count = high_ref.shape[0] // LANES
    diagonal = lax.broadcasted_iota(jnp.int32, (LANES, LANES), 0) == lax.broadcasted_iota(
        jnp.int32, (LANES, LANES), 1
    )
    places_of = {}
    square = jnp.zeros((1, 1), jnp.float32)
    index = 0
    for row in range(count):
        for col in range(row, count):
            places_of[index] = (row, col)
            if row == col:
                block = packed_ref[index].reshape(LANES, LANES)
                square += jnp.sum(jnp.where(diagonal, block, 0.0), keepdims=True)
            index += 1
    scale = 1.0 / (jnp.sqrt(square) + EPS_ORTHO)
    for index, (row, col) in places_of.items():
        block = packed_ref[index].reshape(LANES, LANES) * (scale * scale)
        rows, cols = pl.ds(row * LANES, LANES), pl.ds(col * LANES, LANES)
        high_ref[rows, cols], low_ref[rows, cols] = split(block)
        if row != col:
            high_ref[cols, rows], low_ref[cols, rows] = split(block.T)
    return scale


def orthogonal(high_ref, low_ref, mix_ref, total_ref):
    size = high_ref.shape[0]
    eye = lax.broadcasted_iota(jnp.int32, (size, size), 0) == lax.broadcasted_iota(
        jnp.int32, (size, size), 1
    )
    for turn in range(NS_ITERS):
        high, low = high_ref[...], low_ref[...]
        square = dot(high, high)
        if turn == NS_ITERS - 1:
            square += dot(high, low) + dot(low, high)
        mix_ref[...] = (
            jnp.where(eye, NS_A, 0.0)
            + NS_B * (high.astype(jnp.float32) + low.astype(jnp.float32))
            + NS_C * square
        ).astype(jnp.bfloat16)
        mix = mix_ref[...]
        if turn == 0:
            total_ref[...] = mix.astype(jnp.float32)
        else:
            total_high, total_low = split(total_ref[...])
            total_ref[...] = dot(mix, total_high) + dot(mix, total_low)
        if turn < NS_ITERS - 1:
            turned_high, turned_low = split(dot(mix, high) + dot(mix, low))
            high_ref[...], low_ref[...] = split(dot(turned_high, mix) + dot(turned_low, mix))


def backward_kernel(
    n_exp,
    h_x,
    h_d,
    h_first,
    h_qkv,
    h_lse,
    h_att,
    h_mid,
    h_dsecond,
    h_grads,
    grouter_ref,
    norm_ref,
    h_wqkv,
    h_wproj,
    h_out,
    h_min,
    h_mout,
    h_mqkv,
    h_mproj,
    mnorm_ref,
    mrouter_ref,
    out_ref,
    dx_ref,
    gexp_ref,
    step_ref,
    whole_ref,
    sums_ref,
    squares_ref,
    x_ref,
    d_ref,
    first_ref,
    qkv_ref,
    lse_ref,
    att_ref,
    mid_ref,
    dsecond_ref,
    own_grads,
    passed_ref,
    wqkv_ref,
    wproj_ref,
    out_own,
    mexp_ref,
    mqkv_ref,
    mproj_ref,
    out_recv,
    z_recv,
    dmid_ref,
    dbranch_ref,
    datt_ref,
    dqkv_ref,
    dx_send,
    shared_ref,
    half_recv,
    sum_one,
    ctx_recv,
    piece_send,
    piece_recv,
    mat_ref,
    packed_ref,
    packed_recv,
    gathered_ref,
    high_ref,
    low_ref,
    mix_ref,
    total_ref,
    small_ref,
    small_twin,
    small_ctx,
    small_z,
    in_sems,
    out_sems,
    z_sems,
    f_sems,
    dx_sems,
    h_sems,
    c_sems,
    s_sems,
    p_sems,
    w_sems,
    g_sems,
    a_sems,
    x_sems,
    n_sems,
):
    expert, ctx, dp = places()
    own_images, n_ctx, seq_dev, width = dx_send.shape
    seq = n_ctx * seq_dev
    half = width // 2
    cols = width // n_ctx
    loads = {}

    def load(name, source, target):
        loads[name] = pltpu.make_async_copy(source, target, in_sems.at[len(loads)])
        return loads[name]

    def take(*names):
        for name in names:
            loads[name].wait()

    for name, source, target in (
        ("mid", h_mid, mid_ref),
        ("dsecond", h_dsecond, dsecond_ref),
        ("d", h_d, d_ref),
        ("wproj", h_wproj, wproj_ref),
        ("qkv", h_qkv, qkv_ref),
        ("lse", h_lse, lse_ref),
        ("att", h_att, att_ref),
        ("first", h_first, first_ref),
        ("wqkv", h_wqkv, wqkv_ref),
        ("x", h_x, x_ref),
        ("grads", h_grads.at[expert], own_grads),
        ("passed", h_grads.at[jnp.where(expert < n_exp // 2, n_exp - 1, 0)], passed_ref),
        ("out", h_out.at[:, :, ctx], out_own),
        ("mqkv", h_mqkv, mqkv_ref),
        ("mproj", h_mproj, mproj_ref),
    ):
        load(name, source, target).start()
    moment = [
        pltpu.make_async_copy(source.at[0], mexp_ref, in_sems.at[len(loads)])
        for source in (h_min, h_mout)
    ]
    pl.when(dp == 0)(moment[0].start)
    pl.when(dp == 1)(moment[1].start)
    ctx_ids = [(expert, ctx_partner(ctx, step), dp) for step in range(1, n_ctx)]
    z_steps = [1, n_exp - 1] + list(range(2, n_exp - 1))
    z_ids = [(z_partner(expert, step, n_exp), ctx, dp) for step in z_steps]
    twin = (expert, ctx, 1 - dp)
    greeted = ctx_ids + z_ids + [twin]
    greet(greeted)

    def to_each(partners, source, target, sems):
        return [
            send(source(at, partner), target(at, partner), sems.at[0, at], sems.at[1, at], partner)
            for at, partner in enumerate(partners)
        ]

    await_greetings(greeted)
    low_side = expert < n_exp // 2
    near_end = jnp.where(low_side, 0, n_exp - 1)
    far_end = n_exp - 1 - near_end
    near_mid = jnp.where(low_side, 1, n_exp - 2)
    far_mid = n_exp - 1 - near_mid
    at_end = expert == near_end

    def z_copy(target, source, slot, order):
        return pltpu.make_async_remote_copy(
            src_ref=source,
            dst_ref=z_recv.at[slot],
            send_sem=z_sems.at[0, order],
            recv_sem=z_sems.at[1, slot],
            device_id=(target, ctx, dp),
            device_id_type=MESH,
        )

    def end_copies():
        return [
            z_copy(near_mid, h_grads.at[far_end], 3, 0),
            z_copy(far_mid, h_grads.at[far_mid], 1, 1),
            z_copy(near_mid, h_grads.at[near_mid], 0, 2),
        ]

    def mid_copies():
        return [
            z_copy(far_mid, h_grads.at[far_mid], 2, 0),
            z_copy(near_end, h_grads.at[near_end], 0, 1),
            z_copy(far_end, passed_ref, 1, 2),
        ]

    @pl.when(at_end)
    def _():
        end_copies()[0].start()

    @pl.when(jnp.logical_not(at_end))
    def _():
        for copy in mid_copies()[:2]:
            copy.start()

    def send_out(step):
        first_image = ctx_partner(ctx, step) * own_images
        return to_each(
            ctx_ids,
            lambda at, partner: h_out.at[step, :, partner[1]],
            lambda at, partner: out_recv.at[ctx, pl.ds(first_image, own_images)],
            out_sems.at[step],
        )

    out_copies = []
    for step in range(1, n_ctx):
        out_copies += send_out(step)
    gain_one, gain_two = norm_ref[0:1], norm_ref[2:3]
    sums = [jnp.zeros((1, width), jnp.float32) for _ in range(4)]
    take("mid", "dsecond", "d", "wproj")
    for image in range(own_images):
        rows = pl.ds(image * seq, seq)
        unit, scale = normalize(mid_ref[rows])
        grad = dsecond_ref[rows]
        sums[2] += jnp.sum(grad * unit, axis=0, keepdims=True)
        sums[3] += jnp.sum(grad, axis=0, keepdims=True)
        dmid = normalize_back(grad * gain_two, unit, scale) + d_ref[rows].astype(jnp.float32)
        dmid_ref[rows] = dmid
        dbranch = dmid.astype(jnp.bfloat16)
        dbranch_ref[rows] = dbranch
        datt_ref[rows] = dot_nt(dbranch, wproj_ref[...]).astype(jnp.bfloat16)
    take("att")
    gproj = dot_tn(att_ref[...], dbranch_ref[...]).astype(jnp.bfloat16)
    for place in range(n_ctx):
        shared_ref[place, :, 3 * cols :] = gproj[:, place * cols : (place + 1) * cols]
    own_half = pl.ds(pl.multiple_of(dp * half, half), half)
    other_half = pl.ds(pl.multiple_of((1 - dp) * half, half), half)

    def to_twin(which, lanes):
        return send(
            shared_ref.at[:, other_half, lanes],
            half_recv.at[:, :, lanes],
            h_sems.at[0, which],
            h_sems.at[1, which],
            twin,
        )

    def to_owners(which, lanes):
        for place in range(n_ctx):
            sum_one[place, :, lanes] = (
                shared_ref[place, own_half, lanes].astype(jnp.float32)
                + half_recv[place, :, lanes].astype(jnp.float32)
            ).astype(jnp.bfloat16)
        return to_each(
            ctx_ids,
            lambda at, partner: sum_one.at[partner[1], :, lanes],
            lambda at, partner: ctx_recv.at[at, :, lanes],
            c_sems.at[which],
        )

    qkv_lanes, proj_lanes = pl.ds(0, 3 * cols), pl.ds(3 * cols, cols)
    h_copy = to_twin(0, proj_lanes)
    take("qkv", "lse")
    lane = lax.broadcasted_iota(jnp.int32, (seq, LANES), 1)
    low_half = lane < HEAD_DIM
    factor = HEAD_DIM**-0.5
    for image in range(own_images):
        rows = pl.ds(image * seq, seq)
        totals = lse_ref[rows].T
        bias = lse_ref[rows, HEADS : HEADS + 1]
        for pair in range(HEADS // 2):
            at = pair * LANES
            query = qkv_ref[rows, at : at + LANES] * jnp.bfloat16(factor)
            keys = qkv_ref[rows, width + at : width + at + LANES]
            heads = qkv_ref[rows, 2 * width + at : 2 * width + at + LANES]
            datt = datt_ref[rows, at : at + LANES]
            dquery, dkeys, dheads = [], [], []
            for part in range(2):
                chosen = low_half if part == 0 else ~low_half
                scores = dot_nt(keys, jnp.where(chosen, query, jnp.zeros_like(query))) + bias
                head = 2 * pair + part
                weights = jnp.exp(scores - totals[head : head + 1])
                dprobs = dot_nt(heads, jnp.where(chosen, datt, jnp.zeros_like(datt)))
                delta = jnp.sum(weights * dprobs, axis=0, keepdims=True)
                dscores = (weights * (dprobs - delta)).astype(jnp.bfloat16)
                dquery.append(dot_tn(dscores, keys))
                dkeys.append(dot(dscores, query))
                dheads.append(dot(weights.astype(jnp.bfloat16), datt))
            dqkv_ref[rows, at : at + LANES] = (
                jnp.where(low_half, dquery[0], dquery[1]) * factor
            ).astype(jnp.bfloat16)
            dqkv_ref[rows, width + at : width + at + LANES] = jnp.where(
                low_half, dkeys[0], dkeys[1]
            ).astype(jnp.bfloat16)
            dqkv_ref[rows, 2 * width + at : 2 * width + at + LANES] = jnp.where(
                low_half, dheads[0], dheads[1]
            ).astype(jnp.bfloat16)
        if image == 0:
            h_copy.wait()
            c_copies = to_owners(0, proj_lanes)
            take("passed")

            @pl.when(jnp.logical_not(at_end))
            def _():
                copies = mid_copies()
                copies[0].wait_send()
                z_copy(near_mid, passed_ref, 3, 0).wait_recv()
                passed_ref[...] = (
                    passed_ref[...].astype(jnp.float32) + z_recv[3].astype(jnp.float32)
                ).astype(jnp.bfloat16)
                copies[2].start()

            @pl.when(at_end)
            def _():
                copies = end_copies()
                copies[0].wait_send()
                copies[1].start()
                copies[2].start()

    take("first")
    gqkv = dot_tn(first_ref[...], dqkv_ref[...]).astype(jnp.bfloat16)
    for place in range(n_ctx):
        shared_ref[place, :, : 3 * cols] = gqkv[:, 3 * cols * place : 3 * cols * (place + 1)]
    h_copy = to_twin(1, qkv_lanes)
    take("wqkv", "x")
    for image in range(own_images):
        rows = pl.ds(image * seq, seq)
        grad = dot_nt(dqkv_ref[rows], wqkv_ref[...])
        unit, scale = normalize(x_ref[rows].astype(jnp.float32))
        sums[0] += jnp.sum(grad * unit, axis=0, keepdims=True)
        sums[1] += jnp.sum(grad, axis=0, keepdims=True)
        dx = dmid_ref[rows] + normalize_back(grad * gain_one, unit, scale)
        dx_send[image] = dx.astype(jnp.bfloat16).reshape(n_ctx, seq_dev, width)
        if image == 0:
            h_copy.wait()
            c_copies += to_owners(1, qkv_lanes)
    for at, total in enumerate(sums):
        small_ref[at : at + 1] = total
    small_ref[4:8] = jnp.zeros((4, width), jnp.float32)
    small_ref[8:16] = grouter_ref[...]
    s_copy = send(small_ref, small_twin, h_sems.at[0, 2], h_sems.at[1, 2], twin)
    s_copy.wait()
    small_ctx[ctx] = small_ref[...] + small_twin[...]
    s_copies = to_each(
        ctx_ids, lambda at, partner: small_ctx.at[ctx], lambda at, partner: small_ctx.at[ctx], s_sems
    )
    for copy in c_copies:
        copy.wait()
    total = sum_one[ctx].astype(jnp.float32)
    for at in range(n_ctx - 1):
        total += ctx_recv[at].astype(jnp.float32)
    piece_send[...] = total.astype(jnp.bfloat16).reshape(piece_send.shape)
    p_copies = to_each(
        z_ids,
        lambda at, partner: piece_send.at[partner[0]],
        lambda at, partner: piece_recv.at[at],
        p_sems,
    )
    out_copies += send_out(0)
    dx_copies = to_each(
        ctx_ids,
        lambda at, partner: dx_send.at[:, partner[1]],
        lambda at, partner: dx_ref.at[pl.ds(ctx * own_images, own_images)],
        dx_sems,
    )
    for image in range(own_images):
        dx_ref[ctx * own_images + image] = dx_send[image, ctx]
    for copy in s_copies:
        copy.wait()
    total = small_ctx[0]
    for place in range(1, n_ctx):
        total += small_ctx[place]
    small_z[expert] = total
    s_copies = to_each(
        z_ids,
        lambda at, partner: small_z.at[expert],
        lambda at, partner: small_z.at[expert],
        n_sems.at[0],
    )

    def gram_start(which, matrix):
        gram_blocks(matrix.astype(jnp.bfloat16), packed_ref.at[which])
        return to_each(
            ctx_ids,
            lambda at, partner: packed_ref.at[which, :, partner[1]],
            lambda at, partner: packed_recv.at[which, at],
            g_sems.at[which],
        )

    def gram_middle(which, copies):
        for copy in copies:
            copy.wait()
        total = packed_ref[which, :, ctx]
        for at in range(n_ctx - 1):
            total += packed_recv[which, at]
        gathered_ref[which, :, ctx] = total
        return to_each(
            ctx_ids,
            lambda at, partner: gathered_ref.at[which, :, ctx],
            lambda at, partner: gathered_ref.at[which, :, ctx],
            a_sems.at[which],
        )

    def step_of(which, matrix, scale):
        total_high, total_low = split(total_ref[...])
        high, low = split(matrix * scale)
        cut = pl.ds(0, matrix.shape[1])
        step_ref[which, dp, :, cut] = (
            dot(total_high, high) + dot(total_high, low) + dot(total_low, high)
        ).astype(jnp.bfloat16)
        return send(
            step_ref.at[which, dp, :, cut],
            step_ref.at[which, dp, :, cut],
            x_sems.at[0, which],
            x_sems.at[1, which],
            twin,
        )

    take("grads")

    @pl.when(at_end)
    def _():
        copies = end_copies()
        copies[1].wait_send()
        copies[2].wait_send()
        copies[1].wait_recv()
        copies[2].wait_recv()
        total = own_grads[...].astype(jnp.float32)
        for slot in range(2):
            total += z_recv[slot].astype(jnp.float32)
        gexp_ref[dp] = total.astype(jnp.bfloat16)

    @pl.when(jnp.logical_not(at_end))
    def _():
        copies = mid_copies()
        copies[1].wait_send()
        copies[2].wait_send()
        for copy in copies:
            copy.wait_recv()
        total = own_grads[...].astype(jnp.float32)
        for slot in range(3):
            total += z_recv[slot].astype(jnp.float32)
        gexp_ref[dp] = total.astype(jnp.bfloat16)

    f_copy = send(gexp_ref.at[dp], gexp_ref.at[dp], f_sems.at[0], f_sems.at[1], twin)
    moment[0].wait()
    mat_ref[0] = DECAY * mexp_ref[...] + gexp_ref[dp].astype(jnp.float32)
    exp_copies = gram_start(0, mat_ref[0])
    for copy in p_copies:
        copy.wait()
    total = piece_send[expert].astype(jnp.float32)
    for at in range(n_exp - 1):
        total += piece_recv[at].astype(jnp.float32)
    whole_ref[dp, expert] = total.astype(jnp.bfloat16)
    p_copies = to_each(
        z_ids,
        lambda at, partner: whole_ref.at[dp, expert],
        lambda at, partner: whole_ref.at[dp, expert],
        w_sems,
    )
    for copy in p_copies:
        copy.wait()
    w_copy = send(whole_ref.at[dp], whole_ref.at[dp], f_sems.at[2], f_sems.at[3], twin)
    exp_copies = gram_middle(0, exp_copies)
    for copy in s_copies:
        copy.wait()
    total = small_z[0]
    for place in range(1, n_exp):
        total += small_z[place]
    sums_ref[...] = total
    lane_part = pl.ds(pl.multiple_of(ctx * cols, cols), cols)
    fresh_norm = DECAY * mnorm_ref[...] + sums_ref[0:4, lane_part]
    fresh_router = DECAY * mrouter_ref[...] + sums_ref[pl.ds(8 + ctx, 1)]
    row = lax.broadcasted_iota(jnp.int32, (8, LANES), 0)
    squares_ref[ctx] = jnp.where(
        row == 0,
        jnp.sum(fresh_norm * fresh_norm, keepdims=True),
        jnp.sum(fresh_router * fresh_router, keepdims=True),
    )
    n_copies = to_each(
        ctx_ids,
        lambda at, partner: squares_ref.at[ctx],
        lambda at, partner: squares_ref.at[ctx],
        n_sems.at[1],
    )
    w_copy.wait()
    take("mqkv", "mproj")
    grad = whole_ref[...].reshape(width, width).astype(jnp.float32)
    mat_ref[1, :, : 3 * cols] = DECAY * mqkv_ref[...] + grad[:, : 3 * cols]
    mat_ref[2, :, :cols] = DECAY * mproj_ref[...] + grad[:, 3 * cols :]
    mat_ref[2, :, cols : 3 * cols] = jnp.zeros((width, 2 * cols), jnp.float32)
    shared_copies = [gram_start(1, mat_ref[1 + dp, :, : 3 * cols])]
    for copy in exp_copies:
        copy.wait()
    exp_scale = gram_whole(gathered_ref.at[0], high_ref, low_ref)
    orthogonal(high_ref, low_ref, mix_ref, total_ref)
    exp_step = step_of(0, mat_ref[0], exp_scale)
    shared_copies[0] = gram_middle(1, shared_copies[0])
    for copy in shared_copies[0]:
        copy.wait()
    shared_scale = gram_whole(gathered_ref.at[1], high_ref, low_ref)
    orthogonal(high_ref, low_ref, mix_ref, total_ref)
    shared_step = step_of(1, mat_ref[1 + dp, :, : 3 * cols], shared_scale)
    take("out")
    for copy in out_copies:
        copy.wait()
    for step in range(n_ctx):
        start = ctx_partner(ctx, step) * own_images
        for image in range(own_images):
            total = out_own[step, image].astype(jnp.float32)
            for at in range(n_ctx - 1):
                total += out_recv[ctx_partner(ctx, at + 1), start + image].astype(jnp.float32)
            out_ref[start + image] = total.astype(jnp.bfloat16)
    for copy in dx_copies + n_copies + [f_copy, exp_step, shared_step]:
        copy.wait()


def finish_kernel(
    experts,
    n_ctx,
    width,
    ctx_ref,
    gexp_ref,
    step_ref,
    whole_ref,
    sums_ref,
    squares_ref,
    dx_in,
    out_in,
    min_ref,
    mout_ref,
    mqkv_ref,
    mproj_ref,
    mnorm_ref,
    mrouter_ref,
    win_ref,
    wout_ref,
    wqkv_ref,
    wproj_ref,
    norm_ref,
    router_ref,
    o_out,
    o_dx,
    o_gnorm,
    o_grouter,
    o_gqkv,
    o_gproj,
    o_gin,
    o_gout,
    o_mnorm,
    o_mrouter,
    o_mqkv,
    o_mproj,
    o_min,
    o_mout,
    o_nnorm,
    o_nrouter,
    o_nqkv,
    o_nproj,
    o_nin,
    o_nout,
    o_bqkv,
    o_bproj,
    o_bin,
    o_bout,
):
    cols = width // n_ctx
    o_out[...] = out_in[...]
    o_dx[...] = dx_in[...].astype(jnp.float32)

    def update(grad, moment, weight, step, columns, outs):
        o_g, o_m, o_n, o_b = outs
        rate = RATE_MAT * 0.2 * math.sqrt(max(width, columns))
        new = weight.astype(jnp.float32) - rate * step.astype(jnp.float32)
        o_g[...] = grad.reshape(o_g.shape)
        o_m[...] = (DECAY * moment + grad).reshape(o_m.shape)
        o_n[...] = new.reshape(o_n.shape)
        o_b[...] = new.astype(jnp.bfloat16).reshape(o_b.shape)

    for index, outs in enumerate(((o_gin, o_min, o_nin, o_bin), (o_gout, o_mout, o_nout, o_bout))):
        update(
            gexp_ref[index].astype(jnp.float32),
            (min_ref, mout_ref)[index][0],
            (win_ref, wout_ref)[index][0],
            step_ref[0, index],
            n_ctx * gexp_ref.shape[2],
            outs,
        )
    grad = whole_ref[...].astype(jnp.float32)
    update(
        grad[:, : 3 * cols],
        mqkv_ref[...],
        wqkv_ref[...],
        step_ref[1, 0, :, : 3 * cols],
        3 * width,
        (o_gqkv, o_mqkv, o_nqkv, o_bqkv),
    )
    update(
        grad[:, 3 * cols :],
        mproj_ref[...],
        wproj_ref[...],
        step_ref[1, 1, :, :cols],
        width,
        (o_gproj, o_mproj, o_nproj, o_bproj),
    )
    ctx = ctx_ref[0]
    own_norm = sums_ref[0:4, pl.ds(pl.multiple_of(ctx * cols, cols), cols)]
    own_router = sums_ref[pl.ds(8 + ctx, 1)]
    fresh_norm = DECAY * mnorm_ref[...] + own_norm
    fresh_router = DECAY * mrouter_ref[...] + own_router
    o_gnorm[...] = own_norm
    o_grouter[...] = own_router
    o_mnorm[...] = fresh_norm
    o_mrouter[...] = fresh_router
    squares = squares_ref[0]
    for place in range(1, n_ctx):
        squares += squares_ref[place]
    o_nnorm[...] = norm_ref[...] - (
        RATE_GAIN * fresh_norm * lax.rsqrt(squares[0:1] / (4 * width) + EPS_NORM)
    )
    o_nrouter[...] = router_ref[pl.ds(ctx, 1)] - RATE_ROUTER * fresh_router * lax.rsqrt(
        squares[1:2, 0:1] / (width * experts) + EPS_NORM
    )


def call(kernel, ident, outs, scratch, operands, spaces, out_spaces=None):
    out_spaces = out_spaces or [pltpu.VMEM] * len(outs)
    return pl.pallas_call(
        kernel,
        out_shape=[jax.ShapeDtypeStruct(shape, dtype) for shape, dtype in outs],
        in_specs=[pl.BlockSpec(memory_space=space) for space in spaces],
        out_specs=[pl.BlockSpec(memory_space=space) for space in out_spaces],
        scratch_shapes=scratch,
        compiler_params=pltpu.CompilerParams(
            collective_id=ident, has_side_effects=True, vmem_limit_bytes=VMEM_LIMIT
        ),
    )(*operands)


def gathered(
    x_in,
    d_out,
    key_mask,
    expert_ids,
    norm_params,
    w_qkv,
    w_proj,
    w_router,
    w_in,
    w_out,
    mom_norm,
    mom_router,
    mom_qkv,
    mom_proj,
    mom_in,
    mom_out,
):
    n_exp = lax.axis_size("expert")
    n_ctx = lax.axis_size("ctx")
    ctx = lax.axis_index("ctx")
    images, seq_dev, width = x_in.shape
    experts = w_router.shape[1]
    own_images = images // n_ctx
    seq = n_ctx * seq_dev
    rows = own_images * seq
    hid = w_in.shape[2]
    low, full = jnp.bfloat16, jnp.float32
    dma = lambda *shape: pltpu.SemaphoreType.DMA(shape)
    vmem = lambda shape, dtype: pltpu.VMEM(shape, dtype)

    vm, anywhere = pltpu.VMEM, pl.ANY
    block = (own_images, n_ctx, seq_dev, width)
    kept = [
        (block, low),
        ((rows, width), low),
        ((rows, 3 * width), low),
        ((rows, LANES), full),
        ((rows, width), low),
        ((rows, width), full),
        (block, low),
        ((n_ctx,) + block, low),
        ((rows, width), full),
        ((n_exp, width, hid), low),
        ((8, width), full),
    ]
    router_turned = w_router.T
    (x_all, first, qkv, lse, att, mid, d_own, out_parts, dsecond, grads, grouter) = call(
        functools.partial(forward_kernel, n_exp, experts),
        1,
        kept,
        [vmem(*kept[at]) for at in range(6)]
        + [vmem((2,) + block, low), vmem((rows, width), full)]
        + [
            vmem((n_exp, width, hid), low),
            vmem((8, width), full),
            vmem((n_ctx,) + block, low),
            vmem((2, n_exp, width, hid), low),
            vmem((n_ctx, own_images, seq, width), low),
            vmem((images, 8, LANES), full),
            vmem((n_ctx, images, 8, LANES), full),
            vmem((width, 3 * width), low),
            vmem((width, width), low),
            vmem((2, LANES, width), full),
            vmem((n_ctx - 1, rows, width), low),
            vmem((n_ctx - 1, rows, width), low),
            vmem((2, rows, width), full),
            vmem((2, rows, width), full),
            vmem((2, n_ctx * rows, LANES), low),
            vmem((n_ctx, rows, LANES), full),
            vmem((n_ctx, rows, LANES), full),
            vmem((width, n_ctx * rows), low),
            vmem((width, n_ctx * rows), low),
            vmem((n_exp, n_ctx * rows, hid), low),
            vmem((n_exp, n_ctx * rows, hid), low),
            dma(2, own_images, n_ctx - 1),
            dma(2, n_ctx - 1),
            dma(2, n_ctx - 1, n_ctx),
            dma(2, 2, 2),
            dma(2, n_ctx - 1),
            dma(2, 2, n_ctx),
            dma(2, 2),
            dma(2, n_exp - 1, 2),
            dma(2, n_exp - 1, 2),
            dma(2, n_exp),
            dma(6),
            dma(15 + n_exp),
        ],
        (
            x_in,
            d_out.reshape(n_ctx, own_images, seq_dev, width),
            expert_ids.swapaxes(1, 2),
            key_mask,
            w_in,
            w_out,
            norm_params,
            w_qkv,
            w_proj,
            router_turned,
        ),
        [anywhere, anywhere, vm, vm, anywhere, anywhere, vm, anywhere, anywhere, vm],
        [anywhere] * 11,
    )
    cols = width // n_ctx
    blocks = (width // LANES) * (width // LANES + 1) // 2
    block_rows = LANES // n_ctx
    quarter = (n_exp, width // 2 // n_exp, width)
    moments = (mom_in, mom_out, mom_qkv, mom_proj, mom_norm, mom_router.reshape(1, width))
    out_low, dx_low, gexp, steps, whole, sums, squares = call(
        functools.partial(backward_kernel, n_exp),
        2,
        [
            ((images, seq_dev, width), low),
            ((images, seq_dev, width), low),
            ((2, width, hid), low),
            ((2, 2, width, hid), low),
            ((2,) + quarter, low),
            ((16, width), full),
            ((n_ctx, 8, LANES), full),
        ],
        [
            vmem((rows, width), low),
            vmem((rows, width), low),
            vmem((rows, width), low),
            vmem((rows, 3 * width), low),
            vmem((rows, LANES), full),
            vmem((rows, width), low),
            vmem((rows, width), full),
            vmem((rows, width), full),
            vmem((width, hid), low),
            vmem((width, hid), low),
            vmem((width, 3 * width), low),
            vmem((width, width), low),
            vmem((n_ctx, own_images, seq_dev, width), low),
            vmem((width, hid), full),
            vmem((width, 3 * cols), full),
            vmem((width, cols), full),
            vmem((n_ctx, images, seq_dev, width), low),
            vmem((n_exp, width, hid), low),
            vmem((rows, width), full),
            vmem((rows, width), low),
            vmem((rows, width), low),
            vmem((rows, 3 * width), low),
            vmem(block, low),
            vmem((n_ctx, width, width), low),
            vmem((n_ctx, width // 2, width), low),
            vmem((n_ctx, width // 2, width), low),
            vmem((n_ctx - 1, width // 2, width), low),
            vmem(quarter, low),
            vmem((n_exp - 1,) + quarter[1:], low),
            vmem((3, width, hid), full),
            vmem((2, blocks, n_ctx, block_rows, LANES), full),
            vmem((2, n_ctx - 1, blocks, block_rows, LANES), full),
            vmem((2, blocks, n_ctx, block_rows, LANES), full),
            vmem((width, width), low),
            vmem((width, width), low),
            vmem((width, width), low),
            vmem((width, width), full),
            vmem((16, width), full),
            vmem((16, width), full),
            vmem((n_ctx, 16, width), full),
            vmem((n_exp, 16, width), full),
            dma(17),
            dma(n_ctx, 2, n_ctx - 1),
            dma(2, n_exp),
            dma(4),
            dma(2, n_ctx - 1),
            dma(2, 3),
            dma(2, 2, n_ctx - 1),
            dma(2, n_ctx - 1),
            dma(2, n_exp - 1),
            dma(2, n_exp - 1),
            dma(2, 2, n_ctx - 1),
            dma(2, 2, n_ctx - 1),
            dma(2, 2),
            dma(2, 2, max(n_ctx, n_exp) - 1),
        ],
        (
            x_all.reshape(rows, width),
            d_own.reshape(rows, width),
            first,
            qkv,
            lse,
            att,
            mid,
            dsecond,
            grads,
            grouter,
            norm_params,
            w_qkv,
            w_proj,
            out_parts,
        )
        + moments,
        [anywhere] * 9 + [vm, vm] + [anywhere] * 7 + [vm, vm],
    )
    pieces = ((4, cols), (1, width), (width, 3 * cols), (width, cols), (1, width, hid), (1, width, hid))
    parts = width // LANES
    outs = (
        [((images, seq_dev, width), low), ((images, seq_dev, width), full)]
        + [(piece, full) for piece in pieces * 3]
        + [(piece, low) for piece in pieces[2:]]
    )

    def strip(shape, axis, last=None):
        def index_map(at, ctx_ref):
            place = [0] * len(shape)
            if axis is not None:
                place[axis] = at
            if last is not None:
                place[-1] = ctx_ref[0]
            return tuple(place)

        size = list(shape)
        if axis is not None:
            size[axis] //= parts
        if last is not None:
            size[-1] = last
        return pl.BlockSpec(tuple(size), index_map)

    def strips(shape):
        if len(shape) == 3:
            return strip(shape, 0 if shape[0] == images else 1)
        return strip(shape, 0 if shape[0] == width else None)

    results = pl.pallas_call(
        functools.partial(finish_kernel, experts, n_ctx, width),
        out_shape=[jax.ShapeDtypeStruct(shape, dtype) for shape, dtype in outs],
        grid_spec=pltpu.PrefetchScalarGridSpec(
            num_scalar_prefetch=1,
            grid=(parts,),
            in_specs=[
                strip((2, width, hid), 1),
                strip((2, 2, width, hid), 2),
                strip((width, width), 0),
                strip((16, width), None),
                strip((n_ctx, 8, LANES), None),
                strip((images, seq_dev, width), 0),
                strip((images, seq_dev, width), 0),
                strip((1, width, hid), 1),
                strip((1, width, hid), 1),
                strip((width, 3 * cols), 0),
                strip((width, cols), 0),
                strip((4, cols), None),
                strip((1, width), None),
                strip((1, width, hid), 1),
                strip((1, width, hid), 1),
                strip((width, 3 * width), 0, 3 * cols),
                strip((width, width), 0, cols),
                strip((4, width), None, cols),
                strip((experts, width), None),
            ],
            out_specs=[strips(shape) for shape, _ in outs],
        ),
        compiler_params=pltpu.CompilerParams(vmem_limit_bytes=VMEM_LIMIT),
    )(
        ctx.reshape(1),
        gexp,
        steps,
        whole.reshape(width, width),
        sums,
        squares,
        dx_low,
        out_low,
        *moments,
        w_in,
        w_out,
        w_qkv,
        w_proj,
        norm_params,
        router_turned,
    )
    return tuple(
        value.reshape(width, 1) if value.shape == (1, width) else value for value in results
    )


def solution(mesh):
    in_specs = (
        P(("expert", "dp"), "ctx", None),
        P(("expert", "dp"), "ctx", None),
        P(("expert", "dp"), "ctx"),
        P(("expert", "dp"), "ctx", None),
        P(),
        P(),
        P(),
        P(),
        P("expert", None, "ctx"),
        P("expert", None, "ctx"),
        P(None, "ctx"),
        P(None, "ctx"),
        P(None, "ctx"),
        P(None, "ctx"),
        P("expert", None, "ctx"),
        P("expert", None, "ctx"),
    )
    out_specs = (
        P(("expert", "dp"), "ctx", None),
        P(("expert", "dp"), "ctx", None),
        P(None, "ctx"),
        P(None, "ctx"),
        P(None, "ctx"),
        P(None, "ctx"),
        P("expert", None, "ctx"),
        P("expert", None, "ctx"),
        P(None, "ctx"),
        P(None, "ctx"),
        P(None, "ctx"),
        P(None, "ctx"),
        P("expert", None, "ctx"),
        P("expert", None, "ctx"),
        P(None, "ctx"),
        P(None, "ctx"),
        P(None, "ctx"),
        P(None, "ctx"),
        P("expert", None, "ctx"),
        P("expert", None, "ctx"),
        P(None, "ctx"),
        P(None, "ctx"),
        P("expert", None, "ctx"),
        P("expert", None, "ctx"),
    )
    experts = mesh.shape["expert"]
    square = mesh.shape["ctx"] == 4 and mesh.shape["dp"] == 2

    def local(*arrays):
        whole = (
            square
            and arrays[7].shape[1] == experts <= 7
            and arrays[8].shape[0] == 1
            and 2 * arrays[0].shape[1] == LANES
        )
        return (gathered if whole else exchanged)(*arrays)

    return jax.shard_map(local, mesh=mesh, in_specs=in_specs, out_specs=out_specs, check_vma=False)
```

```python
import functools
import math

import jax
import jax.numpy as jnp
from jax import lax
from jax.experimental import pallas as pl
from jax.experimental.pallas import tpu as pltpu
from jax.sharding import PartitionSpec as P

HEADS = 8
HEAD_DIM = 64
MICRO = 2
NS_ITERS = 4


HIGH = lax.Precision.HIGHEST
NS_A = 3.4445
NS_B = -4.775
NS_C = 2.0315
DECAY = 0.5
RATE_MAT = 0.3
RATE_GAIN = 0.3
RATE_ROUTER = 0.05
EPS_NORM = 1e-06
EPS_ORTHO = 1e-07
NEG = -1e30
LANES = 128
VMEM_LIMIT = 60 * 2**20
MESH = pl.DeviceIdType.MESH


def as_sent(array):
    return jax.tree.map(lambda a: a.astype(jnp.bfloat16) if a.dtype == jnp.float32 else a, array)


def layer_norm(values, gain, shift):
    center = jnp.mean(values, axis=-1, keepdims=True)
    spread = values - center
    power = jnp.mean(spread * spread, axis=-1, keepdims=True)
    return spread * lax.rsqrt(power + EPS_NORM) * gain + shift


def gelu_exact(values):
    return jax.nn.gelu(values, approximate=False)


def add_block(total, piece):
    return total + piece


def masked_scores(query, key_piece, mask_piece, factor):
    scores = (
        jnp.einsum("bqhd,bkhd->bhqk", query, key_piece, preferred_element_type=jnp.float32) * factor
    )
    return jnp.where(mask_piece[:, None, None, :] > 0, scores, NEG)


def gram_list(matrices):
    return tuple(
        (jnp.einsum("...ik,...jk->...ij", matrix, matrix, precision=HIGH) for matrix in matrices)
    )


def schulz_turn(matrices, grams):
    result = []
    for matrix, gram in zip(matrices, grams):
        square = jnp.einsum("...ij,...jk->...ik", gram, gram, precision=HIGH)
        mixer = NS_B * gram + NS_C * square
        result.append(
            NS_A * matrix + jnp.einsum("...ij,...jk->...ik", mixer, matrix, precision=HIGH)
        )
    return tuple(result)


def exchanged(
    x_in,
    d_out,
    key_mask,
    expert_ids,
    norm_params,
    w_qkv,
    w_proj,
    w_router,
    w_in,
    w_out,
    mom_norm,
    mom_router,
    mom_qkv,
    mom_proj,
    mom_in,
    mom_out,
):
    ctx_count = lax.axis_size("ctx")
    ctx_place = lax.axis_index("ctx")
    owner_count = lax.axis_size("expert")
    local_images = x_in.shape[0]
    seq_dev = x_in.shape[1]
    width = x_in.shape[2]
    top_count = expert_ids.shape[-1]
    experts = w_router.shape[1]
    exp_dev = w_in.shape[0]
    hid_part = w_in.shape[2]
    capacity = max(2, (5 * top_count * seq_dev + 4 * experts - 1) // (4 * experts))
    batch = local_images // MICRO
    slot_count = batch * capacity
    seq_all = seq_dev * ctx_count
    factor = HEAD_DIM ** (-0.5)
    expert_iota = jnp.arange(experts, dtype=jnp.int32)
    recv_shape = (owner_count, exp_dev, slot_count, width)
    head_shape = (batch, seq_dev, HEADS, HEAD_DIM)

    def hidden_fold(step_fn, init):
        folded = step_fn(
            init,
            (
                lax.all_gather(w_in, "ctx", axis=2, tiled=True),
                lax.all_gather(w_out, "ctx", axis=2, tiled=True),
            ),
            jnp.int32(0),
        )
        return folded

    def to_owner(rows):
        return lax.all_to_all(rows, "expert", split_axis=0, concat_axis=0, tiled=True)

    def to_source(rows):
        return lax.all_to_all(rows, "expert", split_axis=0, concat_axis=0, tiled=True)

    def key_fold(keys, values, mask_low, step_fn, init):
        return step_fn(
            init,
            (
                lax.all_gather(keys, "ctx", axis=1, tiled=True),
                lax.all_gather(values, "ctx", axis=1, tiled=True),
                lax.all_gather(mask_low, "ctx", axis=1, tiled=True),
            ),
            jnp.int32(0),
        )

    grad_qkv = jnp.zeros(w_qkv.shape, jnp.float32)
    grad_proj = jnp.zeros(w_proj.shape, jnp.float32)
    grad_router = jnp.zeros(w_router.shape, jnp.float32)
    grad_norm = jnp.zeros((4, width), jnp.float32)
    grad_in = jnp.zeros((exp_dev, width, hid_part * ctx_count), jnp.float32)
    grad_out = jnp.zeros((exp_dev, width, hid_part * ctx_count), jnp.float32)
    outputs = []
    input_grads = []
    for micro_index in range(MICRO):
        first_image = micro_index * batch
        last_image = first_image + batch
        x_part = x_in[first_image:last_image].astype(jnp.float32)
        cotangent = d_out[first_image:last_image].astype(jnp.float32)
        mask_low = key_mask[first_image:last_image].astype(jnp.bfloat16)
        idents = expert_ids[first_image:last_image]
        normed_first, pull_first = jax.vjp(layer_norm, x_part, norm_params[0], norm_params[1])
        first_low = normed_first.astype(jnp.bfloat16).reshape(-1, width)
        qkv = jnp.dot(first_low, w_qkv, preferred_element_type=jnp.float32).astype(jnp.bfloat16)
        qkv = qkv.reshape(batch, seq_dev, 3, HEADS, HEAD_DIM)
        query = qkv[:, :, 0]
        keys = qkv[:, :, 1]
        values = qkv[:, :, 2]
        peak_old = jnp.full((batch, HEADS, seq_dev), NEG, jnp.float32)
        key_piece = lax.all_gather(keys, "ctx", axis=1, tiled=True)
        mask_piece = lax.all_gather(mask_low, "ctx", axis=1, tiled=True)
        scores = masked_scores(query, key_piece, mask_piece, factor)
        peak_new = jnp.maximum(peak_old, jnp.max(scores, axis=-1))
        total_new = jnp.sum(jnp.exp(scores - peak_new[..., None]), axis=-1)
        log_total = peak_new + jnp.log(total_new)

        def attend_step(acc, pieces, start):
            key_piece, value_piece, mask_piece = pieces
            weights = jnp.exp(
                masked_scores(query, key_piece, mask_piece, factor) - log_total[..., None]
            )
            return jnp.einsum(
                "bhqk,bkhd->bqhd",
                weights.astype(jnp.bfloat16),
                value_piece,
                preferred_element_type=jnp.float32,
            )

        attended = key_fold(keys, values, mask_low, attend_step, jnp.zeros(head_shape, jnp.float32))
        attended_low = attended.astype(jnp.bfloat16).reshape(-1, width)
        branch = jnp.dot(attended_low, w_proj, preferred_element_type=jnp.float32).reshape(
            batch, seq_dev, width
        )
        mid = x_part + branch
        normed_second, pull_second = jax.vjp(layer_norm, mid, norm_params[2], norm_params[3])
        routed_low = normed_second.astype(jnp.bfloat16)
        logits = jnp.einsum("bsd,de->bse", normed_second, w_router, precision=HIGH)
        onehot = (idents[..., None] == expert_iota).astype(jnp.float32)
        chosen = jnp.sum(onehot * logits[:, :, None, :], axis=-1)
        gates = jax.nn.softmax(chosen, axis=-1)
        flat_ids = idents.reshape(batch, seq_dev * top_count)
        hits = (flat_ids[..., None] == expert_iota).astype(jnp.int32)
        ranked = jnp.sum((jnp.cumsum(hits, axis=1) - hits) * hits, axis=-1)
        slot = (ranked + (jnp.arange(batch, dtype=jnp.int32) * capacity)[:, None]).reshape(-1)
        target = flat_ids.reshape(-1)
        routed_rows = jnp.broadcast_to(
            routed_low[:, :, None, :], (batch, seq_dev, top_count, width)
        ).reshape(-1, width)
        send = (
            jnp.zeros((experts, slot_count, width), jnp.bfloat16).at[target, slot].set(routed_rows)
        )
        received = to_owner(send.reshape(recv_shape))

        def expert_step(acc, pieces, start):
            piece_in, piece_out = pieces
            pre = jnp.einsum(
                "nesd,edh->nesh", received, piece_in, preferred_element_type=jnp.float32
            )
            act = gelu_exact(pre).astype(jnp.bfloat16)
            return jnp.einsum("nesh,edh->nesd", act, piece_out, preferred_element_type=jnp.float32)

        made = hidden_fold(expert_step, jnp.zeros(recv_shape, jnp.float32))
        back_rows = to_source(made.astype(jnp.bfloat16)).reshape(experts, slot_count, width)
        returned = (
            back_rows[target, slot].reshape(batch, seq_dev, top_count, width).astype(jnp.float32)
        )
        result = mid + jnp.sum(gates[..., None] * returned, axis=2)
        outputs.append(result.astype(jnp.bfloat16))
        dgates = jnp.sum(cotangent[:, :, None, :] * returned, axis=-1)
        dchosen = gates * (dgates - jnp.sum(gates * dgates, axis=-1, keepdims=True))
        dlogits = jnp.sum(dchosen[..., None] * onehot, axis=2)
        grad_router = grad_router + jnp.einsum(
            "bsd,bse->de", normed_second, dlogits, precision=HIGH
        )
        dsecond = jnp.einsum("bse,de->bsd", dlogits, w_router, precision=HIGH)
        dreturned = (
            (gates[..., None] * cotangent[:, :, None, :]).astype(jnp.bfloat16).reshape(-1, width)
        )
        dsend = (
            jnp.zeros((experts, slot_count, width), jnp.bfloat16).at[target, slot].set(dreturned)
        )
        dreceived = to_owner(dsend.reshape(recv_shape))

        def expert_back(carry, pieces, start):
            drows, dins, douts = carry
            piece_in, piece_out = pieces
            pre = jnp.einsum(
                "nesd,edh->nesh", received, piece_in, preferred_element_type=jnp.float32
            )
            act_full, pull_act = jax.vjp(gelu_exact, pre)
            act = act_full.astype(jnp.bfloat16)
            dact = jnp.einsum(
                "nesd,edh->nesh", dreceived, piece_out, preferred_element_type=jnp.float32
            )
            dpre = pull_act(dact)[0].astype(jnp.bfloat16)
            douts = add_block(
                douts,
                jnp.einsum("nesd,nesh->edh", dreceived, act, preferred_element_type=jnp.float32),
            )
            dins = add_block(
                dins,
                jnp.einsum("nesd,nesh->edh", received, dpre, preferred_element_type=jnp.float32),
            )
            drows = jnp.einsum("nesh,edh->nesd", dpre, piece_in, preferred_element_type=jnp.float32)
            return (drows, dins, douts)

        drows, grad_in, grad_out = hidden_fold(
            expert_back, (jnp.zeros(recv_shape, jnp.float32), grad_in, grad_out)
        )
        dback = to_source(drows.astype(jnp.bfloat16)).reshape(experts, slot_count, width)
        dsecond = dsecond + jnp.sum(
            dback[target, slot].reshape(batch, seq_dev, top_count, width).astype(jnp.float32),
            axis=2,
        )
        dmid, dgain_two, dshift_two = pull_second(dsecond)
        dmid = dmid + cotangent
        dbranch = dmid.astype(jnp.bfloat16).reshape(-1, width)
        grad_proj = grad_proj + jnp.einsum(
            "sd,se->de", attended_low, dbranch, preferred_element_type=jnp.float32
        )
        dattended = jnp.einsum("se,de->sd", dbranch, w_proj, preferred_element_type=jnp.float32)
        dattended = dattended.astype(jnp.bfloat16).reshape(head_shape)
        delta = jnp.einsum("bqhd,bqhd->bhq", dattended.astype(jnp.float32), attended)

        def attend_back(carry, pieces, start):
            dquery, dkeys, dvalues = carry
            key_piece, value_piece, mask_piece = pieces
            weights = jnp.exp(
                masked_scores(query, key_piece, mask_piece, factor) - log_total[..., None]
            )
            probs = weights.astype(jnp.bfloat16)
            dvalue_piece = jnp.einsum(
                "bhqk,bqhd->bkhd", probs, dattended, preferred_element_type=jnp.float32
            )
            dprobs = jnp.einsum(
                "bqhd,bkhd->bhqk", dattended, value_piece, preferred_element_type=jnp.float32
            )
            dscores = (weights * (dprobs - delta[..., None])).astype(jnp.bfloat16)
            dquery = factor * jnp.einsum(
                "bhqk,bkhd->bqhd", dscores, key_piece, preferred_element_type=jnp.float32
            )
            dkey_piece = factor * jnp.einsum(
                "bhqk,bqhd->bkhd", dscores, query, preferred_element_type=jnp.float32
            )
            return (dquery, add_block(dkeys, dkey_piece), add_block(dvalues, dvalue_piece))

        all_shape = (batch, seq_all, HEADS, HEAD_DIM)
        back_init = (
            jnp.zeros(head_shape, jnp.float32),
            jnp.zeros(all_shape, jnp.float32),
            jnp.zeros(all_shape, jnp.float32),
        )
        dquery, dkeys_all, dvalues_all = key_fold(keys, values, mask_low, attend_back, back_init)
        dkeys, dvalues = (
            lax.psum_scatter(
                dkeys_all.astype(jnp.bfloat16), "ctx", scatter_dimension=1, tiled=True
            ).astype(jnp.float32),
            lax.psum_scatter(
                dvalues_all.astype(jnp.bfloat16), "ctx", scatter_dimension=1, tiled=True
            ).astype(jnp.float32),
        )
        dqkv = (
            jnp.stack([dquery, dkeys, dvalues], axis=2).astype(jnp.bfloat16).reshape(-1, 3 * width)
        )
        grad_qkv = grad_qkv + jnp.einsum(
            "sd,se->de", first_low, dqkv, preferred_element_type=jnp.float32
        )
        dfirst = jnp.einsum("se,de->sd", dqkv, w_qkv, preferred_element_type=jnp.float32).reshape(
            batch, seq_dev, width
        )
        dx_part, dgain_one, dshift_one = pull_first(dfirst)
        grad_norm = grad_norm + jnp.stack([dgain_one, dshift_one, dgain_two, dshift_two])
        input_grads.append(dx_part + dmid)
    block_out = jnp.concatenate(outputs, axis=0)
    d_x = jnp.concatenate(input_grads, axis=0)
    shared = (
        lax.psum_scatter(
            grad_in.astype(jnp.bfloat16), "ctx", scatter_dimension=2, tiled=True
        ).astype(jnp.float32),
        lax.psum_scatter(
            grad_out.astype(jnp.bfloat16), "ctx", scatter_dimension=2, tiled=True
        ).astype(jnp.float32),
        lax.psum_scatter(
            grad_qkv[None].astype(jnp.bfloat16), "ctx", scatter_dimension=2, tiled=True
        ).astype(jnp.float32),
        lax.psum_scatter(
            grad_proj[None].astype(jnp.bfloat16), "ctx", scatter_dimension=2, tiled=True
        ).astype(jnp.float32),
        lax.psum_scatter(
            grad_norm[None].astype(jnp.bfloat16), "ctx", scatter_dimension=2, tiled=True
        ).astype(jnp.float32),
        lax.psum_scatter(
            grad_router[None].astype(jnp.bfloat16), "ctx", scatter_dimension=2, tiled=True
        ).astype(jnp.float32),
    )
    g_in, g_out = (
        lax.psum(shared[0].astype(jnp.bfloat16), "dp").astype(jnp.float32),
        lax.psum(shared[1].astype(jnp.bfloat16), "dp").astype(jnp.float32),
    )
    g_qkv, g_proj, g_norm, g_router = lax.psum(
        (shared[2][0], shared[3][0], shared[4][0], shared[5][0]), ("expert", "dp")
    )
    own_qkv = lax.dynamic_slice_in_dim(w_qkv, ctx_place * g_qkv.shape[1], g_qkv.shape[1], 1).astype(
        jnp.float32
    )
    own_proj = lax.dynamic_slice_in_dim(
        w_proj, ctx_place * g_proj.shape[1], g_proj.shape[1], 1
    ).astype(jnp.float32)
    own_norm = lax.dynamic_slice_in_dim(
        norm_params, ctx_place * g_norm.shape[1], g_norm.shape[1], 1
    )
    own_router = lax.dynamic_slice_in_dim(
        w_router, ctx_place * g_router.shape[1], g_router.shape[1], 1
    )
    m_qkv = DECAY * mom_qkv + g_qkv
    m_proj = DECAY * mom_proj + g_proj
    m_in = DECAY * mom_in + g_in
    m_out = DECAY * mom_out + g_out
    m_norm = DECAY * mom_norm + g_norm
    m_router = DECAY * mom_router + g_router
    matrices = (m_qkv, m_proj, m_in, m_out)
    vector_squares = (jnp.sum(m_norm * m_norm), jnp.sum(m_router * m_router))
    sums = lax.psum(
        tuple((jnp.sum(matrix * matrix, axis=(-2, -1)) for matrix in matrices)) + vector_squares,
        "ctx",
    )
    vector_totals = sums[4:]
    iterates = tuple(
        (
            matrix / jnp.expand_dims(jnp.sqrt(square) + EPS_ORTHO, (-2, -1))
            for matrix, square in zip(matrices, sums[:4])
        )
    )
    for turn_index in range(NS_ITERS):
        iterates = schulz_turn(
            iterates,
            jax.tree.map(
                lambda part: part.astype(jnp.float32), lax.psum(as_sent(gram_list(iterates)), "ctx")
            ),
        )
    n_qkv = (
        own_qkv - RATE_MAT * 0.2 * math.sqrt(max(width, g_qkv.shape[1] * ctx_count)) * iterates[0]
    )
    n_proj = (
        own_proj - RATE_MAT * 0.2 * math.sqrt(max(width, g_proj.shape[1] * ctx_count)) * iterates[1]
    )
    n_in = (
        w_in.astype(jnp.float32)
        - RATE_MAT * 0.2 * math.sqrt(max(width, hid_part * ctx_count)) * iterates[2]
    )
    n_out = (
        w_out.astype(jnp.float32)
        - RATE_MAT * 0.2 * math.sqrt(max(width, hid_part * ctx_count)) * iterates[3]
    )
    n_norm = own_norm - RATE_GAIN * m_norm * lax.rsqrt(vector_totals[0] / (4 * width) + EPS_NORM)
    n_router = own_router - RATE_ROUTER * m_router * lax.rsqrt(
        vector_totals[1] / (width * experts) + EPS_NORM
    )
    return (
        block_out,
        d_x,
        g_norm,
        g_router,
        g_qkv,
        g_proj,
        g_in,
        g_out,
        m_norm,
        m_router,
        m_qkv,
        m_proj,
        m_in,
        m_out,
        n_norm,
        n_router,
        n_qkv,
        n_proj,
        n_in,
        n_out,
        n_qkv.astype(jnp.bfloat16),
        n_proj.astype(jnp.bfloat16),
        n_in.astype(jnp.bfloat16),
        n_out.astype(jnp.bfloat16),
    )


def dot(left, right, precision=None):
    return jnp.dot(left, right, precision=precision, preferred_element_type=jnp.float32)


def dot_nt(left, right, precision=None):
    return lax.dot_general(
        left, right, (((1,), (1,)), ((), ())), precision=precision, preferred_element_type=jnp.float32
    )


def dot_tn(left, right, precision=None):
    return lax.dot_general(
        left, right, (((0,), (0,)), ((), ())), precision=precision, preferred_element_type=jnp.float32
    )


def places():
    return lax.axis_index("expert"), lax.axis_index("ctx"), lax.axis_index("dp")


def ctx_partner(ctx, step):
    column, row = lax.rem(ctx, 2), ctx // 2
    column = lax.rem(column + lax.rem(step, 2), 2)
    row = lax.rem(row + step // 2, 2)
    return row * 2 + column


def z_partner(expert, step, count):
    return lax.rem(expert + step, count)


def greet(partners):
    for partner in partners:
        pl.semaphore_signal(
            pltpu.get_barrier_semaphore(), inc=1, device_id=partner, device_id_type=MESH
        )


def await_greetings(partners):
    pl.semaphore_wait(pltpu.get_barrier_semaphore(), len(partners))


def send(source, target, send_sem, recv_sem, partner):
    copy = pltpu.make_async_remote_copy(
        src_ref=source,
        dst_ref=target,
        send_sem=send_sem,
        recv_sem=recv_sem,
        device_id=partner,
        device_id_type=MESH,
    )
    copy.start()
    return copy


def normalize(values):
    center = jnp.mean(values, axis=-1, keepdims=True)
    spread = values - center
    power = jnp.mean(spread * spread, axis=-1, keepdims=True)
    scale = lax.rsqrt(power + EPS_NORM)
    return spread * scale, scale


def normalize_back(grad, unit, scale):
    first = jnp.mean(grad, axis=-1, keepdims=True)
    second = jnp.mean(grad * unit, axis=-1, keepdims=True)
    return scale * (grad - first - unit * second)


def group_rows(meta_ref, image):
    pairs = [
        meta_ref[2 * half, image] + meta_ref[2 * half + 1, image]
        for half in range(meta_ref.shape[0] // 2)
    ]
    return jnp.concatenate(pairs, axis=1)


def split(values):
    high = values.astype(jnp.bfloat16)
    return high, (values - high.astype(jnp.float32)).astype(jnp.bfloat16)


def gelu_parts(values):
    cdf = 0.5 + 0.5 * lax.erf(values * (0.5**0.5))
    return cdf, jnp.exp(-0.5 * values * values) * (1.0 / math.sqrt(2 * math.pi))


def forward_kernel(
    n_exp,
    experts,
    x_ref,
    d_ref,
    ids_ref,
    mask_ref,
    win_ref,
    wout_ref,
    norm_ref,
    wqkv_hbm,
    wproj_hbm,
    wrouter_ref,
    o_x,
    o_first,
    o_qkv,
    o_lse,
    o_att,
    o_mid,
    o_d,
    o_out,
    o_dsecond,
    o_grads,
    o_grouter,
    x_all,
    first_ref,
    qkv_ref,
    lse_ref,
    att_ref,
    mid_ref,
    out_send,
    dsecond_ref,
    grads_recv,
    grouter_ref,
    d_all,
    w_all,
    r_all,
    meta_ref,
    meta_all,
    wqkv_ref,
    wproj_ref,
    router_ref,
    ds_send,
    ds_recv,
    acc_out,
    acc_ds,
    dlogits_ref,
    gates_ref,
    dgates_ref,
    r_turn,
    d_turn,
    act_all,
    dpre_all,
    x_sems,
    m_sems,
    d_sems,
    r_sems,
    ds_sems,
    dr_sems,
    rr_sems,
    z_sems,
    s_sems,
    t_sems,
    own_sem,
    o_sems,
):
    expert, ctx, dp = places()
    own_images, n_ctx, seq_dev, width = x_all.shape
    seq = n_ctx * seq_dev
    rows = own_images * seq
    ctx_ids = [(expert, ctx_partner(ctx, step), dp) for step in range(1, n_ctx)]
    side_ids = ctx_ids[:2]
    twin = (expert, ctx, 1 - dp)
    right, left = lax.rem(expert + 1, n_exp), lax.rem(expert + n_exp - 1, n_exp)
    greeted = ctx_ids + [(right, ctx, dp), (left, ctx, dp), twin]
    greet(greeted)
    row = lax.broadcasted_iota(jnp.int32, (8, seq_dev), 0)
    odd = lax.rem(ctx, 2).astype(jnp.float32)
    for image in range(ids_ref.shape[0]):
        named = jnp.zeros((8, seq_dev), jnp.bool_)
        for choice in range(ids_ref.shape[1]):
            named = named | (ids_ref[image, choice : choice + 1] == row)
        values = jnp.where(
            row == experts, mask_ref[image : image + 1].astype(jnp.float32), named.astype(jnp.float32)
        )
        meta_ref[image, :, :seq_dev] = values * (1.0 - odd)
        meta_ref[image, :, seq_dev:] = values * odd
    router_ref[...] = jnp.zeros_like(router_ref)
    router_high, router_low = split(wrouter_ref[...])
    router_ref[0, :experts] = router_high.astype(jnp.float32)
    router_ref[1, :experts] = router_low.astype(jnp.float32)
    own = [
        pltpu.make_async_copy(source, target, own_sem.at[at])
        for at, (source, target) in enumerate(
            (
                (win_ref.at[0], w_all.at[0, expert]),
                (wout_ref.at[0], w_all.at[1, expert]),
                (x_ref.at[pl.ds(ctx * own_images, own_images)], x_all.at[:, ctx]),
                (wqkv_hbm, wqkv_ref),
                (wproj_hbm, wproj_ref),
                (d_ref, d_all.at[:, :, ctx]),
            )
        )
    ]
    for copy in own:
        copy.start()
    meta_all[ctx] = meta_ref[...]
    await_greetings(greeted)
    x_copies = []
    for image in range(own_images):
        x_copies.append(
            [
                send(
                    x_ref.at[partner[1] * own_images + image],
                    x_all.at[image, ctx],
                    x_sems.at[0, image, at],
                    x_sems.at[1, image, at],
                    partner,
                )
                for at, partner in enumerate(ctx_ids)
            ]
        )
        if image == 0:
            m_copies = [
                send(meta_ref, meta_all.at[ctx], m_sems.at[0, at], m_sems.at[1, at], partner)
                for at, partner in enumerate(ctx_ids)
            ]

    def hop(phase, side):
        share = expert - phase if side == 0 else expert + phase
        able = (share >= 0) & (expert < n_exp - 1) if side == 0 else (share < n_exp) & (expert > 0)
        share = jnp.clip(share, 0, n_exp - 1)
        return able, pltpu.make_async_remote_copy(
            src_ref=w_all.at[dp, share],
            dst_ref=w_all.at[dp, share],
            send_sem=z_sems.at[0, phase, side],
            recv_sem=z_sems.at[1, phase, side],
            device_id=(right if side == 0 else left, ctx, dp),
            device_id_type=MESH,
        )

    def landed(phase, side):
        share = expert - 1 - phase if side == 0 else expert + 1 + phase
        able = share >= 0 if side == 0 else share < n_exp
        share = jnp.clip(share, 0, n_exp - 1)
        place = w_all.at[dp, share]
        return (
            able,
            pltpu.make_async_remote_copy(
                src_ref=place,
                dst_ref=place,
                send_sem=z_sems.at[0, phase, side],
                recv_sem=z_sems.at[1, phase, side],
                device_id=(left if side == 0 else right, ctx, dp),
                device_id_type=MESH,
            ),
            pltpu.make_async_remote_copy(
                src_ref=place,
                dst_ref=place,
                send_sem=s_sems.at[0, phase, side],
                recv_sem=s_sems.at[1, phase, side],
                device_id=twin,
                device_id_type=MESH,
            ),
        )

    def start_hops(phase):
        for side in range(2):
            able, copy = hop(phase, side)
            pl.when(able)(copy.start)

    def take_hops(phase):
        for side in range(2):
            able, copy, shared = landed(phase, side)

            @pl.when(able)
            def _():
                copy.wait_recv()
                shared.start()

    def take_shared(phase):
        for side in range(2):
            able, _, shared = landed(phase, side)
            pl.when(able)(shared.wait_recv)

    own[0].wait()
    own[1].wait()
    start_hops(0)
    for copy in own[2:]:
        copy.wait()

    def d_copy(at, order):
        group = ctx_partner(ctx_ids[at][1], order)
        return pltpu.make_async_remote_copy(
            src_ref=d_ref.at[group],
            dst_ref=d_all.at[group, :, ctx],
            send_sem=d_sems.at[0, at, order],
            recv_sem=d_sems.at[1, at, order],
            device_id=ctx_ids[at],
            device_id_type=MESH,
        )

    def d_relay(image, order):
        target = side_ids[1 - image]
        place = d_all.at[ctx_partner(target[1], order), image, side_ids[image][1]]
        return pltpu.make_async_remote_copy(
            src_ref=place,
            dst_ref=place,
            send_sem=dr_sems.at[0, image, order],
            recv_sem=dr_sems.at[1, image, order],
            device_id=target,
            device_id_type=MESH,
        )

    def r_copy(at, image):
        return pltpu.make_async_remote_copy(
            src_ref=r_all.at[ctx, image],
            dst_ref=r_all.at[ctx, image],
            send_sem=r_sems.at[0, at, image],
            recv_sem=r_sems.at[1, at, image],
            device_id=side_ids[at],
            device_id_type=MESH,
        )

    def r_relay(image):
        place = r_all.at[side_ids[image][1], image]
        return pltpu.make_async_remote_copy(
            src_ref=place,
            dst_ref=place,
            send_sem=rr_sems.at[0, image],
            recv_sem=rr_sems.at[1, image],
            device_id=side_ids[1 - image],
            device_id_type=MESH,
        )

    for at in range(n_ctx - 1):
        d_copy(at, 0).start()
    for copy in x_copies[0] + m_copies:
        copy.wait()
    for order in (3, 1):
        for at in range(2):
            d_copy(at, order).start()
    lane = lax.broadcasted_iota(jnp.int32, (seq, LANES), 1)
    low_half = lane < HEAD_DIM
    for image in range(own_images):
        part = pl.ds(image * seq, seq)
        if image > 0:
            for copy in x_copies[image]:
                copy.wait()
        values = x_all[image].reshape(seq, width).astype(jnp.float32)
        unit, _ = normalize(values)
        first = (unit * norm_ref[0:1] + norm_ref[1:2]).astype(jnp.bfloat16)
        first_ref[part] = first
        qkv_ref[part] = dot(first, wqkv_ref[...]).astype(jnp.bfloat16)
        key_mask = group_rows(meta_all, ctx * own_images + image)[experts : experts + 1]
        bias = jnp.where(key_mask > 0, 0.0, NEG)
        column = jnp.broadcast_to(bias, (LANES, seq)).T
        totals = jnp.where(lane == HEADS, column, 0.0)
        for pair in range(HEADS // 2):
            query = qkv_ref[part, pair * LANES : (pair + 1) * LANES]
            keys = qkv_ref[part, width + pair * LANES : width + (pair + 1) * LANES]
            heads = qkv_ref[part, 2 * width + pair * LANES : 2 * width + (pair + 1) * LANES]
            query = query * jnp.bfloat16(HEAD_DIM**-0.5)
            parts = []
            for half in range(2):
                chosen = low_half if half == 0 else ~low_half
                scores = dot_nt(jnp.where(chosen, query, jnp.zeros_like(query)), keys) + bias
                peak = jnp.max(scores, axis=-1, keepdims=True)
                raised = jnp.exp(scores - peak)
                total = jnp.sum(raised, axis=-1, keepdims=True)
                probs = (raised * (1.0 / total)).astype(jnp.bfloat16)
                parts.append(dot(probs, heads))
                totals = jnp.where(lane == 2 * pair + half, peak + jnp.log(total), totals)
            att_ref[part, pair * LANES : (pair + 1) * LANES] = jnp.where(
                low_half, parts[0], parts[1]
            ).astype(jnp.bfloat16)
        lse_ref[part] = totals
        mid = values + dot(att_ref[part], wproj_ref[...])
        mid_ref[part] = mid
        unit, _ = normalize(mid)
        r_all[ctx, image] = (unit * norm_ref[2:3] + norm_ref[3:4]).astype(jnp.bfloat16)
        for at in range(2):
            r_copy(at, image).start()
        if image == 0:
            take_hops(0)
            start_hops(1)
        if image == own_images - 1:
            for at in range(2):
                d_copy(at, 2).start()

    kept_copies = [
        pltpu.make_async_copy(source, target, o_sems.at[at])
        for at, (source, target) in enumerate(
            (
                (x_all, o_x),
                (first_ref, o_first),
                (qkv_ref, o_qkv),
                (lse_ref, o_lse),
                (att_ref, o_att),
                (mid_ref, o_mid),
            )
        )
    ]
    for copy in kept_copies:
        copy.start()

    def out_copy(chunk):
        return pltpu.make_async_copy(
            out_send.at[chunk % 2], o_out.at[chunk], o_sems.at[8 + chunk]
        )

    wide = lax.broadcasted_iota(jnp.int32, (rows, LANES), 1)
    near = jnp.where(expert < n_exp // 2, expert + 1, expert - 1)
    last = jnp.where(expert < n_exp // 2, n_exp - 1, 0)
    middle = n_exp * (n_exp - 1) // 2 - expert - near - last

    def start_chunk(chunk, owner):
        routed = r_all[owner].reshape(rows, width)
        present = jnp.concatenate(
            [group_rows(meta_all, owner * own_images + image) for image in range(own_images)], axis=1
        )
        present = jnp.concatenate(
            [present, jnp.zeros((LANES - present.shape[0], rows), jnp.float32)], axis=0
        ).T
        present = (present > 0) & (wide < experts)
        logits = dot_nt(routed, router_ref[0].astype(jnp.bfloat16)) + dot_nt(
            routed, router_ref[1].astype(jnp.bfloat16)
        )
        peak = jnp.max(jnp.where(present, logits, NEG), axis=-1, keepdims=True)
        raised = jnp.where(present, jnp.exp(jnp.where(present, logits - peak, 0.0)), 0.0)
        gates_ref[chunk] = raised / jnp.sum(raised, axis=-1, keepdims=True)
        dgates_ref[chunk] = jnp.zeros((rows, LANES), jnp.float32)

    def end_chunk(chunk):
        slot = 0 if chunk == 0 else 1
        gates = gates_ref[chunk]
        dgates = jnp.where(gates > 0, dgates_ref[chunk], 0.0)
        dlogits = gates * (dgates - jnp.sum(gates * dgates, axis=-1, keepdims=True))
        high, low = split(dlogits)
        dlogits_ref[0, chunk * rows : (chunk + 1) * rows] = high
        dlogits_ref[1, chunk * rows : (chunk + 1) * rows] = low
        total = (
            acc_ds[slot]
            + dot(high, router_ref[0].astype(jnp.bfloat16))
            + dot(high, router_ref[1].astype(jnp.bfloat16))
            + dot(low, router_ref[0].astype(jnp.bfloat16))
        )
        if chunk == 0:
            dsecond_ref[...] = total
        else:
            ds_send[chunk - 1] = total.astype(jnp.bfloat16)
            ds_copy(chunk).start()
        out = acc_out[slot]
        if chunk == 0:
            out += mid_ref[...]
        if chunk in (3, 0):
            out_copy(1 if chunk == 3 else 2).wait()
        out_send[chunk % 2] = out.astype(jnp.bfloat16).reshape(out_send.shape[1:])
        out_copy(chunk).start()
        if chunk in (1, 2):
            acc_out[slot] = jnp.zeros(acc_out.shape[1:], jnp.float32)
            acc_ds[slot] = jnp.zeros(acc_ds.shape[1:], jnp.float32)

    def ds_copy(chunk):
        return pltpu.make_async_remote_copy(
            src_ref=ds_send.at[chunk - 1],
            dst_ref=ds_recv.at[chunk - 1],
            send_sem=ds_sems.at[0, chunk - 1],
            recv_sem=ds_sems.at[1, chunk - 1],
            device_id=ctx_ids[chunk - 1],
            device_id_type=MESH,
        )

    acc_out[...] = jnp.zeros_like(acc_out)
    acc_ds[...] = jnp.zeros_like(acc_ds)

    def place_of(step):
        own_chunk = (step < 3) | (step == n_ctx * n_exp - 1)
        chunk = jnp.where(own_chunk, 0, 1 + (step - 3) // n_exp)
        rank = jnp.where(step < 3, step, jnp.where(own_chunk, n_exp - 1, lax.rem(step - 3, n_exp)))
        index = jnp.where(
            rank == 0, expert, jnp.where(rank == 1, near, jnp.where(rank == 2, middle, last))
        )
        return chunk, jnp.where(own_chunk, 0, 1), index

    def hidden_products(step, image):
        chunk, _, index = place_of(step)
        owner = ctx_partner(ctx, chunk)
        return (
            dot(r_all[owner, image], w_all[0, index]),
            dot(d_all[owner, image].reshape(seq, width), w_all[1, index]),
        )

    def hidden(step, image, pre, dact):
        chunk, _, index = place_of(step)
        part = pl.ds(image * seq, seq)
        gate = jnp.sum(jnp.where(lane == index, gates_ref[chunk, part], 0.0), axis=-1, keepdims=True)
        cdf, density = gelu_parts(pre)
        act = pre * cdf
        dgate = jnp.sum(dact * act, axis=-1, keepdims=True)
        dgates_ref[chunk, part] = jnp.where(lane == index, dgate, dgates_ref[chunk, part])
        kept = pl.ds(pl.multiple_of(chunk * rows + image * seq, seq), seq)
        act_all[index, kept] = (gate * act).astype(jnp.bfloat16)
        dpre_all[index, kept] = (gate * dact * (cdf + pre * density)).astype(jnp.bfloat16)

    def back_out(step, image):
        chunk, slot, index = place_of(step)
        part = pl.ds(image * seq, seq)
        kept = pl.ds(pl.multiple_of(chunk * rows + image * seq, seq), seq)
        acc_out[slot, part] += dot_nt(act_all[index, kept], w_all[1, index])
        acc_ds[slot, part] += dot_nt(dpre_all[index, kept], w_all[0, index])

    for at in range(n_ctx - 1):
        d_copy(at, 0).wait_recv()
    start_chunk(0, ctx)
    for image in range(own_images):
        hidden(0, image, *hidden_products(0, image))

    def one_step(step, carry):
        @pl.when(step == 1)
        def _():
            take_shared(0)
            for order in (3, 1):
                for at in range(2):
                    d_copy(at, order).wait_recv()
            for order in range(1, n_ctx):
                d_relay(0, order).start()
            for order in (1, 2):
                d_relay(1, order).start()

        @pl.when(step == 2)
        def _():
            take_hops(1)
            start_hops(2)
            take_shared(1)

        @pl.when(step == 3)
        def _():
            for image in range(2):
                r_copy(0, image).wait_recv()
                d_relay(image, 1).wait_recv()
            r_relay(0).start()
            start_chunk(1, ctx_ids[0][1])

        @pl.when(step == 4)
        def _():
            for image in range(2):
                r_copy(1, image).wait_recv()
            r_relay(1).start()
            for at in range(2):
                d_copy(at, 2).wait_recv()
            d_relay(1, 3).start()

        @pl.when(step == 6)
        def _():
            take_hops(2)
            take_shared(2)

        @pl.when(step == 7)
        def _():
            for image in range(2):
                d_relay(image, 2).wait_recv()
            start_chunk(2, ctx_ids[1][1])

        @pl.when(step == 11)
        def _():
            for image in range(2):
                d_relay(image, 3).wait_recv()
                r_relay(image).wait_recv()
            start_chunk(3, ctx_ids[2][1])

        for image in range(own_images):
            products = hidden_products(step, image)
            back_out(step - 1, image)
            hidden(step, image, *products)

        for chunk in range(1, n_ctx):
            pl.when(step == 3 + chunk * n_exp)(functools.partial(end_chunk, chunk))

        return carry

    lax.fori_loop(1, n_ctx * n_exp, one_step, 0)
    for image in range(own_images):
        back_out(n_ctx * n_exp - 1, image)
    end_chunk(0)
    for chunk in range(n_ctx):
        owner = ctx_partner(ctx, chunk)
        r_turn[:, chunk * rows : (chunk + 1) * rows] = r_all[owner].reshape(rows, width).T
        d_turn[:, chunk * rows : (chunk + 1) * rows] = d_all[owner].reshape(rows, width).T

    d_kept = pltpu.make_async_copy(d_all.at[ctx], o_d, o_sems.at[7])
    d_kept.start()

    def grad_at(which, index):
        return act_all.at[index, pl.ds(pl.multiple_of(which * width, width), width)]

    def t_copy(index):
        return pltpu.make_async_remote_copy(
            src_ref=grad_at(1 - dp, index),
            dst_ref=grads_recv.at[index],
            send_sem=t_sems.at[0, index],
            recv_sem=t_sems.at[1, index],
            device_id=twin,
            device_id_type=MESH,
        )

    def one_expert(index, carry):
        grad_out = dot(d_turn[...], act_all[index]).astype(jnp.bfloat16)
        grad_at(0, index)[...] = dot(r_turn[...], dpre_all[index]).astype(jnp.bfloat16)
        grad_at(1, index)[...] = grad_out
        t_copy(index).start()
        return carry

    lax.fori_loop(0, n_exp, one_expert, 0)
    grouter = dot(r_turn[...], dlogits_ref[0]) + dot(r_turn[...], dlogits_ref[1])
    grouter_ref[...] = grouter.T[: grouter_ref.shape[0]]
    for index in range(n_exp):
        t_copy(index).wait()
        grad_at(dp, index)[...] = (
            grad_at(dp, index)[...].astype(jnp.float32) + grads_recv[index].astype(jnp.float32)
        ).astype(jnp.bfloat16)
    last_copies = [pltpu.make_async_copy(grouter_ref, o_grouter, o_sems.at[13])] + [
        pltpu.make_async_copy(grad_at(dp, index), o_grads.at[index], o_sems.at[15 + index])
        for index in range(n_exp)
    ]
    for copy in last_copies:
        copy.start()
    for phase in range(n_exp - 1):
        for side in range(2):
            able, copy = hop(phase, side)
            pl.when(able)(copy.wait_send)
            able, _, shared = landed(phase, side)
            pl.when(able)(shared.wait_send)
    for at in range(n_ctx - 1):
        for order in range(n_ctx if at < 2 else 1):
            d_copy(at, order).wait_send()
    for image in range(2):
        r_relay(image).wait_send()
        for at in range(2):
            r_copy(at, image).wait_send()
        for order in range(1, n_ctx):
            d_relay(image, order).wait_send()
    for chunk in range(1, n_ctx):
        ds_copy(chunk).wait()
        dsecond_ref[...] += ds_recv[chunk - 1].astype(jnp.float32)
    last_copies.append(pltpu.make_async_copy(dsecond_ref, o_dsecond, o_sems.at[14]))
    last_copies[-1].start()
    for copy in kept_copies + [d_kept] + last_copies:
        copy.wait()
    out_copy(3).wait()
    out_copy(0).wait()


def gram_blocks(matrix, packed_ref):
    size = matrix.shape[0]
    index = 0
    for row in range(size // LANES):
        strip = dot_nt(matrix[row * LANES : (row + 1) * LANES], matrix[row * LANES :])
        for col in range(size // LANES - row):
            packed_ref[index] = strip[:, col * LANES : (col + 1) * LANES].reshape(
                packed_ref.shape[1:]
            )
            index += 1


def gram_whole(packed_ref, high_ref, low_ref):
    count = high_ref.shape[0] // LANES
    diagonal = lax.broadcasted_iota(jnp.int32, (LANES, LANES), 0) == lax.broadcasted_iota(
        jnp.int32, (LANES, LANES), 1
    )
    places_of = {}
    square = jnp.zeros((1, 1), jnp.float32)
    index = 0
    for row in range(count):
        for col in range(row, count):
            places_of[index] = (row, col)
            if row == col:
                block = packed_ref[index].reshape(LANES, LANES)
                square += jnp.sum(jnp.where(diagonal, block, 0.0), keepdims=True)
            index += 1
    scale = 1.0 / (jnp.sqrt(square) + EPS_ORTHO)
    for index, (row, col) in places_of.items():
        block = packed_ref[index].reshape(LANES, LANES) * (scale * scale)
        rows, cols = pl.ds(row * LANES, LANES), pl.ds(col * LANES, LANES)
        high_ref[rows, cols], low_ref[rows, cols] = split(block)
        if row != col:
            high_ref[cols, rows], low_ref[cols, rows] = split(block.T)
    return scale


def orthogonal(high_ref, low_ref, mix_ref, total_ref):
    size = high_ref.shape[0]
    eye = lax.broadcasted_iota(jnp.int32, (size, size), 0) == lax.broadcasted_iota(
        jnp.int32, (size, size), 1
    )
    for turn in range(NS_ITERS):
        high, low = high_ref[...], low_ref[...]
        square = dot(high, high)
        if turn == NS_ITERS - 1:
            square += dot(high, low) + dot(low, high)
        mix_ref[...] = (
            jnp.where(eye, NS_A, 0.0)
            + NS_B * (high.astype(jnp.float32) + low.astype(jnp.float32))
            + NS_C * square
        ).astype(jnp.bfloat16)
        mix = mix_ref[...]
        if turn == 0:
            total_ref[...] = mix.astype(jnp.float32)
        else:
            total_high, total_low = split(total_ref[...])
            total_ref[...] = dot(mix, total_high) + dot(mix, total_low)
        if turn < NS_ITERS - 1:
            turned_high, turned_low = split(dot(mix, high) + dot(mix, low))
            high_ref[...], low_ref[...] = split(dot(turned_high, mix) + dot(turned_low, mix))


def backward_kernel(
    n_exp,
    h_x,
    h_d,
    h_first,
    h_qkv,
    h_lse,
    h_att,
    h_mid,
    h_dsecond,
    h_grads,
    grouter_ref,
    norm_ref,
    h_wqkv,
    h_wproj,
    h_out,
    h_min,
    h_mout,
    h_mqkv,
    h_mproj,
    mnorm_ref,
    mrouter_ref,
    out_ref,
    dx_ref,
    gexp_ref,
    step_ref,
    whole_ref,
    sums_ref,
    squares_ref,
    x_ref,
    d_ref,
    first_ref,
    qkv_ref,
    lse_ref,
    att_ref,
    mid_ref,
    dsecond_ref,
    own_grads,
    passed_ref,
    wqkv_ref,
    wproj_ref,
    out_own,
    mexp_ref,
    mqkv_ref,
    mproj_ref,
    out_recv,
    z_recv,
    dmid_ref,
    dbranch_ref,
    datt_ref,
    dqkv_ref,
    dx_send,
    shared_ref,
    half_recv,
    sum_one,
    ctx_recv,
    piece_send,
    piece_recv,
    mat_ref,
    packed_ref,
    packed_recv,
    gathered_ref,
    high_ref,
    low_ref,
    mix_ref,
    total_ref,
    small_ref,
    small_twin,
    small_ctx,
    small_z,
    in_sems,
    out_sems,
    z_sems,
    f_sems,
    dx_sems,
    h_sems,
    c_sems,
    s_sems,
    p_sems,
    w_sems,
    g_sems,
    a_sems,
    x_sems,
    n_sems,
):
    expert, ctx, dp = places()
    own_images, n_ctx, seq_dev, width = dx_send.shape
    seq = n_ctx * seq_dev
    half = width // 2
    cols = width // n_ctx
    loads = {}

    def load(name, source, target):
        loads[name] = pltpu.make_async_copy(source, target, in_sems.at[len(loads)])
        return loads[name]

    def take(*names):
        for name in names:
            loads[name].wait()

    for name, source, target in (
        ("mid", h_mid, mid_ref),
        ("dsecond", h_dsecond, dsecond_ref),
        ("d", h_d, d_ref),
        ("wproj", h_wproj, wproj_ref),
        ("qkv", h_qkv, qkv_ref),
        ("lse", h_lse, lse_ref),
        ("att", h_att, att_ref),
        ("first", h_first, first_ref),
        ("wqkv", h_wqkv, wqkv_ref),
        ("x", h_x, x_ref),
        ("grads", h_grads.at[expert], own_grads),
        ("passed", h_grads.at[jnp.where(expert < n_exp // 2, n_exp - 1, 0)], passed_ref),
        ("out", h_out.at[:, :, ctx], out_own),
        ("mqkv", h_mqkv, mqkv_ref),
        ("mproj", h_mproj, mproj_ref),
    ):
        load(name, source, target).start()
    moment = [
        pltpu.make_async_copy(source.at[0], mexp_ref, in_sems.at[len(loads)])
        for source in (h_min, h_mout)
    ]
    pl.when(dp == 0)(moment[0].start)
    pl.when(dp == 1)(moment[1].start)
    ctx_ids = [(expert, ctx_partner(ctx, step), dp) for step in range(1, n_ctx)]
    z_steps = [1, n_exp - 1] + list(range(2, n_exp - 1))
    z_ids = [(z_partner(expert, step, n_exp), ctx, dp) for step in z_steps]
    twin = (expert, ctx, 1 - dp)
    greeted = ctx_ids + z_ids + [twin]
    greet(greeted)

    def to_each(partners, source, target, sems):
        return [
            send(source(at, partner), target(at, partner), sems.at[0, at], sems.at[1, at], partner)
            for at, partner in enumerate(partners)
        ]

    await_greetings(greeted)
    low_side = expert < n_exp // 2
    near_end = jnp.where(low_side, 0, n_exp - 1)
    far_end = n_exp - 1 - near_end
    near_mid = jnp.where(low_side, 1, n_exp - 2)
    far_mid = n_exp - 1 - near_mid
    at_end = expert == near_end

    def z_copy(target, source, slot, order):
        return pltpu.make_async_remote_copy(
            src_ref=source,
            dst_ref=z_recv.at[slot],
            send_sem=z_sems.at[0, order],
            recv_sem=z_sems.at[1, slot],
            device_id=(target, ctx, dp),
            device_id_type=MESH,
        )

    def end_copies():
        return [
            z_copy(near_mid, h_grads.at[far_end], 3, 0),
            z_copy(far_mid, h_grads.at[far_mid], 1, 1),
            z_copy(near_mid, h_grads.at[near_mid], 0, 2),
        ]

    def mid_copies():
        return [
            z_copy(far_mid, h_grads.at[far_mid], 2, 0),
            z_copy(near_end, h_grads.at[near_end], 0, 1),
            z_copy(far_end, passed_ref, 1, 2),
        ]

    @pl.when(at_end)
    def _():
        end_copies()[0].start()

    @pl.when(jnp.logical_not(at_end))
    def _():
        for copy in mid_copies()[:2]:
            copy.start()

    def send_out(step):
        first_image = ctx_partner(ctx, step) * own_images
        return to_each(
            ctx_ids,
            lambda at, partner: h_out.at[step, :, partner[1]],
            lambda at, partner: out_recv.at[ctx, pl.ds(first_image, own_images)],
            out_sems.at[step],
        )

    out_copies = []
    for step in range(1, n_ctx):
        out_copies += send_out(step)
    gain_one, gain_two = norm_ref[0:1], norm_ref[2:3]
    sums = [jnp.zeros((1, width), jnp.float32) for _ in range(4)]
    take("mid", "dsecond", "d", "wproj")
    for image in range(own_images):
        rows = pl.ds(image * seq, seq)
        unit, scale = normalize(mid_ref[rows])
        grad = dsecond_ref[rows]
        sums[2] += jnp.sum(grad * unit, axis=0, keepdims=True)
        sums[3] += jnp.sum(grad, axis=0, keepdims=True)
        dmid = normalize_back(grad * gain_two, unit, scale) + d_ref[rows].astype(jnp.float32)
        dmid_ref[rows] = dmid
        dbranch = dmid.astype(jnp.bfloat16)
        dbranch_ref[rows] = dbranch
        datt_ref[rows] = dot_nt(dbranch, wproj_ref[...]).astype(jnp.bfloat16)
    take("att")
    gproj = dot_tn(att_ref[...], dbranch_ref[...]).astype(jnp.bfloat16)
    for place in range(n_ctx):
        shared_ref[place, :, 3 * cols :] = gproj[:, place * cols : (place + 1) * cols]
    own_half = pl.ds(pl.multiple_of(dp * half, half), half)
    other_half = pl.ds(pl.multiple_of((1 - dp) * half, half), half)

    def to_twin(which, lanes):
        return send(
            shared_ref.at[:, other_half, lanes],
            half_recv.at[:, :, lanes],
            h_sems.at[0, which],
            h_sems.at[1, which],
            twin,
        )

    def to_owners(which, lanes):
        for place in range(n_ctx):
            sum_one[place, :, lanes] = (
                shared_ref[place, own_half, lanes].astype(jnp.float32)
                + half_recv[place, :, lanes].astype(jnp.float32)
            ).astype(jnp.bfloat16)
        return to_each(
            ctx_ids,
            lambda at, partner: sum_one.at[partner[1], :, lanes],
            lambda at, partner: ctx_recv.at[at, :, lanes],
            c_sems.at[which],
        )

    qkv_lanes, proj_lanes = pl.ds(0, 3 * cols), pl.ds(3 * cols, cols)
    h_copy = to_twin(0, proj_lanes)
    take("qkv", "lse")
    lane = lax.broadcasted_iota(jnp.int32, (seq, LANES), 1)
    low_half = lane < HEAD_DIM
    factor = HEAD_DIM**-0.5
    for image in range(own_images):
        rows = pl.ds(image * seq, seq)
        totals = lse_ref[rows].T
        bias = lse_ref[rows, HEADS : HEADS + 1]
        for pair in range(HEADS // 2):
            at = pair * LANES
            query = qkv_ref[rows, at : at + LANES] * jnp.bfloat16(factor)
            keys = qkv_ref[rows, width + at : width + at + LANES]
            heads = qkv_ref[rows, 2 * width + at : 2 * width + at + LANES]
            datt = datt_ref[rows, at : at + LANES]
            dquery, dkeys, dheads = [], [], []
            for part in range(2):
                chosen = low_half if part == 0 else ~low_half
                scores = dot_nt(keys, jnp.where(chosen, query, jnp.zeros_like(query))) + bias
                head = 2 * pair + part
                weights = jnp.exp(scores - totals[head : head + 1])
                dprobs = dot_nt(heads, jnp.where(chosen, datt, jnp.zeros_like(datt)))
                delta = jnp.sum(weights * dprobs, axis=0, keepdims=True)
                dscores = (weights * (dprobs - delta)).astype(jnp.bfloat16)
                dquery.append(dot_tn(dscores, keys))
                dkeys.append(dot(dscores, query))
                dheads.append(dot(weights.astype(jnp.bfloat16), datt))
            dqkv_ref[rows, at : at + LANES] = (
                jnp.where(low_half, dquery[0], dquery[1]) * factor
            ).astype(jnp.bfloat16)
            dqkv_ref[rows, width + at : width + at + LANES] = jnp.where(
                low_half, dkeys[0], dkeys[1]
            ).astype(jnp.bfloat16)
            dqkv_ref[rows, 2 * width + at : 2 * width + at + LANES] = jnp.where(
                low_half, dheads[0], dheads[1]
            ).astype(jnp.bfloat16)
        if image == 0:
            h_copy.wait()
            c_copies = to_owners(0, proj_lanes)
            take("passed")

            @pl.when(jnp.logical_not(at_end))
            def _():
                copies = mid_copies()
                copies[0].wait_send()
                z_copy(near_mid, passed_ref, 3, 0).wait_recv()
                passed_ref[...] = (
                    passed_ref[...].astype(jnp.float32) + z_recv[3].astype(jnp.float32)
                ).astype(jnp.bfloat16)
                copies[2].start()

            @pl.when(at_end)
            def _():
                copies = end_copies()
                copies[0].wait_send()
                copies[1].start()
                copies[2].start()

    take("first")
    gqkv = dot_tn(first_ref[...], dqkv_ref[...]).astype(jnp.bfloat16)
    for place in range(n_ctx):
        shared_ref[place, :, : 3 * cols] = gqkv[:, 3 * cols * place : 3 * cols * (place + 1)]
    h_copy = to_twin(1, qkv_lanes)
    take("wqkv", "x")
    for image in range(own_images):
        rows = pl.ds(image * seq, seq)
        grad = dot_nt(dqkv_ref[rows], wqkv_ref[...])
        unit, scale = normalize(x_ref[rows].astype(jnp.float32))
        sums[0] += jnp.sum(grad * unit, axis=0, keepdims=True)
        sums[1] += jnp.sum(grad, axis=0, keepdims=True)
        dx = dmid_ref[rows] + normalize_back(grad * gain_one, unit, scale)
        dx_send[image] = dx.astype(jnp.bfloat16).reshape(n_ctx, seq_dev, width)
        if image == 0:
            h_copy.wait()
            c_copies += to_owners(1, qkv_lanes)
    for at, total in enumerate(sums):
        small_ref[at : at + 1] = total
    small_ref[4:8] = jnp.zeros((4, width), jnp.float32)
    small_ref[8:16] = grouter_ref[...]
    s_copy = send(small_ref, small_twin, h_sems.at[0, 2], h_sems.at[1, 2], twin)
    s_copy.wait()
    small_ctx[ctx] = small_ref[...] + small_twin[...]
    s_copies = to_each(
        ctx_ids, lambda at, partner: small_ctx.at[ctx], lambda at, partner: small_ctx.at[ctx], s_sems
    )
    for copy in c_copies:
        copy.wait()
    total = sum_one[ctx].astype(jnp.float32)
    for at in range(n_ctx - 1):
        total += ctx_recv[at].astype(jnp.float32)
    piece_send[...] = total.astype(jnp.bfloat16).reshape(piece_send.shape)
    p_copies = to_each(
        z_ids,
        lambda at, partner: piece_send.at[partner[0]],
        lambda at, partner: piece_recv.at[at],
        p_sems,
    )
    out_copies += send_out(0)
    dx_copies = to_each(
        ctx_ids,
        lambda at, partner: dx_send.at[:, partner[1]],
        lambda at, partner: dx_ref.at[pl.ds(ctx * own_images, own_images)],
        dx_sems,
    )
    for image in range(own_images):
        dx_ref[ctx * own_images + image] = dx_send[image, ctx]
    for copy in s_copies:
        copy.wait()
    total = small_ctx[0]
    for place in range(1, n_ctx):
        total += small_ctx[place]
    small_z[expert] = total
    s_copies = to_each(
        z_ids,
        lambda at, partner: small_z.at[expert],
        lambda at, partner: small_z.at[expert],
        n_sems.at[0],
    )

    def gram_start(which, matrix):
        gram_blocks(matrix.astype(jnp.bfloat16), packed_ref.at[which])
        return to_each(
            ctx_ids,
            lambda at, partner: packed_ref.at[which, :, partner[1]],
            lambda at, partner: packed_recv.at[which, at],
            g_sems.at[which],
        )

    def gram_middle(which, copies):
        for copy in copies:
            copy.wait()
        total = packed_ref[which, :, ctx]
        for at in range(n_ctx - 1):
            total += packed_recv[which, at]
        gathered_ref[which, :, ctx] = total
        return to_each(
            ctx_ids,
            lambda at, partner: gathered_ref.at[which, :, ctx],
            lambda at, partner: gathered_ref.at[which, :, ctx],
            a_sems.at[which],
        )

    def step_of(which, matrix, scale):
        total_high, total_low = split(total_ref[...])
        high, low = split(matrix * scale)
        cut = pl.ds(0, matrix.shape[1])
        step_ref[which, dp, :, cut] = (
            dot(total_high, high) + dot(total_high, low) + dot(total_low, high)
        ).astype(jnp.bfloat16)
        return send(
            step_ref.at[which, dp, :, cut],
            step_ref.at[which, dp, :, cut],
            x_sems.at[0, which],
            x_sems.at[1, which],
            twin,
        )

    take("grads")

    @pl.when(at_end)
    def _():
        copies = end_copies()
        copies[1].wait_send()
        copies[2].wait_send()
        copies[1].wait_recv()
        copies[2].wait_recv()
        total = own_grads[...].astype(jnp.float32)
        for slot in range(2):
            total += z_recv[slot].astype(jnp.float32)
        gexp_ref[dp] = total.astype(jnp.bfloat16)

    @pl.when(jnp.logical_not(at_end))
    def _():
        copies = mid_copies()
        copies[1].wait_send()
        copies[2].wait_send()
        for copy in copies:
            copy.wait_recv()
        total = own_grads[...].astype(jnp.float32)
        for slot in range(3):
            total += z_recv[slot].astype(jnp.float32)
        gexp_ref[dp] = total.astype(jnp.bfloat16)

    f_copy = send(gexp_ref.at[dp], gexp_ref.at[dp], f_sems.at[0], f_sems.at[1], twin)
    moment[0].wait()
    mat_ref[0] = DECAY * mexp_ref[...] + gexp_ref[dp].astype(jnp.float32)
    exp_copies = gram_start(0, mat_ref[0])
    for copy in p_copies:
        copy.wait()
    total = piece_send[expert].astype(jnp.float32)
    for at in range(n_exp - 1):
        total += piece_recv[at].astype(jnp.float32)
    whole_ref[dp, expert] = total.astype(jnp.bfloat16)
    p_copies = to_each(
        z_ids,
        lambda at, partner: whole_ref.at[dp, expert],
        lambda at, partner: whole_ref.at[dp, expert],
        w_sems,
    )
    for copy in p_copies:
        copy.wait()
    w_copy = send(whole_ref.at[dp], whole_ref.at[dp], f_sems.at[2], f_sems.at[3], twin)
    exp_copies = gram_middle(0, exp_copies)
    for copy in s_copies:
        copy.wait()
    total = small_z[0]
    for place in range(1, n_exp):
        total += small_z[place]
    sums_ref[...] = total
    lane_part = pl.ds(pl.multiple_of(ctx * cols, cols), cols)
    fresh_norm = DECAY * mnorm_ref[...] + sums_ref[0:4, lane_part]
    fresh_router = DECAY * mrouter_ref[...] + sums_ref[pl.ds(8 + ctx, 1)]
    row = lax.broadcasted_iota(jnp.int32, (8, LANES), 0)
    squares_ref[ctx] = jnp.where(
        row == 0,
        jnp.sum(fresh_norm * fresh_norm, keepdims=True),
        jnp.sum(fresh_router * fresh_router, keepdims=True),
    )
    n_copies = to_each(
        ctx_ids,
        lambda at, partner: squares_ref.at[ctx],
        lambda at, partner: squares_ref.at[ctx],
        n_sems.at[1],
    )
    w_copy.wait()
    take("mqkv", "mproj")
    grad = whole_ref[...].reshape(width, width).astype(jnp.float32)
    mat_ref[1, :, : 3 * cols] = DECAY * mqkv_ref[...] + grad[:, : 3 * cols]
    mat_ref[2, :, :cols] = DECAY * mproj_ref[...] + grad[:, 3 * cols :]
    mat_ref[2, :, cols : 3 * cols] = jnp.zeros((width, 2 * cols), jnp.float32)
    shared_copies = [gram_start(1, mat_ref[1 + dp, :, : 3 * cols])]
    for copy in exp_copies:
        copy.wait()
    exp_scale = gram_whole(gathered_ref.at[0], high_ref, low_ref)
    orthogonal(high_ref, low_ref, mix_ref, total_ref)
    exp_step = step_of(0, mat_ref[0], exp_scale)
    shared_copies[0] = gram_middle(1, shared_copies[0])
    for copy in shared_copies[0]:
        copy.wait()
    shared_scale = gram_whole(gathered_ref.at[1], high_ref, low_ref)
    orthogonal(high_ref, low_ref, mix_ref, total_ref)
    shared_step = step_of(1, mat_ref[1 + dp, :, : 3 * cols], shared_scale)
    take("out")
    for copy in out_copies:
        copy.wait()
    for step in range(n_ctx):
        start = ctx_partner(ctx, step) * own_images
        for image in range(own_images):
            total = out_own[step, image].astype(jnp.float32)
            for at in range(n_ctx - 1):
                total += out_recv[ctx_partner(ctx, at + 1), start + image].astype(jnp.float32)
            out_ref[start + image] = total.astype(jnp.bfloat16)
    for copy in dx_copies + n_copies + [f_copy, exp_step, shared_step]:
        copy.wait()


def finish_kernel(
    experts,
    n_ctx,
    width,
    ctx_ref,
    gexp_ref,
    step_ref,
    whole_ref,
    sums_ref,
    squares_ref,
    dx_in,
    out_in,
    min_ref,
    mout_ref,
    mqkv_ref,
    mproj_ref,
    mnorm_ref,
    mrouter_ref,
    win_ref,
    wout_ref,
    wqkv_ref,
    wproj_ref,
    norm_ref,
    router_ref,
    o_out,
    o_dx,
    o_gnorm,
    o_grouter,
    o_gqkv,
    o_gproj,
    o_gin,
    o_gout,
    o_mnorm,
    o_mrouter,
    o_mqkv,
    o_mproj,
    o_min,
    o_mout,
    o_nnorm,
    o_nrouter,
    o_nqkv,
    o_nproj,
    o_nin,
    o_nout,
    o_bqkv,
    o_bproj,
    o_bin,
    o_bout,
):
    cols = width // n_ctx
    o_out[...] = out_in[...]
    o_dx[...] = dx_in[...].astype(jnp.float32)

    def update(grad, moment, weight, step, columns, outs):
        o_g, o_m, o_n, o_b = outs
        rate = RATE_MAT * 0.2 * math.sqrt(max(width, columns))
        new = weight.astype(jnp.float32) - rate * step.astype(jnp.float32)
        o_g[...] = grad.reshape(o_g.shape)
        o_m[...] = (DECAY * moment + grad).reshape(o_m.shape)
        o_n[...] = new.reshape(o_n.shape)
        o_b[...] = new.astype(jnp.bfloat16).reshape(o_b.shape)

    for index, outs in enumerate(((o_gin, o_min, o_nin, o_bin), (o_gout, o_mout, o_nout, o_bout))):
        update(
            gexp_ref[index].astype(jnp.float32),
            (min_ref, mout_ref)[index][0],
            (win_ref, wout_ref)[index][0],
            step_ref[0, index],
            n_ctx * gexp_ref.shape[2],
            outs,
        )
    grad = whole_ref[...].astype(jnp.float32)
    update(
        grad[:, : 3 * cols],
        mqkv_ref[...],
        wqkv_ref[...],
        step_ref[1, 0, :, : 3 * cols],
        3 * width,
        (o_gqkv, o_mqkv, o_nqkv, o_bqkv),
    )
    update(
        grad[:, 3 * cols :],
        mproj_ref[...],
        wproj_ref[...],
        step_ref[1, 1, :, :cols],
        width,
        (o_gproj, o_mproj, o_nproj, o_bproj),
    )
    ctx = ctx_ref[0]
    own_norm = sums_ref[0:4, pl.ds(pl.multiple_of(ctx * cols, cols), cols)]
    own_router = sums_ref[pl.ds(8 + ctx, 1)]
    fresh_norm = DECAY * mnorm_ref[...] + own_norm
    fresh_router = DECAY * mrouter_ref[...] + own_router
    o_gnorm[...] = own_norm
    o_grouter[...] = own_router
    o_mnorm[...] = fresh_norm
    o_mrouter[...] = fresh_router
    squares = squares_ref[0]
    for place in range(1, n_ctx):
        squares += squares_ref[place]
    o_nnorm[...] = norm_ref[...] - (
        RATE_GAIN * fresh_norm * lax.rsqrt(squares[0:1] / (4 * width) + EPS_NORM)
    )
    o_nrouter[...] = router_ref[pl.ds(ctx, 1)] - RATE_ROUTER * fresh_router * lax.rsqrt(
        squares[1:2, 0:1] / (width * experts) + EPS_NORM
    )


def call(kernel, ident, outs, scratch, operands, spaces, out_spaces=None):
    out_spaces = out_spaces or [pltpu.VMEM] * len(outs)
    return pl.pallas_call(
        kernel,
        out_shape=[jax.ShapeDtypeStruct(shape, dtype) for shape, dtype in outs],
        in_specs=[pl.BlockSpec(memory_space=space) for space in spaces],
        out_specs=[pl.BlockSpec(memory_space=space) for space in out_spaces],
        scratch_shapes=scratch,
        compiler_params=pltpu.CompilerParams(
            collective_id=ident, has_side_effects=True, vmem_limit_bytes=VMEM_LIMIT
        ),
    )(*operands)


def gathered(
    x_in,
    d_out,
    key_mask,
    expert_ids,
    norm_params,
    w_qkv,
    w_proj,
    w_router,
    w_in,
    w_out,
    mom_norm,
    mom_router,
    mom_qkv,
    mom_proj,
    mom_in,
    mom_out,
):
    n_exp = lax.axis_size("expert")
    n_ctx = lax.axis_size("ctx")
    ctx = lax.axis_index("ctx")
    images, seq_dev, width = x_in.shape
    experts = w_router.shape[1]
    own_images = images // n_ctx
    seq = n_ctx * seq_dev
    rows = own_images * seq
    hid = w_in.shape[2]
    low, full = jnp.bfloat16, jnp.float32
    dma = lambda *shape: pltpu.SemaphoreType.DMA(shape)
    vmem = lambda shape, dtype: pltpu.VMEM(shape, dtype)

    vm, anywhere = pltpu.VMEM, pl.ANY
    block = (own_images, n_ctx, seq_dev, width)
    kept = [
        (block, low),
        ((rows, width), low),
        ((rows, 3 * width), low),
        ((rows, LANES), full),
        ((rows, width), low),
        ((rows, width), full),
        (block, low),
        ((n_ctx,) + block, low),
        ((rows, width), full),
        ((n_exp, width, hid), low),
        ((8, width), full),
    ]
    router_turned = w_router.T
    (x_all, first, qkv, lse, att, mid, d_own, out_parts, dsecond, grads, grouter) = call(
        functools.partial(forward_kernel, n_exp, experts),
        1,
        kept,
        [vmem(*kept[at]) for at in range(6)]
        + [vmem((2,) + block, low), vmem((rows, width), full)]
        + [
            vmem((n_exp, width, hid), low),
            vmem((8, width), full),
            vmem((n_ctx,) + block, low),
            vmem((2, n_exp, width, hid), low),
            vmem((n_ctx, own_images, seq, width), low),
            vmem((images, 8, LANES), full),
            vmem((n_ctx, images, 8, LANES), full),
            vmem((width, 3 * width), low),
            vmem((width, width), low),
            vmem((2, LANES, width), full),
            vmem((n_ctx - 1, rows, width), low),
            vmem((n_ctx - 1, rows, width), low),
            vmem((2, rows, width), full),
            vmem((2, rows, width), full),
            vmem((2, n_ctx * rows, LANES), low),
            vmem((n_ctx, rows, LANES), full),
            vmem((n_ctx, rows, LANES), full),
            vmem((width, n_ctx * rows), low),
            vmem((width, n_ctx * rows), low),
            vmem((n_exp, n_ctx * rows, hid), low),
            vmem((n_exp, n_ctx * rows, hid), low),
            dma(2, own_images, n_ctx - 1),
            dma(2, n_ctx - 1),
            dma(2, n_ctx - 1, n_ctx),
            dma(2, 2, 2),
            dma(2, n_ctx - 1),
            dma(2, 2, n_ctx),
            dma(2, 2),
            dma(2, n_exp - 1, 2),
            dma(2, n_exp - 1, 2),
            dma(2, n_exp),
            dma(6),
            dma(15 + n_exp),
        ],
        (
            x_in,
            d_out.reshape(n_ctx, own_images, seq_dev, width),
            expert_ids.swapaxes(1, 2),
            key_mask,
            w_in,
            w_out,
            norm_params,
            w_qkv,
            w_proj,
            router_turned,
        ),
        [anywhere, anywhere, vm, vm, anywhere, anywhere, vm, anywhere, anywhere, vm],
        [anywhere] * 11,
    )
    cols = width // n_ctx
    blocks = (width // LANES) * (width // LANES + 1) // 2
    block_rows = LANES // n_ctx
    quarter = (n_exp, width // 2 // n_exp, width)
    moments = (mom_in, mom_out, mom_qkv, mom_proj, mom_norm, mom_router.reshape(1, width))
    out_low, dx_low, gexp, steps, whole, sums, squares = call(
        functools.partial(backward_kernel, n_exp),
        2,
        [
            ((images, seq_dev, width), low),
            ((images, seq_dev, width), low),
            ((2, width, hid), low),
            ((2, 2, width, hid), low),
            ((2,) + quarter, low),
            ((16, width), full),
            ((n_ctx, 8, LANES), full),
        ],
        [
            vmem((rows, width), low),
            vmem((rows, width), low),
            vmem((rows, width), low),
            vmem((rows, 3 * width), low),
            vmem((rows, LANES), full),
            vmem((rows, width), low),
            vmem((rows, width), full),
            vmem((rows, width), full),
            vmem((width, hid), low),
            vmem((width, hid), low),
            vmem((width, 3 * width), low),
            vmem((width, width), low),
            vmem((n_ctx, own_images, seq_dev, width), low),
            vmem((width, hid), full),
            vmem((width, 3 * cols), full),
            vmem((width, cols), full),
            vmem((n_ctx, images, seq_dev, width), low),
            vmem((n_exp, width, hid), low),
            vmem((rows, width), full),
            vmem((rows, width), low),
            vmem((rows, width), low),
            vmem((rows, 3 * width), low),
            vmem(block, low),
            vmem((n_ctx, width, width), low),
            vmem((n_ctx, width // 2, width), low),
            vmem((n_ctx, width // 2, width), low),
            vmem((n_ctx - 1, width // 2, width), low),
            vmem(quarter, low),
            vmem((n_exp - 1,) + quarter[1:], low),
            vmem((3, width, hid), full),
            vmem((2, blocks, n_ctx, block_rows, LANES), full),
            vmem((2, n_ctx - 1, blocks, block_rows, LANES), full),
            vmem((2, blocks, n_ctx, block_rows, LANES), full),
            vmem((width, width), low),
            vmem((width, width), low),
            vmem((width, width), low),
            vmem((width, width), full),
            vmem((16, width), full),
            vmem((16, width), full),
            vmem((n_ctx, 16, width), full),
            vmem((n_exp, 16, width), full),
            dma(17),
            dma(n_ctx, 2, n_ctx - 1),
            dma(2, n_exp),
            dma(4),
            dma(2, n_ctx - 1),
            dma(2, 3),
            dma(2, 2, n_ctx - 1),
            dma(2, n_ctx - 1),
            dma(2, n_exp - 1),
            dma(2, n_exp - 1),
            dma(2, 2, n_ctx - 1),
            dma(2, 2, n_ctx - 1),
            dma(2, 2),
            dma(2, 2, max(n_ctx, n_exp) - 1),
        ],
        (
            x_all.reshape(rows, width),
            d_own.reshape(rows, width),
            first,
            qkv,
            lse,
            att,
            mid,
            dsecond,
            grads,
            grouter,
            norm_params,
            w_qkv,
            w_proj,
            out_parts,
        )
        + moments,
        [anywhere] * 9 + [vm, vm] + [anywhere] * 7 + [vm, vm],
    )
    pieces = ((4, cols), (1, width), (width, 3 * cols), (width, cols), (1, width, hid), (1, width, hid))
    parts = width // LANES
    outs = (
        [((images, seq_dev, width), low), ((images, seq_dev, width), full)]
        + [(piece, full) for piece in pieces * 3]
        + [(piece, low) for piece in pieces[2:]]
    )

    def strip(shape, axis, last=None):
        def index_map(at, ctx_ref):
            place = [0] * len(shape)
            if axis is not None:
                place[axis] = at
            if last is not None:
                place[-1] = ctx_ref[0]
            return tuple(place)

        size = list(shape)
        if axis is not None:
            size[axis] //= parts
        if last is not None:
            size[-1] = last
        return pl.BlockSpec(tuple(size), index_map)

    def strips(shape):
        if len(shape) == 3:
            return strip(shape, 0 if shape[0] == images else 1)
        return strip(shape, 0 if shape[0] == width else None)

    results = pl.pallas_call(
        functools.partial(finish_kernel, experts, n_ctx, width),
        out_shape=[jax.ShapeDtypeStruct(shape, dtype) for shape, dtype in outs],
        grid_spec=pltpu.PrefetchScalarGridSpec(
            num_scalar_prefetch=1,
            grid=(parts,),
            in_specs=[
                strip((2, width, hid), 1),
                strip((2, 2, width, hid), 2),
                strip((width, width), 0),
                strip((16, width), None),
                strip((n_ctx, 8, LANES), None),
                strip((images, seq_dev, width), 0),
                strip((images, seq_dev, width), 0),
                strip((1, width, hid), 1),
                strip((1, width, hid), 1),
                strip((width, 3 * cols), 0),
                strip((width, cols), 0),
                strip((4, cols), None),
                strip((1, width), None),
                strip((1, width, hid), 1),
                strip((1, width, hid), 1),
                strip((width, 3 * width), 0, 3 * cols),
                strip((width, width), 0, cols),
                strip((4, width), None, cols),
                strip((experts, width), None),
            ],
            out_specs=[strips(shape) for shape, _ in outs],
        ),
        compiler_params=pltpu.CompilerParams(vmem_limit_bytes=VMEM_LIMIT),
    )(
        ctx.reshape(1),
        gexp,
        steps,
        whole.reshape(width, width),
        sums,
        squares,
        dx_low,
        out_low,
        *moments,
        w_in,
        w_out,
        w_qkv,
        w_proj,
        norm_params,
        router_turned,
    )
    return tuple(
        value.reshape(width, 1) if value.shape == (1, width) else value for value in results
    )


def solution(mesh):
    in_specs = (
        P(("expert", "dp"), "ctx", None),
        P(("expert", "dp"), "ctx", None),
        P(("expert", "dp"), "ctx"),
        P(("expert", "dp"), "ctx", None),
        P(),
        P(),
        P(),
        P(),
        P("expert", None, "ctx"),
        P("expert", None, "ctx"),
        P(None, "ctx"),
        P(None, "ctx"),
        P(None, "ctx"),
        P(None, "ctx"),
        P("expert", None, "ctx"),
        P("expert", None, "ctx"),
    )
    out_specs = (
        P(("expert", "dp"), "ctx", None),
        P(("expert", "dp"), "ctx", None),
        P(None, "ctx"),
        P(None, "ctx"),
        P(None, "ctx"),
        P(None, "ctx"),
        P("expert", None, "ctx"),
        P("expert", None, "ctx"),
        P(None, "ctx"),
        P(None, "ctx"),
        P(None, "ctx"),
        P(None, "ctx"),
        P("expert", None, "ctx"),
        P("expert", None, "ctx"),
        P(None, "ctx"),
        P(None, "ctx"),
        P(None, "ctx"),
        P(None, "ctx"),
        P("expert", None, "ctx"),
        P("expert", None, "ctx"),
        P(None, "ctx"),
        P(None, "ctx"),
        P("expert", None, "ctx"),
        P("expert", None, "ctx"),
    )
    experts = mesh.shape["expert"]
    square = mesh.shape["ctx"] == 4 and mesh.shape["dp"] == 2

    def local(*arrays):
        whole = (
            square
            and arrays[7].shape[1] == experts <= 7
            and arrays[8].shape[0] == 1
            and 2 * arrays[0].shape[1] == LANES
        )
        return (gathered if whole else exchanged)(*arrays)

    return jax.shard_map(local, mesh=mesh, in_specs=in_specs, out_specs=out_specs, check_vma=False)
```

```python
import functools
import math

import jax
import jax.numpy as jnp
from jax import lax
from jax.experimental import pallas as pl
from jax.experimental.pallas import tpu as pltpu
from jax.sharding import PartitionSpec as P

HEADS = 8
HEAD_DIM = 64
MICRO = 2
NS_ITERS = 4


HIGH = lax.Precision.HIGHEST
NS_A = 3.4445
NS_B = -4.775
NS_C = 2.0315
DECAY = 0.5
RATE_MAT = 0.3
RATE_GAIN = 0.3
RATE_ROUTER = 0.05
EPS_NORM = 1e-06
EPS_ORTHO = 1e-07
NEG = -1e30
LANES = 128
VMEM_LIMIT = 60 * 2**20
MESH = pl.DeviceIdType.MESH


def as_sent(array):
    return jax.tree.map(lambda a: a.astype(jnp.bfloat16) if a.dtype == jnp.float32 else a, array)


def layer_norm(values, gain, shift):
    center = jnp.mean(values, axis=-1, keepdims=True)
    spread = values - center
    power = jnp.mean(spread * spread, axis=-1, keepdims=True)
    return spread * lax.rsqrt(power + EPS_NORM) * gain + shift


def gelu_exact(values):
    return jax.nn.gelu(values, approximate=False)


def add_block(total, piece):
    return total + piece


def masked_scores(query, key_piece, mask_piece, factor):
    scores = (
        jnp.einsum("bqhd,bkhd->bhqk", query, key_piece, preferred_element_type=jnp.float32) * factor
    )
    return jnp.where(mask_piece[:, None, None, :] > 0, scores, NEG)


def gram_list(matrices):
    return tuple(
        (jnp.einsum("...ik,...jk->...ij", matrix, matrix, precision=HIGH) for matrix in matrices)
    )


def schulz_turn(matrices, grams):
    result = []
    for matrix, gram in zip(matrices, grams):
        square = jnp.einsum("...ij,...jk->...ik", gram, gram, precision=HIGH)
        mixer = NS_B * gram + NS_C * square
        result.append(
            NS_A * matrix + jnp.einsum("...ij,...jk->...ik", mixer, matrix, precision=HIGH)
        )
    return tuple(result)


def exchanged(
    x_in,
    d_out,
    key_mask,
    expert_ids,
    norm_params,
    w_qkv,
    w_proj,
    w_router,
    w_in,
    w_out,
    mom_norm,
    mom_router,
    mom_qkv,
    mom_proj,
    mom_in,
    mom_out,
):
    ctx_count = lax.axis_size("ctx")
    ctx_place = lax.axis_index("ctx")
    owner_count = lax.axis_size("expert")
    local_images = x_in.shape[0]
    seq_dev = x_in.shape[1]
    width = x_in.shape[2]
    top_count = expert_ids.shape[-1]
    experts = w_router.shape[1]
    exp_dev = w_in.shape[0]
    hid_part = w_in.shape[2]
    capacity = max(2, (5 * top_count * seq_dev + 4 * experts - 1) // (4 * experts))
    batch = local_images // MICRO
    slot_count = batch * capacity
    seq_all = seq_dev * ctx_count
    factor = HEAD_DIM ** (-0.5)
    expert_iota = jnp.arange(experts, dtype=jnp.int32)
    recv_shape = (owner_count, exp_dev, slot_count, width)
    head_shape = (batch, seq_dev, HEADS, HEAD_DIM)

    def hidden_fold(step_fn, init):
        folded = step_fn(
            init,
            (
                lax.all_gather(w_in, "ctx", axis=2, tiled=True),
                lax.all_gather(w_out, "ctx", axis=2, tiled=True),
            ),
            jnp.int32(0),
        )
        return folded

    def to_owner(rows):
        return lax.all_to_all(rows, "expert", split_axis=0, concat_axis=0, tiled=True)

    def to_source(rows):
        return lax.all_to_all(rows, "expert", split_axis=0, concat_axis=0, tiled=True)

    def key_fold(keys, values, mask_low, step_fn, init):
        return step_fn(
            init,
            (
                lax.all_gather(keys, "ctx", axis=1, tiled=True),
                lax.all_gather(values, "ctx", axis=1, tiled=True),
                lax.all_gather(mask_low, "ctx", axis=1, tiled=True),
            ),
            jnp.int32(0),
        )

    grad_qkv = jnp.zeros(w_qkv.shape, jnp.float32)
    grad_proj = jnp.zeros(w_proj.shape, jnp.float32)
    grad_router = jnp.zeros(w_router.shape, jnp.float32)
    grad_norm = jnp.zeros((4, width), jnp.float32)
    grad_in = jnp.zeros((exp_dev, width, hid_part * ctx_count), jnp.float32)
    grad_out = jnp.zeros((exp_dev, width, hid_part * ctx_count), jnp.float32)
    outputs = []
    input_grads = []
    for micro_index in range(MICRO):
        first_image = micro_index * batch
        last_image = first_image + batch
        x_part = x_in[first_image:last_image].astype(jnp.float32)
        cotangent = d_out[first_image:last_image].astype(jnp.float32)
        mask_low = key_mask[first_image:last_image].astype(jnp.bfloat16)
        idents = expert_ids[first_image:last_image]
        normed_first, pull_first = jax.vjp(layer_norm, x_part, norm_params[0], norm_params[1])
        first_low = normed_first.astype(jnp.bfloat16).reshape(-1, width)
        qkv = jnp.dot(first_low, w_qkv, preferred_element_type=jnp.float32).astype(jnp.bfloat16)
        qkv = qkv.reshape(batch, seq_dev, 3, HEADS, HEAD_DIM)
        query = qkv[:, :, 0]
        keys = qkv[:, :, 1]
        values = qkv[:, :, 2]
        peak_old = jnp.full((batch, HEADS, seq_dev), NEG, jnp.float32)
        key_piece = lax.all_gather(keys, "ctx", axis=1, tiled=True)
        mask_piece = lax.all_gather(mask_low, "ctx", axis=1, tiled=True)
        scores = masked_scores(query, key_piece, mask_piece, factor)
        peak_new = jnp.maximum(peak_old, jnp.max(scores, axis=-1))
        total_new = jnp.sum(jnp.exp(scores - peak_new[..., None]), axis=-1)
        log_total = peak_new + jnp.log(total_new)

        def attend_step(acc, pieces, start):
            key_piece, value_piece, mask_piece = pieces
            weights = jnp.exp(
                masked_scores(query, key_piece, mask_piece, factor) - log_total[..., None]
            )
            return jnp.einsum(
                "bhqk,bkhd->bqhd",
                weights.astype(jnp.bfloat16),
                value_piece,
                preferred_element_type=jnp.float32,
            )

        attended = key_fold(keys, values, mask_low, attend_step, jnp.zeros(head_shape, jnp.float32))
        attended_low = attended.astype(jnp.bfloat16).reshape(-1, width)
        branch = jnp.dot(attended_low, w_proj, preferred_element_type=jnp.float32).reshape(
            batch, seq_dev, width
        )
        mid = x_part + branch
        normed_second, pull_second = jax.vjp(layer_norm, mid, norm_params[2], norm_params[3])
        routed_low = normed_second.astype(jnp.bfloat16)
        logits = jnp.einsum("bsd,de->bse", normed_second, w_router, precision=HIGH)
        onehot = (idents[..., None] == expert_iota).astype(jnp.float32)
        chosen = jnp.sum(onehot * logits[:, :, None, :], axis=-1)
        gates = jax.nn.softmax(chosen, axis=-1)
        flat_ids = idents.reshape(batch, seq_dev * top_count)
        hits = (flat_ids[..., None] == expert_iota).astype(jnp.int32)
        ranked = jnp.sum((jnp.cumsum(hits, axis=1) - hits) * hits, axis=-1)
        slot = (ranked + (jnp.arange(batch, dtype=jnp.int32) * capacity)[:, None]).reshape(-1)
        target = flat_ids.reshape(-1)
        routed_rows = jnp.broadcast_to(
            routed_low[:, :, None, :], (batch, seq_dev, top_count, width)
        ).reshape(-1, width)
        send = (
            jnp.zeros((experts, slot_count, width), jnp.bfloat16).at[target, slot].set(routed_rows)
        )
        received = to_owner(send.reshape(recv_shape))

        def expert_step(acc, pieces, start):
            piece_in, piece_out = pieces
            pre = jnp.einsum(
                "nesd,edh->nesh", received, piece_in, preferred_element_type=jnp.float32
            )
            act = gelu_exact(pre).astype(jnp.bfloat16)
            return jnp.einsum("nesh,edh->nesd", act, piece_out, preferred_element_type=jnp.float32)

        made = hidden_fold(expert_step, jnp.zeros(recv_shape, jnp.float32))
        back_rows = to_source(made.astype(jnp.bfloat16)).reshape(experts, slot_count, width)
        returned = (
            back_rows[target, slot].reshape(batch, seq_dev, top_count, width).astype(jnp.float32)
        )
        result = mid + jnp.sum(gates[..., None] * returned, axis=2)
        outputs.append(result.astype(jnp.bfloat16))
        dgates = jnp.sum(cotangent[:, :, None, :] * returned, axis=-1)
        dchosen = gates * (dgates - jnp.sum(gates * dgates, axis=-1, keepdims=True))
        dlogits = jnp.sum(dchosen[..., None] * onehot, axis=2)
        grad_router = grad_router + jnp.einsum(
            "bsd,bse->de", normed_second, dlogits, precision=HIGH
        )
        dsecond = jnp.einsum("bse,de->bsd", dlogits, w_router, precision=HIGH)
        dreturned = (
            (gates[..., None] * cotangent[:, :, None, :]).astype(jnp.bfloat16).reshape(-1, width)
        )
        dsend = (
            jnp.zeros((experts, slot_count, width), jnp.bfloat16).at[target, slot].set(dreturned)
        )
        dreceived = to_owner(dsend.reshape(recv_shape))

        def expert_back(carry, pieces, start):
            drows, dins, douts = carry
            piece_in, piece_out = pieces
            pre = jnp.einsum(
                "nesd,edh->nesh", received, piece_in, preferred_element_type=jnp.float32
            )
            act_full, pull_act = jax.vjp(gelu_exact, pre)
            act = act_full.astype(jnp.bfloat16)
            dact = jnp.einsum(
                "nesd,edh->nesh", dreceived, piece_out, preferred_element_type=jnp.float32
            )
            dpre = pull_act(dact)[0].astype(jnp.bfloat16)
            douts = add_block(
                douts,
                jnp.einsum("nesd,nesh->edh", dreceived, act, preferred_element_type=jnp.float32),
            )
            dins = add_block(
                dins,
                jnp.einsum("nesd,nesh->edh", received, dpre, preferred_element_type=jnp.float32),
            )
            drows = jnp.einsum("nesh,edh->nesd", dpre, piece_in, preferred_element_type=jnp.float32)
            return (drows, dins, douts)

        drows, grad_in, grad_out = hidden_fold(
            expert_back, (jnp.zeros(recv_shape, jnp.float32), grad_in, grad_out)
        )
        dback = to_source(drows.astype(jnp.bfloat16)).reshape(experts, slot_count, width)
        dsecond = dsecond + jnp.sum(
            dback[target, slot].reshape(batch, seq_dev, top_count, width).astype(jnp.float32),
            axis=2,
        )
        dmid, dgain_two, dshift_two = pull_second(dsecond)
        dmid = dmid + cotangent
        dbranch = dmid.astype(jnp.bfloat16).reshape(-1, width)
        grad_proj = grad_proj + jnp.einsum(
            "sd,se->de", attended_low, dbranch, preferred_element_type=jnp.float32
        )
        dattended = jnp.einsum("se,de->sd", dbranch, w_proj, preferred_element_type=jnp.float32)
        dattended = dattended.astype(jnp.bfloat16).reshape(head_shape)
        delta = jnp.einsum("bqhd,bqhd->bhq", dattended.astype(jnp.float32), attended)

        def attend_back(carry, pieces, start):
            dquery, dkeys, dvalues = carry
            key_piece, value_piece, mask_piece = pieces
            weights = jnp.exp(
                masked_scores(query, key_piece, mask_piece, factor) - log_total[..., None]
            )
            probs = weights.astype(jnp.bfloat16)
            dvalue_piece = jnp.einsum(
                "bhqk,bqhd->bkhd", probs, dattended, preferred_element_type=jnp.float32
            )
            dprobs = jnp.einsum(
                "bqhd,bkhd->bhqk", dattended, value_piece, preferred_element_type=jnp.float32
            )
            dscores = (weights * (dprobs - delta[..., None])).astype(jnp.bfloat16)
            dquery = factor * jnp.einsum(
                "bhqk,bkhd->bqhd", dscores, key_piece, preferred_element_type=jnp.float32
            )
            dkey_piece = factor * jnp.einsum(
                "bhqk,bqhd->bkhd", dscores, query, preferred_element_type=jnp.float32
            )
            return (dquery, add_block(dkeys, dkey_piece), add_block(dvalues, dvalue_piece))

        all_shape = (batch, seq_all, HEADS, HEAD_DIM)
        back_init = (
            jnp.zeros(head_shape, jnp.float32),
            jnp.zeros(all_shape, jnp.float32),
            jnp.zeros(all_shape, jnp.float32),
        )
        dquery, dkeys_all, dvalues_all = key_fold(keys, values, mask_low, attend_back, back_init)
        dkeys, dvalues = (
            lax.psum_scatter(
                dkeys_all.astype(jnp.bfloat16), "ctx", scatter_dimension=1, tiled=True
            ).astype(jnp.float32),
            lax.psum_scatter(
                dvalues_all.astype(jnp.bfloat16), "ctx", scatter_dimension=1, tiled=True
            ).astype(jnp.float32),
        )
        dqkv = (
            jnp.stack([dquery, dkeys, dvalues], axis=2).astype(jnp.bfloat16).reshape(-1, 3 * width)
        )
        grad_qkv = grad_qkv + jnp.einsum(
            "sd,se->de", first_low, dqkv, preferred_element_type=jnp.float32
        )
        dfirst = jnp.einsum("se,de->sd", dqkv, w_qkv, preferred_element_type=jnp.float32).reshape(
            batch, seq_dev, width
        )
        dx_part, dgain_one, dshift_one = pull_first(dfirst)
        grad_norm = grad_norm + jnp.stack([dgain_one, dshift_one, dgain_two, dshift_two])
        input_grads.append(dx_part + dmid)
    block_out = jnp.concatenate(outputs, axis=0)
    d_x = jnp.concatenate(input_grads, axis=0)
    shared = (
        lax.psum_scatter(
            grad_in.astype(jnp.bfloat16), "ctx", scatter_dimension=2, tiled=True
        ).astype(jnp.float32),
        lax.psum_scatter(
            grad_out.astype(jnp.bfloat16), "ctx", scatter_dimension=2, tiled=True
        ).astype(jnp.float32),
        lax.psum_scatter(
            grad_qkv[None].astype(jnp.bfloat16), "ctx", scatter_dimension=2, tiled=True
        ).astype(jnp.float32),
        lax.psum_scatter(
            grad_proj[None].astype(jnp.bfloat16), "ctx", scatter_dimension=2, tiled=True
        ).astype(jnp.float32),
        lax.psum_scatter(
            grad_norm[None].astype(jnp.bfloat16), "ctx", scatter_dimension=2, tiled=True
        ).astype(jnp.float32),
        lax.psum_scatter(
            grad_router[None].astype(jnp.bfloat16), "ctx", scatter_dimension=2, tiled=True
        ).astype(jnp.float32),
    )
    g_in, g_out = (
        lax.psum(shared[0].astype(jnp.bfloat16), "dp").astype(jnp.float32),
        lax.psum(shared[1].astype(jnp.bfloat16), "dp").astype(jnp.float32),
    )
    g_qkv, g_proj, g_norm, g_router = lax.psum(
        (shared[2][0], shared[3][0], shared[4][0], shared[5][0]), ("expert", "dp")
    )
    own_qkv = lax.dynamic_slice_in_dim(w_qkv, ctx_place * g_qkv.shape[1], g_qkv.shape[1], 1).astype(
        jnp.float32
    )
    own_proj = lax.dynamic_slice_in_dim(
        w_proj, ctx_place * g_proj.shape[1], g_proj.shape[1], 1
    ).astype(jnp.float32)
    own_norm = lax.dynamic_slice_in_dim(
        norm_params, ctx_place * g_norm.shape[1], g_norm.shape[1], 1
    )
    own_router = lax.dynamic_slice_in_dim(
        w_router, ctx_place * g_router.shape[1], g_router.shape[1], 1
    )
    m_qkv = DECAY * mom_qkv + g_qkv
    m_proj = DECAY * mom_proj + g_proj
    m_in = DECAY * mom_in + g_in
    m_out = DECAY * mom_out + g_out
    m_norm = DECAY * mom_norm + g_norm
    m_router = DECAY * mom_router + g_router
    matrices = (m_qkv, m_proj, m_in, m_out)
    vector_squares = (jnp.sum(m_norm * m_norm), jnp.sum(m_router * m_router))
    sums = lax.psum(
        tuple((jnp.sum(matrix * matrix, axis=(-2, -1)) for matrix in matrices)) + vector_squares,
        "ctx",
    )
    vector_totals = sums[4:]
    iterates = tuple(
        (
            matrix / jnp.expand_dims(jnp.sqrt(square) + EPS_ORTHO, (-2, -1))
            for matrix, square in zip(matrices, sums[:4])
        )
    )
    for turn_index in range(NS_ITERS):
        iterates = schulz_turn(
            iterates,
            jax.tree.map(
                lambda part: part.astype(jnp.float32), lax.psum(as_sent(gram_list(iterates)), "ctx")
            ),
        )
    n_qkv = (
        own_qkv - RATE_MAT * 0.2 * math.sqrt(max(width, g_qkv.shape[1] * ctx_count)) * iterates[0]
    )
    n_proj = (
        own_proj - RATE_MAT * 0.2 * math.sqrt(max(width, g_proj.shape[1] * ctx_count)) * iterates[1]
    )
    n_in = (
        w_in.astype(jnp.float32)
        - RATE_MAT * 0.2 * math.sqrt(max(width, hid_part * ctx_count)) * iterates[2]
    )
    n_out = (
        w_out.astype(jnp.float32)
        - RATE_MAT * 0.2 * math.sqrt(max(width, hid_part * ctx_count)) * iterates[3]
    )
    n_norm = own_norm - RATE_GAIN * m_norm * lax.rsqrt(vector_totals[0] / (4 * width) + EPS_NORM)
    n_router = own_router - RATE_ROUTER * m_router * lax.rsqrt(
        vector_totals[1] / (width * experts) + EPS_NORM
    )
    return (
        block_out,
        d_x,
        g_norm,
        g_router,
        g_qkv,
        g_proj,
        g_in,
        g_out,
        m_norm,
        m_router,
        m_qkv,
        m_proj,
        m_in,
        m_out,
        n_norm,
        n_router,
        n_qkv,
        n_proj,
        n_in,
        n_out,
        n_qkv.astype(jnp.bfloat16),
        n_proj.astype(jnp.bfloat16),
        n_in.astype(jnp.bfloat16),
        n_out.astype(jnp.bfloat16),
    )


def dot(left, right, precision=None):
    return jnp.dot(left, right, precision=precision, preferred_element_type=jnp.float32)


def dot_nt(left, right, precision=None):
    return lax.dot_general(
        left, right, (((1,), (1,)), ((), ())), precision=precision, preferred_element_type=jnp.float32
    )


def dot_tn(left, right, precision=None):
    return lax.dot_general(
        left, right, (((0,), (0,)), ((), ())), precision=precision, preferred_element_type=jnp.float32
    )


def places():
    return lax.axis_index("expert"), lax.axis_index("ctx"), lax.axis_index("dp")


def ctx_partner(ctx, step):
    column, row = lax.rem(ctx, 2), ctx // 2
    column = lax.rem(column + lax.rem(step, 2), 2)
    row = lax.rem(row + step // 2, 2)
    return row * 2 + column


def z_partner(expert, step, count):
    return lax.rem(expert + step, count)


def greet(partners):
    for partner in partners:
        pl.semaphore_signal(
            pltpu.get_barrier_semaphore(), inc=1, device_id=partner, device_id_type=MESH
        )


def await_greetings(partners):
    pl.semaphore_wait(pltpu.get_barrier_semaphore(), len(partners))


def send(source, target, send_sem, recv_sem, partner):
    copy = pltpu.make_async_remote_copy(
        src_ref=source,
        dst_ref=target,
        send_sem=send_sem,
        recv_sem=recv_sem,
        device_id=partner,
        device_id_type=MESH,
    )
    copy.start()
    return copy


def normalize(values):
    center = jnp.mean(values, axis=-1, keepdims=True)
    spread = values - center
    power = jnp.mean(spread * spread, axis=-1, keepdims=True)
    scale = lax.rsqrt(power + EPS_NORM)
    return spread * scale, scale


def normalize_back(grad, unit, scale):
    first = jnp.mean(grad, axis=-1, keepdims=True)
    second = jnp.mean(grad * unit, axis=-1, keepdims=True)
    return scale * (grad - first - unit * second)


def group_rows(meta_ref, image):
    pairs = [
        meta_ref[2 * half, image] + meta_ref[2 * half + 1, image]
        for half in range(meta_ref.shape[0] // 2)
    ]
    return jnp.concatenate(pairs, axis=1)


def split(values):
    high = values.astype(jnp.bfloat16)
    return high, (values - high.astype(jnp.float32)).astype(jnp.bfloat16)


def gelu_parts(values):
    cdf = 0.5 + 0.5 * lax.erf(values * (0.5**0.5))
    return cdf, jnp.exp(-0.5 * values * values) * (1.0 / math.sqrt(2 * math.pi))


def forward_kernel(
    n_exp,
    experts,
    x_ref,
    d_ref,
    ids_ref,
    mask_ref,
    win_ref,
    wout_ref,
    norm_ref,
    wqkv_hbm,
    wproj_hbm,
    wrouter_ref,
    o_x,
    o_first,
    o_qkv,
    o_lse,
    o_att,
    o_mid,
    o_d,
    o_out,
    o_dsecond,
    o_grads,
    o_grouter,
    x_all,
    first_ref,
    qkv_ref,
    lse_ref,
    att_ref,
    mid_ref,
    out_send,
    dsecond_ref,
    grads_recv,
    grouter_ref,
    d_all,
    w_all,
    r_all,
    meta_ref,
    meta_all,
    wqkv_ref,
    wproj_ref,
    router_ref,
    ds_send,
    ds_recv,
    acc_out,
    acc_ds,
    dlogits_ref,
    gates_ref,
    dgates_ref,
    r_turn,
    d_turn,
    act_all,
    dpre_all,
    x_sems,
    m_sems,
    d_sems,
    r_sems,
    ds_sems,
    dr_sems,
    rr_sems,
    z_sems,
    s_sems,
    t_sems,
    own_sem,
    o_sems,
):
    expert, ctx, dp = places()
    own_images, n_ctx, seq_dev, width = x_all.shape
    seq = n_ctx * seq_dev
    rows = own_images * seq
    ctx_ids = [(expert, ctx_partner(ctx, step), dp) for step in range(1, n_ctx)]
    side_ids = ctx_ids[:2]
    twin = (expert, ctx, 1 - dp)
    right, left = lax.rem(expert + 1, n_exp), lax.rem(expert + n_exp - 1, n_exp)
    greeted = ctx_ids + [(right, ctx, dp), (left, ctx, dp), twin]
    greet(greeted)
    row = lax.broadcasted_iota(jnp.int32, (8, seq_dev), 0)
    odd = lax.rem(ctx, 2).astype(jnp.float32)
    for image in range(ids_ref.shape[0]):
        named = jnp.zeros((8, seq_dev), jnp.bool_)
        for choice in range(ids_ref.shape[1]):
            named = named | (ids_ref[image, choice : choice + 1] == row)
        values = jnp.where(
            row == experts, mask_ref[image : image + 1].astype(jnp.float32), named.astype(jnp.float32)
        )
        meta_ref[image, :, :seq_dev] = values * (1.0 - odd)
        meta_ref[image, :, seq_dev:] = values * odd
    router_ref[...] = jnp.zeros_like(router_ref)
    router_high, router_low = split(wrouter_ref[...])
    router_ref[0, :experts] = router_high.astype(jnp.float32)
    router_ref[1, :experts] = router_low.astype(jnp.float32)
    own = [
        pltpu.make_async_copy(source, target, own_sem.at[at])
        for at, (source, target) in enumerate(
            (
                (win_ref.at[0], w_all.at[0, expert]),
                (wout_ref.at[0], w_all.at[1, expert]),
                (x_ref.at[pl.ds(ctx * own_images, own_images)], x_all.at[:, ctx]),
                (wqkv_hbm, wqkv_ref),
                (wproj_hbm, wproj_ref),
                (d_ref, d_all.at[:, :, ctx]),
            )
        )
    ]
    for copy in own:
        copy.start()
    meta_all[ctx] = meta_ref[...]
    await_greetings(greeted)
    x_copies = []
    for image in range(own_images):
        x_copies.append(
            [
                send(
                    x_ref.at[partner[1] * own_images + image],
                    x_all.at[image, ctx],
                    x_sems.at[0, image, at],
                    x_sems.at[1, image, at],
                    partner,
                )
                for at, partner in enumerate(ctx_ids)
            ]
        )
        if image == 0:
            m_copies = [
                send(meta_ref, meta_all.at[ctx], m_sems.at[0, at], m_sems.at[1, at], partner)
                for at, partner in enumerate(ctx_ids)
            ]

    def hop(phase, side):
        share = expert - phase if side == 0 else expert + phase
        able = (share >= 0) & (expert < n_exp - 1) if side == 0 else (share < n_exp) & (expert > 0)
        share = jnp.clip(share, 0, n_exp - 1)
        return able, pltpu.make_async_remote_copy(
            src_ref=w_all.at[dp, share],
            dst_ref=w_all.at[dp, share],
            send_sem=z_sems.at[0, phase, side],
            recv_sem=z_sems.at[1, phase, side],
            device_id=(right if side == 0 else left, ctx, dp),
            device_id_type=MESH,
        )

    def landed(phase, side):
        share = expert - 1 - phase if side == 0 else expert + 1 + phase
        able = share >= 0 if side == 0 else share < n_exp
        share = jnp.clip(share, 0, n_exp - 1)
        place = w_all.at[dp, share]
        return (
            able,
            pltpu.make_async_remote_copy(
                src_ref=place,
                dst_ref=place,
                send_sem=z_sems.at[0, phase, side],
                recv_sem=z_sems.at[1, phase, side],
                device_id=(left if side == 0 else right, ctx, dp),
                device_id_type=MESH,
            ),
            pltpu.make_async_remote_copy(
                src_ref=place,
                dst_ref=place,
                send_sem=s_sems.at[0, phase, side],
                recv_sem=s_sems.at[1, phase, side],
                device_id=twin,
                device_id_type=MESH,
            ),
        )

    def start_hops(phase):
        for side in range(2):
            able, copy = hop(phase, side)
            pl.when(able)(copy.start)

    def take_hops(phase):
        for side in range(2):
            able, copy, shared = landed(phase, side)

            @pl.when(able)
            def _():
                copy.wait_recv()
                shared.start()

    def take_shared(phase):
        for side in range(2):
            able, _, shared = landed(phase, side)
            pl.when(able)(shared.wait_recv)

    own[0].wait()
    own[1].wait()
    start_hops(0)
    for copy in own[2:]:
        copy.wait()

    def d_copy(at, order):
        group = ctx_partner(ctx_ids[at][1], order)
        return pltpu.make_async_remote_copy(
            src_ref=d_ref.at[group],
            dst_ref=d_all.at[group, :, ctx],
            send_sem=d_sems.at[0, at, order],
            recv_sem=d_sems.at[1, at, order],
            device_id=ctx_ids[at],
            device_id_type=MESH,
        )

    def d_relay(image, order):
        target = side_ids[1 - image]
        place = d_all.at[ctx_partner(target[1], order), image, side_ids[image][1]]
        return pltpu.make_async_remote_copy(
            src_ref=place,
            dst_ref=place,
            send_sem=dr_sems.at[0, image, order],
            recv_sem=dr_sems.at[1, image, order],
            device_id=target,
            device_id_type=MESH,
        )

    def r_copy(at, image):
        return pltpu.make_async_remote_copy(
            src_ref=r_all.at[ctx, image],
            dst_ref=r_all.at[ctx, image],
            send_sem=r_sems.at[0, at, image],
            recv_sem=r_sems.at[1, at, image],
            device_id=side_ids[at],
            device_id_type=MESH,
        )

    def r_relay(image):
        place = r_all.at[side_ids[image][1], image]
        return pltpu.make_async_remote_copy(
            src_ref=place,
            dst_ref=place,
            send_sem=rr_sems.at[0, image],
            recv_sem=rr_sems.at[1, image],
            device_id=side_ids[1 - image],
            device_id_type=MESH,
        )

    for at in range(n_ctx - 1):
        d_copy(at, 0).start()
    for copy in x_copies[0] + m_copies:
        copy.wait()
    for order in (3, 1):
        for at in range(2):
            d_copy(at, order).start()
    lane = lax.broadcasted_iota(jnp.int32, (seq, LANES), 1)
    low_half = lane < HEAD_DIM
    for image in range(own_images):
        part = pl.ds(image * seq, seq)
        if image > 0:
            for copy in x_copies[image]:
                copy.wait()
        values = x_all[image].reshape(seq, width).astype(jnp.float32)
        unit, _ = normalize(values)
        first = (unit * norm_ref[0:1] + norm_ref[1:2]).astype(jnp.bfloat16)
        first_ref[part] = first
        qkv_ref[part] = dot(first, wqkv_ref[...]).astype(jnp.bfloat16)
        key_mask = group_rows(meta_all, ctx * own_images + image)[experts : experts + 1]
        bias = jnp.where(key_mask > 0, 0.0, NEG)
        column = jnp.broadcast_to(bias, (LANES, seq)).T
        totals = jnp.where(lane == HEADS, column, 0.0)
        for pair in range(HEADS // 2):
            query = qkv_ref[part, pair * LANES : (pair + 1) * LANES]
            keys = qkv_ref[part, width + pair * LANES : width + (pair + 1) * LANES]
            heads = qkv_ref[part, 2 * width + pair * LANES : 2 * width + (pair + 1) * LANES]
            query = query * jnp.bfloat16(HEAD_DIM**-0.5)
            parts = []
            for half in range(2):
                chosen = low_half if half == 0 else ~low_half
                scores = dot_nt(jnp.where(chosen, query, jnp.zeros_like(query)), keys) + bias
                peak = jnp.max(scores, axis=-1, keepdims=True)
                raised = jnp.exp(scores - peak)
                total = jnp.sum(raised, axis=-1, keepdims=True)
                probs = (raised * (1.0 / total)).astype(jnp.bfloat16)
                parts.append(dot(probs, heads))
                totals = jnp.where(lane == 2 * pair + half, peak + jnp.log(total), totals)
            att_ref[part, pair * LANES : (pair + 1) * LANES] = jnp.where(
                low_half, parts[0], parts[1]
            ).astype(jnp.bfloat16)
        lse_ref[part] = totals
        mid = values + dot(att_ref[part], wproj_ref[...])
        mid_ref[part] = mid
        unit, _ = normalize(mid)
        r_all[ctx, image] = (unit * norm_ref[2:3] + norm_ref[3:4]).astype(jnp.bfloat16)
        for at in range(2):
            r_copy(at, image).start()
        if image == own_images - 1:
            take_hops(0)
            start_hops(1)
            for at in range(2):
                d_copy(at, 2).start()

    kept_copies = [
        pltpu.make_async_copy(source, target, o_sems.at[at])
        for at, (source, target) in enumerate(
            (
                (x_all, o_x),
                (first_ref, o_first),
                (qkv_ref, o_qkv),
                (lse_ref, o_lse),
                (att_ref, o_att),
                (mid_ref, o_mid),
            )
        )
    ]
    for copy in kept_copies:
        copy.start()

    def out_copy(chunk):
        return pltpu.make_async_copy(
            out_send.at[chunk % 2], o_out.at[chunk], o_sems.at[8 + chunk]
        )

    wide = lax.broadcasted_iota(jnp.int32, (rows, LANES), 1)
    near = jnp.where(expert < n_exp // 2, expert + 1, expert - 1)
    last = jnp.where(expert < n_exp // 2, n_exp - 1, 0)
    middle = n_exp * (n_exp - 1) // 2 - expert - near - last

    def start_chunk(chunk, owner):
        routed = r_all[owner].reshape(rows, width)
        present = jnp.concatenate(
            [group_rows(meta_all, owner * own_images + image) for image in range(own_images)], axis=1
        )
        present = jnp.concatenate(
            [present, jnp.zeros((LANES - present.shape[0], rows), jnp.float32)], axis=0
        ).T
        present = (present > 0) & (wide < experts)
        logits = dot_nt(routed, router_ref[0].astype(jnp.bfloat16)) + dot_nt(
            routed, router_ref[1].astype(jnp.bfloat16)
        )
        peak = jnp.max(jnp.where(present, logits, NEG), axis=-1, keepdims=True)
        raised = jnp.where(present, jnp.exp(jnp.where(present, logits - peak, 0.0)), 0.0)
        gates_ref[chunk] = raised / jnp.sum(raised, axis=-1, keepdims=True)
        dgates_ref[chunk] = jnp.zeros((rows, LANES), jnp.float32)

    def end_chunk(chunk):
        slot = (0, 1, 2, 1)[chunk]
        gates = gates_ref[chunk]
        dgates = jnp.where(gates > 0, dgates_ref[chunk], 0.0)
        dlogits = gates * (dgates - jnp.sum(gates * dgates, axis=-1, keepdims=True))
        high, low = split(dlogits)
        dlogits_ref[0, chunk * rows : (chunk + 1) * rows] = high
        dlogits_ref[1, chunk * rows : (chunk + 1) * rows] = low
        total = (
            acc_ds[slot]
            + dot(high, router_ref[0].astype(jnp.bfloat16))
            + dot(high, router_ref[1].astype(jnp.bfloat16))
            + dot(low, router_ref[0].astype(jnp.bfloat16))
        )
        if chunk == 0:
            dsecond_ref[...] = total
        else:
            ds_send[chunk - 1] = total.astype(jnp.bfloat16)
            ds_copy(chunk).start()
        out = acc_out[slot]
        if chunk == 0:
            out += mid_ref[...]
        if chunk in (3, 0):
            out_copy(1 if chunk == 3 else 2).wait()
        out_send[chunk % 2] = out.astype(jnp.bfloat16).reshape(out_send.shape[1:])
        out_copy(chunk).start()
        if chunk == 1:
            acc_out[slot] = jnp.zeros(acc_out.shape[1:], jnp.float32)
            acc_ds[slot] = jnp.zeros(acc_ds.shape[1:], jnp.float32)

    def ds_copy(chunk):
        return pltpu.make_async_remote_copy(
            src_ref=ds_send.at[chunk - 1],
            dst_ref=ds_recv.at[chunk - 1],
            send_sem=ds_sems.at[0, chunk - 1],
            recv_sem=ds_sems.at[1, chunk - 1],
            device_id=ctx_ids[chunk - 1],
            device_id_type=MESH,
        )

    acc_out[...] = jnp.zeros_like(acc_out)
    acc_ds[...] = jnp.zeros_like(acc_ds)

    def place_of(step):
        own_chunk = (step < 3) | (step == n_ctx * n_exp - 1)
        chunk = jnp.where(
            own_chunk, 0, jnp.where(step < 9, 1 + (step - 3) // 3, jnp.where(step < 11, step - 8, 3))
        )
        rank = jnp.where(
            step < 3,
            step,
            jnp.where(
                step < 9,
                lax.rem(step - 3, 3),
                jnp.where(own_chunk | (step < 11), n_exp - 1, step - 11),
            ),
        )
        index = jnp.where(
            rank == 0, expert, jnp.where(rank == 1, near, jnp.where(rank == 2, middle, last))
        )
        return chunk, jnp.where(own_chunk, 0, jnp.where(chunk == 2, 2, 1)), index

    def hidden_products(step, image):
        chunk, _, index = place_of(step)
        owner = ctx_partner(ctx, chunk)
        return (
            dot(r_all[owner, image], w_all[0, index]),
            dot(d_all[owner, image].reshape(seq, width), w_all[1, index]),
        )

    def hidden(step, image, pre, dact):
        chunk, _, index = place_of(step)
        part = pl.ds(image * seq, seq)
        gate = jnp.sum(jnp.where(lane == index, gates_ref[chunk, part], 0.0), axis=-1, keepdims=True)
        cdf, density = gelu_parts(pre)
        act = pre * cdf
        dgate = jnp.sum(dact * act, axis=-1, keepdims=True)
        dgates_ref[chunk, part] = jnp.where(lane == index, dgate, dgates_ref[chunk, part])
        kept = pl.ds(pl.multiple_of(chunk * rows + image * seq, seq), seq)
        act_all[index, kept] = (gate * act).astype(jnp.bfloat16)
        dpre_all[index, kept] = (gate * dact * (cdf + pre * density)).astype(jnp.bfloat16)

    def back_out(step, image):
        chunk, slot, index = place_of(step)
        part = pl.ds(image * seq, seq)
        kept = pl.ds(pl.multiple_of(chunk * rows + image * seq, seq), seq)
        acc_out[slot, part] += dot_nt(act_all[index, kept], w_all[1, index])
        acc_ds[slot, part] += dot_nt(dpre_all[index, kept], w_all[0, index])

    for at in range(n_ctx - 1):
        d_copy(at, 0).wait_recv()
    start_chunk(0, ctx)
    for image in range(own_images):
        hidden(0, image, *hidden_products(0, image))

    def one_step(step, carry):
        @pl.when(step == 1)
        def _():
            take_shared(0)
            for order in (3, 1):
                for at in range(2):
                    d_copy(at, order).wait_recv()
            for order in range(1, n_ctx):
                d_relay(0, order).start()
            for order in (1, 2):
                d_relay(1, order).start()

        @pl.when(step == 2)
        def _():
            take_hops(1)
            start_hops(2)
            take_shared(1)

        @pl.when(step == 3)
        def _():
            for image in range(2):
                r_copy(0, image).wait_recv()
                d_relay(image, 1).wait_recv()
            r_relay(0).start()
            start_chunk(1, ctx_ids[0][1])

        @pl.when(step == 4)
        def _():
            for image in range(2):
                r_copy(1, image).wait_recv()
            r_relay(1).start()
            for at in range(2):
                d_copy(at, 2).wait_recv()
            d_relay(1, 3).start()

        @pl.when(step == 9)
        def _():
            take_hops(2)
            take_shared(2)

        @pl.when(step == 6)
        def _():
            for image in range(2):
                d_relay(image, 2).wait_recv()
            start_chunk(2, ctx_ids[1][1])

        @pl.when(step == 11)
        def _():
            for image in range(2):
                d_relay(image, 3).wait_recv()
                r_relay(image).wait_recv()
            start_chunk(3, ctx_ids[2][1])

        for image in range(own_images):
            products = hidden_products(step, image)
            back_out(step - 1, image)
            hidden(step, image, *products)

        for chunk, after in ((1, 10), (2, 11), (3, 15)):
            pl.when(step == after)(functools.partial(end_chunk, chunk))

        return carry

    lax.fori_loop(1, n_ctx * n_exp, one_step, 0)
    for image in range(own_images):
        back_out(n_ctx * n_exp - 1, image)
    end_chunk(0)
    for chunk in range(n_ctx):
        owner = ctx_partner(ctx, chunk)
        r_turn[:, chunk * rows : (chunk + 1) * rows] = r_all[owner].reshape(rows, width).T
        d_turn[:, chunk * rows : (chunk + 1) * rows] = d_all[owner].reshape(rows, width).T

    d_kept = pltpu.make_async_copy(d_all.at[ctx], o_d, o_sems.at[7])
    d_kept.start()

    def grad_at(which, index):
        return act_all.at[index, pl.ds(pl.multiple_of(which * width, width), width)]

    def t_copy(index):
        return pltpu.make_async_remote_copy(
            src_ref=grad_at(1 - dp, index),
            dst_ref=grads_recv.at[index],
            send_sem=t_sems.at[0, index],
            recv_sem=t_sems.at[1, index],
            device_id=twin,
            device_id_type=MESH,
        )

    def one_expert(index, carry):
        grad_out = dot(d_turn[...], act_all[index]).astype(jnp.bfloat16)
        grad_at(0, index)[...] = dot(r_turn[...], dpre_all[index]).astype(jnp.bfloat16)
        grad_at(1, index)[...] = grad_out
        t_copy(index).start()
        return carry

    lax.fori_loop(0, n_exp, one_expert, 0)
    grouter = dot(r_turn[...], dlogits_ref[0]) + dot(r_turn[...], dlogits_ref[1])
    grouter_ref[...] = grouter.T[: grouter_ref.shape[0]]
    for index in range(n_exp):
        t_copy(index).wait()
        grad_at(dp, index)[...] = (
            grad_at(dp, index)[...].astype(jnp.float32) + grads_recv[index].astype(jnp.float32)
        ).astype(jnp.bfloat16)
    last_copies = [pltpu.make_async_copy(grouter_ref, o_grouter, o_sems.at[13])] + [
        pltpu.make_async_copy(grad_at(dp, index), o_grads.at[index], o_sems.at[15 + index])
        for index in range(n_exp)
    ]
    for copy in last_copies:
        copy.start()
    for phase in range(n_exp - 1):
        for side in range(2):
            able, copy = hop(phase, side)
            pl.when(able)(copy.wait_send)
            able, _, shared = landed(phase, side)
            pl.when(able)(shared.wait_send)
    for at in range(n_ctx - 1):
        for order in range(n_ctx if at < 2 else 1):
            d_copy(at, order).wait_send()
    for image in range(2):
        r_relay(image).wait_send()
        for at in range(2):
            r_copy(at, image).wait_send()
        for order in range(1, n_ctx):
            d_relay(image, order).wait_send()
    for chunk in range(1, n_ctx):
        ds_copy(chunk).wait()
        dsecond_ref[...] += ds_recv[chunk - 1].astype(jnp.float32)
    last_copies.append(pltpu.make_async_copy(dsecond_ref, o_dsecond, o_sems.at[14]))
    last_copies[-1].start()
    for copy in kept_copies + [d_kept] + last_copies:
        copy.wait()
    out_copy(3).wait()
    out_copy(0).wait()


def gram_blocks(matrix, packed_ref):
    size = matrix.shape[0]
    index = 0
    for row in range(size // LANES):
        strip = dot_nt(matrix[row * LANES : (row + 1) * LANES], matrix[row * LANES :])
        for col in range(size // LANES - row):
            packed_ref[index] = strip[:, col * LANES : (col + 1) * LANES].reshape(
                packed_ref.shape[1:]
            )
            index += 1


def gram_whole(packed_ref, high_ref, low_ref):
    count = high_ref.shape[0] // LANES
    diagonal = lax.broadcasted_iota(jnp.int32, (LANES, LANES), 0) == lax.broadcasted_iota(
        jnp.int32, (LANES, LANES), 1
    )
    places_of = {}
    square = jnp.zeros((1, 1), jnp.float32)
    index = 0
    for row in range(count):
        for col in range(row, count):
            places_of[index] = (row, col)
            if row == col:
                block = packed_ref[index].reshape(LANES, LANES)
                square += jnp.sum(jnp.where(diagonal, block, 0.0), keepdims=True)
            index += 1
    scale = 1.0 / (jnp.sqrt(square) + EPS_ORTHO)
    for index, (row, col) in places_of.items():
        block = packed_ref[index].reshape(LANES, LANES) * (scale * scale)
        rows, cols = pl.ds(row * LANES, LANES), pl.ds(col * LANES, LANES)
        high_ref[rows, cols], low_ref[rows, cols] = split(block)
        if row != col:
            high_ref[cols, rows], low_ref[cols, rows] = split(block.T)
    return scale


def orthogonal(high_ref, low_ref, mix_ref, total_ref):
    size = high_ref.shape[0]
    eye = lax.broadcasted_iota(jnp.int32, (size, size), 0) == lax.broadcasted_iota(
        jnp.int32, (size, size), 1
    )
    for turn in range(NS_ITERS):
        high, low = high_ref[...], low_ref[...]
        square = dot(high, high)
        if turn == NS_ITERS - 1:
            square += dot(high, low) + dot(low, high)
        mix_ref[...] = (
            jnp.where(eye, NS_A, 0.0)
            + NS_B * (high.astype(jnp.float32) + low.astype(jnp.float32))
            + NS_C * square
        ).astype(jnp.bfloat16)
        mix = mix_ref[...]
        if turn == 0:
            total_ref[...] = mix.astype(jnp.float32)
        else:
            total_high, total_low = split(total_ref[...])
            total_ref[...] = dot(mix, total_high) + dot(mix, total_low)
        if turn < NS_ITERS - 1:
            turned_high, turned_low = split(dot(mix, high) + dot(mix, low))
            high_ref[...], low_ref[...] = split(dot(turned_high, mix) + dot(turned_low, mix))


def backward_kernel(
    n_exp,
    h_x,
    h_d,
    h_first,
    h_qkv,
    h_lse,
    h_att,
    h_mid,
    h_dsecond,
    h_grads,
    grouter_ref,
    norm_ref,
    h_wqkv,
    h_wproj,
    h_out,
    h_min,
    h_mout,
    h_mqkv,
    h_mproj,
    mnorm_ref,
    mrouter_ref,
    out_ref,
    dx_ref,
    gexp_ref,
    step_ref,
    whole_ref,
    sums_ref,
    squares_ref,
    x_ref,
    d_ref,
    first_ref,
    qkv_ref,
    lse_ref,
    att_ref,
    mid_ref,
    dsecond_ref,
    own_grads,
    passed_ref,
    wqkv_ref,
    wproj_ref,
    out_own,
    mexp_ref,
    mqkv_ref,
    mproj_ref,
    out_recv,
    z_recv,
    dmid_ref,
    dbranch_ref,
    datt_ref,
    dqkv_ref,
    dx_send,
    shared_ref,
    half_recv,
    sum_one,
    ctx_recv,
    piece_send,
    piece_recv,
    mat_ref,
    packed_ref,
    packed_recv,
    gathered_ref,
    high_ref,
    low_ref,
    mix_ref,
    total_ref,
    small_ref,
    small_twin,
    small_ctx,
    small_z,
    in_sems,
    out_sems,
    z_sems,
    f_sems,
    dx_sems,
    h_sems,
    c_sems,
    s_sems,
    p_sems,
    w_sems,
    g_sems,
    a_sems,
    x_sems,
    n_sems,
):
    expert, ctx, dp = places()
    own_images, n_ctx, seq_dev, width = dx_send.shape
    seq = n_ctx * seq_dev
    half = width // 2
    cols = width // n_ctx
    loads = {}

    def load(name, source, target):
        loads[name] = pltpu.make_async_copy(source, target, in_sems.at[len(loads)])
        return loads[name]

    def take(*names):
        for name in names:
            loads[name].wait()

    for name, source, target in (
        ("mid", h_mid, mid_ref),
        ("dsecond", h_dsecond, dsecond_ref),
        ("d", h_d, d_ref),
        ("wproj", h_wproj, wproj_ref),
        ("qkv", h_qkv, qkv_ref),
        ("lse", h_lse, lse_ref),
        ("att", h_att, att_ref),
        ("first", h_first, first_ref),
        ("wqkv", h_wqkv, wqkv_ref),
        ("x", h_x, x_ref),
        ("grads", h_grads.at[expert], own_grads),
        ("passed", h_grads.at[jnp.where(expert < n_exp // 2, n_exp - 1, 0)], passed_ref),
        ("out", h_out.at[:, :, ctx], out_own),
        ("mqkv", h_mqkv, mqkv_ref),
        ("mproj", h_mproj, mproj_ref),
    ):
        load(name, source, target).start()
    moment = [
        pltpu.make_async_copy(source.at[0], mexp_ref, in_sems.at[len(loads)])
        for source in (h_min, h_mout)
    ]
    pl.when(dp == 0)(moment[0].start)
    pl.when(dp == 1)(moment[1].start)
    ctx_ids = [(expert, ctx_partner(ctx, step), dp) for step in range(1, n_ctx)]
    z_steps = [1, n_exp - 1] + list(range(2, n_exp - 1))
    z_ids = [(z_partner(expert, step, n_exp), ctx, dp) for step in z_steps]
    twin = (expert, ctx, 1 - dp)
    greeted = ctx_ids + z_ids + [twin]
    greet(greeted)

    def to_each(partners, source, target, sems):
        return [
            send(source(at, partner), target(at, partner), sems.at[0, at], sems.at[1, at], partner)
            for at, partner in enumerate(partners)
        ]

    await_greetings(greeted)
    low_side = expert < n_exp // 2
    near_end = jnp.where(low_side, 0, n_exp - 1)
    far_end = n_exp - 1 - near_end
    near_mid = jnp.where(low_side, 1, n_exp - 2)
    far_mid = n_exp - 1 - near_mid
    at_end = expert == near_end

    def z_copy(target, source, slot, order):
        return pltpu.make_async_remote_copy(
            src_ref=source,
            dst_ref=z_recv.at[slot],
            send_sem=z_sems.at[0, order],
            recv_sem=z_sems.at[1, slot],
            device_id=(target, ctx, dp),
            device_id_type=MESH,
        )

    def end_copies():
        return [
            z_copy(near_mid, h_grads.at[far_end], 3, 0),
            z_copy(far_mid, h_grads.at[far_mid], 1, 1),
            z_copy(near_mid, h_grads.at[near_mid], 0, 2),
        ]

    def mid_copies():
        return [
            z_copy(far_mid, h_grads.at[far_mid], 2, 0),
            z_copy(near_end, h_grads.at[near_end], 0, 1),
            z_copy(far_end, passed_ref, 1, 2),
        ]

    @pl.when(at_end)
    def _():
        end_copies()[0].start()

    @pl.when(jnp.logical_not(at_end))
    def _():
        for copy in mid_copies()[:2]:
            copy.start()

    def send_out(step):
        first_image = ctx_partner(ctx, step) * own_images
        return to_each(
            ctx_ids,
            lambda at, partner: h_out.at[step, :, partner[1]],
            lambda at, partner: out_recv.at[ctx, pl.ds(first_image, own_images)],
            out_sems.at[step],
        )

    out_copies = []
    for step in range(1, n_ctx):
        out_copies += send_out(step)
    gain_one, gain_two = norm_ref[0:1], norm_ref[2:3]
    sums = [jnp.zeros((1, width), jnp.float32) for _ in range(4)]
    take("mid", "dsecond", "d", "wproj")
    for image in range(own_images):
        rows = pl.ds(image * seq, seq)
        unit, scale = normalize(mid_ref[rows])
        grad = dsecond_ref[rows]
        sums[2] += jnp.sum(grad * unit, axis=0, keepdims=True)
        sums[3] += jnp.sum(grad, axis=0, keepdims=True)
        dmid = normalize_back(grad * gain_two, unit, scale) + d_ref[rows].astype(jnp.float32)
        dmid_ref[rows] = dmid
        dbranch = dmid.astype(jnp.bfloat16)
        dbranch_ref[rows] = dbranch
        datt_ref[rows] = dot_nt(dbranch, wproj_ref[...]).astype(jnp.bfloat16)
    take("att")
    gproj = dot_tn(att_ref[...], dbranch_ref[...]).astype(jnp.bfloat16)
    for place in range(n_ctx):
        shared_ref[place, :, 3 * cols :] = gproj[:, place * cols : (place + 1) * cols]
    own_half = pl.ds(pl.multiple_of(dp * half, half), half)
    other_half = pl.ds(pl.multiple_of((1 - dp) * half, half), half)

    def to_twin(which, lanes):
        return send(
            shared_ref.at[:, other_half, lanes],
            half_recv.at[:, :, lanes],
            h_sems.at[0, which],
            h_sems.at[1, which],
            twin,
        )

    def to_owners(which, lanes):
        for place in range(n_ctx):
            sum_one[place, :, lanes] = (
                shared_ref[place, own_half, lanes].astype(jnp.float32)
                + half_recv[place, :, lanes].astype(jnp.float32)
            ).astype(jnp.bfloat16)
        return to_each(
            ctx_ids,
            lambda at, partner: sum_one.at[partner[1], :, lanes],
            lambda at, partner: ctx_recv.at[at, :, lanes],
            c_sems.at[which],
        )

    qkv_lanes, proj_lanes = pl.ds(0, 3 * cols), pl.ds(3 * cols, cols)
    h_copy = to_twin(0, proj_lanes)
    take("qkv", "lse")
    lane = lax.broadcasted_iota(jnp.int32, (seq, LANES), 1)
    low_half = lane < HEAD_DIM
    factor = HEAD_DIM**-0.5
    for image in range(own_images):
        rows = pl.ds(image * seq, seq)
        totals = lse_ref[rows].T
        bias = lse_ref[rows, HEADS : HEADS + 1]
        for pair in range(HEADS // 2):
            at = pair * LANES
            query = qkv_ref[rows, at : at + LANES] * jnp.bfloat16(factor)
            keys = qkv_ref[rows, width + at : width + at + LANES]
            heads = qkv_ref[rows, 2 * width + at : 2 * width + at + LANES]
            datt = datt_ref[rows, at : at + LANES]
            dquery, dkeys, dheads = [], [], []
            for part in range(2):
                chosen = low_half if part == 0 else ~low_half
                scores = dot_nt(keys, jnp.where(chosen, query, jnp.zeros_like(query))) + bias
                head = 2 * pair + part
                weights = jnp.exp(scores - totals[head : head + 1])
                dprobs = dot_nt(heads, jnp.where(chosen, datt, jnp.zeros_like(datt)))
                delta = jnp.sum(weights * dprobs, axis=0, keepdims=True)
                dscores = (weights * (dprobs - delta)).astype(jnp.bfloat16)
                dquery.append(dot_tn(dscores, keys))
                dkeys.append(dot(dscores, query))
                dheads.append(dot(weights.astype(jnp.bfloat16), datt))
            dqkv_ref[rows, at : at + LANES] = (
                jnp.where(low_half, dquery[0], dquery[1]) * factor
            ).astype(jnp.bfloat16)
            dqkv_ref[rows, width + at : width + at + LANES] = jnp.where(
                low_half, dkeys[0], dkeys[1]
            ).astype(jnp.bfloat16)
            dqkv_ref[rows, 2 * width + at : 2 * width + at + LANES] = jnp.where(
                low_half, dheads[0], dheads[1]
            ).astype(jnp.bfloat16)
        if image == 0:
            h_copy.wait()
            c_copies = to_owners(0, proj_lanes)
            take("passed")

            @pl.when(jnp.logical_not(at_end))
            def _():
                copies = mid_copies()
                copies[0].wait_send()
                z_copy(near_mid, passed_ref, 3, 0).wait_recv()
                passed_ref[...] = (
                    passed_ref[...].astype(jnp.float32) + z_recv[3].astype(jnp.float32)
                ).astype(jnp.bfloat16)
                copies[2].start()

            @pl.when(at_end)
            def _():
                copies = end_copies()
                copies[0].wait_send()
                copies[1].start()
                copies[2].start()

    take("first")
    gqkv = dot_tn(first_ref[...], dqkv_ref[...]).astype(jnp.bfloat16)
    for place in range(n_ctx):
        shared_ref[place, :, : 3 * cols] = gqkv[:, 3 * cols * place : 3 * cols * (place + 1)]
    h_copy = to_twin(1, qkv_lanes)
    take("wqkv", "x")
    for image in range(own_images):
        rows = pl.ds(image * seq, seq)
        grad = dot_nt(dqkv_ref[rows], wqkv_ref[...])
        unit, scale = normalize(x_ref[rows].astype(jnp.float32))
        sums[0] += jnp.sum(grad * unit, axis=0, keepdims=True)
        sums[1] += jnp.sum(grad, axis=0, keepdims=True)
        dx = dmid_ref[rows] + normalize_back(grad * gain_one, unit, scale)
        dx_send[image] = dx.astype(jnp.bfloat16).reshape(n_ctx, seq_dev, width)
        if image == 0:
            h_copy.wait()
            c_copies += to_owners(1, qkv_lanes)
    for at, total in enumerate(sums):
        small_ref[at : at + 1] = total
    small_ref[4:8] = jnp.zeros((4, width), jnp.float32)
    small_ref[8:16] = grouter_ref[...]
    s_copy = send(small_ref, small_twin, h_sems.at[0, 2], h_sems.at[1, 2], twin)
    s_copy.wait()
    small_ctx[ctx] = small_ref[...] + small_twin[...]
    s_copies = to_each(
        ctx_ids, lambda at, partner: small_ctx.at[ctx], lambda at, partner: small_ctx.at[ctx], s_sems
    )
    for copy in c_copies:
        copy.wait()
    total = sum_one[ctx].astype(jnp.float32)
    for at in range(n_ctx - 1):
        total += ctx_recv[at].astype(jnp.float32)
    piece_send[...] = total.astype(jnp.bfloat16).reshape(piece_send.shape)
    p_copies = to_each(
        z_ids,
        lambda at, partner: piece_send.at[partner[0]],
        lambda at, partner: piece_recv.at[at],
        p_sems,
    )
    out_copies += send_out(0)
    dx_copies = to_each(
        ctx_ids,
        lambda at, partner: dx_send.at[:, partner[1]],
        lambda at, partner: dx_ref.at[pl.ds(ctx * own_images, own_images)],
        dx_sems,
    )
    for image in range(own_images):
        dx_ref[ctx * own_images + image] = dx_send[image, ctx]
    for copy in s_copies:
        copy.wait()
    total = small_ctx[0]
    for place in range(1, n_ctx):
        total += small_ctx[place]
    small_z[expert] = total
    s_copies = to_each(
        z_ids,
        lambda at, partner: small_z.at[expert],
        lambda at, partner: small_z.at[expert],
        n_sems.at[0],
    )

    def gram_start(which, matrix):
        gram_blocks(matrix.astype(jnp.bfloat16), packed_ref.at[which])
        return to_each(
            ctx_ids,
            lambda at, partner: packed_ref.at[which, :, partner[1]],
            lambda at, partner: packed_recv.at[which, at],
            g_sems.at[which],
        )

    def gram_middle(which, copies):
        for copy in copies:
            copy.wait()
        total = packed_ref[which, :, ctx]
        for at in range(n_ctx - 1):
            total += packed_recv[which, at]
        gathered_ref[which, :, ctx] = total
        return to_each(
            ctx_ids,
            lambda at, partner: gathered_ref.at[which, :, ctx],
            lambda at, partner: gathered_ref.at[which, :, ctx],
            a_sems.at[which],
        )

    def step_of(which, matrix, scale):
        total_high, total_low = split(total_ref[...])
        high, low = split(matrix * scale)
        cut = pl.ds(0, matrix.shape[1])
        step_ref[which, dp, :, cut] = (
            dot(total_high, high) + dot(total_high, low) + dot(total_low, high)
        ).astype(jnp.bfloat16)
        return send(
            step_ref.at[which, dp, :, cut],
            step_ref.at[which, dp, :, cut],
            x_sems.at[0, which],
            x_sems.at[1, which],
            twin,
        )

    take("grads")

    @pl.when(at_end)
    def _():
        copies = end_copies()
        copies[1].wait_send()
        copies[2].wait_send()
        copies[1].wait_recv()
        copies[2].wait_recv()
        total = own_grads[...].astype(jnp.float32)
        for slot in range(2):
            total += z_recv[slot].astype(jnp.float32)
        gexp_ref[dp] = total.astype(jnp.bfloat16)

    @pl.when(jnp.logical_not(at_end))
    def _():
        copies = mid_copies()
        copies[1].wait_send()
        copies[2].wait_send()
        for copy in copies:
            copy.wait_recv()
        total = own_grads[...].astype(jnp.float32)
        for slot in range(3):
            total += z_recv[slot].astype(jnp.float32)
        gexp_ref[dp] = total.astype(jnp.bfloat16)

    f_copy = send(gexp_ref.at[dp], gexp_ref.at[dp], f_sems.at[0], f_sems.at[1], twin)
    moment[0].wait()
    mat_ref[0] = DECAY * mexp_ref[...] + gexp_ref[dp].astype(jnp.float32)
    exp_copies = gram_start(0, mat_ref[0])
    for copy in p_copies:
        copy.wait()
    total = piece_send[expert].astype(jnp.float32)
    for at in range(n_exp - 1):
        total += piece_recv[at].astype(jnp.float32)
    whole_ref[dp, expert] = total.astype(jnp.bfloat16)
    p_copies = to_each(
        z_ids,
        lambda at, partner: whole_ref.at[dp, expert],
        lambda at, partner: whole_ref.at[dp, expert],
        w_sems,
    )
    for copy in p_copies:
        copy.wait()
    w_copy = send(whole_ref.at[dp], whole_ref.at[dp], f_sems.at[2], f_sems.at[3], twin)
    exp_copies = gram_middle(0, exp_copies)
    for copy in s_copies:
        copy.wait()
    total = small_z[0]
    for place in range(1, n_exp):
        total += small_z[place]
    sums_ref[...] = total
    lane_part = pl.ds(pl.multiple_of(ctx * cols, cols), cols)
    fresh_norm = DECAY * mnorm_ref[...] + sums_ref[0:4, lane_part]
    fresh_router = DECAY * mrouter_ref[...] + sums_ref[pl.ds(8 + ctx, 1)]
    row = lax.broadcasted_iota(jnp.int32, (8, LANES), 0)
    squares_ref[ctx] = jnp.where(
        row == 0,
        jnp.sum(fresh_norm * fresh_norm, keepdims=True),
        jnp.sum(fresh_router * fresh_router, keepdims=True),
    )
    n_copies = to_each(
        ctx_ids,
        lambda at, partner: squares_ref.at[ctx],
        lambda at, partner: squares_ref.at[ctx],
        n_sems.at[1],
    )
    w_copy.wait()
    take("mqkv", "mproj")
    grad = whole_ref[...].reshape(width, width).astype(jnp.float32)
    mat_ref[1, :, : 3 * cols] = DECAY * mqkv_ref[...] + grad[:, : 3 * cols]
    mat_ref[2, :, :cols] = DECAY * mproj_ref[...] + grad[:, 3 * cols :]
    mat_ref[2, :, cols : 3 * cols] = jnp.zeros((width, 2 * cols), jnp.float32)
    shared_copies = [gram_start(1, mat_ref[1 + dp, :, : 3 * cols])]
    for copy in exp_copies:
        copy.wait()
    exp_scale = gram_whole(gathered_ref.at[0], high_ref, low_ref)
    orthogonal(high_ref, low_ref, mix_ref, total_ref)
    exp_step = step_of(0, mat_ref[0], exp_scale)
    shared_copies[0] = gram_middle(1, shared_copies[0])
    for copy in shared_copies[0]:
        copy.wait()
    shared_scale = gram_whole(gathered_ref.at[1], high_ref, low_ref)
    orthogonal(high_ref, low_ref, mix_ref, total_ref)
    shared_step = step_of(1, mat_ref[1 + dp, :, : 3 * cols], shared_scale)
    take("out")
    for copy in out_copies:
        copy.wait()
    for step in range(n_ctx):
        start = ctx_partner(ctx, step) * own_images
        for image in range(own_images):
            total = out_own[step, image].astype(jnp.float32)
            for at in range(n_ctx - 1):
                total += out_recv[ctx_partner(ctx, at + 1), start + image].astype(jnp.float32)
            out_ref[start + image] = total.astype(jnp.bfloat16)
    for copy in dx_copies + n_copies + [f_copy, exp_step, shared_step]:
        copy.wait()


def finish_kernel(
    experts,
    n_ctx,
    width,
    ctx_ref,
    gexp_ref,
    step_ref,
    whole_ref,
    sums_ref,
    squares_ref,
    dx_in,
    out_in,
    min_ref,
    mout_ref,
    mqkv_ref,
    mproj_ref,
    mnorm_ref,
    mrouter_ref,
    win_ref,
    wout_ref,
    wqkv_ref,
    wproj_ref,
    norm_ref,
    router_ref,
    o_out,
    o_dx,
    o_gnorm,
    o_grouter,
    o_gqkv,
    o_gproj,
    o_gin,
    o_gout,
    o_mnorm,
    o_mrouter,
    o_mqkv,
    o_mproj,
    o_min,
    o_mout,
    o_nnorm,
    o_nrouter,
    o_nqkv,
    o_nproj,
    o_nin,
    o_nout,
    o_bqkv,
    o_bproj,
    o_bin,
    o_bout,
):
    cols = width // n_ctx
    o_out[...] = out_in[...]
    o_dx[...] = dx_in[...].astype(jnp.float32)

    def update(grad, moment, weight, step, columns, outs):
        o_g, o_m, o_n, o_b = outs
        rate = RATE_MAT * 0.2 * math.sqrt(max(width, columns))
        new = weight.astype(jnp.float32) - rate * step.astype(jnp.float32)
        o_g[...] = grad.reshape(o_g.shape)
        o_m[...] = (DECAY * moment + grad).reshape(o_m.shape)
        o_n[...] = new.reshape(o_n.shape)
        o_b[...] = new.astype(jnp.bfloat16).reshape(o_b.shape)

    for index, outs in enumerate(((o_gin, o_min, o_nin, o_bin), (o_gout, o_mout, o_nout, o_bout))):
        update(
            gexp_ref[index].astype(jnp.float32),
            (min_ref, mout_ref)[index][0],
            (win_ref, wout_ref)[index][0],
            step_ref[0, index],
            n_ctx * gexp_ref.shape[2],
            outs,
        )
    grad = whole_ref[...].astype(jnp.float32)
    update(
        grad[:, : 3 * cols],
        mqkv_ref[...],
        wqkv_ref[...],
        step_ref[1, 0, :, : 3 * cols],
        3 * width,
        (o_gqkv, o_mqkv, o_nqkv, o_bqkv),
    )
    update(
        grad[:, 3 * cols :],
        mproj_ref[...],
        wproj_ref[...],
        step_ref[1, 1, :, :cols],
        width,
        (o_gproj, o_mproj, o_nproj, o_bproj),
    )
    ctx = ctx_ref[0]
    own_norm = sums_ref[0:4, pl.ds(pl.multiple_of(ctx * cols, cols), cols)]
    own_router = sums_ref[pl.ds(8 + ctx, 1)]
    fresh_norm = DECAY * mnorm_ref[...] + own_norm
    fresh_router = DECAY * mrouter_ref[...] + own_router
    o_gnorm[...] = own_norm
    o_grouter[...] = own_router
    o_mnorm[...] = fresh_norm
    o_mrouter[...] = fresh_router
    squares = squares_ref[0]
    for place in range(1, n_ctx):
        squares += squares_ref[place]
    o_nnorm[...] = norm_ref[...] - (
        RATE_GAIN * fresh_norm * lax.rsqrt(squares[0:1] / (4 * width) + EPS_NORM)
    )
    o_nrouter[...] = router_ref[pl.ds(ctx, 1)] - RATE_ROUTER * fresh_router * lax.rsqrt(
        squares[1:2, 0:1] / (width * experts) + EPS_NORM
    )


def call(kernel, ident, outs, scratch, operands, spaces, out_spaces=None):
    out_spaces = out_spaces or [pltpu.VMEM] * len(outs)
    return pl.pallas_call(
        kernel,
        out_shape=[jax.ShapeDtypeStruct(shape, dtype) for shape, dtype in outs],
        in_specs=[pl.BlockSpec(memory_space=space) for space in spaces],
        out_specs=[pl.BlockSpec(memory_space=space) for space in out_spaces],
        scratch_shapes=scratch,
        compiler_params=pltpu.CompilerParams(
            collective_id=ident, has_side_effects=True, vmem_limit_bytes=VMEM_LIMIT
        ),
    )(*operands)


def gathered(
    x_in,
    d_out,
    key_mask,
    expert_ids,
    norm_params,
    w_qkv,
    w_proj,
    w_router,
    w_in,
    w_out,
    mom_norm,
    mom_router,
    mom_qkv,
    mom_proj,
    mom_in,
    mom_out,
):
    n_exp = lax.axis_size("expert")
    n_ctx = lax.axis_size("ctx")
    ctx = lax.axis_index("ctx")
    images, seq_dev, width = x_in.shape
    experts = w_router.shape[1]
    own_images = images // n_ctx
    seq = n_ctx * seq_dev
    rows = own_images * seq
    hid = w_in.shape[2]
    low, full = jnp.bfloat16, jnp.float32
    dma = lambda *shape: pltpu.SemaphoreType.DMA(shape)
    vmem = lambda shape, dtype: pltpu.VMEM(shape, dtype)

    vm, anywhere = pltpu.VMEM, pl.ANY
    block = (own_images, n_ctx, seq_dev, width)
    kept = [
        (block, low),
        ((rows, width), low),
        ((rows, 3 * width), low),
        ((rows, LANES), full),
        ((rows, width), low),
        ((rows, width), full),
        (block, low),
        ((n_ctx,) + block, low),
        ((rows, width), full),
        ((n_exp, width, hid), low),
        ((8, width), full),
    ]
    router_turned = w_router.T
    (x_all, first, qkv, lse, att, mid, d_own, out_parts, dsecond, grads, grouter) = call(
        functools.partial(forward_kernel, n_exp, experts),
        1,
        kept,
        [vmem(*kept[at]) for at in range(6)]
        + [vmem((2,) + block, low), vmem((rows, width), full)]
        + [
            vmem((n_exp, width, hid), low),
            vmem((8, width), full),
            vmem((n_ctx,) + block, low),
            vmem((2, n_exp, width, hid), low),
            vmem((n_ctx, own_images, seq, width), low),
            vmem((images, 8, LANES), full),
            vmem((n_ctx, images, 8, LANES), full),
            vmem((width, 3 * width), low),
            vmem((width, width), low),
            vmem((2, LANES, width), full),
            vmem((n_ctx - 1, rows, width), low),
            vmem((n_ctx - 1, rows, width), low),
            vmem((3, rows, width), full),
            vmem((3, rows, width), full),
            vmem((2, n_ctx * rows, LANES), low),
            vmem((n_ctx, rows, LANES), full),
            vmem((n_ctx, rows, LANES), full),
            vmem((width, n_ctx * rows), low),
            vmem((width, n_ctx * rows), low),
            vmem((n_exp, n_ctx * rows, hid), low),
            vmem((n_exp, n_ctx * rows, hid), low),
            dma(2, own_images, n_ctx - 1),
            dma(2, n_ctx - 1),
            dma(2, n_ctx - 1, n_ctx),
            dma(2, 2, 2),
            dma(2, n_ctx - 1),
            dma(2, 2, n_ctx),
            dma(2, 2),
            dma(2, n_exp - 1, 2),
            dma(2, n_exp - 1, 2),
            dma(2, n_exp),
            dma(6),
            dma(15 + n_exp),
        ],
        (
            x_in,
            d_out.reshape(n_ctx, own_images, seq_dev, width),
            expert_ids.swapaxes(1, 2),
            key_mask,
            w_in,
            w_out,
            norm_params,
            w_qkv,
            w_proj,
            router_turned,
        ),
        [anywhere, anywhere, vm, vm, anywhere, anywhere, vm, anywhere, anywhere, vm],
        [anywhere] * 11,
    )
    cols = width // n_ctx
    blocks = (width // LANES) * (width // LANES + 1) // 2
    block_rows = LANES // n_ctx
    quarter = (n_exp, width // 2 // n_exp, width)
    moments = (mom_in, mom_out, mom_qkv, mom_proj, mom_norm, mom_router.reshape(1, width))
    out_low, dx_low, gexp, steps, whole, sums, squares = call(
        functools.partial(backward_kernel, n_exp),
        2,
        [
            ((images, seq_dev, width), low),
            ((images, seq_dev, width), low),
            ((2, width, hid), low),
            ((2, 2, width, hid), low),
            ((2,) + quarter, low),
            ((16, width), full),
            ((n_ctx, 8, LANES), full),
        ],
        [
            vmem((rows, width), low),
            vmem((rows, width), low),
            vmem((rows, width), low),
            vmem((rows, 3 * width), low),
            vmem((rows, LANES), full),
            vmem((rows, width), low),
            vmem((rows, width), full),
            vmem((rows, width), full),
            vmem((width, hid), low),
            vmem((width, hid), low),
            vmem((width, 3 * width), low),
            vmem((width, width), low),
            vmem((n_ctx, own_images, seq_dev, width), low),
            vmem((width, hid), full),
            vmem((width, 3 * cols), full),
            vmem((width, cols), full),
            vmem((n_ctx, images, seq_dev, width), low),
            vmem((n_exp, width, hid), low),
            vmem((rows, width), full),
            vmem((rows, width), low),
            vmem((rows, width), low),
            vmem((rows, 3 * width), low),
            vmem(block, low),
            vmem((n_ctx, width, width), low),
            vmem((n_ctx, width // 2, width), low),
            vmem((n_ctx, width // 2, width), low),
            vmem((n_ctx - 1, width // 2, width), low),
            vmem(quarter, low),
            vmem((n_exp - 1,) + quarter[1:], low),
            vmem((3, width, hid), full),
            vmem((2, blocks, n_ctx, block_rows, LANES), full),
            vmem((2, n_ctx - 1, blocks, block_rows, LANES), full),
            vmem((2, blocks, n_ctx, block_rows, LANES), full),
            vmem((width, width), low),
            vmem((width, width), low),
            vmem((width, width), low),
            vmem((width, width), full),
            vmem((16, width), full),
            vmem((16, width), full),
            vmem((n_ctx, 16, width), full),
            vmem((n_exp, 16, width), full),
            dma(17),
            dma(n_ctx, 2, n_ctx - 1),
            dma(2, n_exp),
            dma(4),
            dma(2, n_ctx - 1),
            dma(2, 3),
            dma(2, 2, n_ctx - 1),
            dma(2, n_ctx - 1),
            dma(2, n_exp - 1),
            dma(2, n_exp - 1),
            dma(2, 2, n_ctx - 1),
            dma(2, 2, n_ctx - 1),
            dma(2, 2),
            dma(2, 2, max(n_ctx, n_exp) - 1),
        ],
        (
            x_all.reshape(rows, width),
            d_own.reshape(rows, width),
            first,
            qkv,
            lse,
            att,
            mid,
            dsecond,
            grads,
            grouter,
            norm_params,
            w_qkv,
            w_proj,
            out_parts,
        )
        + moments,
        [anywhere] * 9 + [vm, vm] + [anywhere] * 7 + [vm, vm],
    )
    pieces = ((4, cols), (1, width), (width, 3 * cols), (width, cols), (1, width, hid), (1, width, hid))
    parts = width // LANES
    outs = (
        [((images, seq_dev, width), low), ((images, seq_dev, width), full)]
        + [(piece, full) for piece in pieces * 3]
        + [(piece, low) for piece in pieces[2:]]
    )

    def strip(shape, axis, last=None):
        def index_map(at, ctx_ref):
            place = [0] * len(shape)
            if axis is not None:
                place[axis] = at
            if last is not None:
                place[-1] = ctx_ref[0]
            return tuple(place)

        size = list(shape)
        if axis is not None:
            size[axis] //= parts
        if last is not None:
            size[-1] = last
        return pl.BlockSpec(tuple(size), index_map)

    def strips(shape):
        if len(shape) == 3:
            return strip(shape, 0 if shape[0] == images else 1)
        return strip(shape, 0 if shape[0] == width else None)

    results = pl.pallas_call(
        functools.partial(finish_kernel, experts, n_ctx, width),
        out_shape=[jax.ShapeDtypeStruct(shape, dtype) for shape, dtype in outs],
        grid_spec=pltpu.PrefetchScalarGridSpec(
            num_scalar_prefetch=1,
            grid=(parts,),
            in_specs=[
                strip((2, width, hid), 1),
                strip((2, 2, width, hid), 2),
                strip((width, width), 0),
                strip((16, width), None),
                strip((n_ctx, 8, LANES), None),
                strip((images, seq_dev, width), 0),
                strip((images, seq_dev, width), 0),
                strip((1, width, hid), 1),
                strip((1, width, hid), 1),
                strip((width, 3 * cols), 0),
                strip((width, cols), 0),
                strip((4, cols), None),
                strip((1, width), None),
                strip((1, width, hid), 1),
                strip((1, width, hid), 1),
                strip((width, 3 * width), 0, 3 * cols),
                strip((width, width), 0, cols),
                strip((4, width), None, cols),
                strip((experts, width), None),
            ],
            out_specs=[strips(shape) for shape, _ in outs],
        ),
        compiler_params=pltpu.CompilerParams(vmem_limit_bytes=VMEM_LIMIT),
    )(
        ctx.reshape(1),
        gexp,
        steps,
        whole.reshape(width, width),
        sums,
        squares,
        dx_low,
        out_low,
        *moments,
        w_in,
        w_out,
        w_qkv,
        w_proj,
        norm_params,
        router_turned,
    )
    return tuple(
        value.reshape(width, 1) if value.shape == (1, width) else value for value in results
    )


def solution(mesh):
    in_specs = (
        P(("expert", "dp"), "ctx", None),
        P(("expert", "dp"), "ctx", None),
        P(("expert", "dp"), "ctx"),
        P(("expert", "dp"), "ctx", None),
        P(),
        P(),
        P(),
        P(),
        P("expert", None, "ctx"),
        P("expert", None, "ctx"),
        P(None, "ctx"),
        P(None, "ctx"),
        P(None, "ctx"),
        P(None, "ctx"),
        P("expert", None, "ctx"),
        P("expert", None, "ctx"),
    )
    out_specs = (
        P(("expert", "dp"), "ctx", None),
        P(("expert", "dp"), "ctx", None),
        P(None, "ctx"),
        P(None, "ctx"),
        P(None, "ctx"),
        P(None, "ctx"),
        P("expert", None, "ctx"),
        P("expert", None, "ctx"),
        P(None, "ctx"),
        P(None, "ctx"),
        P(None, "ctx"),
        P(None, "ctx"),
        P("expert", None, "ctx"),
        P("expert", None, "ctx"),
        P(None, "ctx"),
        P(None, "ctx"),
        P(None, "ctx"),
        P(None, "ctx"),
        P("expert", None, "ctx"),
        P("expert", None, "ctx"),
        P(None, "ctx"),
        P(None, "ctx"),
        P("expert", None, "ctx"),
        P("expert", None, "ctx"),
    )
    experts = mesh.shape["expert"]
    square = mesh.shape["ctx"] == 4 and mesh.shape["dp"] == 2

    def local(*arrays):
        whole = (
            square
            and arrays[7].shape[1] == experts <= 7
            and arrays[8].shape[0] == 1
            and 2 * arrays[0].shape[1] == LANES
        )
        return (gathered if whole else exchanged)(*arrays)

    return jax.shard_map(local, mesh=mesh, in_specs=in_specs, out_specs=out_specs, check_vma=False)
```
